32 devices in a mesh: dp: 8 (over z, x), chan: 4 (over y, core).
Axes of the slice: x: 2, y: 2, z: 4, core: 2. Of those that a mesh axis runs over, the one named last changes fastest.
Arguments:
- input_a: bfloat16 [256, 25088], P('dp'), may hold values from -24 to 24, as said below
- input_b: bfloat16 [256, 9216], P('dp'), may hold values from -24 to 24, as said below
- boxes_a: int32 [128, 4], P('dp'), may hold values from 0 to 7, as said below
- boxes_b: int32 [256, 4], P('dp'), may hold values from 0 to 3, as said below
- weight_first: bfloat16 [9, 256, 512], P(None, None, 'chan'), may hold values from -0.125 to 0.125
- weight_second: bfloat16 [9, 512, 512], P(None, None, 'chan'), may hold values from -0.09375 to 0.09375
- weight_short: bfloat16 [256, 512], P(None, 'chan'), may hold values from -0.375 to 0.375
- gain_first: float32 [512], P('chan'), may hold values from 0.5 to 1.5
- shift_first: float32 [512], P('chan'), may hold values from -0.5 to 0.5
- gain_second: float32 [512], P('chan'), may hold values from 0.5 to 1.5
- shift_second: float32 [512], P('chan'), may hold values from -0.5 to 0.5
- gain_short: float32 [512], P('chan'), may hold values from 0.5 to 1.5
- shift_short: float32 [512], P('chan'), may hold values from -0.5 to 0.5
- upstream_a: bfloat16 [512, 6272], P('chan', 'dp'), may hold values from -6 to 6
- upstream_b: bfloat16 [512, 2304], P('chan', 'dp'), may hold values from -6 to 6
Outputs:
- out_a: bfloat16 [512, 6272], P('chan', 'dp')
- out_b: bfloat16 [512, 2304], P('chan', 'dp')
- grad_input_a: bfloat16 [256, 8, 4, 784], P('dp', None, 'chan')
- grad_input_b: bfloat16 [256, 8, 4, 288], P('dp', None, 'chan')
- grad_first: float32 [9, 256, 512], P(None, 'dp', 'chan')
- grad_second: float32 [9, 512, 512], P(None, 'dp', 'chan')
- grad_short: float32 [256, 512], P('dp', 'chan')
- grad_gain_first: float32 [512], P('chan')
- grad_shift_first: float32 [512], P('chan')
- grad_gain_second: float32 [512], P('chan')
- grad_shift_second: float32 [512], P('chan')
- grad_gain_short: float32 [512], P('chan')
- grad_shift_short: float32 [512], P('chan')
The draws below stay inside these ranges and needn't reach their ends.
Inputs may be any that keep to these rules, and one draw needn't show every extreme that they name: `input_a`: entries of order one. `input_b`: entries of order one. `boxes_a`: each row is (first row, first column, height, width) of a box inside the output grid of side 14/2, height and width at least 1. `boxes_b`: each row is (first row, first column, height, width) of a box inside the output grid of side 6/2, height and width at least 1.
All inputs are finite; a program needn't handle non-finite values.
Results may differ from the reference program's by a relative error of at most 0.017.
Values may be sent and summed in bfloat16 or wider, within the bound.
A program may use at most 320 MiB of HBM per device.

```python
import jax
import jax.numpy as jnp
from jax import lax

IN_WIDTH = 256
WIDTH = 512
SA = 14
SB = 6
QA = 4
QB = 8
IMG_A = 128
IMG_B = 256
N_DP = 8
N_CHAN = 4


def scaled_images(noise_field, scale_key, image_count, extent):
    positions = jnp.arange(image_count * extent * extent, dtype=jnp.int32) // (extent * extent)
    image_ramp = 1.0 + 2.0 * positions.astype(jnp.float32) / image_count
    channel_scale = jax.random.uniform(scale_key, (IN_WIDTH, 1), minval=0.5, maxval=2.0)
    return noise_field * image_ramp[None, :] * channel_scale


def box_draw(key, image_count, extent):
    subkeys = jax.random.split(key, 4)
    upper_edge = jax.random.randint(subkeys[0], (image_count,), 0, extent)
    left_edge = jax.random.randint(subkeys[1], (image_count,), 0, extent)
    box_height = jax.random.randint(subkeys[2], (image_count,), 1, extent - upper_edge + 1)
    box_width = jax.random.randint(subkeys[3], (image_count,), 1, extent - left_edge + 1)
    leading = jnp.arange(image_count, dtype=jnp.int32) == 0
    upper_edge = jnp.where(leading, 0, upper_edge)
    left_edge = jnp.where(leading, 0, left_edge)
    box_height = jnp.where(leading, extent, box_height)
    box_width = jnp.where(leading, extent, box_width)
    return jnp.stack([upper_edge, left_edge, box_height, box_width], axis=1).astype(jnp.int32)


def draw_input_a(key, part):
    key = jax.random.fold_in(key, 5)
    extent_shape = (IN_WIDTH, IMG_A * SA * SA)
    noise_field = jnp.clip(jax.random.normal(key, extent_shape), -4.0, 4.0)
    return scaled_images(noise_field, jax.random.fold_in(key, 17), IMG_A, SA).astype(jnp.bfloat16)


def draw_input_b(key, part):
    key = jax.random.fold_in(key, 6)
    extent_shape = (IN_WIDTH, IMG_B * SB * SB)
    noise_field = jnp.clip(jax.random.normal(key, extent_shape), -4.0, 4.0)
    return scaled_images(noise_field, jax.random.fold_in(key, 19), IMG_B, SB).astype(jnp.bfloat16)


def draw_boxes_a(key, part):
    key = jax.random.fold_in(key, 7)
    return box_draw(key, IMG_A, SA // 2)


def draw_boxes_b(key, part):
    key = jax.random.fold_in(key, 8)
    return box_draw(key, IMG_B, SB // 2)


def levels(rng, shape, cuts, least, high):
    level, own = 1.0, jax.random.fold_in(rng, 6)
    for dim, parts in cuts:
        draws = jnp.exp(jax.random.uniform(jax.random.fold_in(own, dim), (parts,), jnp.float32, least / len(cuts), high / len(cuts)))
        level = level * jnp.repeat(draws, shape[dim] // parts).reshape([-1 if axis == dim else 1 for axis in range(len(shape))])
    return level


def gaussian(key, shape, scale, limit, pieces=(), kind=jnp.bfloat16):
    array = scale * jax.random.normal(key, shape, jnp.float32)
    if pieces:
        array = array * levels(key, shape, pieces, -0.22, 0.18)
    return jnp.clip(array, -limit, limit).astype(kind)


def setup_inputs(seed: int = 0) -> dict:
    streams_of = jax.random.split(jax.random.key(seed), 16)
    input_a = draw_input_a(jax.random.fold_in(streams_of[15], 71), 0)
    input_b = draw_input_b(jax.random.fold_in(streams_of[15], 71), 0)
    boxes_a = draw_boxes_a(jax.random.fold_in(streams_of[15], 71), 0)
    boxes_b = draw_boxes_b(jax.random.fold_in(streams_of[15], 71), 0)
    weight_first = gaussian(streams_of[4], (9, IN_WIDTH, WIDTH), (9 * IN_WIDTH) ** -0.5, 0.125, ((2, 4),))
    weight_second = gaussian(streams_of[5], (9, WIDTH, WIDTH), (9 * WIDTH) ** -0.5, 0.09375, ((2, 4),))
    weight_short = gaussian(streams_of[6], (IN_WIDTH, WIDTH), IN_WIDTH ** -0.5, 0.375, ((1, 4),))
    gain_first = jnp.clip(0.5 + 1.0 * jax.random.uniform(streams_of[7], (WIDTH,), jnp.float32) ** levels(streams_of[7], (WIDTH,), ((0, 4),), -0.2, 0.2), 0.5, 1.5)
    shift_first = jnp.clip(jax.random.uniform(streams_of[8], (WIDTH,), jnp.float32, -0.5, 0.5) * levels(streams_of[8], (WIDTH,), ((0, 4),), -0.4, 0.0), -0.5, 0.5)
    gain_second = jnp.clip(0.5 + 1.0 * jax.random.uniform(streams_of[9], (WIDTH,), jnp.float32) ** levels(streams_of[9], (WIDTH,), ((0, 4),), -0.2, 0.2), 0.5, 1.5)
    shift_second = jnp.clip(jax.random.uniform(streams_of[10], (WIDTH,), jnp.float32, -0.5, 0.5) * levels(streams_of[10], (WIDTH,), ((0, 4),), -0.4, 0.0), -0.5, 0.5)
    gain_short = jnp.clip(0.5 + 1.0 * jax.random.uniform(streams_of[11], (WIDTH,), jnp.float32) ** levels(streams_of[11], (WIDTH,), ((0, 4),), -0.2, 0.2), 0.5, 1.5)
    shift_short = jnp.clip(jax.random.uniform(streams_of[12], (WIDTH,), jnp.float32, -0.5, 0.5) * levels(streams_of[12], (WIDTH,), ((0, 4),), -0.4, 0.0), -0.5, 0.5)
    upstream_a = gaussian(streams_of[13], (WIDTH, IMG_A * (SA // 2) ** 2), 1.0, 6.0, ((0, 4), (1, 8)))
    upstream_b = gaussian(streams_of[14], (WIDTH, IMG_B * (SB // 2) ** 2), 1.0, 6.0, ((0, 4), (1, 8)))
    return {"input_a": input_a, "input_b": input_b, "boxes_a": boxes_a, "boxes_b": boxes_b, "weight_first": weight_first, "weight_second": weight_second, "weight_short": weight_short, "gain_first": gain_first, "shift_first": shift_first, "gain_second": gain_second, "shift_second": shift_second, "gain_short": gain_short, "shift_short": shift_short, "upstream_a": upstream_a, "upstream_b": upstream_b}


epsilon = 1e-05

@jax.custom_vjp
def low(v):
    return lax.optimization_barrier(v.astype(jnp.bfloat16)).astype(jnp.float32)

@jax.custom_vjp
def low_back(v):
    return v

def low_keep(v):
    return (low(v), None)

def low_pass(kept, grad):
    return (grad,)

def back_keep(v):
    return (v, None)

def back_low(kept, grad):
    return (low(grad),)
low.defvjp(low_keep, low_pass)
low_back.defvjp(back_keep, back_low)

def box_mask(box_rows, extent):
    positions = jnp.arange(extent, dtype=jnp.int32)[None, :]
    row_inside = (positions >= box_rows[:, 0:1]) & (positions < box_rows[:, 0:1] + box_rows[:, 2:3])
    col_inside = (positions >= box_rows[:, 1:2]) & (positions < box_rows[:, 1:2] + box_rows[:, 3:4])
    return (row_inside[:, :, None] & col_inside[:, None, :]).astype(jnp.float32)

def convolve(images, kernel, stride, padding):
    return lax.conv_general_dilated(images, kernel, (stride, stride), ((padding, padding), (padding, padding)), dimension_numbers=('NCHW', 'HWIO', 'NCHW'), precision=lax.Precision.HIGHEST)

def channel_view(vector):
    return vector[None, :, None, None]

def normalize(fields, valid_list, population, gain_values, shift_values):
    running = sum((lax.optimization_barrier(jnp.sum(feature * valid, axis=(0, 2, 3))) for feature, valid in zip(fields, valid_list)))
    squares = sum((lax.optimization_barrier(jnp.sum(feature * feature * valid, axis=(0, 2, 3))) for feature, valid in zip(fields, valid_list)))
    mean_value = running / population
    variance = squares / population - mean_value * mean_value
    scaling = lax.rsqrt(variance + epsilon)
    return [(feature - channel_view(mean_value)) * channel_view(scaling) * channel_view(gain_values) + channel_view(shift_values) for feature in fields]

def layer(parameters, inputs, valid_list):
    weight_first, weight_second, weight_short, gain_first, shift_first, gain_second, shift_second, gain_short, shift_short = parameters
    kernel_first = weight_first.reshape(3, 3, IN_WIDTH, WIDTH)
    kernel_second = weight_second.reshape(3, 3, WIDTH, WIDTH)
    kernel_short = weight_short.reshape(1, 1, IN_WIDTH, WIDTH)
    first_out = [low_back(low(convolve(images, kernel_first, 2, 1))) for images in inputs]
    short_out = [low_back(low(convolve(images, kernel_short, 2, 0))) for images in inputs]
    population = sum((jnp.sum(valid) for valid in valid_list))
    first_norm = normalize(first_out, valid_list, population, gain_first, shift_first)
    hidden = [low(jax.nn.silu(normed) * valid) for normed, valid in zip(first_norm, valid_list)]
    second_out = [low_back(low(convolve(feature, kernel_second, 1, 1))) for feature in hidden]
    second_norm = normalize(second_out, valid_list, population, gain_second, shift_second)
    short_norm = normalize(short_out, valid_list, population, gain_short, shift_short)
    return tuple((jax.nn.silu(main_part + side_part) * valid for main_part, side_part, valid in zip(second_norm, short_norm, valid_list)))

def to_images(flat, channels, count, extent):
    return flat.astype(jnp.float32).reshape(channels, count, extent, extent).transpose(1, 0, 2, 3)

def reference(input_a, input_b, boxes_a, boxes_b, weight_first, weight_second, weight_short, gain_first, shift_first, gain_second, shift_second, gain_short, shift_short, upstream_a, upstream_b):
    out_side_a = SA // 2
    out_side_b = SB // 2
    valid_list = (box_mask(boxes_a, out_side_a)[:, None], box_mask(boxes_b, out_side_b)[:, None])
    images = (to_images(input_a, IN_WIDTH, IMG_A, SA), to_images(input_b, IN_WIDTH, IMG_B, SB))
    parameters = (weight_first.astype(jnp.float32), weight_second.astype(jnp.float32), weight_short.astype(jnp.float32), gain_first, shift_first, gain_second, shift_second, gain_short, shift_short)

    def wrapped(parameters, images):
        return layer(parameters, images, valid_list)
    outputs, pullback = jax.vjp(wrapped, parameters, images)
    cotangents = (to_images(upstream_a, WIDTH, IMG_A, out_side_a), to_images(upstream_b, WIDTH, IMG_B, out_side_b))
    param_grads, image_grads = pullback(cotangents)
    out_a = outputs[0].transpose(1, 0, 2, 3).reshape(WIDTH, IMG_A * out_side_a * out_side_a).astype(jnp.bfloat16)
    out_b = outputs[1].transpose(1, 0, 2, 3).reshape(WIDTH, IMG_B * out_side_b * out_side_b).astype(jnp.bfloat16)
    grad_input_a = image_grads[0].transpose(1, 0, 2, 3).reshape(IN_WIDTH, N_DP, N_CHAN, QA * SA * SA).astype(jnp.bfloat16)
    grad_input_b = image_grads[1].transpose(1, 0, 2, 3).reshape(IN_WIDTH, N_DP, N_CHAN, QB * SB * SB).astype(jnp.bfloat16)
    return (out_a, out_b, grad_input_a, grad_input_b, param_grads[0], param_grads[1], param_grads[2], param_grads[3], param_grads[4], param_grads[5], param_grads[6], param_grads[7], param_grads[8])
```

```python
import jax
import jax.numpy as jnp
from jax import lax
import numpy as np
from jax.experimental import pallas as pl
from jax.experimental.pallas import tpu as pltpu
from jax.sharding import PartitionSpec as P

SA = 14
SB = 6


epsilon = 1e-05


def box_mask(box_rows, extent):
    positions = jnp.arange(extent, dtype=jnp.int32)[None, :]
    row_inside = (positions >= box_rows[:, 0:1]) & (positions < box_rows[:, 0:1] + box_rows[:, 2:3])
    col_inside = (positions >= box_rows[:, 1:2]) & (positions < box_rows[:, 1:2] + box_rows[:, 3:4])
    return (row_inside[:, :, None] & col_inside[:, None, :]).astype(jnp.float32)


def taps_strided(feature, image_count, extent):
    channels = feature.shape[0]
    output_side = extent // 2
    padded = jnp.pad(
        feature.reshape(channels, image_count, extent, extent), ((0, 0), (0, 0), (1, 1), (1, 1))
    )
    pieces = [
        padded[:, :, tap_row : tap_row + extent : 2, tap_col : tap_col + extent : 2]
        for tap_row in range(3)
        for tap_col in range(3)
    ]
    return jnp.stack(pieces, axis=0).reshape(9 * channels, image_count * output_side * output_side)


def taps_plain(feature, image_count, extent):
    channels = feature.shape[0]
    padded = jnp.pad(
        feature.reshape(channels, image_count, extent, extent), ((0, 0), (0, 0), (1, 1), (1, 1))
    )
    pieces = [
        padded[:, :, tap_row : tap_row + extent, tap_col : tap_col + extent]
        for tap_row in range(3)
        for tap_col in range(3)
    ]
    return jnp.stack(pieces, axis=0).reshape(9 * channels, image_count * extent * extent)


def untaps_plain(columns, channels, image_count, extent):
    pieces = columns.reshape(9, channels, image_count, extent, extent)
    running = jnp.zeros((channels, image_count, extent + 2, extent + 2), jnp.float32)
    for tap_row in range(3):
        for tap_col in range(3):
            running = running + jnp.pad(
                pieces[3 * tap_row + tap_col],
                ((0, 0), (0, 0), (tap_row, 2 - tap_row), (tap_col, 2 - tap_col)),
            )
    return running[:, :, 1:-1, 1:-1].reshape(channels, image_count * extent * extent)


def untaps_strided(columns, shortcut, channels, image_count, extent):
    output_side = extent // 2
    pieces = columns.reshape(9, channels, image_count, output_side, output_side)
    parity_sums = {}
    for tap_row in range(3):
        for tap_col in range(3):
            block_row = tap_row // 2
            block_col = tap_col // 2
            placed = jnp.pad(
                pieces[3 * tap_row + tap_col],
                ((0, 0), (0, 0), (block_row, 1 - block_row), (block_col, 1 - block_col)),
            )
            parity = (tap_row % 2, tap_col % 2)
            parity_sums[parity] = (
                placed if parity not in parity_sums else parity_sums[parity] + placed
            )
    direct = jnp.pad(
        shortcut.reshape(channels, image_count, output_side, output_side),
        ((0, 0), (0, 0), (0, 1), (0, 1)),
    )
    parity_sums[1, 1] = parity_sums[1, 1] + direct
    rows_even = jnp.stack([parity_sums[0, 0], parity_sums[0, 1]], axis=-1)
    rows_odd = jnp.stack([parity_sums[1, 0], parity_sums[1, 1]], axis=-1)
    padded = jnp.stack([rows_even, rows_odd], axis=3).reshape(
        channels, image_count, extent + 2, extent + 2
    )
    return padded[:, :, 1:-1, 1:-1].reshape(channels, image_count * extent * extent)


def contract_first(weights, columns):
    return lax.dot_general(
        weights, columns, (((0,), (0,)), ((), ())), preferred_element_type=jnp.float32
    )


def weight_product(columns, gradient):
    return lax.dot_general(
        columns, gradient, (((1,), (1,)), ((), ())), preferred_element_type=jnp.float32
    )


def swish_slope(values):
    logistic = jax.nn.sigmoid(values)
    return logistic * (1.0 + values * (1.0 - logistic))


def moments(values, valid_list):
    running = 0.0
    squares = 0.0
    for tensor, valid in zip(values, valid_list):
        widened = tensor.astype(jnp.float32)
        running = running + jnp.sum(widened * valid, axis=1)
        squares = squares + jnp.sum(widened * widened * valid, axis=1)
    return (running, squares)


def standardize(values, running, squares, population):
    mean_value = running / population
    variance = squares / population - mean_value * mean_value
    scaling = lax.rsqrt(variance + epsilon)
    return (
        [
            (tensor.astype(jnp.float32) - mean_value[:, None]) * scaling[:, None]
            for tensor in values
        ],
        scaling,
    )


def norm_back(gradient, normed, valid, scaling, gain_values, shift_sum, gain_sum, population):
    return (gain_values * scaling)[:, None] * (
        gradient - valid * (shift_sum[:, None] + normed * gain_sum[:, None]) / population
    )


def plain_body(
    input_a,
    input_b,
    boxes_a,
    boxes_b,
    weight_first,
    weight_second,
    weight_short,
    gain_first,
    shift_first,
    gain_second,
    shift_second,
    gain_short,
    shift_short,
    upstream_a,
    upstream_b,
):
    image_groups = lax.axis_size("dp")
    in_local = input_a.shape[0]
    chan_in = weight_first.shape[1]
    chan_part = weight_first.shape[2]
    chan_full = weight_second.shape[1]
    image_counts = (boxes_a.shape[0], boxes_b.shape[0])
    extents = (SA, SB)
    whole_a, whole_b = (
        lax.all_to_all(
            input_a.reshape(in_local, image_groups, -1),
            "dp",
            split_axis=1,
            concat_axis=0,
            tiled=True,
        ),
        lax.all_to_all(
            input_b.reshape(in_local, image_groups, -1),
            "dp",
            split_axis=1,
            concat_axis=0,
            tiled=True,
        ),
    )
    features = (whole_a.reshape(chan_in, -1), whole_b.reshape(chan_in, -1))
    valid_list = (
        box_mask(boxes_a, SA // 2).reshape(1, -1),
        box_mask(boxes_b, SB // 2).reshape(1, -1),
    )
    first_mat = weight_first.reshape(9 * chan_in, chan_part)
    second_mat = weight_second.reshape(9 * chan_full, chan_part)
    first_cols = []
    sampled = []
    first_z = []
    short_z = []
    for feature, image_count, extent in zip(features, image_counts, extents):
        columns = taps_strided(feature, image_count, extent)
        picked = feature.reshape(chan_in, image_count, extent, extent)[:, :, ::2, ::2].reshape(
            chan_in, -1
        )
        first_cols.append(columns)
        sampled.append(picked)
        first_z.append(contract_first(first_mat, columns).astype(jnp.bfloat16))
        short_z.append(contract_first(weight_short, picked).astype(jnp.bfloat16))
    sum_first, square_first = moments(first_z, valid_list)
    sum_short, square_short = moments(short_z, valid_list)
    population = jnp.sum(valid_list[0]) + jnp.sum(valid_list[1])
    sum_first, square_first, sum_short, square_short, population = lax.psum(
        (sum_first, square_first, sum_short, square_short, population), "dp"
    )
    normed_first, scaling_first = standardize(first_z, sum_first, square_first, population)
    normed_short, scaling_short = standardize(short_z, sum_short, square_short, population)
    before_first = [normed * gain_first[:, None] + shift_first[:, None] for normed in normed_first]
    outgoing_a = (jax.nn.silu(before_first[0]) * valid_list[0]).astype(jnp.bfloat16)
    outgoing_b = (jax.nn.silu(before_first[1]) * valid_list[1]).astype(jnp.bfloat16)
    gathered_a, gathered_b = (
        lax.all_gather(outgoing_a, "chan", axis=0, tiled=True),
        lax.all_gather(outgoing_b, "chan", axis=0, tiled=True),
    )
    second_cols = []
    second_z = []
    for gathered, image_count, extent in zip((gathered_a, gathered_b), image_counts, extents):
        columns = taps_plain(gathered, image_count, extent // 2)
        second_cols.append(columns)
        second_z.append(contract_first(second_mat, columns).astype(jnp.bfloat16))
    sum_second, square_second = moments(second_z, valid_list)
    sum_second, square_second = lax.psum((sum_second, square_second), "dp")
    normed_second, scaling_second = standardize(second_z, sum_second, square_second, population)
    summed_pre = [
        main_part * gain_second[:, None]
        + shift_second[:, None]
        + side_part * gain_short[:, None]
        + shift_short[:, None]
        for main_part, side_part in zip(normed_second, normed_short)
    ]
    outputs = [
        (jax.nn.silu(tensor) * valid).astype(jnp.bfloat16)
        for tensor, valid in zip(summed_pre, valid_list)
    ]
    tail_grads = [
        upstream.astype(jnp.float32) * valid * swish_slope(tensor)
        for upstream, valid, tensor in zip((upstream_a, upstream_b), valid_list, summed_pre)
    ]
    shift_tail = sum((jnp.sum(gradient, axis=1) for gradient in tail_grads))
    gain_tail = sum(
        (jnp.sum(gradient * normed, axis=1) for gradient, normed in zip(tail_grads, normed_second))
    )
    gain_side = sum(
        (jnp.sum(gradient * normed, axis=1) for gradient, normed in zip(tail_grads, normed_short))
    )
    shift_tail, gain_tail, gain_side = lax.psum((shift_tail, gain_tail, gain_side), "dp")
    grad_second_local = 0.0
    partial_hidden = []
    short_dz = []
    for index_group in range(2):
        valid = valid_list[index_group]
        dz_second = norm_back(
            tail_grads[index_group],
            normed_second[index_group],
            valid,
            scaling_second,
            gain_second,
            shift_tail,
            gain_tail,
            population,
        ).astype(jnp.bfloat16)
        dz_short = norm_back(
            tail_grads[index_group],
            normed_short[index_group],
            valid,
            scaling_short,
            gain_short,
            shift_tail,
            gain_side,
            population,
        ).astype(jnp.bfloat16)
        short_dz.append(dz_short)
        grad_second_local = grad_second_local + weight_product(second_cols[index_group], dz_second)
        back_cols = jnp.dot(second_mat, dz_second, preferred_element_type=jnp.float32)
        partial_hidden.append(
            untaps_plain(back_cols, chan_full, image_counts[index_group], extents[index_group] // 2)
        )
    hidden_a, hidden_b = (
        lax.psum_scatter(
            partial_hidden[0].astype(jnp.bfloat16), "chan", scatter_dimension=0, tiled=True
        ).astype(jnp.float32),
        lax.psum_scatter(
            partial_hidden[1].astype(jnp.bfloat16), "chan", scatter_dimension=0, tiled=True
        ).astype(jnp.float32),
    )
    head_grads = [
        hidden * valid * swish_slope(tensor)
        for hidden, valid, tensor in zip((hidden_a, hidden_b), valid_list, before_first)
    ]
    shift_head = sum((jnp.sum(gradient, axis=1) for gradient in head_grads))
    gain_head = sum(
        (jnp.sum(gradient * normed, axis=1) for gradient, normed in zip(head_grads, normed_first))
    )
    shift_head, gain_head = lax.psum((shift_head, gain_head), "dp")
    grad_first_local = 0.0
    grad_short_local = 0.0
    partial_inputs = []
    for index_group in range(2):
        valid = valid_list[index_group]
        dz_first = norm_back(
            head_grads[index_group],
            normed_first[index_group],
            valid,
            scaling_first,
            gain_first,
            shift_head,
            gain_head,
            population,
        ).astype(jnp.bfloat16)
        grad_first_local = grad_first_local + weight_product(first_cols[index_group], dz_first)
        grad_short_local = grad_short_local + weight_product(
            sampled[index_group], short_dz[index_group]
        )
        back_cols = jnp.dot(first_mat, dz_first, preferred_element_type=jnp.float32)
        back_short = jnp.dot(
            weight_short, short_dz[index_group], preferred_element_type=jnp.float32
        )
        flat_input = untaps_strided(
            back_cols, back_short, chan_in, image_counts[index_group], extents[index_group]
        )
        partial_inputs.append(flat_input.reshape(chan_in, 1, lax.axis_size("chan"), -1))
    arrived_a, arrived_b = (
        lax.all_to_all(
            partial_inputs[0].astype(jnp.bfloat16), "dp", split_axis=0, concat_axis=1, tiled=True
        ).astype(jnp.float32),
        lax.all_to_all(
            partial_inputs[1].astype(jnp.bfloat16), "dp", split_axis=0, concat_axis=1, tiled=True
        ).astype(jnp.float32),
    )
    summed_a, summed_b = (
        lax.psum_scatter(
            arrived_a.astype(jnp.bfloat16), "chan", scatter_dimension=2, tiled=True
        ).astype(jnp.float32),
        lax.psum_scatter(
            arrived_b.astype(jnp.bfloat16), "chan", scatter_dimension=2, tiled=True
        ).astype(jnp.float32),
    )
    grad_input_a = summed_a.astype(jnp.bfloat16)
    grad_input_b = summed_b.astype(jnp.bfloat16)
    grad_first_local = grad_first_local.reshape(9, chan_in, chan_part)
    grad_second_local = grad_second_local.reshape(9, chan_full, chan_part)
    total_first, total_second, total_short = lax.psum(
        (grad_first_local, grad_second_local, grad_short_local), "dp"
    )
    position = lax.axis_index("dp")
    rows_first = chan_in // image_groups
    rows_second = chan_full // image_groups
    grad_first = lax.dynamic_slice_in_dim(total_first, position * rows_first, rows_first, 1)
    grad_second = lax.dynamic_slice_in_dim(total_second, position * rows_second, rows_second, 1)
    grad_short = lax.dynamic_slice_in_dim(total_short, position * rows_first, rows_first, 0)
    return (
        outputs[0],
        outputs[1],
        grad_input_a,
        grad_input_b,
        grad_first,
        grad_second,
        grad_short,
        gain_head,
        shift_head,
        gain_tail,
        shift_tail,
        gain_side,
        shift_tail,
    )


MESH = pl.DeviceIdType.MESH
TAPS = tuple((a, b) for a in range(3) for b in range(3))
PLANE_TAPS = (
    ((1, 1),),
    ((1, 0), (1, 2)),
    ((0, 1), (2, 1)),
    ((0, 0), (0, 2), (2, 0), (2, 2)),
)
ORDER = [tap for taps in PLANE_TAPS for tap in taps]
LANES = 128


def quarter_order(images, side, row_offset, lanes):
    half = side // 2
    matrix = np.zeros((half * half * 4 * images, lanes), np.float32)
    for image in range(images):
        for row in range(side):
            for col in range(side):
                plane = 2 * (row % 2) + col % 2
                cell = (row // 2) * half + col // 2
                target = (cell * 4 + plane) * images + image
                matrix[target, row_offset + (image * side + row) * side + col] = 1.0
    return matrix


class Links:
    def __init__(self, send_sems, recv_sems):
        self.send_sems, self.recv_sems = send_sems, recv_sems
        self.sends = self.slots = 0
        self.open = []

    def slot(self, count=1):
        first = self.slots
        self.slots += count
        return first

    def send(self, source, target, slot, where):
        copy = pltpu.make_async_remote_copy(
            source, target, self.send_sems.at[self.sends], self.recv_sems.at[slot],
            device_id=where, device_id_type=MESH,
        )
        self.sends += 1
        copy.start()
        self.open.append(copy)

    def arrived(self, target, slot, where):
        pltpu.make_async_remote_copy(
            target, target, self.send_sems.at[0], self.recv_sems.at[slot],
            device_id=where, device_id_type=MESH,
        ).wait_recv()

    def drain(self):
        for copy in self.open:
            copy.wait_send()


def mm(a, b, ca, cb):
    return lax.dot_general(a, b, (((ca,), (cb,)), ((), ())), preferred_element_type=jnp.float32)


def lanes_cat(parts):
    return jnp.concatenate(parts, axis=1) if len(parts) > 1 else parts[0]


def sigma(v):
    return 0.5 * jnp.tanh(0.5 * v) + 0.5


def make_fused(n_dp, in_local, images, sides, chan_in, chan_part, stop):
    halves = tuple(side // 2 for side in sides)
    sizes = tuple(h * h * n for h, n in zip(halves, images))
    rows = sum(sizes)
    quarter = tuple(n // 4 for n in images)
    qlanes = tuple(q * side * side for q, side in zip(quarter, sides))
    slab_lanes = -(-sum(qlanes) // LANES) * LANES
    b_tile = qlanes[0] // LANES * LANES
    b_skip = qlanes[0] - b_tile
    chan_full = 4 * chan_part
    out_rows = chan_full // n_dp
    starts = (0, sizes[0])
    chunks = [
        (g, r, starts[g] + r * halves[g] * images[g], halves[g] * images[g])
        for g in range(2)
        for r in range(halves[g])
    ]
    win = [-(-(qlanes[g] + LANES - 1) // LANES) * LANES for g in range(2)]
    win = [-(-qlanes[0] // LANES) * LANES, -(-qlanes[1] // LANES) * LANES]

    def kernel(xa, xb, bxa, bxb, w1, w2, ws, g1, b1, g2, b2, gs, bs, ua, ub, pa, pb,
               oa, ob, gr, gw1, gw2, vecs,
               xs, xr, zg, zpa, zpb, valid, z1, zs, a1a, a1b, slots, up, outr, gv, dza, dzb, dzsr,
               dd, hp, hr1, hs, hr2, gu, d1a, d1b, wg2, wr2, wx2, wz2, wg1, wr1, wx1, wz1,
               gp, gr1, gsum, gr2, gt, ssem, rsem):
        i, k = lax.axis_index("dp"), lax.axis_index("chan")
        k1 = k + 1 - 2 * (k % 2)
        k2 = (k + 2) % 4
        k3 = (k1 + 2) % 4
        ix = i % 2
        mate = i + 1 - 2 * ix
        net = Links(ssem, rsem)
        zp, a1, dz, d1 = (zpa, zpb), (a1a, a1b), (dza, dzb), (d1a, d1b)
        f32, bf16 = jnp.float32, jnp.bfloat16

        def flat(value):
            return value.reshape(-1, value.shape[-1])

        barrier = pltpu.get_barrier_semaphore()
        for d in range(1, n_dp):
            pl.semaphore_signal(barrier, inc=1, device_id=((i + d) % n_dp, k), device_id_type=MESH)
        pl.semaphore_signal(barrier, inc=1, device_id=(i, k1), device_id_type=MESH)
        pl.semaphore_signal(barrier, inc=1, device_id=(i, k2), device_id_type=MESH)

        lane = lax.broadcasted_iota(jnp.int32, (in_local, LANES), 1)
        for d in range(n_dp):
            j = (i + d) % n_dp
            begin = 4 * qlanes[0] * j + qlanes[0] * k
            tile = begin // LANES
            part_a = xa[:, pl.ds(pl.multiple_of(tile * LANES, LANES), win[0])].astype(f32)
            part_a = pltpu.roll(part_a, (win[0] - (begin - tile * LANES)) % win[0], 1)
            begin = 4 * qlanes[1] * j + qlanes[1] * k
            tile = begin // LANES
            part_b = xb[:, pl.ds(pl.multiple_of(tile * LANES, LANES), win[1])].astype(f32)
            part_b = jnp.concatenate([part_b, jnp.zeros((in_local, LANES), f32)], axis=1)
            wide = win[1] + LANES
            part_b = pltpu.roll(part_b, (wide + b_skip - (begin - tile * LANES)) % wide, 1)
            seam = jnp.where(lane < b_skip, part_a[:, b_tile : b_tile + LANES], part_b[:, :LANES])
            slab = jnp.concatenate(
                [part_a[:, :b_tile], seam, part_b[:, LANES : slab_lanes - b_tile]], axis=1
            ).astype(bf16)
            if d == 0:
                xr[i] = slab
            else:
                xs[j] = slab
        pl.semaphore_wait(barrier, n_dp + 1)
        base = net.slot(n_dp)
        for d in range(1, n_dp):
            j = (i + d) % n_dp
            net.send(xs.at[j], xr.at[i], base + i, (j, k))

        for buf in (zpa, zpb, a1a, a1b, dza, dzb, d1a, d1b):
            side = buf.shape[1] if len(buf.shape) == 5 else buf.shape[0]
            lead = (slice(None),) if len(buf.shape) == 5 else ()
            for edge in (0, side - 1):
                for index in (lead + (edge,), lead + (slice(None), edge)):
                    region = buf.at[index]
                    region[...] = jnp.zeros(region.shape, buf.dtype)
        population = jnp.zeros((8, LANES), f32)
        for g, box in enumerate((bxa, bxb)):
            n, half = images[g], halves[g]
            diag = lax.broadcasted_iota(jnp.int32, (n, n), 0) == lax.broadcasted_iota(jnp.int32, (n, n), 1)
            cols = [
                jnp.sum(jnp.where(diag, box[q : q + 1, :].astype(f32), 0.0), axis=1, keepdims=True)
                for q in range(4)
            ]
            inside = [
                [((p >= cols[q]) & (p < cols[q] + cols[q + 2])).astype(f32) for p in range(half)]
                for q in range(2)
            ]
            for r in range(half):
                for s in range(half):
                    cell = jnp.broadcast_to(inside[0][r] * inside[1][s], (n, LANES))
                    begin = starts[g] + (r * half + s) * n
                    valid[begin : begin + n, :] = cell
                    population = population + jnp.sum(cell.reshape(n // 8, 8, LANES), axis=0)
        population = jnp.sum(population, axis=0, keepdims=True)
        for g, source in enumerate((ua, ub)):
            n, cells = images[g], halves[g] ** 2
            gu[starts[g] : starts[g] + sizes[g], :] = source[...].astype(f32)
            for cell in range(cells):
                up[starts[g] + cell * n : starts[g] + (cell + 1) * n, :] = gu[
                    pl.ds(starts[g] + cell, n, stride=cells), :
                ]

        for d in range(1, n_dp):
            j = (i + d) % n_dp
            net.arrived(xr.at[j], base + j, (j, k))
        if stop == 0:
            return finish(net, locals())
        xall = jnp.concatenate([xr[q] for q in range(n_dp)], axis=0)
        zg[k, : sizes[0], :] = mm(pa[...], xall[:, : pa.shape[1]], 1, 1).astype(bf16)
        zg[k, sizes[0] :, :] = mm(pb[...], xall[:, b_tile:], 1, 1).astype(bf16)
        slot = net.slot(4)
        net.send(zg.at[k], zg.at[k], slot + k, (i, k2))
        net.send(zg.at[k], zg.at[k], slot + k, (i, k1))
        net.arrived(zg.at[k2], slot + k2, (i, k2))
        net.send(zg.at[k2], zg.at[k2], slot + k2, (i, k1))
        net.arrived(zg.at[k1], slot + k1, (i, k1))
        net.arrived(zg.at[k3], slot + k3, (i, k1))
        if stop == 1:
            return finish(net, locals())

        def planes_of(quarters, g):
            step = quarter[g]
            if step % 8 == 0:
                return [
                    jnp.concatenate([v[:, step * p : step * (p + 1)] for v in quarters], axis=1)
                    for p in range(4)
                ]
            low = lax.broadcasted_iota(jnp.int32, (1, 8, 1), 1) < 4
            halves_ = [[v[:, 8 * h : 8 * h + 8] for v in quarters] for h in range(2)]
            turned = [[pltpu.roll(v, 4, 1) for v in side] for side in halves_]
            result = []
            for p in range(4):
                h, odd = p // 2, p % 2
                v, t = halves_[h], turned[h]
                if odd == 0:
                    parts = [jnp.where(low, v[0], t[1]), jnp.where(low, v[2], t[3])]
                else:
                    parts = [jnp.where(low, t[0], v[1]), jnp.where(low, t[2], v[3])]
                result.append(jnp.concatenate(parts, axis=1))
            return result

        for g, r, begin, count in chunks:
            quarters = [
                zg[q, begin : begin + count, :].astype(f32).reshape(halves[g], images[g], chan_in)
                for q in range(4)
            ]
            for p, value in enumerate(planes_of(quarters, g)):
                zp[g][p, 1 + r, 1 : 1 + halves[g]] = value.astype(bf16)
        if stop == 2:
            return finish(net, locals())

        def strided_patch(g, tap):
            a, b = tap
            p = 2 * (a % 2 == 0) + (b % 2 == 0)
            r, s = 1 - (a == 0), 1 - (b == 0)
            return flat(zp[g][p, r : r + halves[g], s : s + halves[g]])

        for g in range(2):
            span = slice(starts[g], starts[g] + sizes[g])
            both = mm(strided_patch(g, (1, 1)), jnp.concatenate([w1[4], ws[...]], axis=1), 1, 0)
            zs[span, :] = both[:, chan_part:]
            acc = both[:, :chan_part]
            for tap in TAPS:
                if tap != (1, 1):
                    acc = acc + mm(strided_patch(g, tap), w1[3 * tap[0] + tap[1]], 1, 0)
            z1[span, :] = acc

        def rowsum(value):
            return jnp.sum(value.reshape(-1, 8, LANES), axis=0)

        def message(sums):
            parts = [jnp.sum(v, axis=0, keepdims=True) if v.shape[0] > 1 else v for v in sums]
            parts.append(jnp.zeros((8 - len(parts), LANES), f32))
            return jnp.concatenate(parts, axis=0)

        def share(rnd, value):
            slots[rnd, i] = value
            first = net.slot(n_dp)
            for d in range(1, n_dp):
                j = (i + d) % n_dp
                net.send(slots.at[rnd, i], slots.at[rnd, i], first + i, (j, k))
            return first

        def total(rnd, first):
            for d in range(1, n_dp):
                j = (i + d) % n_dp
                net.arrived(slots.at[rnd, j], first + j, (j, k))
            return jnp.sum(slots[rnd], axis=0)

        acc = [jnp.zeros((8, LANES), f32)] * 4
        for g, r, begin, count in chunks:
            span = slice(begin, begin + count)
            ok = valid[span, :]
            u, w = z1[span, :], zs[span, :]
            uv, wv = u * ok, w * ok
            acc = [acc[0] + rowsum(uv), acc[1] + rowsum(uv * u), acc[2] + rowsum(wv), acc[3] + rowsum(wv * w)]
        first = share(0, message(acc + [population]))
        tot = total(0, first)
        if stop == 3:
            return finish(net, locals())
        inv_pop = 1.0 / tot[4:5]
        mean1, means = tot[0:1] * inv_pop, tot[2:3] * inv_pop
        sc1 = lax.rsqrt(tot[1:2] * inv_pop - mean1 * mean1 + epsilon)
        scs = lax.rsqrt(tot[3:4] * inv_pop - means * means + epsilon)
        gain1, shift1 = g1[...], b1[...]
        for g, r, begin, count in chunks:
            span = slice(begin, begin + count)
            hat = (z1[span, :] - mean1) * sc1
            z1[span, :] = hat
            v = hat * gain1 + shift1
            act = (v * sigma(v) * valid[span, :]).astype(bf16)
            a1[g][k, 1 + r, 1 : 1 + halves[g]] = act.reshape(halves[g], images[g], chan_part)

        def inner(g, q):
            return a1[g].at[q, 1 : 1 + halves[g], 1 : 1 + halves[g]]

        slot = net.slot(8)
        for where in (k2, k1):
            for g in range(2):
                net.send(inner(g, k), inner(g, k), slot + 4 * g + k, (i, where))
        for g in range(2):
            span = slice(starts[g], starts[g] + sizes[g])
        for g in range(2):
            net.arrived(inner(g, k2), slot + 4 * g + k2, (i, k2))
            net.send(inner(g, k2), inner(g, k2), slot + 4 * g + k2, (i, k1))
        for g in range(2):
            net.arrived(inner(g, k1), slot + 4 * g + k1, (i, k1))
            net.arrived(inner(g, k3), slot + 4 * g + k3, (i, k1))
        if stop == 4:
            return finish(net, locals())

        def plain_patch(g, tap):
            a, b = tap
            return lanes_cat(
                [flat(a1[g][q, a : a + halves[g], b : b + halves[g]]) for q in range(4)]
            )

        z2 = hp
        for g in range(2):
            acc = None
            for tap in TAPS:
                part = mm(plain_patch(g, tap), w2[3 * tap[0] + tap[1]], 1, 0)
                acc = part if acc is None else acc + part
            gv[starts[g] : starts[g] + sizes[g], :] = acc
        acc = [jnp.zeros((8, LANES), f32)] * 2
        for g, r, begin, count in chunks:
            span = slice(begin, begin + count)
            u = gv[span, :]
            uv = u * valid[span, :]
            acc = [acc[0] + rowsum(uv), acc[1] + rowsum(uv * u)]
        first = share(1, message(acc))
        for g, r, begin, count in chunks:
            span = slice(begin, begin + count)
            zs[span, :] = (zs[span, :] - means) * scs
        tot = total(1, first)
        if stop == 5:
            return finish(net, locals())
        mean2 = tot[0:1] * inv_pop
        sc2 = lax.rsqrt(tot[1:2] * inv_pop - mean2 * mean2 + epsilon)
        gain2, gains = g2[...], gs[...]
        shifts = b2[...] + bs[...]
        acc = [jnp.zeros((8, LANES), f32)] * 3
        for g, r, begin, count in chunks:
            span = slice(begin, begin + count)
            ok = valid[span, :]
            hat2 = (gv[span, :] - mean2) * sc2
            hats = zs[span, :]
            v = hat2 * gain2 + hats * gains + shifts
            sig = sigma(v)
            outr[span, :] = v * sig * ok
            grad = up[span, :] * ok * (sig * (1.0 + v * (1.0 - sig)))
            up[span, :] = grad
            gv[span, :] = hat2
            acc = [acc[0] + rowsum(grad), acc[1] + rowsum(grad * hat2), acc[2] + rowsum(grad * hats)]
        first = share(2, message(acc))
        for g, target in enumerate((oa, ob)):
            n, cells = images[g], halves[g] ** 2
            for cell in range(cells):
                gu[pl.ds(starts[g] + cell, n, stride=cells), :] = outr[
                    starts[g] + cell * n : starts[g] + (cell + 1) * n, :
                ]
            target[...] = gu[starts[g] : starts[g] + sizes[g], :].astype(bf16)
        tot = total(2, first)
        sum_tail, sum_gain2, sum_gains = tot[0:1], tot[1:2], tot[2:3]
        if stop == 6:
            return finish(net, locals())

        k2g, ksg = gain2 * sc2, gains * scs
        db, dg2, dgs = sum_tail * inv_pop, sum_gain2 * inv_pop, sum_gains * inv_pop
        for g, r, begin, count in chunks:
            span = slice(begin, begin + count)
            ok = valid[span, :]
            grad = up[span, :]
            shape = (halves[g], images[g], chan_part)
            value = k2g * (grad - ok * (db + gv[span, :] * dg2))
            dz[g][1 + r, 1 : 1 + halves[g]] = value.astype(bf16).reshape(shape)
            value = ksg * (grad - ok * (db + zs[span, :] * dgs))
            dzsr[span, :] = value.astype(bf16)
        for g in range(2):
            for t, (a, b) in enumerate(TAPS):
                dd[starts[g] : starts[g] + sizes[g], t * LANES : (t + 1) * LANES] = flat(
                    dz[g][2 - a : 2 - a + halves[g], 2 - b : 2 - b + halves[g]]
                )

        def back_second(q):
            weights = lanes_cat(
                [w2[t, pl.ds(pl.multiple_of(q * chan_part, LANES), chan_part), :] for t in range(9)]
            )
            hp[q] = mm(dd[...], weights, 1, 1).astype(bf16)

        slot = net.slot(3)
        back_second(k3)
        net.send(hp.at[k3], hr1.at[1], slot + 1, (i, k1))
        back_second(k2)
        net.arrived(hr1.at[1], slot + 1, (i, k1))
        hs[...] = (hp[k2].astype(f32) + hr1[1].astype(f32)).astype(bf16)
        net.send(hs, hr2, slot + 2, (i, k2))
        back_second(k1)
        net.send(hp.at[k1], hr1.at[0], slot, (i, k1))
        back_second(k)

        n_z = n_dp // 2
        acts = [
            lanes_cat([flat(a1[g][q, 1 : 1 + halves[g], 1 : 1 + halves[g]]) for q in range(4)])
            for g in range(2)
        ]
        grad_w2 = mm(acts[0], dd[: sizes[0], :], 0, 0) + mm(acts[1], dd[sizes[0] :, :], 0, 0)
        wg2[...] = grad_w2.astype(bf16).reshape(n_dp, out_rows, 9 * LANES)

        def halve(part, got, slot):
            for z in range(n_z):
                net.send(part.at[2 * z + 1 - ix], got.at[z], slot + z, (mate, k))

        def spread(part, got, both, last, slot, slot_z):
            for z in range(n_z):
                net.arrived(got.at[z], slot + z, (mate, k))
                both[z] = (part[2 * z + ix].astype(f32) + got[z].astype(f32)).astype(bf16)
            iz = i // 2
            for d in range(1, n_z):
                z = (iz + d) % n_z
                net.send(both.at[z], last.at[iz], slot_z + iz, (2 * z + ix, k))

        def collect(both, last, slot_z):
            iz = i // 2
            value = both[iz].astype(f32)
            for d in range(1, n_z):
                z = (iz + d) % n_z
                net.arrived(last.at[z], slot_z + z, (2 * z + ix, k))
                value = value + last[z].astype(f32)
            return value

        slot_w2 = net.slot(2 * n_z)
        halve(wg2, wr2, slot_w2)
        net.arrived(hr1.at[0], slot, (i, k1))
        net.arrived(hr2, slot + 2, (i, k2))
        if stop == 7:
            spread(wg2, wr2, wx2, wz2, slot_w2, slot_w2 + n_z)
            collect(wx2, wz2, slot_w2 + n_z)
            return finish(net, locals())
        acc = [jnp.zeros((8, LANES), f32)] * 2
        for g, r, begin, count in chunks:
            span = slice(begin, begin + count)
            hat = z1[span, :]
            v = hat * gain1 + shift1
            sig = sigma(v)
            grad = hp[k, span, :].astype(f32) + hr1[0, span, :].astype(f32) + hr2[span, :].astype(f32)
            grad = grad * valid[span, :] * (sig * (1.0 + v * (1.0 - sig)))
            gu[span, :] = grad
            acc = [acc[0] + rowsum(grad), acc[1] + rowsum(grad * hat)]
        first = share(3, message(acc))
        spread(wg2, wr2, wx2, wz2, slot_w2, slot_w2 + n_z)
        tot = total(3, first)
        sum_head, sum_gain1 = tot[0:1], tot[1:2]
        if stop == 8:
            collect(wx2, wz2, slot_w2 + n_z)
            return finish(net, locals())
        k1g = gain1 * sc1
        db, dg1 = sum_head * inv_pop, sum_gain1 * inv_pop
        for g, r, begin, count in chunks:
            span = slice(begin, begin + count)
            value = k1g * (gu[span, :] - valid[span, :] * (db + z1[span, :] * dg1))
            d1[g][r, : halves[g]] = value.astype(bf16).reshape(halves[g], images[g], chan_part)

        def back_patch(g, p):
            parts = [
                flat(d1[g][(a == 0) : (a == 0) + halves[g], (b == 0) : (b == 0) + halves[g]])
                for a, b in PLANE_TAPS[p]
            ]
            if p == 0:
                parts.append(dzsr[starts[g] : starts[g] + sizes[g], :])
            return lanes_cat(parts)

        for g in range(2):
            planes = []
            for p in range(4):
                weights = [w1[3 * a + b] for a, b in PLANE_TAPS[p]]
                if p == 0:
                    weights.append(ws[...])
                value = mm(back_patch(g, p), lanes_cat(weights), 1, 1)
                planes.append(value.reshape(halves[g] ** 2, images[g], chan_in))
            for q, value in enumerate(planes_of(planes, g)):
                gp[q, starts[g] : starts[g] + sizes[g], :] = flat(value).astype(bf16)
        slot = net.slot(3)
        net.send(gp.at[k3], gr1.at[1], slot + 1, (i, k1))
        net.send(gp.at[k1], gr1.at[0], slot, (i, k1))
        net.arrived(gr1.at[1], slot + 1, (i, k1))
        for begin in range(0, rows, 16):
            span = slice(begin, begin + 16)
            gsum[span, :] = (gp[k2, span, :].astype(f32) + gr1[1, span, :].astype(f32)).astype(bf16)
        net.send(gsum, gr2, slot + 2, (i, k2))

        blocks = []
        for p in range(4):
            value = 0.0
            for g in range(2):
                cells = flat(zp[g][p, 1 : 1 + halves[g], 1 : 1 + halves[g]])
                value = value + mm(cells, back_patch(g, p), 0, 0)
            blocks.append(value.astype(bf16))
        wg1[...] = lanes_cat(blocks).reshape(n_dp, in_local, 10 * LANES)
        slot_w1 = net.slot(2 * n_z)
        halve(wg1, wr1, slot_w1)
        spread(wg1, wr1, wx1, wz1, slot_w1, slot_w1 + n_z)
        net.arrived(gr1.at[0], slot, (i, k1))
        net.arrived(gr2, slot + 2, (i, k2))
        if stop == 9:
            collect(wx2, wz2, slot_w2 + n_z)
            collect(wx1, wz1, slot_w1 + n_z)
            return finish(net, locals())
        for begin in range(0, rows, 16):
            span = slice(begin, begin + 16)
            gsum_ = gp[k, span, :].astype(f32) + gr1[0, span, :].astype(f32) + gr2[span, :].astype(f32)
            gp[k, span, :] = gsum_.astype(bf16)
        part_a = mm(gp[k, : sizes[0], :], pa[...], 0, 0)
        part_b = mm(gp[k, sizes[0] :, :], pb[...], 0, 0)
        lane = lax.broadcasted_iota(jnp.int32, (chan_in, LANES), 1)
        seam = jnp.where(lane < b_skip, part_a[:, b_tile : b_tile + LANES], part_b[:, :LANES])
        gt[...] = (
            jnp.concatenate([part_a[:, :b_tile], seam, part_b[:, LANES:]], axis=1)
            .astype(bf16)
            .reshape(n_dp, in_local, slab_lanes)
        )
        slot = net.slot(n_dp)
        for d in range(1, n_dp):
            j = (i + d) % n_dp
            net.send(gt.at[j], gr.at[i], slot + i, (j, k))
        gr[i] = gt[i]
        gw2[...] = collect(wx2, wz2, slot_w2 + n_z)
        gw1[...] = collect(wx1, wz1, slot_w1 + n_z)
        vecs[...] = message([sum_gain1, sum_head, sum_gain2, sum_tail, sum_gains])
        for d in range(1, n_dp):
            j = (i + d) % n_dp
            net.arrived(gr.at[j], slot + j, (j, k))
        net.drain()

    def finish(net, env):
        net.drain()

    bf, f = jnp.bfloat16, jnp.float32
    V = pltpu.VMEM
    pads = [(h + 2, h + 2, n, chan_part) for h, n in zip(halves, images)]
    scratch = [
        V((n_dp, in_local, slab_lanes), bf),
        V((n_dp, in_local, slab_lanes), bf),
        V((4, rows, chan_in), bf),
        V((4, halves[0] + 1, halves[0] + 1, images[0], chan_in), bf),
        V((4, halves[1] + 1, halves[1] + 1, images[1], chan_in), bf),
        V((rows, LANES), f),
        V((rows, chan_part), f),
        V((rows, chan_part), f),
        V((4,) + pads[0], bf),
        V((4,) + pads[1], bf),
        V((4, n_dp, 8, LANES), f),
        V((rows, chan_part), f),
        V((rows, chan_part), f),
        V((rows, chan_part), f),
        V(pads[0], bf),
        V(pads[1], bf),
        V((rows, chan_part), bf),
        V((rows, 9 * chan_part), bf),
        V((4, rows, chan_part), bf),
        V((2, rows, chan_part), bf),
        V((rows, chan_part), bf),
        V((rows, chan_part), bf),
        V((rows, chan_part), f),
        V((halves[0] + 1, halves[0] + 1, images[0], chan_part), bf),
        V((halves[1] + 1, halves[1] + 1, images[1], chan_part), bf),
        V((n_dp, out_rows, 9 * LANES), bf),
        V((n_dp // 2, out_rows, 9 * LANES), bf),
        V((n_dp // 2, out_rows, 9 * LANES), bf),
        V((n_dp // 2, out_rows, 9 * LANES), bf),
        V((n_dp, in_local, 10 * LANES), bf),
        V((n_dp // 2, in_local, 10 * LANES), bf),
        V((n_dp // 2, in_local, 10 * LANES), bf),
        V((n_dp // 2, in_local, 10 * LANES), bf),
        V((4, rows, chan_in), bf),
        V((2, rows, chan_in), bf),
        V((rows, chan_in), bf),
        V((rows, chan_in), bf),
        V((n_dp, in_local, slab_lanes), bf),
        pltpu.SemaphoreType.DMA((96,)),
        pltpu.SemaphoreType.DMA((96,)),
    ]
    outs = [
        jax.ShapeDtypeStruct((sizes[0], chan_part), bf),
        jax.ShapeDtypeStruct((sizes[1], chan_part), bf),
        jax.ShapeDtypeStruct((n_dp, in_local, slab_lanes), bf),
        jax.ShapeDtypeStruct((in_local, 10 * LANES), f),
        jax.ShapeDtypeStruct((out_rows, 9 * LANES), f),
        jax.ShapeDtypeStruct((8, LANES), f),
    ]
    vmem = pl.BlockSpec(memory_space=pltpu.VMEM)
    main = pl.pallas_call(
        kernel,
        out_shape=outs,
        in_specs=[vmem] * 17,
        out_specs=[vmem] * len(outs),
        scratch_shapes=scratch,
        compiler_params=pltpu.CompilerParams(
            collective_id=1, has_side_effects=True, vmem_limit_bytes=60 * 2**20
        ),
        name="block",
    )

    def closing(oa, ob, gr, gw1, gw2, vecs, turn, *outs):
        fa, fb, ia, ib, f1, f2, fs, c1, h1, c2, h2, cs, hs = outs
        fa[...] = oa[...]
        fb[...] = ob[...]
        moved = mm(turn[...], gr[...].reshape(n_dp * in_local, slab_lanes), 1, 0)
        ia[...] = moved[:, : qlanes[0]].astype(bf).reshape(in_local, n_dp, qlanes[0])
        ib[...] = moved[:, qlanes[0] : qlanes[0] + qlanes[1]].astype(bf).reshape(in_local, n_dp, qlanes[1])
        for t, tap in enumerate(TAPS):
            f2[t] = gw2[:, t * LANES : (t + 1) * LANES]
            place = ORDER.index(tap)
            place = place + (place > 0)
            f1[t] = gw1[:, place * LANES : (place + 1) * LANES]
        fs[...] = gw1[:, LANES : 2 * LANES]
        for ref, row in ((c1, 0), (h1, 1), (c2, 2), (h2, 3), (cs, 4), (hs, 3)):
            ref[...] = vecs[row : row + 1, :]

    last = pl.pallas_call(
        closing,
        out_shape=[
            jax.ShapeDtypeStruct((sizes[0], chan_part), bf),
            jax.ShapeDtypeStruct((sizes[1], chan_part), bf),
            jax.ShapeDtypeStruct((in_local, n_dp, qlanes[0]), bf),
            jax.ShapeDtypeStruct((in_local, n_dp, qlanes[1]), bf),
            jax.ShapeDtypeStruct((9, in_local, LANES), f),
            jax.ShapeDtypeStruct((9, out_rows, LANES), f),
            jax.ShapeDtypeStruct((in_local, LANES), f),
        ]
        + [jax.ShapeDtypeStruct((1, LANES), f)] * 6,
        in_specs=[vmem] * 7,
        out_specs=[vmem] * 13,
        compiler_params=pltpu.CompilerParams(vmem_limit_bytes=40 * 2**20),
        name="closing",
    )
    order_a = quarter_order(quarter[0], sides[0], 0, win[0]).astype(jnp.bfloat16)
    order_b = quarter_order(quarter[1], sides[1], b_skip, slab_lanes - b_tile).astype(jnp.bfloat16)
    total_rows = n_dp * in_local
    turn = np.zeros((total_rows, total_rows), np.float32)
    for c in range(in_local):
        for j in range(n_dp):
            turn[c * n_dp + j, j * in_local + c] = 1.0
    turn = turn.astype(jnp.bfloat16)
    return main, last, order_a, order_b, turn


STOP = 99


def fused_body(
    input_a, input_b, boxes_a, boxes_b, weight_first, weight_second, weight_short,
    gain_first, shift_first, gain_second, shift_second, gain_short, shift_short,
    upstream_a, upstream_b,
):
    n_dp = lax.axis_size("dp")
    chan_part = weight_first.shape[2]
    main, last, order_a, order_b, turn = make_fused(
        n_dp, input_a.shape[0], (boxes_a.shape[0], boxes_b.shape[0]), (SA, SB),
        weight_first.shape[1], chan_part, STOP,
    )
    vectors = [
        v.reshape(1, chan_part)
        for v in (gain_first, shift_first, gain_second, shift_second, gain_short, shift_short)
    ]
    mid = main(
        input_a, input_b, boxes_a.T, boxes_b.T, weight_first, weight_second, weight_short,
        *vectors, upstream_a.T, upstream_b.T, order_a, order_b,
    )
    res = last(*mid, turn)
    in_local = input_a.shape[0]
    return (
        res[0].T, res[1].T,
        res[2].reshape(in_local, n_dp, 1, -1), res[3].reshape(in_local, n_dp, 1, -1),
        res[4], res[5], res[6],
    ) + tuple(v.reshape(chan_part) for v in res[7:])


def choose_body(mesh):
    return fused_body if mesh.shape["dp"] == 8 and mesh.shape["chan"] == 4 else plain_body


def solution(mesh):
    placed = (
        P("dp", None),
        P("dp", None),
        P("dp", None),
        P("dp", None),
        P(None, None, "chan"),
        P(None, None, "chan"),
        P(None, "chan"),
        P("chan"),
        P("chan"),
        P("chan"),
        P("chan"),
        P("chan"),
        P("chan"),
        P("chan", "dp"),
        P("chan", "dp"),
    )
    return jax.shard_map(
        choose_body(mesh),
        mesh=mesh,
        in_specs=placed,
        out_specs=(
            P("chan", "dp"),
            P("chan", "dp"),
            P("dp", None, "chan", None),
            P("dp", None, "chan", None),
            P(None, "dp", "chan"),
            P(None, "dp", "chan"),
            P("dp", "chan"),
            P("chan"),
            P("chan"),
            P("chan"),
            P("chan"),
            P("chan"),
            P("chan"),
        ),
        check_vma=False,
    )
```

```python
import jax
import jax.numpy as jnp
from jax import lax
import numpy as np
from jax.experimental import pallas as pl
from jax.experimental.pallas import tpu as pltpu
from jax.sharding import PartitionSpec as P

SA = 14
SB = 6


epsilon = 1e-05


def box_mask(box_rows, extent):
    positions = jnp.arange(extent, dtype=jnp.int32)[None, :]
    row_inside = (positions >= box_rows[:, 0:1]) & (positions < box_rows[:, 0:1] + box_rows[:, 2:3])
    col_inside = (positions >= box_rows[:, 1:2]) & (positions < box_rows[:, 1:2] + box_rows[:, 3:4])
    return (row_inside[:, :, None] & col_inside[:, None, :]).astype(jnp.float32)


def taps_strided(feature, image_count, extent):
    channels = feature.shape[0]
    output_side = extent // 2
    padded = jnp.pad(
        feature.reshape(channels, image_count, extent, extent), ((0, 0), (0, 0), (1, 1), (1, 1))
    )
    pieces = [
        padded[:, :, tap_row : tap_row + extent : 2, tap_col : tap_col + extent : 2]
        for tap_row in range(3)
        for tap_col in range(3)
    ]
    return jnp.stack(pieces, axis=0).reshape(9 * channels, image_count * output_side * output_side)


def taps_plain(feature, image_count, extent):
    channels = feature.shape[0]
    padded = jnp.pad(
        feature.reshape(channels, image_count, extent, extent), ((0, 0), (0, 0), (1, 1), (1, 1))
    )
    pieces = [
        padded[:, :, tap_row : tap_row + extent, tap_col : tap_col + extent]
        for tap_row in range(3)
        for tap_col in range(3)
    ]
    return jnp.stack(pieces, axis=0).reshape(9 * channels, image_count * extent * extent)


def untaps_plain(columns, channels, image_count, extent):
    pieces = columns.reshape(9, channels, image_count, extent, extent)
    running = jnp.zeros((channels, image_count, extent + 2, extent + 2), jnp.float32)
    for tap_row in range(3):
        for tap_col in range(3):
            running = running + jnp.pad(
                pieces[3 * tap_row + tap_col],
                ((0, 0), (0, 0), (tap_row, 2 - tap_row), (tap_col, 2 - tap_col)),
            )
    return running[:, :, 1:-1, 1:-1].reshape(channels, image_count * extent * extent)


def untaps_strided(columns, shortcut, channels, image_count, extent):
    output_side = extent // 2
    pieces = columns.reshape(9, channels, image_count, output_side, output_side)
    parity_sums = {}
    for tap_row in range(3):
        for tap_col in range(3):
            block_row = tap_row // 2
            block_col = tap_col // 2
            placed = jnp.pad(
                pieces[3 * tap_row + tap_col],
                ((0, 0), (0, 0), (block_row, 1 - block_row), (block_col, 1 - block_col)),
            )
            parity = (tap_row % 2, tap_col % 2)
            parity_sums[parity] = (
                placed if parity not in parity_sums else parity_sums[parity] + placed
            )
    direct = jnp.pad(
        shortcut.reshape(channels, image_count, output_side, output_side),
        ((0, 0), (0, 0), (0, 1), (0, 1)),
    )
    parity_sums[1, 1] = parity_sums[1, 1] + direct
    rows_even = jnp.stack([parity_sums[0, 0], parity_sums[0, 1]], axis=-1)
    rows_odd = jnp.stack([parity_sums[1, 0], parity_sums[1, 1]], axis=-1)
    padded = jnp.stack([rows_even, rows_odd], axis=3).reshape(
        channels, image_count, extent + 2, extent + 2
    )
    return padded[:, :, 1:-1, 1:-1].reshape(channels, image_count * extent * extent)


def contract_first(weights, columns):
    return lax.dot_general(
        weights, columns, (((0,), (0,)), ((), ())), preferred_element_type=jnp.float32
    )


def weight_product(columns, gradient):
    return lax.dot_general(
        columns, gradient, (((1,), (1,)), ((), ())), preferred_element_type=jnp.float32
    )


def swish_slope(values):
    logistic = jax.nn.sigmoid(values)
    return logistic * (1.0 + values * (1.0 - logistic))


def moments(values, valid_list):
    running = 0.0
    squares = 0.0
    for tensor, valid in zip(values, valid_list):
        widened = tensor.astype(jnp.float32)
        running = running + jnp.sum(widened * valid, axis=1)
        squares = squares + jnp.sum(widened * widened * valid, axis=1)
    return (running, squares)


def standardize(values, running, squares, population):
    mean_value = running / population
    variance = squares / population - mean_value * mean_value
    scaling = lax.rsqrt(variance + epsilon)
    return (
        [
            (tensor.astype(jnp.float32) - mean_value[:, None]) * scaling[:, None]
            for tensor in values
        ],
        scaling,
    )


def norm_back(gradient, normed, valid, scaling, gain_values, shift_sum, gain_sum, population):
    return (gain_values * scaling)[:, None] * (
        gradient - valid * (shift_sum[:, None] + normed * gain_sum[:, None]) / population
    )


def plain_body(
    input_a,
    input_b,
    boxes_a,
    boxes_b,
    weight_first,
    weight_second,
    weight_short,
    gain_first,
    shift_first,
    gain_second,
    shift_second,
    gain_short,
    shift_short,
    upstream_a,
    upstream_b,
):
    image_groups = lax.axis_size("dp")
    in_local = input_a.shape[0]
    chan_in = weight_first.shape[1]
    chan_part = weight_first.shape[2]
    chan_full = weight_second.shape[1]
    image_counts = (boxes_a.shape[0], boxes_b.shape[0])
    extents = (SA, SB)
    whole_a, whole_b = (
        lax.all_to_all(
            input_a.reshape(in_local, image_groups, -1),
            "dp",
            split_axis=1,
            concat_axis=0,
            tiled=True,
        ),
        lax.all_to_all(
            input_b.reshape(in_local, image_groups, -1),
            "dp",
            split_axis=1,
            concat_axis=0,
            tiled=True,
        ),
    )
    features = (whole_a.reshape(chan_in, -1), whole_b.reshape(chan_in, -1))
    valid_list = (
        box_mask(boxes_a, SA // 2).reshape(1, -1),
        box_mask(boxes_b, SB // 2).reshape(1, -1),
    )
    first_mat = weight_first.reshape(9 * chan_in, chan_part)
    second_mat = weight_second.reshape(9 * chan_full, chan_part)
    first_cols = []
    sampled = []
    first_z = []
    short_z = []
    for feature, image_count, extent in zip(features, image_counts, extents):
        columns = taps_strided(feature, image_count, extent)
        picked = feature.reshape(chan_in, image_count, extent, extent)[:, :, ::2, ::2].reshape(
            chan_in, -1
        )
        first_cols.append(columns)
        sampled.append(picked)
        first_z.append(contract_first(first_mat, columns).astype(jnp.bfloat16))
        short_z.append(contract_first(weight_short, picked).astype(jnp.bfloat16))
    sum_first, square_first = moments(first_z, valid_list)
    sum_short, square_short = moments(short_z, valid_list)
    population = jnp.sum(valid_list[0]) + jnp.sum(valid_list[1])
    sum_first, square_first, sum_short, square_short, population = lax.psum(
        (sum_first, square_first, sum_short, square_short, population), "dp"
    )
    normed_first, scaling_first = standardize(first_z, sum_first, square_first, population)
    normed_short, scaling_short = standardize(short_z, sum_short, square_short, population)
    before_first = [normed * gain_first[:, None] + shift_first[:, None] for normed in normed_first]
    outgoing_a = (jax.nn.silu(before_first[0]) * valid_list[0]).astype(jnp.bfloat16)
    outgoing_b = (jax.nn.silu(before_first[1]) * valid_list[1]).astype(jnp.bfloat16)
    gathered_a, gathered_b = (
        lax.all_gather(outgoing_a, "chan", axis=0, tiled=True),
        lax.all_gather(outgoing_b, "chan", axis=0, tiled=True),
    )
    second_cols = []
    second_z = []
    for gathered, image_count, extent in zip((gathered_a, gathered_b), image_counts, extents):
        columns = taps_plain(gathered, image_count, extent // 2)
        second_cols.append(columns)
        second_z.append(contract_first(second_mat, columns).astype(jnp.bfloat16))
    sum_second, square_second = moments(second_z, valid_list)
    sum_second, square_second = lax.psum((sum_second, square_second), "dp")
    normed_second, scaling_second = standardize(second_z, sum_second, square_second, population)
    summed_pre = [
        main_part * gain_second[:, None]
        + shift_second[:, None]
        + side_part * gain_short[:, None]
        + shift_short[:, None]
        for main_part, side_part in zip(normed_second, normed_short)
    ]
    outputs = [
        (jax.nn.silu(tensor) * valid).astype(jnp.bfloat16)
        for tensor, valid in zip(summed_pre, valid_list)
    ]
    tail_grads = [
        upstream.astype(jnp.float32) * valid * swish_slope(tensor)
        for upstream, valid, tensor in zip((upstream_a, upstream_b), valid_list, summed_pre)
    ]
    shift_tail = sum((jnp.sum(gradient, axis=1) for gradient in tail_grads))
    gain_tail = sum(
        (jnp.sum(gradient * normed, axis=1) for gradient, normed in zip(tail_grads, normed_second))
    )
    gain_side = sum(
        (jnp.sum(gradient * normed, axis=1) for gradient, normed in zip(tail_grads, normed_short))
    )
    shift_tail, gain_tail, gain_side = lax.psum((shift_tail, gain_tail, gain_side), "dp")
    grad_second_local = 0.0
    partial_hidden = []
    short_dz = []
    for index_group in range(2):
        valid = valid_list[index_group]
        dz_second = norm_back(
            tail_grads[index_group],
            normed_second[index_group],
            valid,
            scaling_second,
            gain_second,
            shift_tail,
            gain_tail,
            population,
        ).astype(jnp.bfloat16)
        dz_short = norm_back(
            tail_grads[index_group],
            normed_short[index_group],
            valid,
            scaling_short,
            gain_short,
            shift_tail,
            gain_side,
            population,
        ).astype(jnp.bfloat16)
        short_dz.append(dz_short)
        grad_second_local = grad_second_local + weight_product(second_cols[index_group], dz_second)
        back_cols = jnp.dot(second_mat, dz_second, preferred_element_type=jnp.float32)
        partial_hidden.append(
            untaps_plain(back_cols, chan_full, image_counts[index_group], extents[index_group] // 2)
        )
    hidden_a, hidden_b = (
        lax.psum_scatter(
            partial_hidden[0].astype(jnp.bfloat16), "chan", scatter_dimension=0, tiled=True
        ).astype(jnp.float32),
        lax.psum_scatter(
            partial_hidden[1].astype(jnp.bfloat16), "chan", scatter_dimension=0, tiled=True
        ).astype(jnp.float32),
    )
    head_grads = [
        hidden * valid * swish_slope(tensor)
        for hidden, valid, tensor in zip((hidden_a, hidden_b), valid_list, before_first)
    ]
    shift_head = sum((jnp.sum(gradient, axis=1) for gradient in head_grads))
    gain_head = sum(
        (jnp.sum(gradient * normed, axis=1) for gradient, normed in zip(head_grads, normed_first))
    )
    shift_head, gain_head = lax.psum((shift_head, gain_head), "dp")
    grad_first_local = 0.0
    grad_short_local = 0.0
    partial_inputs = []
    for index_group in range(2):
        valid = valid_list[index_group]
        dz_first = norm_back(
            head_grads[index_group],
            normed_first[index_group],
            valid,
            scaling_first,
            gain_first,
            shift_head,
            gain_head,
            population,
        ).astype(jnp.bfloat16)
        grad_first_local = grad_first_local + weight_product(first_cols[index_group], dz_first)
        grad_short_local = grad_short_local + weight_product(
            sampled[index_group], short_dz[index_group]
        )
        back_cols = jnp.dot(first_mat, dz_first, preferred_element_type=jnp.float32)
        back_short = jnp.dot(
            weight_short, short_dz[index_group], preferred_element_type=jnp.float32
        )
        flat_input = untaps_strided(
            back_cols, back_short, chan_in, image_counts[index_group], extents[index_group]
        )
        partial_inputs.append(flat_input.reshape(chan_in, 1, lax.axis_size("chan"), -1))
    arrived_a, arrived_b = (
        lax.all_to_all(
            partial_inputs[0].astype(jnp.bfloat16), "dp", split_axis=0, concat_axis=1, tiled=True
        ).astype(jnp.float32),
        lax.all_to_all(
            partial_inputs[1].astype(jnp.bfloat16), "dp", split_axis=0, concat_axis=1, tiled=True
        ).astype(jnp.float32),
    )
    summed_a, summed_b = (
        lax.psum_scatter(
            arrived_a.astype(jnp.bfloat16), "chan", scatter_dimension=2, tiled=True
        ).astype(jnp.float32),
        lax.psum_scatter(
            arrived_b.astype(jnp.bfloat16), "chan", scatter_dimension=2, tiled=True
        ).astype(jnp.float32),
    )
    grad_input_a = summed_a.astype(jnp.bfloat16)
    grad_input_b = summed_b.astype(jnp.bfloat16)
    grad_first_local = grad_first_local.reshape(9, chan_in, chan_part)
    grad_second_local = grad_second_local.reshape(9, chan_full, chan_part)
    total_first, total_second, total_short = lax.psum(
        (grad_first_local, grad_second_local, grad_short_local), "dp"
    )
    position = lax.axis_index("dp")
    rows_first = chan_in // image_groups
    rows_second = chan_full // image_groups
    grad_first = lax.dynamic_slice_in_dim(total_first, position * rows_first, rows_first, 1)
    grad_second = lax.dynamic_slice_in_dim(total_second, position * rows_second, rows_second, 1)
    grad_short = lax.dynamic_slice_in_dim(total_short, position * rows_first, rows_first, 0)
    return (
        outputs[0],
        outputs[1],
        grad_input_a,
        grad_input_b,
        grad_first,
        grad_second,
        grad_short,
        gain_head,
        shift_head,
        gain_tail,
        shift_tail,
        gain_side,
        shift_tail,
    )


MESH = pl.DeviceIdType.MESH
TAPS = tuple((a, b) for a in range(3) for b in range(3))
PLANE_TAPS = (
    ((1, 1),),
    ((1, 0), (1, 2)),
    ((0, 1), (2, 1)),
    ((0, 0), (0, 2), (2, 0), (2, 2)),
)
ORDER = [tap for taps in PLANE_TAPS for tap in taps]
LANES = 128


class Links:
    def __init__(self, send_sems, recv_sems):
        self.send_sems, self.recv_sems = send_sems, recv_sems
        self.sends = self.slots = 0
        self.open = []

    def slot(self, count=1):
        first = self.slots
        self.slots += count
        return first

    def send(self, source, target, slot, where):
        copy = pltpu.make_async_remote_copy(
            source, target, self.send_sems.at[self.sends], self.recv_sems.at[slot],
            device_id=where, device_id_type=MESH,
        )
        self.sends += 1
        copy.start()
        self.open.append(copy)

    def arrived(self, target, slot, where):
        pltpu.make_async_remote_copy(
            target, target, self.send_sems.at[0], self.recv_sems.at[slot],
            device_id=where, device_id_type=MESH,
        ).wait_recv()

    def drain(self):
        for copy in self.open:
            copy.wait_send()


def mm(a, b, ca, cb):
    return lax.dot_general(a, b, (((ca,), (cb,)), ((), ())), preferred_element_type=jnp.float32)


def lanes_cat(parts):
    return jnp.concatenate(parts, axis=1) if len(parts) > 1 else parts[0]


def regroup(value, runs):
    return jnp.concatenate([value[:, a:b] for a, b in runs], axis=1)


def sigma(v):
    return 0.5 * jnp.tanh(0.5 * v) + 0.5


class Reduce:
    def __init__(self, net, i, k, part, bufs, windows):
        self.net, self.part, self.windows = net, part, windows
        self.b1, self.s1, self.b2, self.s2, self.b3 = bufs
        self.ix, self.pz, self.hz = i % 2, (i // 2) % 2, i // 4
        self.peers = (
            (i + 1 - 2 * self.ix, k),
            (i + 2 - 4 * self.pz, k),
            (i + 4 - 8 * self.hz, k),
        )
        self.slots = [net.slot(3) for _ in windows]

    def first(self, w):
        cols = self.windows[w]
        self.net.send(
            self.part.at[:, :, 1 - self.ix, :, cols], self.b1.at[:, :, :, cols],
            self.slots[w], self.peers[0],
        )

    def second(self, w):
        cols = self.windows[w]
        self.net.arrived(self.b1.at[:, :, :, cols], self.slots[w], self.peers[0])
        for h in range(2):
            for p in range(2):
                value = self.part[h, p, self.ix, :, cols].astype(jnp.float32)
                value = value + self.b1[h, p, :, cols].astype(jnp.float32)
                self.s1[h, p, :, cols] = value.astype(jnp.bfloat16)
        self.net.send(
            self.s1.at[:, 1 - self.pz, :, cols], self.b2.at[:, :, cols],
            self.slots[w] + 1, self.peers[1],
        )

    def third(self, w):
        cols = self.windows[w]
        self.net.arrived(self.b2.at[:, :, cols], self.slots[w] + 1, self.peers[1])
        for h in range(2):
            value = self.s1[h, self.pz, :, cols].astype(jnp.float32)
            value = value + self.b2[h, :, cols].astype(jnp.float32)
            self.s2[h, :, cols] = value.astype(jnp.bfloat16)
        self.net.send(
            self.s2.at[1 - self.hz, :, cols], self.b3.at[:, cols],
            self.slots[w] + 2, self.peers[2],
        )

    def last(self, w):
        cols = self.windows[w]
        self.net.arrived(self.b3.at[:, cols], self.slots[w] + 2, self.peers[2])
        return self.s2[self.hz, :, cols].astype(jnp.float32) + self.b3[:, cols].astype(jnp.float32)


def make_fused(n_dp, in_local, images, sides, chan_in, chan_part, stop):
    f32, bf16 = jnp.float32, jnp.bfloat16
    halves = tuple(side // 2 for side in sides)
    sizes = tuple(h * h * n for h, n in zip(halves, images))
    rows = sum(sizes)
    quarter = tuple(n // 4 for n in images)
    qlanes = tuple(q * side * side for q, side in zip(quarter, sides))
    n_parts = 3
    step = -(-sum(qlanes) // (n_parts * LANES)) * LANES
    slab_lanes = n_parts * step
    b_tile = qlanes[0] // LANES * LANES
    b_skip = qlanes[0] - b_tile
    chan_full = 4 * chan_part
    out_rows = chan_full // n_dp
    starts = (0, sizes[0])
    chunks = [
        (g, r, starts[g] + r * halves[g] * images[g], halves[g] * images[g])
        for g in range(2)
        for r in range(halves[g])
    ]
    win = [-(-q // LANES) * LANES for q in qlanes]
    part_chunks = [[] for _ in range(n_parts)]
    for chunk in chunks:
        part_chunks[n_parts - 1 if chunk[0] else -(-(chunk[2] + chunk[3]) // step) - 1].append(chunk)
    spans = [(part[0][2], part[-1][2] + part[-1][3]) for part in part_chunks]
    pieces = []
    for part in part_chunks:
        found = [[c for c in part if c[0] == g] for g in range(2)]
        pieces.append([(g, f[0][1], f[-1][1] + 1) for g, f in enumerate(found) if f])
    in_win = [(a // LANES * LANES, min(-(-b // LANES) * LANES, slab_lanes)) for a, b in spans]
    out_win = []
    for c in range(n_parts):
        hit = [span for span in spans if span[0] < (c + 1) * step and span[1] > c * step]
        out_win.append((hit[0][0], hit[-1][1]))
    runs = []
    for part in pieces:
        for g, r0, r1 in part:
            side, base = sides[g], (0, qlanes[0])[g]
            runs += [
                (base + (image * side + 2 * r0) * side, base + (image * side + 2 * r1) * side)
                for image in range(quarter[g])
            ]
    runs.append((sum(qlanes), slab_lanes))
    lane_of, order = 0, []
    for a, b in runs:
        order.append((a, lane_of, lane_of + b - a))
        lane_of += b - a
    back_runs = [(a, b) for _, a, b in sorted(order)]
    split = halves[0] // 2 + 1
    act_pieces = [(1, 0, halves[1]), (0, 0, split), (0, split, halves[0])]
    mid = (rows // 32 + 1) * 16
    row_halves = (slice(0, mid), slice(mid, rows))
    cols2 = (slice(0, 5 * LANES), slice(5 * LANES, 9 * LANES))
    cols1 = (slice(0, 10 * LANES),)

    def kernel(*refs):
        (xa_h, xb_h, bxa_h, bxb_h, w1_h, w2_h, ws_h, g1_h, b1_h, g2_h, b2_h, gs_h, bs_h, ua_h, ub_h,
         oa, ob, gr, gw1, gws, gw2, vecs,
         xa, xb, bxa, bxb, w1, w2, ws, g1, b1, g2, b2, gs, bs, ua, ub, cells,
         xs, xt, xr, zg, zpa, zpb, valid, z1, zs, a1a, a1b, slots, up, outr, gv, dza, dzb, dzsr,
         dd, hp, hr1, hs, hr2, gu, d1a, d1b,
         wg2, p21, p22, p23, p24, p25, wg1, p11, p12, p13, p14, p15,
         gp, gr1, gsum, gr2, zt, gt, lsem, ssem, rsem) = refs
        i, k = lax.axis_index("dp"), lax.axis_index("chan")
        k1 = k + 1 - 2 * (k % 2)
        k2 = (k + 2) % 4
        k3 = (k1 + 2) % 4
        net = Links(ssem, rsem)
        zp, a1, dz, d1 = (zpa, zpb), (a1a, a1b), (dza, dzb), (d1a, d1b)

        def flat(value):
            return value.reshape(-1, value.shape[-1])

        def zeros(count):
            return [jnp.zeros((8, LANES), f32)] * count

        loads = {}
        pairs_of = (
            ("xa", xa_h, xa), ("xb", xb_h, xb),
            ("bxa", bxa_h, bxa), ("bxb", bxb_h, bxb), ("ua", ua_h, ua), ("ub", ub_h, ub),
            ("w1", w1_h, w1), ("ws", ws_h, ws), ("g1", g1_h, g1), ("b1", b1_h, b1), ("g2", g2_h, g2),
            ("b2", b2_h, b2), ("gs", gs_h, gs), ("bs", bs_h, bs), ("w2", w2_h, w2),
        )
        for index, (name, source, target) in enumerate(pairs_of):
            loads[name] = pltpu.make_async_copy(source, target, lsem.at[index])
        loads["xa"].start()
        loads["xb"].start()

        def need(*names):
            for name in names:
                loads.pop(name).wait()

        barrier = pltpu.get_barrier_semaphore()
        for d in range(1, n_dp):
            pl.semaphore_signal(barrier, inc=1, device_id=((i + d) % n_dp, k), device_id_type=MESH)
        pl.semaphore_signal(barrier, inc=1, device_id=(i, k1), device_id_type=MESH)
        pl.semaphore_signal(barrier, inc=1, device_id=(i, k2), device_id_type=MESH)

        if stop == -6:
            need("xa", "xb")
            for copy in loads.values():
                copy.start()
            pl.semaphore_wait(barrier, n_dp + 1)
            need(*list(loads))
            return net.drain()
        need("xa", "xb")
        for copy in loads.values():
            copy.start()
        lane = lax.broadcasted_iota(jnp.int32, (in_local, LANES), 1)
        for d in range(n_dp):
            j = (i + d) % n_dp
            begin = 4 * qlanes[0] * j + qlanes[0] * k
            tile = begin // LANES
            part_a = xa[:, pl.ds(pl.multiple_of(tile * LANES, LANES), win[0])].astype(f32)
            part_a = pltpu.roll(part_a, (win[0] - (begin - tile * LANES)) % win[0], 1)
            begin = 4 * qlanes[1] * j + qlanes[1] * k
            tile = begin // LANES
            part_b = xb[:, pl.ds(pl.multiple_of(tile * LANES, LANES), win[1])].astype(f32)
            part_b = jnp.concatenate([part_b, jnp.zeros((in_local, LANES), f32)], axis=1)
            wide = win[1] + LANES
            part_b = pltpu.roll(part_b, (wide + b_skip - (begin - tile * LANES)) % wide, 1)
            seam = jnp.where(lane < b_skip, part_a[:, b_tile : b_tile + LANES], part_b[:, :LANES])
            xs[d * in_local : (d + 1) * in_local, :] = jnp.concatenate(
                [part_a[:, :b_tile], seam, part_b[:, LANES : slab_lanes - b_tile]], axis=1
            ).astype(bf16)
        if stop == -5:
            pl.semaphore_wait(barrier, n_dp + 1)
            need(*list(loads))
            return net.drain()
        slot_x = [net.slot(n_dp) for _ in range(n_parts)]
        for c in range(n_parts):
            cols = slice(c * step, (c + 1) * step)
            if c == 0:
                ordered = regroup(xs[...], runs)
            moved = ordered[:, cols]
            xt[:, :, cols] = moved.reshape(n_dp, in_local, step)
            xr[i, :, cols] = moved[:in_local]
            if c == 0:
                pl.semaphore_wait(barrier, n_dp + 1)
            for d in range(1, n_dp):
                net.send(xt.at[d, :, cols], xr.at[i, :, cols], slot_x[c] + i, ((i + d) % n_dp, k))

        if stop in (-3,-4):
            for c in range(n_parts):
                for d in range(1, n_dp):
                    j = (i + d) % n_dp
                    net.arrived(xr.at[j, :, c*step:(c+1)*step], slot_x[c] + j, (j, k))
            need(*list(loads))
            return net.drain()

        for buf in (zpa, zpb, a1a, a1b, dza, dzb, d1a, d1b):
            side = buf.shape[1] if len(buf.shape) == 5 else buf.shape[0]
            lead = (slice(None),) if len(buf.shape) == 5 else ()
            for edge in (0, side - 1):
                for index in (lead + (edge,), lead + (slice(None), edge)):
                    region = buf.at[index]
                    region[...] = jnp.zeros(region.shape, buf.dtype)
        need("bxa", "bxb", "ua", "ub")
        population = zeros(1)[0]
        for g, box in enumerate((bxa, bxb)):
            n, half = images[g], halves[g]
            diag = lax.broadcasted_iota(jnp.int32, (n, n), 0) == lax.broadcasted_iota(jnp.int32, (n, n), 1)
            ends = [
                jnp.sum(jnp.where(diag, box[q : q + 1, :].astype(f32), 0.0), axis=1, keepdims=True)
                for q in range(4)
            ]
            inside = [
                [((p >= ends[q]) & (p < ends[q] + ends[q + 2])).astype(f32) for p in range(half)]
                for q in range(2)
            ]
            for r in range(half):
                for s in range(half):
                    cell = jnp.broadcast_to(inside[0][r] * inside[1][s], (n, LANES))
                    begin = starts[g] + (r * half + s) * n
                    valid[begin : begin + n, :] = cell
                    population = population + jnp.sum(cell.reshape(n // 8, 8, LANES), axis=0)
        population = jnp.sum(population, axis=0, keepdims=True)
        for g, source in enumerate((ua, ub)):
            n, count = images[g], halves[g] ** 2
            gu[starts[g] : starts[g] + sizes[g], :] = source[...].astype(f32)
            for cell in range(count):
                up[starts[g] + cell * n : starts[g] + (cell + 1) * n, :] = gu[
                    pl.ds(starts[g] + cell, n, stride=count), :
                ]

        lane = lax.broadcasted_iota(jnp.int32, (16, slab_lanes), 1)
        for part, (a, b) in zip(pieces, spans):
            for g, r0, r1 in part:
                n, half, side, width = quarter[g], halves[g], sides[g], halves[g] * images[g]
                for r in range(r0, r1):
                    for begin in range(0, width, 16):
                        at = begin + lax.broadcasted_iota(jnp.int32, (16, 1), 0)
                        image, plane, s = at % n, (at // n) % 4, at // (4 * n)
                        first = starts[g] + r0 * width + 2 * (r - r0) * side
                        place = first + image * (2 * (r1 - r0) * side) + (plane // 2) * side + 2 * s + plane % 2
                        row = starts[g] + r * width + begin
                        cells[row : row + 16, :] = jnp.where(lane == place, 1.0, 0.0).astype(bf16)
        slot_z = [net.slot(4) for _ in range(n_parts)]

        if stop == -2:
            for c in range(n_parts):
                for d in range(1, n_dp):
                    j = (i + d) % n_dp
                    net.arrived(xr.at[j, :, c*step:(c+1)*step], slot_x[c] + j, (j, k))
            need(*list(loads))
            return net.drain()

        def quarter_in(c):
            lo, hi = c * step, (c + 1) * step
            for d in range(1, n_dp):
                j = (i + d) % n_dp
                net.arrived(xr.at[j, :, lo:hi], slot_x[c] + j, (j, k))
            (a, b), (lo, hi) = spans[c], in_win[c]
            whole = jnp.concatenate([xr[q, :, lo:hi] for q in range(n_dp)], axis=0)
            zg[k, a:b, :] = mm(cells[a:b, lo:hi], whole, 1, 1).astype(bf16)
            for where in (k2, k1):
                net.send(zg.at[k, a:b], zg.at[k, a:b], slot_z[c] + k, (i, where))

        def quarter_on(c):
            a, b = spans[c]
            net.arrived(zg.at[k2, a:b], slot_z[c] + k2, (i, k2))
            net.send(zg.at[k2, a:b], zg.at[k2, a:b], slot_z[c] + k2, (i, k1))

        def planes_of(quarters, g):
            count = quarter[g]
            if count % 8 == 0:
                return [
                    jnp.concatenate([v[:, count * p : count * (p + 1)] for v in quarters], axis=1)
                    for p in range(4)
                ]
            low = lax.broadcasted_iota(jnp.int32, (1, 8, 1), 1) < 4
            parts = [[v[:, 8 * h : 8 * h + 8] for v in quarters] for h in range(2)]
            turned = [[pltpu.roll(v, 4, 1) for v in side] for side in parts]
            result = []
            for p in range(4):
                v, t = parts[p // 2], turned[p // 2]
                if p % 2 == 0:
                    both = [jnp.where(low, v[0], t[1]), jnp.where(low, v[2], t[3])]
                else:
                    both = [jnp.where(low, t[0], v[1]), jnp.where(low, t[2], v[3])]
                result.append(jnp.concatenate(both, axis=1))
            return result

        def strided_patch(c, tap):
            a, b = tap
            p = 2 * (a % 2 == 0) + (b % 2 == 0)
            r, s = 1 - (a == 0), 1 - (b == 0)
            return jnp.concatenate(
                [flat(zp[g][p, r0 + r : r1 + r, s : s + halves[g]]) for g, r0, r1 in pieces[c]], axis=0
            )

        def rowsum(value):
            return jnp.sum(value.reshape(-1, 8, LANES), axis=0)

        def first_conv(c, acc):
            a, b = spans[c]
            net.arrived(zg.at[k1, a:b], slot_z[c] + k1, (i, k1))
            net.arrived(zg.at[k3, a:b], slot_z[c] + k3, (i, k1))
            for g, r, begin, count in part_chunks[c]:
                quarters = [
                    zg[q, begin : begin + count, :].astype(f32).reshape(halves[g], images[g], chan_in)
                    for q in range(4)
                ]
                for p, value in enumerate(planes_of(quarters, g)):
                    zp[g][p, 1 + r, 1 : 1 + halves[g]] = value.astype(bf16)
            both = mm(strided_patch(c, (1, 1)), jnp.concatenate([w1[4], ws[...]], axis=1), 1, 0)
            zs[a:b, :] = both[:, chan_part:]
            value = both[:, :chan_part]
            for tap in TAPS:
                if tap != (1, 1):
                    value = value + mm(strided_patch(c, tap), w1[3 * tap[0] + tap[1]], 1, 0)
            z1[a:b, :] = value
            for g, r, begin, count in part_chunks[c]:
                span = slice(begin, begin + count)
                ok = valid[span, :]
                u, w = z1[span, :], zs[span, :]
                uv, wv = u * ok, w * ok
                acc = [
                    acc[0] + rowsum(uv), acc[1] + rowsum(uv * u),
                    acc[2] + rowsum(wv), acc[3] + rowsum(wv * w),
                ]
            return acc

        acc = zeros(4)
        for c in range(n_parts):
            quarter_in(c)
            if c >= 1:
                quarter_on(c - 1)
        if stop == 1:
            quarter_on(n_parts - 1)
            for c in range(n_parts):
                net.arrived(zg.at[k1, spans[c][0]:spans[c][1]], slot_z[c] + k1, (i, k1))
                net.arrived(zg.at[k3, spans[c][0]:spans[c][1]], slot_z[c] + k3, (i, k1))
            need(*list(loads))
            return net.drain()
        need("w1", "ws")
        for c in range(n_parts):
            if c == 1:
                quarter_on(n_parts - 1)
            acc = first_conv(c, acc)

        def message(sums):
            parts = [jnp.sum(v, axis=0, keepdims=True) if v.shape[0] > 1 else v for v in sums]
            parts.append(jnp.zeros((8 - len(parts), LANES), f32))
            return jnp.concatenate(parts, axis=0)

        def share(rnd, value):
            slots[rnd, i] = value
            first = net.slot(n_dp)
            for d in range(1, n_dp):
                net.send(slots.at[rnd, i], slots.at[rnd, i], first + i, ((i + d) % n_dp, k))
            return first

        def total(rnd, first):
            for d in range(1, n_dp):
                j = (i + d) % n_dp
                net.arrived(slots.at[rnd, j], first + j, (j, k))
            return jnp.sum(slots[rnd], axis=0)

        if stop == 2:
            valid[0:8, :] = acc[0] + acc[1] + acc[2] + acc[3]
            need(*list(loads))
            return net.drain()
        first = share(0, message(acc + [population]))
        need(*list(loads))
        tot = total(0, first)
        inv_pop = 1.0 / tot[4:5]
        mean1, means = tot[0:1] * inv_pop, tot[2:3] * inv_pop
        sc1 = lax.rsqrt(tot[1:2] * inv_pop - mean1 * mean1 + epsilon)
        scs = lax.rsqrt(tot[3:4] * inv_pop - means * means + epsilon)
        gain1, shift1 = g1[...], b1[...]
        if stop == 3:
            valid[0:1, :] = sc1 + scs
            return net.drain()

        def act_ref(piece, q):
            g, r0, r1 = piece
            return a1[g].at[q, 1 + r0 : 1 + r1, 1 : 1 + halves[g]]

        slot_a = [net.slot(4) for _ in act_pieces]
        for piece, slot in zip(act_pieces, slot_a):
            for g, r, begin, count in chunks:
                if g == piece[0] and piece[1] <= r < piece[2]:
                    span = slice(begin, begin + count)
                    hat = (z1[span, :] - mean1) * sc1
                    z1[span, :] = hat
                    v = hat * gain1 + shift1
                    act = (v * sigma(v) * valid[span, :]).astype(bf16)
                    a1[g][k, 1 + r, 1 : 1 + halves[g]] = act.reshape(halves[g], images[g], chan_part)
            for where in (k2, k1):
                net.send(act_ref(piece, k), act_ref(piece, k), slot + k, (i, where))

        def act_on(n):
            piece, slot = act_pieces[n], slot_a[n]
            net.arrived(act_ref(piece, k2), slot + k2, (i, k2))
            net.send(act_ref(piece, k2), act_ref(piece, k2), slot + k2, (i, k1))

        def act_in(n):
            piece, slot = act_pieces[n], slot_a[n]
            net.arrived(act_ref(piece, k1), slot + k1, (i, k1))
            net.arrived(act_ref(piece, k3), slot + k3, (i, k1))

        def second_conv(piece, acc):
            g, r0, r1 = piece
            width = halves[g] * images[g]
            begin, end = starts[g] + r0 * width, starts[g] + r1 * width
            value = None
            for a, b in TAPS:
                patch = lanes_cat(
                    [flat(a1[g][q, r0 + a : r1 + a, b : b + halves[g]]) for q in range(4)]
                )
                part = mm(patch, w2[3 * a + b], 1, 0)
                value = part if value is None else value + part
            gv[begin:end, :] = value
            for row in range(begin, end, width):
                span = slice(row, row + width)
                u = gv[span, :]
                uv = u * valid[span, :]
                acc = [acc[0] + rowsum(uv), acc[1] + rowsum(uv * u)]
            return acc

        acc = zeros(2)
        act_on(0)
        act_in(0)
        acc = second_conv((1, 0, halves[1]), acc)
        act_on(1)
        act_in(1)
        acc = second_conv((0, 0, split - 1), acc)
        act_on(2)
        act_in(2)
        acc = second_conv((0, split - 1, halves[0]), acc)
        first = share(1, message(acc))
        for g, r, begin, count in chunks:
            span = slice(begin, begin + count)
            zs[span, :] = (zs[span, :] - means) * scs
        tot = total(1, first)
        mean2 = tot[0:1] * inv_pop
        sc2 = lax.rsqrt(tot[1:2] * inv_pop - mean2 * mean2 + epsilon)
        if stop == 5:
            valid[0:1, :] = sc2
            return net.drain()
        gain2, gains = g2[...], gs[...]
        shifts = b2[...] + bs[...]
        acc = zeros(3)
        for g, r, begin, count in chunks:
            span = slice(begin, begin + count)
            ok = valid[span, :]
            hat2 = (gv[span, :] - mean2) * sc2
            hats = zs[span, :]
            v = hat2 * gain2 + hats * gains + shifts
            sig = sigma(v)
            outr[span, :] = v * sig * ok
            grad = up[span, :] * ok * (sig * (1.0 + v * (1.0 - sig)))
            up[span, :] = grad
            gv[span, :] = hat2
            acc = [acc[0] + rowsum(grad), acc[1] + rowsum(grad * hat2), acc[2] + rowsum(grad * hats)]
        first = share(2, message(acc))
        for g, target in enumerate((oa, ob)):
            n, count = images[g], halves[g] ** 2
            for cell in range(count):
                gu[pl.ds(starts[g] + cell, n, stride=count), :] = outr[
                    starts[g] + cell * n : starts[g] + (cell + 1) * n, :
                ]
            target[...] = gu[starts[g] : starts[g] + sizes[g], :].astype(bf16)
        tot = total(2, first)
        sum_tail, sum_gain2, sum_gains = tot[0:1], tot[1:2], tot[2:3]
        if stop == 6:
            valid[0:1, :] = sum_tail
            return net.drain()

        k2g, ksg = gain2 * sc2, gains * scs
        db, dg2, dgs = sum_tail * inv_pop, sum_gain2 * inv_pop, sum_gains * inv_pop
        for g, r, begin, count in chunks:
            span = slice(begin, begin + count)
            value = k2g * (up[span, :] - valid[span, :] * (db + gv[span, :] * dg2))
            dz[g][1 + r, 1 : 1 + halves[g]] = value.astype(bf16).reshape(halves[g], images[g], chan_part)
        for g in range(2):
            for t, (a, b) in enumerate(TAPS):
                dd[starts[g] : starts[g] + sizes[g], t * LANES : (t + 1) * LANES] = flat(
                    dz[g][2 - a : 2 - a + halves[g], 2 - b : 2 - b + halves[g]]
                )

        def back_second(first, span):
            begin = pl.multiple_of(first * chan_part, LANES)
            weights = lanes_cat([w2[t, pl.ds(begin, 2 * chan_part), :] for t in range(9)])
            value = mm(dd[span, :], weights, 1, 1).astype(bf16)
            hp[first, span, :] = value[:, :chan_part]
            hp[first + 1, span, :] = value[:, chan_part:]

        slot_h = [net.slot(3) for _ in row_halves]
        for span, slot in zip(row_halves, slot_h):
            back_second(2 * (k2 // 2), span)
            net.send(hp.at[k3, span], hr1.at[1, span], slot + 1, (i, k1))
        for span, slot in zip(row_halves, slot_h):
            net.arrived(hr1.at[1, span], slot + 1, (i, k1))
            hs[span, :] = (hp[k2, span, :].astype(f32) + hr1[1, span, :].astype(f32)).astype(bf16)
            net.send(hs.at[span], hr2.at[span], slot + 2, (i, k2))
        back_second(2 * (k // 2), slice(0, rows))
        for span, slot in zip(row_halves, slot_h):
            net.send(hp.at[k1, span], hr1.at[0, span], slot, (i, k1))

        acts = [
            lanes_cat([flat(a1[g][q, 1 : 1 + halves[g], 1 : 1 + halves[g]]) for q in range(4)])
            for g in range(2)
        ]
        sum2 = Reduce(net, i, k, wg2, (p21, p22, p23, p24, p25), cols2)
        for w, cols in enumerate(cols2):
            value = mm(acts[0], dd[: sizes[0], cols], 0, 0) + mm(acts[1], dd[sizes[0] :, cols], 0, 0)
            wg2[:, :, :, :, cols] = value.astype(bf16).reshape(2, 2, 2, out_rows, value.shape[1])
            sum2.first(w)
        for g, r, begin, count in chunks:
            span = slice(begin, begin + count)
            value = ksg * (up[span, :] - valid[span, :] * (db + zs[span, :] * dgs))
            dzsr[span, :] = value.astype(bf16)
        acc = zeros(2)
        for n, (span, slot) in enumerate(zip(row_halves, slot_h)):
            net.arrived(hr1.at[0, span], slot, (i, k1))
            net.arrived(hr2.at[span], slot + 2, (i, k2))
            for begin in range(span.start, span.stop, 16):
                part = slice(begin, begin + 16)
                hat = z1[part, :]
                v = hat * gain1 + shift1
                sig = sigma(v)
                grad = hp[k, part, :].astype(f32) + hr1[0, part, :].astype(f32) + hr2[part, :].astype(f32)
                grad = grad * valid[part, :] * (sig * (1.0 + v * (1.0 - sig)))
                gu[part, :] = grad
                acc = [acc[0] + rowsum(grad), acc[1] + rowsum(grad * hat)]
        first = share(3, message(acc))
        sum2.second(0)
        tot = total(3, first)
        sum_head, sum_gain1 = tot[0:1], tot[1:2]

        def close_second():
            for w, cols in enumerate(cols2):
                value = sum2.last(w)
                for t in range(cols.start // LANES, cols.stop // LANES):
                    gw2[t] = value[:, t * LANES - cols.start : (t + 1) * LANES - cols.start]

        if stop == 8:
            valid[0:1, :] = sum_head
            sum2.second(1)
            for w in range(2):
                sum2.third(w)
            close_second()
            return net.drain()
        k1g = gain1 * sc1
        db, dg1 = sum_head * inv_pop, sum_gain1 * inv_pop
        for g, r, begin, count in chunks:
            span = slice(begin, begin + count)
            value = k1g * (gu[span, :] - valid[span, :] * (db + z1[span, :] * dg1))
            d1[g][r, : halves[g]] = value.astype(bf16).reshape(halves[g], images[g], chan_part)

        def back_patch(pieces, p):
            parts = []
            for g, r0, r1 in pieces:
                width = halves[g] * images[g]
                taps = [
                    flat(d1[g][r0 + (a == 0) : r1 + (a == 0), (b == 0) : (b == 0) + halves[g]])
                    for a, b in PLANE_TAPS[p]
                ]
                if p == 0:
                    taps.append(dzsr[starts[g] + r0 * width : starts[g] + r1 * width, :])
                parts.append(lanes_cat(taps))
            return jnp.concatenate(parts, axis=0) if len(parts) > 1 else parts[0]

        slot_g = [net.slot(3) for _ in range(n_parts)]

        def back_first(c):
            a, b = spans[c]
            planes = []
            for p in range(4):
                weights = [w1[3 * ta + tb] for ta, tb in PLANE_TAPS[p]]
                if p == 0:
                    weights.append(ws[...])
                planes.append(mm(back_patch(pieces[c], p), lanes_cat(weights), 1, 1))
            for g, r, begin, count in part_chunks[c]:
                values = [
                    v[begin - a : begin - a + count].reshape(halves[g], images[g], chan_in)
                    for v in planes
                ]
                for q, value in enumerate(planes_of(values, g)):
                    gp[q, begin : begin + count, :] = flat(value).astype(bf16)
            net.send(gp.at[k3, a:b], gr1.at[1, a:b], slot_g[c] + 1, (i, k1))
            net.send(gp.at[k1, a:b], gr1.at[0, a:b], slot_g[c], (i, k1))

        def back_cross(c):
            a, b = spans[c]
            net.arrived(gr1.at[1, a:b], slot_g[c] + 1, (i, k1))
            for begin in range(a, b, 16):
                span = slice(begin, begin + 16)
                value = gp[k2, span, :].astype(f32) + gr1[1, span, :].astype(f32)
                gsum[span, :] = value.astype(bf16)
            net.send(gsum.at[a:b], gr2.at[a:b], slot_g[c] + 2, (i, k2))

        slot_o = [net.slot(n_dp) for _ in range(n_parts)]

        def back_out(c):
            a, b = spans[c]
            net.arrived(gr1.at[0, a:b], slot_g[c], (i, k1))
            net.arrived(gr2.at[a:b], slot_g[c] + 2, (i, k2))
            for begin in range(a, b, 16):
                span = slice(begin, begin + 16)
                value = gp[k, span, :].astype(f32) + gr1[0, span, :].astype(f32)
                zt[span, :] = (value + gr2[span, :].astype(f32)).astype(bf16)
            cols = slice(c * step, (c + 1) * step)
            a, b = out_win[c]
            value = mm(zt[a:b, :], cells[a:b, cols], 0, 0).astype(bf16)
            gt[:, :, cols] = value.reshape(n_dp, in_local, step)
            for d in range(1, n_dp):
                j = (i + d) % n_dp
                net.send(gt.at[j, :, cols], gr.at[i, :, cols], slot_o[c] + i, (j, k))

        sum1 = Reduce(net, i, k, wg1, (p11, p12, p13, p14, p15), cols1)

        def weight_first():
            everything = [(0, 0, halves[0]), (1, 0, halves[1])]
            blocks = []
            for p in range(4):
                value = 0.0
                for g, r0, r1 in everything:
                    cell = flat(zp[g][p, 1 : 1 + halves[g], 1 : 1 + halves[g]])
                    value = value + mm(cell, back_patch([(g, r0, r1)], p), 0, 0)
                blocks.append(value.astype(bf16))
            wg1[...] = lanes_cat(blocks).reshape(2, 2, 2, in_local, 10 * LANES)
            sum1.first(0)

        order = list(reversed(range(n_parts)))
        for n, c in enumerate(order):
            back_first(c)
            if n >= 1:
                back_cross(order[n - 1])
        back_cross(order[-1])
        weight_first()
        sum2.second(1)
        sum2.third(0)
        for n, c in enumerate(order):
            back_out(c)
            if n == 0:
                sum2.third(1)
            if n == 1:
                sum1.second(0)
        sum1.third(0)
        own = pltpu.make_async_copy(gt.at[i], gr.at[i], lsem.at[len(pairs_of)])
        own.start()
        close_second()
        value = sum1.last(0)
        for t, tap in enumerate(TAPS):
            place = ORDER.index(tap)
            place = place + (place > 0)
            gw1[t] = value[:, place * LANES : (place + 1) * LANES]
        gws[...] = value[:, LANES : 2 * LANES]
        vecs[...] = message([sum_gain1, sum_head, sum_gain2, sum_tail, sum_gains])
        for c in range(n_parts):
            cols = slice(c * step, (c + 1) * step)
            for d in range(1, n_dp):
                j = (i + d) % n_dp
                net.arrived(gr.at[j, :, cols], slot_o[c] + j, (j, k))
        own.wait()
        net.drain()

    V = pltpu.VMEM
    pads = [(h + 2, h + 2, n, chan_part) for h, n in zip(halves, images)]
    half_pads = [(h + 1, h + 1, n) for h, n in zip(halves, images)]

    def ladder(count, width):
        return [
            V((2, 2, 2, count, width), bf16), V((2, 2, count, width), bf16), V((2, 2, count, width), bf16),
            V((2, count, width), bf16), V((2, count, width), bf16), V((count, width), bf16),
        ]

    inputs = [
        V((in_local, n_dp * 4 * qlanes[0]), bf16), V((in_local, n_dp * 4 * qlanes[1]), bf16),
        V((4, images[0]), jnp.int32), V((4, images[1]), jnp.int32),
        V((9, chan_in, chan_part), bf16), V((9, chan_full, chan_part), bf16), V((chan_in, chan_part), bf16),
    ] + [V((1, chan_part), f32)] * 6 + [
        V((sizes[0], chan_part), bf16), V((sizes[1], chan_part), bf16),
    ]
    scratch = inputs + [
        V((rows, slab_lanes), bf16),
        V((n_dp * in_local, slab_lanes), bf16),
        V((n_dp, in_local, slab_lanes), bf16),
        V((n_dp, in_local, slab_lanes), bf16),
        V((4, rows, chan_in), bf16),
        V((4,) + half_pads[0] + (chan_in,), bf16),
        V((4,) + half_pads[1] + (chan_in,), bf16),
        V((rows, LANES), f32),
        V((rows, chan_part), f32),
        V((rows, chan_part), f32),
        V((4,) + pads[0], bf16),
        V((4,) + pads[1], bf16),
        V((4, n_dp, 8, LANES), f32),
        V((rows, chan_part), f32),
        V((rows, chan_part), f32),
        V((rows, chan_part), f32),
        V(pads[0], bf16),
        V(pads[1], bf16),
        V((rows, chan_part), bf16),
        V((rows, 9 * chan_part), bf16),
        V((4, rows, chan_part), bf16),
        V((2, rows, chan_part), bf16),
        V((rows, chan_part), bf16),
        V((rows, chan_part), bf16),
        V((rows, chan_part), f32),
        V(half_pads[0] + (chan_part,), bf16),
        V(half_pads[1] + (chan_part,), bf16),
    ]
    scratch += ladder(out_rows, 9 * LANES) + ladder(in_local, 10 * LANES)
    scratch += [
        V((4, rows, chan_in), bf16),
        V((2, rows, chan_in), bf16),
        V((rows, chan_in), bf16),
        V((rows, chan_in), bf16),
        V((rows, chan_in), bf16),
        V((n_dp, in_local, slab_lanes), bf16),
        pltpu.SemaphoreType.DMA((len(inputs) + 1,)),
        pltpu.SemaphoreType.DMA((160,)),
        pltpu.SemaphoreType.DMA((160,)),
    ]
    mid_outs = [
        jax.ShapeDtypeStruct((sizes[0], chan_part), bf16),
        jax.ShapeDtypeStruct((sizes[1], chan_part), bf16),
        jax.ShapeDtypeStruct((n_dp, in_local, slab_lanes), bf16),
        jax.ShapeDtypeStruct((9, in_local, LANES), f32),
        jax.ShapeDtypeStruct((in_local, LANES), f32),
        jax.ShapeDtypeStruct((9, out_rows, LANES), f32),
        jax.ShapeDtypeStruct((8, LANES), f32),
    ]
    vmem = pl.BlockSpec(memory_space=pltpu.VMEM)
    hbm = pl.BlockSpec(memory_space=pl.ANY)
    main = pl.pallas_call(
        kernel,
        out_shape=mid_outs,
        in_specs=[hbm] * len(inputs),
        out_specs=[vmem, vmem, hbm, vmem, vmem, vmem, vmem],
        scratch_shapes=scratch,
        compiler_params=pltpu.CompilerParams(
            collective_id=1, has_side_effects=True, vmem_limit_bytes=60 * 2**20
        ),
        name="block",
    )

    def closing(oa_h, ob_h, gr_h, gw1_h, gws_h, gw2_h, vecs_h, turn_h,
                fa, fb, ia, ib, f1, f2, fs, c1, h1, c2, h2, cs, hs,
                oa, ob, gr, gw1, gws, gw2, vecs, turn, sems):
        moves = [
            pltpu.make_async_copy(source, target, sems.at[index])
            for index, (source, target) in enumerate(
                (
                    (gr_h, gr), (turn_h, turn), (vecs_h, vecs), (gw2_h, gw2), (gw1_h, gw1),
                    (oa_h, oa), (ob_h, ob), (gws_h, gws),
                )
            )
        ]
        outs = [
            pltpu.make_async_copy(source, target, sems.at[len(moves) + index])
            for index, (source, target) in enumerate(
                ((gw2, f2), (gw1, f1), (oa, fa), (ob, fb), (gws, fs))
            )
        ]
        for move in moves:
            move.start()
        for move in moves[:3]:
            move.wait()
        for move, out in zip(moves[3:], outs):
            move.wait()
            out.start()
        moved = mm(turn[...], gr[...].reshape(n_dp * in_local, slab_lanes), 1, 0)
        natural = regroup(moved, back_runs)
        ia[...] = natural[:, : qlanes[0]].reshape(in_local, n_dp, qlanes[0]).astype(bf16)
        tail = natural[:, qlanes[0] : qlanes[0] + qlanes[1]]
        ib[...] = tail.reshape(in_local, n_dp, qlanes[1]).astype(bf16)
        for ref, row in ((c1, 0), (h1, 1), (c2, 2), (h2, 3), (cs, 4), (hs, 3)):
            ref[...] = vecs[row : row + 1, :]
        for out in outs:
            out.wait()

    last = pl.pallas_call(
        closing,
        out_shape=[
            jax.ShapeDtypeStruct((sizes[0], chan_part), bf16),
            jax.ShapeDtypeStruct((sizes[1], chan_part), bf16),
            jax.ShapeDtypeStruct((in_local, n_dp, qlanes[0]), bf16),
            jax.ShapeDtypeStruct((in_local, n_dp, qlanes[1]), bf16),
            jax.ShapeDtypeStruct((9, in_local, LANES), f32),
            jax.ShapeDtypeStruct((9, out_rows, LANES), f32),
            jax.ShapeDtypeStruct((in_local, LANES), f32),
        ]
        + [jax.ShapeDtypeStruct((1, LANES), f32)] * 6,
        in_specs=[hbm] * 8,
        out_specs=[hbm, hbm, vmem, vmem, hbm, hbm, hbm] + [vmem] * 6,
        scratch_shapes=[V(o.shape, o.dtype) for o in mid_outs]
        + [V((n_dp * in_local, n_dp * in_local), bf16), pltpu.SemaphoreType.DMA((13,))],
        compiler_params=pltpu.CompilerParams(vmem_limit_bytes=60 * 2**20),
        name="closing",
    )
    total_rows = n_dp * in_local
    turn = np.zeros((total_rows, total_rows), np.float32)
    for c in range(in_local):
        for j in range(n_dp):
            turn[c * n_dp + j, j * in_local + c] = 1.0
    return main, last, turn.astype(jnp.bfloat16)


STOP = 99


def fused_body(
    input_a, input_b, boxes_a, boxes_b, weight_first, weight_second, weight_short,
    gain_first, shift_first, gain_second, shift_second, gain_short, shift_short,
    upstream_a, upstream_b,
):
    n_dp = lax.axis_size("dp")
    chan_part = weight_first.shape[2]
    in_local = input_a.shape[0]
    main, last, turn = make_fused(
        n_dp, in_local, (boxes_a.shape[0], boxes_b.shape[0]), (SA, SB),
        weight_first.shape[1], chan_part, STOP,
    )
    vectors = [
        v.reshape(1, chan_part)
        for v in (gain_first, shift_first, gain_second, shift_second, gain_short, shift_short)
    ]
    mid = main(
        input_a, input_b, boxes_a.T, boxes_b.T, weight_first, weight_second, weight_short,
        *vectors, upstream_a.T, upstream_b.T,
    )
    res = last(*mid, turn)
    return (
        res[0].T, res[1].T,
        res[2].reshape(in_local, n_dp, 1, -1), res[3].reshape(in_local, n_dp, 1, -1),
        res[4], res[5], res[6],
    ) + tuple(v.reshape(chan_part) for v in res[7:])


def choose_body(mesh):
    return fused_body if mesh.shape["dp"] == 8 and mesh.shape["chan"] == 4 else plain_body


def solution(mesh):
    placed = (
        P("dp", None),
        P("dp", None),
        P("dp", None),
        P("dp", None),
        P(None, None, "chan"),
        P(None, None, "chan"),
        P(None, "chan"),
        P("chan"),
        P("chan"),
        P("chan"),
        P("chan"),
        P("chan"),
        P("chan"),
        P("chan", "dp"),
        P("chan", "dp"),
    )
    return jax.shard_map(
        choose_body(mesh),
        mesh=mesh,
        in_specs=placed,
        out_specs=(
            P("chan", "dp"),
            P("chan", "dp"),
            P("dp", None, "chan", None),
            P("dp", None, "chan", None),
            P(None, "dp", "chan"),
            P(None, "dp", "chan"),
            P("dp", "chan"),
            P("chan"),
            P("chan"),
            P("chan"),
            P("chan"),
            P("chan"),
            P("chan"),
        ),
        check_vma=False,
    )
```

```python
import jax
import jax.numpy as jnp
from jax import lax
import numpy as np
from jax.experimental import pallas as pl
from jax.experimental.pallas import tpu as pltpu
from jax.sharding import PartitionSpec as P

SA = 14
SB = 6


epsilon = 1e-05


def box_mask(box_rows, extent):
    positions = jnp.arange(extent, dtype=jnp.int32)[None, :]
    row_inside = (positions >= box_rows[:, 0:1]) & (positions < box_rows[:, 0:1] + box_rows[:, 2:3])
    col_inside = (positions >= box_rows[:, 1:2]) & (positions < box_rows[:, 1:2] + box_rows[:, 3:4])
    return (row_inside[:, :, None] & col_inside[:, None, :]).astype(jnp.float32)


def taps_strided(feature, image_count, extent):
    channels = feature.shape[0]
    output_side = extent // 2
    padded = jnp.pad(
        feature.reshape(channels, image_count, extent, extent), ((0, 0), (0, 0), (1, 1), (1, 1))
    )
    pieces = [
        padded[:, :, tap_row : tap_row + extent : 2, tap_col : tap_col + extent : 2]
        for tap_row in range(3)
        for tap_col in range(3)
    ]
    return jnp.stack(pieces, axis=0).reshape(9 * channels, image_count * output_side * output_side)


def taps_plain(feature, image_count, extent):
    channels = feature.shape[0]
    padded = jnp.pad(
        feature.reshape(channels, image_count, extent, extent), ((0, 0), (0, 0), (1, 1), (1, 1))
    )
    pieces = [
        padded[:, :, tap_row : tap_row + extent, tap_col : tap_col + extent]
        for tap_row in range(3)
        for tap_col in range(3)
    ]
    return jnp.stack(pieces, axis=0).reshape(9 * channels, image_count * extent * extent)


def untaps_plain(columns, channels, image_count, extent):
    pieces = columns.reshape(9, channels, image_count, extent, extent)
    running = jnp.zeros((channels, image_count, extent + 2, extent + 2), jnp.float32)
    for tap_row in range(3):
        for tap_col in range(3):
            running = running + jnp.pad(
                pieces[3 * tap_row + tap_col],
                ((0, 0), (0, 0), (tap_row, 2 - tap_row), (tap_col, 2 - tap_col)),
            )
    return running[:, :, 1:-1, 1:-1].reshape(channels, image_count * extent * extent)


def untaps_strided(columns, shortcut, channels, image_count, extent):
    output_side = extent // 2
    pieces = columns.reshape(9, channels, image_count, output_side, output_side)
    parity_sums = {}
    for tap_row in range(3):
        for tap_col in range(3):
            block_row = tap_row // 2
            block_col = tap_col // 2
            placed = jnp.pad(
                pieces[3 * tap_row + tap_col],
                ((0, 0), (0, 0), (block_row, 1 - block_row), (block_col, 1 - block_col)),
            )
            parity = (tap_row % 2, tap_col % 2)
            parity_sums[parity] = (
                placed if parity not in parity_sums else parity_sums[parity] + placed
            )
    direct = jnp.pad(
        shortcut.reshape(channels, image_count, output_side, output_side),
        ((0, 0), (0, 0), (0, 1), (0, 1)),
    )
    parity_sums[1, 1] = parity_sums[1, 1] + direct
    rows_even = jnp.stack([parity_sums[0, 0], parity_sums[0, 1]], axis=-1)
    rows_odd = jnp.stack([parity_sums[1, 0], parity_sums[1, 1]], axis=-1)
    padded = jnp.stack([rows_even, rows_odd], axis=3).reshape(
        channels, image_count, extent + 2, extent + 2
    )
    return padded[:, :, 1:-1, 1:-1].reshape(channels, image_count * extent * extent)


def contract_first(weights, columns):
    return lax.dot_general(
        weights, columns, (((0,), (0,)), ((), ())), preferred_element_type=jnp.float32
    )


def weight_product(columns, gradient):
    return lax.dot_general(
        columns, gradient, (((1,), (1,)), ((), ())), preferred_element_type=jnp.float32
    )


def swish_slope(values):
    logistic = jax.nn.sigmoid(values)
    return logistic * (1.0 + values * (1.0 - logistic))


def moments(values, valid_list):
    running = 0.0
    squares = 0.0
    for tensor, valid in zip(values, valid_list):
        widened = tensor.astype(jnp.float32)
        running = running + jnp.sum(widened * valid, axis=1)
        squares = squares + jnp.sum(widened * widened * valid, axis=1)
    return (running, squares)


def standardize(values, running, squares, population):
    mean_value = running / population
    variance = squares / population - mean_value * mean_value
    scaling = lax.rsqrt(variance + epsilon)
    return (
        [
            (tensor.astype(jnp.float32) - mean_value[:, None]) * scaling[:, None]
            for tensor in values
        ],
        scaling,
    )


def norm_back(gradient, normed, valid, scaling, gain_values, shift_sum, gain_sum, population):
    return (gain_values * scaling)[:, None] * (
        gradient - valid * (shift_sum[:, None] + normed * gain_sum[:, None]) / population
    )


def plain_body(
    input_a,
    input_b,
    boxes_a,
    boxes_b,
    weight_first,
    weight_second,
    weight_short,
    gain_first,
    shift_first,
    gain_second,
    shift_second,
    gain_short,
    shift_short,
    upstream_a,
    upstream_b,
):
    image_groups = lax.axis_size("dp")
    in_local = input_a.shape[0]
    chan_in = weight_first.shape[1]
    chan_part = weight_first.shape[2]
    chan_full = weight_second.shape[1]
    image_counts = (boxes_a.shape[0], boxes_b.shape[0])
    extents = (SA, SB)
    whole_a, whole_b = (
        lax.all_to_all(
            input_a.reshape(in_local, image_groups, -1),
            "dp",
            split_axis=1,
            concat_axis=0,
            tiled=True,
        ),
        lax.all_to_all(
            input_b.reshape(in_local, image_groups, -1),
            "dp",
            split_axis=1,
            concat_axis=0,
            tiled=True,
        ),
    )
    features = (whole_a.reshape(chan_in, -1), whole_b.reshape(chan_in, -1))
    valid_list = (
        box_mask(boxes_a, SA // 2).reshape(1, -1),
        box_mask(boxes_b, SB // 2).reshape(1, -1),
    )
    first_mat = weight_first.reshape(9 * chan_in, chan_part)
    second_mat = weight_second.reshape(9 * chan_full, chan_part)
    first_cols = []
    sampled = []
    first_z = []
    short_z = []
    for feature, image_count, extent in zip(features, image_counts, extents):
        columns = taps_strided(feature, image_count, extent)
        picked = feature.reshape(chan_in, image_count, extent, extent)[:, :, ::2, ::2].reshape(
            chan_in, -1
        )
        first_cols.append(columns)
        sampled.append(picked)
        first_z.append(contract_first(first_mat, columns).astype(jnp.bfloat16))
        short_z.append(contract_first(weight_short, picked).astype(jnp.bfloat16))
    sum_first, square_first = moments(first_z, valid_list)
    sum_short, square_short = moments(short_z, valid_list)
    population = jnp.sum(valid_list[0]) + jnp.sum(valid_list[1])
    sum_first, square_first, sum_short, square_short, population = lax.psum(
        (sum_first, square_first, sum_short, square_short, population), "dp"
    )
    normed_first, scaling_first = standardize(first_z, sum_first, square_first, population)
    normed_short, scaling_short = standardize(short_z, sum_short, square_short, population)
    before_first = [normed * gain_first[:, None] + shift_first[:, None] for normed in normed_first]
    outgoing_a = (jax.nn.silu(before_first[0]) * valid_list[0]).astype(jnp.bfloat16)
    outgoing_b = (jax.nn.silu(before_first[1]) * valid_list[1]).astype(jnp.bfloat16)
    gathered_a, gathered_b = (
        lax.all_gather(outgoing_a, "chan", axis=0, tiled=True),
        lax.all_gather(outgoing_b, "chan", axis=0, tiled=True),
    )
    second_cols = []
    second_z = []
    for gathered, image_count, extent in zip((gathered_a, gathered_b), image_counts, extents):
        columns = taps_plain(gathered, image_count, extent // 2)
        second_cols.append(columns)
        second_z.append(contract_first(second_mat, columns).astype(jnp.bfloat16))
    sum_second, square_second = moments(second_z, valid_list)
    sum_second, square_second = lax.psum((sum_second, square_second), "dp")
    normed_second, scaling_second = standardize(second_z, sum_second, square_second, population)
    summed_pre = [
        main_part * gain_second[:, None]
        + shift_second[:, None]
        + side_part * gain_short[:, None]
        + shift_short[:, None]
        for main_part, side_part in zip(normed_second, normed_short)
    ]
    outputs = [
        (jax.nn.silu(tensor) * valid).astype(jnp.bfloat16)
        for tensor, valid in zip(summed_pre, valid_list)
    ]
    tail_grads = [
        upstream.astype(jnp.float32) * valid * swish_slope(tensor)
        for upstream, valid, tensor in zip((upstream_a, upstream_b), valid_list, summed_pre)
    ]
    shift_tail = sum((jnp.sum(gradient, axis=1) for gradient in tail_grads))
    gain_tail = sum(
        (jnp.sum(gradient * normed, axis=1) for gradient, normed in zip(tail_grads, normed_second))
    )
    gain_side = sum(
        (jnp.sum(gradient * normed, axis=1) for gradient, normed in zip(tail_grads, normed_short))
    )
    shift_tail, gain_tail, gain_side = lax.psum((shift_tail, gain_tail, gain_side), "dp")
    grad_second_local = 0.0
    partial_hidden = []
    short_dz = []
    for index_group in range(2):
        valid = valid_list[index_group]
        dz_second = norm_back(
            tail_grads[index_group],
            normed_second[index_group],
            valid,
            scaling_second,
            gain_second,
            shift_tail,
            gain_tail,
            population,
        ).astype(jnp.bfloat16)
        dz_short = norm_back(
            tail_grads[index_group],
            normed_short[index_group],
            valid,
            scaling_short,
            gain_short,
            shift_tail,
            gain_side,
            population,
        ).astype(jnp.bfloat16)
        short_dz.append(dz_short)
        grad_second_local = grad_second_local + weight_product(second_cols[index_group], dz_second)
        back_cols = jnp.dot(second_mat, dz_second, preferred_element_type=jnp.float32)
        partial_hidden.append(
            untaps_plain(back_cols, chan_full, image_counts[index_group], extents[index_group] // 2)
        )
    hidden_a, hidden_b = (
        lax.psum_scatter(
            partial_hidden[0].astype(jnp.bfloat16), "chan", scatter_dimension=0, tiled=True
        ).astype(jnp.float32),
        lax.psum_scatter(
            partial_hidden[1].astype(jnp.bfloat16), "chan", scatter_dimension=0, tiled=True
        ).astype(jnp.float32),
    )
    head_grads = [
        hidden * valid * swish_slope(tensor)
        for hidden, valid, tensor in zip((hidden_a, hidden_b), valid_list, before_first)
    ]
    shift_head = sum((jnp.sum(gradient, axis=1) for gradient in head_grads))
    gain_head = sum(
        (jnp.sum(gradient * normed, axis=1) for gradient, normed in zip(head_grads, normed_first))
    )
    shift_head, gain_head = lax.psum((shift_head, gain_head), "dp")
    grad_first_local = 0.0
    grad_short_local = 0.0
    partial_inputs = []
    for index_group in range(2):
        valid = valid_list[index_group]
        dz_first = norm_back(
            head_grads[index_group],
            normed_first[index_group],
            valid,
            scaling_first,
            gain_first,
            shift_head,
            gain_head,
            population,
        ).astype(jnp.bfloat16)
        grad_first_local = grad_first_local + weight_product(first_cols[index_group], dz_first)
        grad_short_local = grad_short_local + weight_product(
            sampled[index_group], short_dz[index_group]
        )
        back_cols = jnp.dot(first_mat, dz_first, preferred_element_type=jnp.float32)
        back_short = jnp.dot(
            weight_short, short_dz[index_group], preferred_element_type=jnp.float32
        )
        flat_input = untaps_strided(
            back_cols, back_short, chan_in, image_counts[index_group], extents[index_group]
        )
        partial_inputs.append(flat_input.reshape(chan_in, 1, lax.axis_size("chan"), -1))
    arrived_a, arrived_b = (
        lax.all_to_all(
            partial_inputs[0].astype(jnp.bfloat16), "dp", split_axis=0, concat_axis=1, tiled=True
        ).astype(jnp.float32),
        lax.all_to_all(
            partial_inputs[1].astype(jnp.bfloat16), "dp", split_axis=0, concat_axis=1, tiled=True
        ).astype(jnp.float32),
    )
    summed_a, summed_b = (
        lax.psum_scatter(
            arrived_a.astype(jnp.bfloat16), "chan", scatter_dimension=2, tiled=True
        ).astype(jnp.float32),
        lax.psum_scatter(
            arrived_b.astype(jnp.bfloat16), "chan", scatter_dimension=2, tiled=True
        ).astype(jnp.float32),
    )
    grad_input_a = summed_a.astype(jnp.bfloat16)
    grad_input_b = summed_b.astype(jnp.bfloat16)
    grad_first_local = grad_first_local.reshape(9, chan_in, chan_part)
    grad_second_local = grad_second_local.reshape(9, chan_full, chan_part)
    total_first, total_second, total_short = lax.psum(
        (grad_first_local, grad_second_local, grad_short_local), "dp"
    )
    position = lax.axis_index("dp")
    rows_first = chan_in // image_groups
    rows_second = chan_full // image_groups
    grad_first = lax.dynamic_slice_in_dim(total_first, position * rows_first, rows_first, 1)
    grad_second = lax.dynamic_slice_in_dim(total_second, position * rows_second, rows_second, 1)
    grad_short = lax.dynamic_slice_in_dim(total_short, position * rows_first, rows_first, 0)
    return (
        outputs[0],
        outputs[1],
        grad_input_a,
        grad_input_b,
        grad_first,
        grad_second,
        grad_short,
        gain_head,
        shift_head,
        gain_tail,
        shift_tail,
        gain_side,
        shift_tail,
    )


MESH = pl.DeviceIdType.MESH
TAPS = tuple((a, b) for a in range(3) for b in range(3))
PLANE_TAPS = (
    ((1, 1),),
    ((1, 0), (1, 2)),
    ((0, 1), (2, 1)),
    ((0, 0), (0, 2), (2, 0), (2, 2)),
)
ORDER = [tap for taps in PLANE_TAPS for tap in taps]
LANES = 128


class Links:
    def __init__(self, send_sems, recv_sems):
        self.send_sems, self.recv_sems = send_sems, recv_sems
        self.sends = self.slots = 0
        self.open = []

    def slot(self, count=1):
        first = self.slots
        self.slots += count
        return first

    def send(self, source, target, slot, where):
        copy = pltpu.make_async_remote_copy(
            source, target, self.send_sems.at[self.sends], self.recv_sems.at[slot],
            device_id=where, device_id_type=MESH,
        )
        self.sends += 1
        copy.start()
        self.open.append(copy)

    def arrived(self, target, slot, where):
        pltpu.make_async_remote_copy(
            target, target, self.send_sems.at[0], self.recv_sems.at[slot],
            device_id=where, device_id_type=MESH,
        ).wait_recv()

    def drain(self):
        for copy in self.open:
            copy.wait_send()


def mm(a, b, ca, cb):
    return lax.dot_general(a, b, (((ca,), (cb,)), ((), ())), preferred_element_type=jnp.float32)


def lanes_cat(parts):
    return jnp.concatenate(parts, axis=1) if len(parts) > 1 else parts[0]


def quarter_matrices(images, sides, segments, seg_lane, seg_row, q_rows, lanes):
    def lane(g, image, row, col):
        for (seg_g, r0, r1), first in zip(segments, seg_lane):
            if seg_g == g and 2 * r0 <= row < 2 * r1:
                return first + (image * 2 * (r1 - r0) + row - 2 * r0) * sides[g] + col

    taps = np.zeros((9, q_rows, lanes), np.float32)
    for (g, r0, r1), first in zip(segments, seg_row):
        half = sides[g] // 2
        for r in range(r0, r1):
            for s in range(half):
                for image in range(images[g]):
                    target = first + ((r - r0) * half + s) * images[g] + image
                    for t, (a, b) in enumerate(TAPS):
                        row, col = 2 * r + a - 1, 2 * s + b - 1
                        if row >= 0 and col >= 0:
                            taps[t, target, lane(g, image, row, col)] = 1.0
    sizes = [n * side * side for n, side in zip(images, sides)]
    cells = np.zeros((sum(sizes), lanes), np.float32)
    for g, (n, side) in enumerate(zip(images, sides)):
        for image in range(n):
            for row in range(side):
                for col in range(side):
                    cell = (row // 2) * (side // 2) + col // 2
                    target = g * sizes[0] + (cell * 4 + 2 * (row % 2) + col % 2) * n + image
                    cells[target, lane(g, image, row, col)] = 1.0
    return taps, cells


def regroup(value, runs):
    return jnp.concatenate([value[:, a:b] for a, b in runs], axis=1)


def sigma(v):
    return 0.5 * jnp.tanh(0.5 * v) + 0.5


class Reduce:
    def __init__(self, net, i, k, part, bufs, windows):
        self.net, self.part, self.windows = net, part, windows
        self.b1, self.s1, self.b2, self.s2, self.b3 = bufs
        self.ix, self.pz, self.hz = i % 2, (i // 2) % 2, i // 4
        self.peers = (
            (i + 1 - 2 * self.ix, k),
            (i + 2 - 4 * self.pz, k),
            (i + 4 - 8 * self.hz, k),
        )
        self.slots = [net.slot(3) for _ in windows]

    def first(self, w):
        cols = self.windows[w]
        self.net.send(
            self.part.at[:, :, 1 - self.ix, :, cols], self.b1.at[:, :, :, cols],
            self.slots[w], self.peers[0],
        )

    def second(self, w):
        cols = self.windows[w]
        self.net.arrived(self.b1.at[:, :, :, cols], self.slots[w], self.peers[0])
        for h in range(2):
            for p in range(2):
                value = self.part[h, p, self.ix, :, cols].astype(jnp.float32)
                value = value + self.b1[h, p, :, cols].astype(jnp.float32)
                self.s1[h, p, :, cols] = value.astype(jnp.bfloat16)
        self.net.send(
            self.s1.at[:, 1 - self.pz, :, cols], self.b2.at[:, :, cols],
            self.slots[w] + 1, self.peers[1],
        )

    def third(self, w):
        cols = self.windows[w]
        self.net.arrived(self.b2.at[:, :, cols], self.slots[w] + 1, self.peers[1])
        for h in range(2):
            value = self.s1[h, self.pz, :, cols].astype(jnp.float32)
            value = value + self.b2[h, :, cols].astype(jnp.float32)
            self.s2[h, :, cols] = value.astype(jnp.bfloat16)
        self.net.send(
            self.s2.at[1 - self.hz, :, cols], self.b3.at[:, cols],
            self.slots[w] + 2, self.peers[2],
        )

    def last(self, w):
        cols = self.windows[w]
        self.net.arrived(self.b3.at[:, cols], self.slots[w] + 2, self.peers[2])
        return self.s2[self.hz, :, cols].astype(jnp.float32) + self.b3[:, cols].astype(jnp.float32)


def make_fused(n_dp, in_local, images, sides, chan_in, chan_part, stop):
    f32, bf16 = jnp.float32, jnp.bfloat16
    halves = tuple(side // 2 for side in sides)
    sizes = tuple(h * h * n for h, n in zip(halves, images))
    rows = sum(sizes)
    quarter = tuple(n // 4 for n in images)
    qlanes = tuple(q * side * side for q, side in zip(quarter, sides))
    slab_lanes = -(-sum(qlanes) // LANES) * LANES
    chan_full = 4 * chan_part
    out_rows = chan_full // n_dp
    starts = (0, sizes[0])
    widths = tuple(h * n for h, n in zip(halves, images))
    chunks = [(g, r, starts[g] + r * widths[g], widths[g]) for g in range(2) for r in range(halves[g])]
    win = [-(-q // LANES) * LANES for q in qlanes]
    b_tile = qlanes[0] // LANES * LANES
    b_skip = qlanes[0] - b_tile
    rs = halves[0] // 2
    segments = [(1, 0, halves[1]), (0, 0, rs), (0, rs, halves[0])]
    seg_lane, runs = [], []
    lane_of = 0
    for g, r0, r1 in segments:
        side, base = sides[g], (0, qlanes[0])[g]
        seg_lane.append(lane_of)
        lane_of += quarter[g] * 2 * (r1 - r0) * side
        runs += [
            (base + (image * side + 2 * r0) * side, base + (image * side + 2 * r1) * side)
            for image in range(quarter[g])
        ]
    runs.append((sum(qlanes), slab_lanes))
    at, order = 0, []
    for a, b in runs:
        order.append((a, at, at + b - a))
        at += b - a
    back_runs = [(a, b) for _, a, b in sorted(order)]
    cut_lane = -(-seg_lane[2] // LANES) * LANES
    lane_parts = (slice(0, cut_lane), slice(cut_lane, slab_lanes))
    seg_cells = [(r1 - r0) * halves[g] for g, r0, r1 in segments]
    seg_rows = [cells * quarter[seg[0]] for cells, seg in zip(seg_cells, segments)]
    top = -(-(seg_rows[0] + seg_rows[1]) // 16) * 16
    seg_row = [0, seg_rows[0], top]
    q_rows = top + -(-seg_rows[2] // 16) * 16
    row_parts = (slice(0, top), slice(top, q_rows))
    patch_win = (slice(0, cut_lane), slice(seg_lane[1] // LANES * LANES, slab_lanes))
    patch_m, cells_m = quarter_matrices(
        quarter, sides, segments, seg_lane, seg_row, q_rows, slab_lanes
    )
    patch_ms = [
        np.concatenate([m[rows_, lanes_] for m in patch_m], axis=0)
        for rows_, lanes_ in zip(row_parts, patch_win)
    ]
    spans = [
        (starts[g] + r0 * widths[g], starts[g] + r1 * widths[g])
        for g, r0, r1 in (segments[0], segments[2], segments[1])
    ]
    pieces = [[segments[0]], [segments[2]], [segments[1]]]
    part_chunks = [
        [ch for ch in chunks if ch[0] == p[0][0] and p[0][1] <= ch[1] < p[0][2]] for p in pieces
    ]
    low_lane = seg_lane[1] // LANES * LANES
    out_lanes = [slice(0, low_lane), slice(cut_lane, slab_lanes), slice(low_lane, cut_lane)]
    out_win = [spans[0], spans[1], (0, rows)]
    n_parts = 3
    mid = (rows // 32 + 1) * 16
    row_halves = (slice(0, mid), slice(mid, rows))
    cols2 = (slice(0, 5 * LANES), slice(5 * LANES, 9 * LANES))
    cols1 = (slice(0, 10 * LANES),)

    def kernel(*refs):
        (xa_h, xb_h, bxa_h, bxb_h, w1_h, w2_h, ws_h, g1_h, b1_h, g2_h, b2_h, gs_h, bs_h, ua_h, ub_h,
         pm0_h, pm1_h, cells_h,
         oa, ob, gr, gw1, gws, gw2, vecs,
         xa, xb, bxa, bxb, w1g, w2, wsg, vg, g2, b2, gs, bs, ua, ub, pm0, pm1, cells,
         xs, xt, xr, zb, zsq, zsr, zg, zpa, zpb, valid, vq, hat, mask, zs, a1a, a1b,
         cslots, slots, stat, up, outr, gv, dza, dzb, dzsr,
         dd, hp, hr1, hs, hr2, gu, d1a, d1b,
         wg2, p21, p22, p23, p24, p25, wg1, p11, p12, p13, p14, p15,
         gp, gr1, gsum, gr2, zt, gt, lsem, ssem, rsem) = refs
        i, k = lax.axis_index("dp"), lax.axis_index("chan")
        k1 = k + 1 - 2 * (k % 2)
        k2 = (k + 2) % 4
        k3 = (k1 + 2) % 4
        net = Links(ssem, rsem)
        zp, a1, dz, d1 = (zpa, zpb), (a1a, a1b), (dza, dzb), (d1a, d1b)

        def flat(value):
            return value.reshape(-1, value.shape[-1])

        def zeros(count):
            return [jnp.zeros((8, LANES), f32)] * count

        loads = {}
        pairs_of = (
            ("xa", xa_h, xa), ("xb", xb_h, xb),
            ("w1", w1_h, w1g.at[k]), ("ws", ws_h, wsg.at[k]), ("g1", g1_h, vg.at[k, 0]), ("b1", b1_h, vg.at[k, 1]),
            ("bxa", bxa_h, bxa), ("bxb", bxb_h, bxb), ("pm0", pm0_h, pm0), ("pm1", pm1_h, pm1),
            ("ua", ua_h, ua), ("ub", ub_h, ub), ("g2", g2_h, g2),
            ("b2", b2_h, b2), ("gs", gs_h, gs), ("bs", bs_h, bs), ("w2", w2_h, w2), ("cells", cells_h, cells),
        )
        for index, (name, source, target) in enumerate(pairs_of):
            loads[name] = pltpu.make_async_copy(source, target, lsem.at[index])
        loads["xa"].start()
        loads["xb"].start()

        def need(*names):
            for name in names:
                loads.pop(name).wait()

        barrier = pltpu.get_barrier_semaphore()
        for d in range(1, n_dp):
            pl.semaphore_signal(barrier, inc=1, device_id=((i + d) % n_dp, k), device_id_type=MESH)
        for where in (k1, k2, k3):
            pl.semaphore_signal(barrier, inc=1, device_id=(i, where), device_id_type=MESH)

        need("xa", "xb")
        for copy in loads.values():
            copy.start()
        lane = lax.broadcasted_iota(jnp.int32, (in_local, LANES), 1)
        for d in range(n_dp):
            j = (i + d) % n_dp
            begin = 4 * qlanes[0] * j + qlanes[0] * k
            tile = begin // LANES
            part_a = xa[:, pl.ds(pl.multiple_of(tile * LANES, LANES), win[0])].astype(f32)
            part_a = pltpu.roll(part_a, (win[0] - (begin - tile * LANES)) % win[0], 1)
            begin = 4 * qlanes[1] * j + qlanes[1] * k
            tile = begin // LANES
            part_b = xb[:, pl.ds(pl.multiple_of(tile * LANES, LANES), win[1])].astype(f32)
            part_b = jnp.concatenate([part_b, jnp.zeros((in_local, LANES), f32)], axis=1)
            wide = win[1] + LANES
            part_b = pltpu.roll(part_b, (wide + b_skip - (begin - tile * LANES)) % wide, 1)
            seam = jnp.where(lane < b_skip, part_a[:, b_tile : b_tile + LANES], part_b[:, :LANES])
            xs[d * in_local : (d + 1) * in_local, :] = jnp.concatenate(
                [part_a[:, :b_tile], seam, part_b[:, LANES : slab_lanes - b_tile]], axis=1
            ).astype(bf16)
        slot_x = [net.slot(n_dp) for _ in lane_parts]
        w_taps = (slice(0, 3), slice(3, 6), slice(6, 9))
        slot_w = [net.slot(4) for _ in range(len(w_taps) + 2)]

        def weight_refs(q):
            return [w1g.at[q, taps] for taps in w_taps] + [wsg.at[q], vg.at[q]]

        ordered = regroup(xs[...], runs)
        for c, cols in enumerate(lane_parts):
            moved = ordered[:, cols]
            xt[:, :, cols] = moved.reshape(n_dp, in_local, moved.shape[1])
            xr[i, :, cols] = moved[:in_local]
            if c == 0:
                pl.semaphore_wait(barrier, n_dp + 2)
            for d in range(1, n_dp):
                net.send(xt.at[d, :, cols], xr.at[i, :, cols], slot_x[c] + i, ((i + d) % n_dp, k))
            if c == 0:
                need("w1", "ws", "g1", "b1")
                for where in (k2, k1):
                    for ref, slot in zip(weight_refs(k), slot_w):
                        net.send(ref, ref, slot + k, (i, where))

        def weights_on(n):
            ref = weight_refs(k2)[n]
            net.arrived(ref, slot_w[n] + k2, (i, k2))
            net.send(ref, ref, slot_w[n] + k2, (i, k1))

        def weights_in():
            for q in (k1, k3):
                for ref, slot in zip(weight_refs(q), slot_w):
                    net.arrived(ref, slot + q, (i, k1))

        for buf in (zpa, zpb, a1a, a1b, dza, dzb, d1a, d1b):
            side = buf.shape[1] if len(buf.shape) == 5 else buf.shape[0]
            lead = (slice(None),) if len(buf.shape) == 5 else ()
            for edge in (0, side - 1):
                for index in (lead + (edge,), lead + (slice(None), edge)):
                    region = buf.at[index]
                    region[...] = jnp.zeros(region.shape, buf.dtype)
        need("bxa", "bxb", "ua", "ub")
        population = zeros(1)[0]
        low = lax.broadcasted_iota(jnp.int32, (8, LANES), 0) < 4
        for g, box in enumerate((bxa, bxb)):
            n, half, count = images[g], halves[g], quarter[g]
            diag = lax.broadcasted_iota(jnp.int32, (n, n), 0) == lax.broadcasted_iota(jnp.int32, (n, n), 1)
            ends = [
                jnp.sum(jnp.where(diag, box[q : q + 1, :].astype(f32), 0.0), axis=1, keepdims=True)
                for q in range(4)
            ]
            ends = [jnp.broadcast_to(e, (n, LANES)) for e in ends]
            ends[2], ends[3] = ends[0] + ends[2], ends[1] + ends[3]

            def inside(ends, r, s):
                both = (r >= ends[0]) & (r < ends[2]) & (s >= ends[1]) & (s < ends[3])
                return both.astype(f32)

            for r in range(half):
                for s in range(half):
                    cell = inside(ends, r, s)
                    begin = starts[g] + (r * half + s) * n
                    valid[begin : begin + n, :] = cell
                    population = population + jnp.sum(cell.reshape(n // 8, 8, LANES), axis=0)
            mine = [pltpu.roll(e, (n - count * k) % n, 0)[:8] for e in ends]
            if count < 8:
                mine = [jnp.where(low, e, pltpu.roll(e, 4, 0)) for e in mine]
            for (seg_g, r0, r1), first, cells_n in zip(segments, seg_row, seg_cells):
                if seg_g != g:
                    continue
                per = 8 // count
                for t in range(-(-cells_n // per)):
                    spots = [divmod(min(per * t + e, cells_n - 1), half) for e in range(per)]
                    spots = [(float(r0 + r), float(s)) for r, s in spots]
                    if per == 2:
                        r, s = (jnp.where(low, spots[0][e], spots[1][e]) for e in range(2))
                    else:
                        r, s = spots[0]
                    cell = inside(mine, r, s)
                    if per == 2 and per * t + 1 >= cells_n:
                        cell = jnp.where(low, cell, 0.0)
                    vq[first + 8 * t : first + 8 * t + 8, :] = cell
        population = jnp.broadcast_to(jnp.sum(population, axis=0, keepdims=True), (8, LANES))
        for g, source in enumerate((ua, ub)):
            n, count = images[g], halves[g] ** 2
            gu[starts[g] : starts[g] + sizes[g], :] = source[...].astype(f32)
            for cell in range(count):
                up[starts[g] + cell * n : starts[g] + (cell + 1) * n, :] = gu[
                    pl.ds(starts[g] + cell, n, stride=count), :
                ]

        def rowsum(value):
            return jnp.sum(value.reshape(-1, 8, value.shape[-1]), axis=0)

        def message(sums):
            parts = [jnp.sum(v, axis=0, keepdims=True) if v.shape[0] > 1 else v for v in sums]
            if len(parts) % 8:
                parts.append(jnp.zeros((8 - len(parts) % 8, LANES), f32))
            return jnp.concatenate(parts, axis=0)

        def by_chan(value):
            return [value[:, q * LANES : (q + 1) * LANES] for q in range(4)]

        def share(rnd, value):
            mine = slots.at[rnd, i, : value.shape[0]]
            mine[...] = value
            first = net.slot(n_dp)
            for d in range(1, n_dp):
                net.send(mine, mine, first + i, ((i + d) % n_dp, k))
            return first

        def total(rnd, first, count=8):
            for d in range(1, n_dp):
                j = (i + d) % n_dp
                net.arrived(slots.at[rnd, j, :count], first + j, (j, k))
            return jnp.sum(slots[rnd, :, :count], axis=0)

        def chan_share(rnd, value):
            mine = cslots.at[rnd, k, : value.shape[0]]
            mine[...] = value
            first = net.slot(4)
            for where in (k2, k3, k1):
                net.send(mine, mine, first + k, (i, where))
            return first

        def chan_total(rnd, first, count=8):
            for where in (k1, k2, k3):
                net.arrived(cslots.at[rnd, where, :count], first + where, (i, where))
            return jnp.sum(cslots[rnd, :, :count], axis=0)

        pop_first = share(4, population)

        def quarter_in(c):
            for d in range(1, n_dp):
                j = (i + d) % n_dp
                net.arrived(xr.at[j, :, lane_parts[c]], slot_x[c] + j, (j, k))

        def patches(c):
            whole = jnp.concatenate([xr[q, :, patch_win[c]] for q in range(n_dp)], axis=0)
            value = mm((pm0, pm1)[c][...], whole, 1, 1).astype(bf16)
            count = value.shape[0] // 9
            return [value[t * count : (t + 1) * count] for t in range(9)]

        slot_z = [net.slot(4) for _ in row_parts]
        slot_s = net.slot(4)

        def first_conv(c, taps, acc):
            part = row_parts[c]
            weights = lanes_cat([w1g[q].reshape(9 * chan_in, chan_part) for q in range(4)])
            value = mm(lanes_cat(taps), weights, 1, 0).astype(bf16)
            zb[k, part, :] = value
            for where in (k2, k1):
                net.send(zb.at[k, part], zb.at[k, part], slot_z[c] + k, (i, where))
            side = mm(taps[4], lanes_cat([wsg[q] for q in range(4)]), 1, 0).astype(bf16)
            ok = lanes_cat([vq[part, :]] * 4)
            for n, z in enumerate((value, side)):
                z = z.astype(f32)
                u = z * ok
                acc[2 * n] = acc[2 * n] + rowsum(u)
                acc[2 * n + 1] = acc[2 * n + 1] + rowsum(u * z)
            for q, z in enumerate(by_chan(side)):
                zsq[q, part, :] = z
            return acc

        def act_on(c):
            part = row_parts[c]
            net.arrived(zb.at[k2, part], slot_z[c] + k2, (i, k2))
            net.send(zb.at[k2, part], zb.at[k2, part], slot_z[c] + k2, (i, k1))

        def act_in(c):
            part = row_parts[c]
            net.arrived(zb.at[k1, part], slot_z[c] + k1, (i, k1))
            net.arrived(zb.at[k3, part], slot_z[c] + k3, (i, k1))

        acc = [jnp.zeros((8, chan_full), f32)] * 4
        need("pm0", "pm1")
        weights_on(0)
        weights_on(1)
        quarter_in(0)
        taps = patches(0)
        for n in range(2, 5):
            weights_on(n)
        weights_in()
        acc = first_conv(0, taps, acc)
        quarter_in(1)
        acc = first_conv(1, patches(1), acc)
        acc = [jnp.sum(v, axis=0, keepdims=True) for v in acc]
        first = chan_share(0, message(sum((by_chan(v) for v in acc), [])))
        for where in (k2, k3, k1):
            net.send(zsq.at[where], zsr.at[k], slot_s + k, (i, where))
        zsr[k] = zsq[k]
        act_on(0)
        value = chan_total(0, first, 16)
        first = share(0, value)
        act_on(1)
        need(*list(loads))
        inv_pop = 1.0 / total(4, pop_first)[0:1]
        act_in(0)
        tot = total(0, first, 16)
        stat[...] = tot
        tot_first = (stat[pl.ds(k, 1), :], stat[pl.ds(4 + k, 1), :])
        if stop == 3:
            act_in(1)
            for where in (k2, k3, k1):
                net.arrived(zsr.at[where], slot_s + where, (i, where))
            valid[0:1, :] = inv_pop
            return net.drain()

        def moments(total_, square):
            mean = total_ * inv_pop
            return mean, lax.rsqrt(square * inv_pop - mean * mean + epsilon)

        mean1, sc1 = moments(tot[0:4], tot[4:8])
        mean1, sc1 = (lanes_cat([v[q : q + 1] for q in range(4)]) for v in (mean1, sc1))
        gain1, shift1 = (lanes_cat([vg[q, e] for q in range(4)]) for e in range(2))

        turn_low = lax.broadcasted_iota(jnp.int32, (8, 1), 0) < 4

        def whole_cells(read, c):
            for begin in range(row_parts[c].start, row_parts[c].stop, 16):
                blocks = [read(q, slice(begin, begin + 16)).astype(f32) for q in range(4)]
                for at in (begin, begin + 8):
                    seg = max(e for e in range(3) if seg_row[e] <= at)
                    g, r0, r1 = segments[seg]
                    per = 8 // quarter[g]
                    v = [block[at - begin : at - begin + 8] for block in blocks]
                    cell = (at - seg_row[seg]) // 8 * per
                    if per == 1:
                        found = [jnp.concatenate(v, axis=0)]
                    else:
                        t = [pltpu.roll(e, 4, 0) for e in v]
                        found = [
                            jnp.concatenate(
                                [jnp.where(turn_low, v[0], t[1]), jnp.where(turn_low, v[2], t[3])], axis=0
                            ),
                            jnp.concatenate(
                                [jnp.where(turn_low, t[0], v[1]), jnp.where(turn_low, t[2], v[3])], axis=0
                            ),
                        ]
                    for e, value in enumerate(found):
                        if cell + e < seg_cells[seg]:
                            r, s = divmod(cell + e, halves[g])
                            yield g, r0 + r, s, value

        def activate(c):
            for g, r, s, z in whole_cells(lambda q, span: zb[q, span, :], c):
                begin = starts[g] + (r * halves[g] + s) * images[g]
                span = slice(begin, begin + images[g])
                h = (z - mean1) * sc1
                hat[span, :] = h
                v = h * gain1 + shift1
                act = v * sigma(v) * lanes_cat([valid[span, :]] * 4)
                a1[g][1 + r, 1 + s] = act.astype(bf16)

        def second_conv(parts, acc):
            value = None
            for a, b in TAPS:
                patch = jnp.concatenate(
                    [flat(a1[g][r0 + a : r1 + a, b : b + halves[g]]) for g, r0, r1 in parts], axis=0
                )
                part = mm(patch, w2[3 * a + b], 1, 0)
                value = part if value is None else value + part
            at = 0
            for g, r0, r1 in parts:
                for r in range(r0, r1):
                    begin = starts[g] + r * widths[g]
                    span = slice(begin, begin + widths[g])
                    u = value[at : at + widths[g]]
                    at += widths[g]
                    gv[span, :] = u
                    uv = u * valid[span, :]
                    acc = [acc[0] + rowsum(uv), acc[1] + rowsum(uv * u)]
            return acc

        activate(0)
        acc = second_conv([(1, 0, halves[1]), (0, 0, rs - 1)], zeros(2))
        act_in(1)
        activate(1)
        acc = second_conv([(0, rs - 1, halves[0])], acc)
        first = share(1, message(acc))

        for where in (k2, k3, k1):
            net.arrived(zsr.at[where], slot_s + where, (i, where))
        means, scs = moments(stat[pl.ds(8 + k, 1), :], stat[pl.ds(12 + k, 1), :])
        for c in range(2):
            for g, r, s, z in whole_cells(lambda q, span: zsr[q, span, :], c):
                begin = starts[g] + (r * halves[g] + s) * images[g]
                zs[begin : begin + images[g], :] = (z - means) * scs
        row_cuts = (slice(0, rows // 32 * 16), slice(rows // 32 * 16, rows))
        slot_g0 = [net.slot(4) for _ in row_cuts]
        whole = jnp.concatenate([xr[q] for q in range(n_dp)], axis=0)
        for span, slot in zip(row_cuts, slot_g0):
            zg[k, span, :] = mm(cells[span, :], whole, 1, 1).astype(bf16)
            for where in (k2, k1):
                net.send(zg.at[k, span], zg.at[k, span], slot + k, (i, where))

        def slab_on(n):
            span, slot = row_cuts[n], slot_g0[n]
            net.arrived(zg.at[k2, span], slot + k2, (i, k2))
            net.send(zg.at[k2, span], zg.at[k2, span], slot + k2, (i, k1))

        def slab_in(n):
            span, slot = row_cuts[n], slot_g0[n]
            net.arrived(zg.at[k1, span], slot + k1, (i, k1))
            net.arrived(zg.at[k3, span], slot + k3, (i, k1))

        def planes_of(quarters, g):
            count = quarter[g]
            if count % 8 == 0:
                return [
                    jnp.concatenate([v[:, count * p : count * (p + 1)] for v in quarters], axis=1)
                    for p in range(4)
                ]
            low = lax.broadcasted_iota(jnp.int32, (1, 8, 1), 1) < 4
            parts = [[v[:, 8 * h : 8 * h + 8] for v in quarters] for h in range(2)]
            turned = [[pltpu.roll(v, 4, 1) for v in side] for side in parts]
            result = []
            for p in range(4):
                v, t = parts[p // 2], turned[p // 2]
                if p % 2 == 0:
                    both = [jnp.where(low, v[0], t[1]), jnp.where(low, v[2], t[3])]
                else:
                    both = [jnp.where(low, t[0], v[1]), jnp.where(low, t[2], v[3])]
                result.append(jnp.concatenate(both, axis=1))
            return result

        def make_planes():
            for g, r, begin, count in chunks:
                quarters = [
                    zg[q, begin : begin + count, :].astype(f32).reshape(halves[g], images[g], chan_in)
                    for q in range(4)
                ]
                for p, value in enumerate(planes_of(quarters, g)):
                    zp[g][p, 1 + r, 1 : 1 + halves[g]] = value.astype(bf16)

        tot = total(1, first)
        mean2, sc2 = moments(tot[0:1], tot[1:2])
        if stop == 5:
            valid[0:1, :] = sc2
            for n in range(2):
                slab_on(n)
            for n in range(2):
                slab_in(n)
            return net.drain()
        gain2, gains = g2[...], gs[...]
        shifts = b2[...] + bs[...]
        acc = zeros(3)
        for g, r, begin, count in chunks:
            span = slice(begin, begin + count)
            ok = valid[span, :]
            hat2 = (gv[span, :] - mean2) * sc2
            hats = zs[span, :]
            v = hat2 * gain2 + hats * gains + shifts
            sig = sigma(v)
            outr[span, :] = v * sig * ok
            grad = up[span, :] * ok * (sig * (1.0 + v * (1.0 - sig)))
            up[span, :] = grad
            gv[span, :] = hat2
            acc = [acc[0] + rowsum(grad), acc[1] + rowsum(grad * hat2), acc[2] + rowsum(grad * hats)]
        first = share(2, message(acc))
        for g, target in enumerate((oa, ob)):
            n, count = images[g], halves[g] ** 2
            for cell in range(count):
                gu[pl.ds(starts[g] + cell, n, stride=count), :] = outr[
                    starts[g] + cell * n : starts[g] + (cell + 1) * n, :
                ]
            target[...] = gu[starts[g] : starts[g] + sizes[g], :].astype(bf16)
        for begin in range(0, rows, 16):
            span = slice(begin, begin + 16)
            v = hat[span, :] * gain1 + shift1
            sig = sigma(v)
            mask[span, :] = sig * (1.0 + v * (1.0 - sig)) * lanes_cat([valid[span, :]] * 4)
        tot = total(2, first)
        sum_tail, sum_gain2, sum_gains = tot[0:1], tot[1:2], tot[2:3]
        if stop == 6:
            valid[0:1, :] = sum_tail
            for n in range(2):
                slab_on(n)
            for n in range(2):
                slab_in(n)
            return net.drain()

        k2g, ksg = gain2 * sc2, gains * scs
        db, dg2, dgs = sum_tail * inv_pop, sum_gain2 * inv_pop, sum_gains * inv_pop
        for g, r, begin, count in chunks:
            span = slice(begin, begin + count)
            value = k2g * (up[span, :] - valid[span, :] * (db + gv[span, :] * dg2))
            dz[g][1 + r, 1 : 1 + halves[g]] = value.astype(bf16).reshape(halves[g], images[g], chan_part)
        for g in range(2):
            for t, (a, b) in enumerate(TAPS):
                dd[starts[g] : starts[g] + sizes[g], t * LANES : (t + 1) * LANES] = flat(
                    dz[g][2 - a : 2 - a + halves[g], 2 - b : 2 - b + halves[g]]
                )

        def back_second(first, span):
            begin = pl.multiple_of(first * chan_part, LANES)
            weights = lanes_cat([w2[t, pl.ds(begin, 2 * chan_part), :] for t in range(9)])
            value = mm(dd[span, :], weights, 1, 1).astype(bf16)
            hp[first, span, :] = value[:, :chan_part]
            hp[first + 1, span, :] = value[:, chan_part:]

        slot_h = [net.slot(3) for _ in row_halves]
        for span, slot in zip(row_halves, slot_h):
            back_second(2 * (k2 // 2), span)
            net.send(hp.at[k3, span], hr1.at[1, span], slot + 1, (i, k1))
        for span, slot in zip(row_halves, slot_h):
            net.arrived(hr1.at[1, span], slot + 1, (i, k1))
            hs[span, :] = (hp[k2, span, :].astype(f32) + hr1[1, span, :].astype(f32)).astype(bf16)
            net.send(hs.at[span], hr2.at[span], slot + 2, (i, k2))
        back_second(2 * (k // 2), slice(0, rows))
        for span, slot in zip(row_halves, slot_h):
            net.send(hp.at[k1, span], hr1.at[0, span], slot, (i, k1))

        acc = [jnp.zeros((8, chan_full), f32)] * 2
        for begin in range(0, rows, 16):
            span = slice(begin, begin + 16)
            part = lanes_cat([hp[q, span, :] for q in range(4)]).astype(f32) * mask[span, :]
            acc = [acc[0] + rowsum(part), acc[1] + rowsum(part * hat[span, :])]
        acc = [jnp.sum(v, axis=0, keepdims=True) for v in acc]
        first = chan_share(1, message(sum((by_chan(v) for v in acc), [])))

        acts = [flat(a1[g][1 : 1 + halves[g], 1 : 1 + halves[g]]) for g in range(2)]
        sum2 = Reduce(net, i, k, wg2, (p21, p22, p23, p24, p25), cols2)
        for w, cols in enumerate(cols2):
            value = mm(acts[0], dd[: sizes[0], cols], 0, 0) + mm(acts[1], dd[sizes[0] :, cols], 0, 0)
            wg2[:, :, :, :, cols] = value.astype(bf16).reshape(2, 2, 2, out_rows, value.shape[1])
            sum2.first(w)
            if w == 0:
                first = share(3, chan_total(1, first))
        for g, r, begin, count in chunks:
            span = slice(begin, begin + count)
            value = ksg * (up[span, :] - valid[span, :] * (db + zs[span, :] * dgs))
            dzsr[span, :] = value.astype(bf16)
        for n in range(2):
            slab_on(n)
        for n in range(2):
            slab_in(n)
        make_planes()
        tot = total(3, first)
        stat[0:8, :] = tot
        sum_head, sum_gain1 = stat[pl.ds(k, 1), :], stat[pl.ds(4 + k, 1), :]

        def close_second():
            for w, cols in enumerate(cols2):
                value = sum2.last(w)
                for t in range(cols.start // LANES, cols.stop // LANES):
                    gw2[t] = value[:, t * LANES - cols.start : (t + 1) * LANES - cols.start]

        own = pl.ds(pl.multiple_of(k * chan_part, LANES), chan_part)
        mean1, sc1 = moments(tot_first[0], tot_first[1])
        k1g = vg[k, 0] * sc1
        db, dg1 = sum_head * inv_pop, sum_gain1 * inv_pop
        per_cell = [(g, r, s) for g in range(2) for r in range(halves[g]) for s in range(halves[g])]
        waiting = list(zip(row_halves, slot_h))
        for g, r, s in per_cell:
            begin = starts[g] + (r * halves[g] + s) * images[g]
            part = slice(begin, begin + images[g])
            while waiting and waiting[0][0].start < part.stop:
                span, slot = waiting.pop(0)
                net.arrived(hr1.at[0, span], slot, (i, k1))
                net.arrived(hr2.at[span], slot + 2, (i, k2))
            grad = hp[k, part, :].astype(f32) + hr1[0, part, :].astype(f32) + hr2[part, :].astype(f32)
            grad = grad * mask[part, own]
            value = k1g * (grad - valid[part, :] * (db + hat[part, own] * dg1))
            d1[g][r, s] = value.astype(bf16)
        if stop == 8:
            valid[0:1, :] = sum_head
            for w in range(2):
                sum2.second(w)
            for w in range(2):
                sum2.third(w)
            close_second()
            return net.drain()

        def back_patch(pieces, p):
            parts = []
            for g, r0, r1 in pieces:
                width = halves[g] * images[g]
                taps = [
                    flat(d1[g][r0 + (a == 0) : r1 + (a == 0), (b == 0) : (b == 0) + halves[g]])
                    for a, b in PLANE_TAPS[p]
                ]
                if p == 0:
                    taps.append(dzsr[starts[g] + r0 * width : starts[g] + r1 * width, :])
                parts.append(lanes_cat(taps))
            return jnp.concatenate(parts, axis=0) if len(parts) > 1 else parts[0]

        slot_g = [net.slot(3) for _ in range(n_parts)]

        def back_first(c):
            a, b = spans[c]
            planes = []
            for p in range(4):
                weights = [w1g[k, 3 * ta + tb] for ta, tb in PLANE_TAPS[p]]
                if p == 0:
                    weights.append(wsg[k])
                planes.append(mm(back_patch(pieces[c], p), lanes_cat(weights), 1, 1))
            for g, r, begin, count in part_chunks[c]:
                values = [
                    v[begin - a : begin - a + count].reshape(halves[g], images[g], chan_in)
                    for v in planes
                ]
                for q, value in enumerate(planes_of(values, g)):
                    gp[q, begin : begin + count, :] = flat(value).astype(bf16)
            net.send(gp.at[k3, a:b], gr1.at[1, a:b], slot_g[c] + 1, (i, k1))
            net.send(gp.at[k1, a:b], gr1.at[0, a:b], slot_g[c], (i, k1))

        def back_cross(c):
            a, b = spans[c]
            net.arrived(gr1.at[1, a:b], slot_g[c] + 1, (i, k1))
            for begin in range(a, b, 16):
                span = slice(begin, begin + 16)
                value = gp[k2, span, :].astype(f32) + gr1[1, span, :].astype(f32)
                gsum[span, :] = value.astype(bf16)
            net.send(gsum.at[a:b], gr2.at[a:b], slot_g[c] + 2, (i, k2))

        slot_o = [net.slot(n_dp) for _ in range(n_parts)]

        def back_out(c):
            a, b = spans[c]
            net.arrived(gr1.at[0, a:b], slot_g[c], (i, k1))
            net.arrived(gr2.at[a:b], slot_g[c] + 2, (i, k2))
            for begin in range(a, b, 16):
                span = slice(begin, begin + 16)
                value = gp[k, span, :].astype(f32) + gr1[0, span, :].astype(f32)
                zt[span, :] = (value + gr2[span, :].astype(f32)).astype(bf16)
            cols = out_lanes[c]
            a, b = out_win[c]
            value = mm(zt[a:b, :], cells[a:b, cols], 0, 0).astype(bf16)
            gt[:, :, cols] = value.reshape(n_dp, in_local, value.shape[1])
            for d in range(1, n_dp):
                j = (i + d) % n_dp
                net.send(gt.at[j, :, cols], gr.at[i, :, cols], slot_o[c] + i, (j, k))

        sum1 = Reduce(net, i, k, wg1, (p11, p12, p13, p14, p15), cols1)

        def weight_first():
            everything = [(0, 0, halves[0]), (1, 0, halves[1])]
            blocks = []
            for p in range(4):
                value = 0.0
                for g, r0, r1 in everything:
                    cell = flat(zp[g][p, 1 : 1 + halves[g], 1 : 1 + halves[g]])
                    value = value + mm(cell, back_patch([(g, r0, r1)], p), 0, 0)
                blocks.append(value.astype(bf16))
            wg1[...] = lanes_cat(blocks).reshape(2, 2, 2, in_local, 10 * LANES)
            sum1.first(0)

        back_first(0)
        back_first(1)
        back_cross(0)
        sum2.second(0)
        back_first(2)
        back_cross(1)
        back_cross(2)
        weight_first()
        sum2.second(1)
        back_out(0)
        sum2.third(0)
        back_out(1)
        sum2.third(1)
        sum1.second(0)
        back_out(2)
        sum1.third(0)
        kept = pltpu.make_async_copy(gt.at[i], gr.at[i], lsem.at[len(pairs_of)])
        kept.start()
        close_second()
        value = sum1.last(0)
        for t, tap in enumerate(TAPS):
            place = ORDER.index(tap)
            place = place + (place > 0)
            gw1[t] = value[:, place * LANES : (place + 1) * LANES]
        gws[...] = value[:, LANES : 2 * LANES]
        vecs[...] = message([sum_gain1, sum_head, sum_gain2, sum_tail, sum_gains])
        for c in range(n_parts):
            cols = out_lanes[c]
            for d in range(1, n_dp):
                j = (i + d) % n_dp
                net.arrived(gr.at[j, :, cols], slot_o[c] + j, (j, k))
        kept.wait()
        net.drain()

    V = pltpu.VMEM
    pads = [(h + 2, h + 2, n, chan_part) for h, n in zip(halves, images)]
    half_pads = [(h + 1, h + 1, n) for h, n in zip(halves, images)]

    def ladder(count, width):
        return [
            V((2, 2, 2, count, width), bf16), V((2, 2, count, width), bf16), V((2, 2, count, width), bf16),
            V((2, count, width), bf16), V((2, count, width), bf16), V((count, width), bf16),
        ]

    inputs = [
        V((in_local, n_dp * 4 * qlanes[0]), bf16), V((in_local, n_dp * 4 * qlanes[1]), bf16),
        V((4, images[0]), jnp.int32), V((4, images[1]), jnp.int32),
        V((4, 9, chan_in, chan_part), bf16), V((9, chan_full, chan_part), bf16),
        V((4, chan_in, chan_part), bf16), V((4, 2, 1, chan_part), f32),
    ] + [V((1, chan_part), f32)] * 4 + [
        V((sizes[0], chan_part), bf16), V((sizes[1], chan_part), bf16),
    ] + [V(m.shape, bf16) for m in patch_ms] + [V((rows, slab_lanes), bf16)]
    scratch = inputs + [
        V((n_dp * in_local, slab_lanes), bf16),
        V((n_dp, in_local, slab_lanes), bf16),
        V((n_dp, in_local, slab_lanes), bf16),
        V((4, q_rows, chan_full), bf16),
        V((4, q_rows, chan_part), bf16),
        V((4, q_rows, chan_part), bf16),
        V((4, rows, chan_in), bf16),
        V((4,) + half_pads[0] + (chan_in,), bf16),
        V((4,) + half_pads[1] + (chan_in,), bf16),
        V((rows, LANES), f32),
        V((q_rows, LANES), f32),
        V((rows, chan_full), f32),
        V((rows, chan_full), f32),
        V((rows, chan_part), f32),
        V(pads[0][:3] + (chan_full,), bf16),
        V(pads[1][:3] + (chan_full,), bf16),
        V((2, 4, 16, LANES), f32),
        V((5, n_dp, 16, LANES), f32),
        V((16, LANES), f32),
        V((rows, chan_part), f32),
        V((rows, chan_part), f32),
        V((rows, chan_part), f32),
        V(pads[0], bf16),
        V(pads[1], bf16),
        V((rows, chan_part), bf16),
        V((rows, 9 * chan_part), bf16),
        V((4, rows, chan_part), bf16),
        V((2, rows, chan_part), bf16),
        V((rows, chan_part), bf16),
        V((rows, chan_part), bf16),
        V((rows, chan_part), f32),
        V(half_pads[0] + (chan_part,), bf16),
        V(half_pads[1] + (chan_part,), bf16),
    ]
    scratch += ladder(out_rows, 9 * LANES) + ladder(in_local, 10 * LANES)
    scratch += [
        V((4, rows, chan_in), bf16),
        V((2, rows, chan_in), bf16),
        V((rows, chan_in), bf16),
        V((rows, chan_in), bf16),
        V((rows, chan_in), bf16),
        V((n_dp, in_local, slab_lanes), bf16),
        pltpu.SemaphoreType.DMA((19,)),
        pltpu.SemaphoreType.DMA((192,)),
        pltpu.SemaphoreType.DMA((192,)),
    ]
    mid_outs = [
        jax.ShapeDtypeStruct((sizes[0], chan_part), bf16),
        jax.ShapeDtypeStruct((sizes[1], chan_part), bf16),
        jax.ShapeDtypeStruct((n_dp, in_local, slab_lanes), bf16),
        jax.ShapeDtypeStruct((9, in_local, LANES), f32),
        jax.ShapeDtypeStruct((in_local, LANES), f32),
        jax.ShapeDtypeStruct((9, out_rows, LANES), f32),
        jax.ShapeDtypeStruct((8, LANES), f32),
    ]
    vmem = pl.BlockSpec(memory_space=pltpu.VMEM)
    hbm = pl.BlockSpec(memory_space=pl.ANY)
    main = pl.pallas_call(
        kernel,
        out_shape=mid_outs,
        in_specs=[hbm] * 18,
        out_specs=[vmem, vmem, hbm, vmem, vmem, vmem, vmem],
        scratch_shapes=scratch,
        compiler_params=pltpu.CompilerParams(
            collective_id=1, has_side_effects=True, vmem_limit_bytes=60 * 2**20
        ),
        name="block",
    )

    def closing(oa_h, ob_h, gr_h, gw1_h, gws_h, gw2_h, vecs_h, turn_h,
                fa, fb, ia, ib, f1, f2, fs, c1, h1, c2, h2, cs, hs,
                oa, ob, gr, gw1, gws, gw2, vecs, turn, sems):
        moves = [
            pltpu.make_async_copy(source, target, sems.at[index])
            for index, (source, target) in enumerate(
                (
                    (gr_h, gr), (turn_h, turn), (vecs_h, vecs), (gw2_h, gw2), (gw1_h, gw1),
                    (oa_h, oa), (ob_h, ob), (gws_h, gws),
                )
            )
        ]
        outs = [
            pltpu.make_async_copy(source, target, sems.at[len(moves) + index])
            for index, (source, target) in enumerate(
                ((gw2, f2), (gw1, f1), (oa, fa), (ob, fb), (gws, fs))
            )
        ]
        for move in moves:
            move.start()
        for move in moves[:3]:
            move.wait()
        for move, out in zip(moves[3:], outs):
            move.wait()
            out.start()
        moved = mm(turn[...], gr[...].reshape(n_dp * in_local, slab_lanes), 1, 0)
        natural = regroup(moved, back_runs)
        ia[...] = natural[:, : qlanes[0]].reshape(in_local, n_dp, qlanes[0]).astype(bf16)
        tail = natural[:, qlanes[0] : qlanes[0] + qlanes[1]]
        ib[...] = tail.reshape(in_local, n_dp, qlanes[1]).astype(bf16)
        for ref, row in ((c1, 0), (h1, 1), (c2, 2), (h2, 3), (cs, 4), (hs, 3)):
            ref[...] = vecs[row : row + 1, :]
        for out in outs:
            out.wait()

    last = pl.pallas_call(
        closing,
        out_shape=[
            jax.ShapeDtypeStruct((sizes[0], chan_part), bf16),
            jax.ShapeDtypeStruct((sizes[1], chan_part), bf16),
            jax.ShapeDtypeStruct((in_local, n_dp, qlanes[0]), bf16),
            jax.ShapeDtypeStruct((in_local, n_dp, qlanes[1]), bf16),
            jax.ShapeDtypeStruct((9, in_local, LANES), f32),
            jax.ShapeDtypeStruct((9, out_rows, LANES), f32),
            jax.ShapeDtypeStruct((in_local, LANES), f32),
        ]
        + [jax.ShapeDtypeStruct((1, LANES), f32)] * 6,
        in_specs=[hbm] * 8,
        out_specs=[hbm, hbm, vmem, vmem, hbm, hbm, hbm] + [vmem] * 6,
        scratch_shapes=[V(o.shape, o.dtype) for o in mid_outs]
        + [V((n_dp * in_local, n_dp * in_local), bf16), pltpu.SemaphoreType.DMA((13,))],
        compiler_params=pltpu.CompilerParams(vmem_limit_bytes=60 * 2**20),
        name="closing",
    )
    total_rows = n_dp * in_local
    turn = np.zeros((total_rows, total_rows), np.float32)
    for c in range(in_local):
        for j in range(n_dp):
            turn[c * n_dp + j, j * in_local + c] = 1.0
    return (main, last) + tuple(m.astype(jnp.bfloat16) for m in (turn, *patch_ms, cells_m))


STOP = 99


def fused_body(
    input_a, input_b, boxes_a, boxes_b, weight_first, weight_second, weight_short,
    gain_first, shift_first, gain_second, shift_second, gain_short, shift_short,
    upstream_a, upstream_b,
):
    n_dp = lax.axis_size("dp")
    chan_part = weight_first.shape[2]
    in_local = input_a.shape[0]
    main, last, turn, *matrices = make_fused(
        n_dp, in_local, (boxes_a.shape[0], boxes_b.shape[0]), (SA, SB),
        weight_first.shape[1], chan_part, STOP,
    )
    vectors = [
        v.reshape(1, chan_part)
        for v in (gain_first, shift_first, gain_second, shift_second, gain_short, shift_short)
    ]
    mid = main(
        input_a, input_b, boxes_a.T, boxes_b.T, weight_first, weight_second, weight_short,
        *vectors, upstream_a.T, upstream_b.T, *matrices,
    )
    res = last(*mid, turn)
    return (
        res[0].T, res[1].T,
        res[2].reshape(in_local, n_dp, 1, -1), res[3].reshape(in_local, n_dp, 1, -1),
        res[4], res[5], res[6],
    ) + tuple(v.reshape(chan_part) for v in res[7:])


def choose_body(mesh):
    return fused_body if mesh.shape["dp"] == 8 and mesh.shape["chan"] == 4 else plain_body


def solution(mesh):
    placed = (
        P("dp", None),
        P("dp", None),
        P("dp", None),
        P("dp", None),
        P(None, None, "chan"),
        P(None, None, "chan"),
        P(None, "chan"),
        P("chan"),
        P("chan"),
        P("chan"),
        P("chan"),
        P("chan"),
        P("chan"),
        P("chan", "dp"),
        P("chan", "dp"),
    )
    return jax.shard_map(
        choose_body(mesh),
        mesh=mesh,
        in_specs=placed,
        out_specs=(
            P("chan", "dp"),
            P("chan", "dp"),
            P("dp", None, "chan", None),
            P("dp", None, "chan", None),
            P(None, "dp", "chan"),
            P(None, "dp", "chan"),
            P("dp", "chan"),
            P("chan"),
            P("chan"),
            P("chan"),
            P("chan"),
            P("chan"),
            P("chan"),
        ),
        check_vma=False,
    )
```

```python
import jax
import jax.numpy as jnp
from jax import lax
import numpy as np
from jax.experimental import pallas as pl
from jax.experimental.pallas import tpu as pltpu
from jax.sharding import PartitionSpec as P

SA = 14
SB = 6


epsilon = 1e-05


def box_mask(box_rows, extent):
    positions = jnp.arange(extent, dtype=jnp.int32)[None, :]
    row_inside = (positions >= box_rows[:, 0:1]) & (positions < box_rows[:, 0:1] + box_rows[:, 2:3])
    col_inside = (positions >= box_rows[:, 1:2]) & (positions < box_rows[:, 1:2] + box_rows[:, 3:4])
    return (row_inside[:, :, None] & col_inside[:, None, :]).astype(jnp.float32)


def taps_strided(feature, image_count, extent):
    channels = feature.shape[0]
    output_side = extent // 2
    padded = jnp.pad(
        feature.reshape(channels, image_count, extent, extent), ((0, 0), (0, 0), (1, 1), (1, 1))
    )
    pieces = [
        padded[:, :, tap_row : tap_row + extent : 2, tap_col : tap_col + extent : 2]
        for tap_row in range(3)
        for tap_col in range(3)
    ]
    return jnp.stack(pieces, axis=0).reshape(9 * channels, image_count * output_side * output_side)


def taps_plain(feature, image_count, extent):
    channels = feature.shape[0]
    padded = jnp.pad(
        feature.reshape(channels, image_count, extent, extent), ((0, 0), (0, 0), (1, 1), (1, 1))
    )
    pieces = [
        padded[:, :, tap_row : tap_row + extent, tap_col : tap_col + extent]
        for tap_row in range(3)
        for tap_col in range(3)
    ]
    return jnp.stack(pieces, axis=0).reshape(9 * channels, image_count * extent * extent)


def untaps_plain(columns, channels, image_count, extent):
    pieces = columns.reshape(9, channels, image_count, extent, extent)
    running = jnp.zeros((channels, image_count, extent + 2, extent + 2), jnp.float32)
    for tap_row in range(3):
        for tap_col in range(3):
            running = running + jnp.pad(
                pieces[3 * tap_row + tap_col],
                ((0, 0), (0, 0), (tap_row, 2 - tap_row), (tap_col, 2 - tap_col)),
            )
    return running[:, :, 1:-1, 1:-1].reshape(channels, image_count * extent * extent)


def untaps_strided(columns, shortcut, channels, image_count, extent):
    output_side = extent // 2
    pieces = columns.reshape(9, channels, image_count, output_side, output_side)
    parity_sums = {}
    for tap_row in range(3):
        for tap_col in range(3):
            block_row = tap_row // 2
            block_col = tap_col // 2
            placed = jnp.pad(
                pieces[3 * tap_row + tap_col],
                ((0, 0), (0, 0), (block_row, 1 - block_row), (block_col, 1 - block_col)),
            )
            parity = (tap_row % 2, tap_col % 2)
            parity_sums[parity] = (
                placed if parity not in parity_sums else parity_sums[parity] + placed
            )
    direct = jnp.pad(
        shortcut.reshape(channels, image_count, output_side, output_side),
        ((0, 0), (0, 0), (0, 1), (0, 1)),
    )
    parity_sums[1, 1] = parity_sums[1, 1] + direct
    rows_even = jnp.stack([parity_sums[0, 0], parity_sums[0, 1]], axis=-1)
    rows_odd = jnp.stack([parity_sums[1, 0], parity_sums[1, 1]], axis=-1)
    padded = jnp.stack([rows_even, rows_odd], axis=3).reshape(
        channels, image_count, extent + 2, extent + 2
    )
    return padded[:, :, 1:-1, 1:-1].reshape(channels, image_count * extent * extent)


def contract_first(weights, columns):
    return lax.dot_general(
        weights, columns, (((0,), (0,)), ((), ())), preferred_element_type=jnp.float32
    )


def weight_product(columns, gradient):
    return lax.dot_general(
        columns, gradient, (((1,), (1,)), ((), ())), preferred_element_type=jnp.float32
    )


def swish_slope(values):
    logistic = jax.nn.sigmoid(values)
    return logistic * (1.0 + values * (1.0 - logistic))


def moments(values, valid_list):
    running = 0.0
    squares = 0.0
    for tensor, valid in zip(values, valid_list):
        widened = tensor.astype(jnp.float32)
        running = running + jnp.sum(widened * valid, axis=1)
        squares = squares + jnp.sum(widened * widened * valid, axis=1)
    return (running, squares)


def standardize(values, running, squares, population):
    mean_value = running / population
    variance = squares / population - mean_value * mean_value
    scaling = lax.rsqrt(variance + epsilon)
    return (
        [
            (tensor.astype(jnp.float32) - mean_value[:, None]) * scaling[:, None]
            for tensor in values
        ],
        scaling,
    )


def norm_back(gradient, normed, valid, scaling, gain_values, shift_sum, gain_sum, population):
    return (gain_values * scaling)[:, None] * (
        gradient - valid * (shift_sum[:, None] + normed * gain_sum[:, None]) / population
    )


def plain_body(
    input_a,
    input_b,
    boxes_a,
    boxes_b,
    weight_first,
    weight_second,
    weight_short,
    gain_first,
    shift_first,
    gain_second,
    shift_second,
    gain_short,
    shift_short,
    upstream_a,
    upstream_b,
):
    image_groups = lax.axis_size("dp")
    in_local = input_a.shape[0]
    chan_in = weight_first.shape[1]
    chan_part = weight_first.shape[2]
    chan_full = weight_second.shape[1]
    image_counts = (boxes_a.shape[0], boxes_b.shape[0])
    extents = (SA, SB)
    whole_a, whole_b = (
        lax.all_to_all(
            input_a.reshape(in_local, image_groups, -1),
            "dp",
            split_axis=1,
            concat_axis=0,
            tiled=True,
        ),
        lax.all_to_all(
            input_b.reshape(in_local, image_groups, -1),
            "dp",
            split_axis=1,
            concat_axis=0,
            tiled=True,
        ),
    )
    features = (whole_a.reshape(chan_in, -1), whole_b.reshape(chan_in, -1))
    valid_list = (
        box_mask(boxes_a, SA // 2).reshape(1, -1),
        box_mask(boxes_b, SB // 2).reshape(1, -1),
    )
    first_mat = weight_first.reshape(9 * chan_in, chan_part)
    second_mat = weight_second.reshape(9 * chan_full, chan_part)
    first_cols = []
    sampled = []
    first_z = []
    short_z = []
    for feature, image_count, extent in zip(features, image_counts, extents):
        columns = taps_strided(feature, image_count, extent)
        picked = feature.reshape(chan_in, image_count, extent, extent)[:, :, ::2, ::2].reshape(
            chan_in, -1
        )
        first_cols.append(columns)
        sampled.append(picked)
        first_z.append(contract_first(first_mat, columns).astype(jnp.bfloat16))
        short_z.append(contract_first(weight_short, picked).astype(jnp.bfloat16))
    sum_first, square_first = moments(first_z, valid_list)
    sum_short, square_short = moments(short_z, valid_list)
    population = jnp.sum(valid_list[0]) + jnp.sum(valid_list[1])
    sum_first, square_first, sum_short, square_short, population = lax.psum(
        (sum_first, square_first, sum_short, square_short, population), "dp"
    )
    normed_first, scaling_first = standardize(first_z, sum_first, square_first, population)
    normed_short, scaling_short = standardize(short_z, sum_short, square_short, population)
    before_first = [normed * gain_first[:, None] + shift_first[:, None] for normed in normed_first]
    outgoing_a = (jax.nn.silu(before_first[0]) * valid_list[0]).astype(jnp.bfloat16)
    outgoing_b = (jax.nn.silu(before_first[1]) * valid_list[1]).astype(jnp.bfloat16)
    gathered_a, gathered_b = (
        lax.all_gather(outgoing_a, "chan", axis=0, tiled=True),
        lax.all_gather(outgoing_b, "chan", axis=0, tiled=True),
    )
    second_cols = []
    second_z = []
    for gathered, image_count, extent in zip((gathered_a, gathered_b), image_counts, extents):
        columns = taps_plain(gathered, image_count, extent // 2)
        second_cols.append(columns)
        second_z.append(contract_first(second_mat, columns).astype(jnp.bfloat16))
    sum_second, square_second = moments(second_z, valid_list)
    sum_second, square_second = lax.psum((sum_second, square_second), "dp")
    normed_second, scaling_second = standardize(second_z, sum_second, square_second, population)
    summed_pre = [
        main_part * gain_second[:, None]
        + shift_second[:, None]
        + side_part * gain_short[:, None]
        + shift_short[:, None]
        for main_part, side_part in zip(normed_second, normed_short)
    ]
    outputs = [
        (jax.nn.silu(tensor) * valid).astype(jnp.bfloat16)
        for tensor, valid in zip(summed_pre, valid_list)
    ]
    tail_grads = [
        upstream.astype(jnp.float32) * valid * swish_slope(tensor)
        for upstream, valid, tensor in zip((upstream_a, upstream_b), valid_list, summed_pre)
    ]
    shift_tail = sum((jnp.sum(gradient, axis=1) for gradient in tail_grads))
    gain_tail = sum(
        (jnp.sum(gradient * normed, axis=1) for gradient, normed in zip(tail_grads, normed_second))
    )
    gain_side = sum(
        (jnp.sum(gradient * normed, axis=1) for gradient, normed in zip(tail_grads, normed_short))
    )
    shift_tail, gain_tail, gain_side = lax.psum((shift_tail, gain_tail, gain_side), "dp")
    grad_second_local = 0.0
    partial_hidden = []
    short_dz = []
    for index_group in range(2):
        valid = valid_list[index_group]
        dz_second = norm_back(
            tail_grads[index_group],
            normed_second[index_group],
            valid,
            scaling_second,
            gain_second,
            shift_tail,
            gain_tail,
            population,
        ).astype(jnp.bfloat16)
        dz_short = norm_back(
            tail_grads[index_group],
            normed_short[index_group],
            valid,
            scaling_short,
            gain_short,
            shift_tail,
            gain_side,
            population,
        ).astype(jnp.bfloat16)
        short_dz.append(dz_short)
        grad_second_local = grad_second_local + weight_product(second_cols[index_group], dz_second)
        back_cols = jnp.dot(second_mat, dz_second, preferred_element_type=jnp.float32)
        partial_hidden.append(
            untaps_plain(back_cols, chan_full, image_counts[index_group], extents[index_group] // 2)
        )
    hidden_a, hidden_b = (
        lax.psum_scatter(
            partial_hidden[0].astype(jnp.bfloat16), "chan", scatter_dimension=0, tiled=True
        ).astype(jnp.float32),
        lax.psum_scatter(
            partial_hidden[1].astype(jnp.bfloat16), "chan", scatter_dimension=0, tiled=True
        ).astype(jnp.float32),
    )
    head_grads = [
        hidden * valid * swish_slope(tensor)
        for hidden, valid, tensor in zip((hidden_a, hidden_b), valid_list, before_first)
    ]
    shift_head = sum((jnp.sum(gradient, axis=1) for gradient in head_grads))
    gain_head = sum(
        (jnp.sum(gradient * normed, axis=1) for gradient, normed in zip(head_grads, normed_first))
    )
    shift_head, gain_head = lax.psum((shift_head, gain_head), "dp")
    grad_first_local = 0.0
    grad_short_local = 0.0
    partial_inputs = []
    for index_group in range(2):
        valid = valid_list[index_group]
        dz_first = norm_back(
            head_grads[index_group],
            normed_first[index_group],
            valid,
            scaling_first,
            gain_first,
            shift_head,
            gain_head,
            population,
        ).astype(jnp.bfloat16)
        grad_first_local = grad_first_local + weight_product(first_cols[index_group], dz_first)
        grad_short_local = grad_short_local + weight_product(
            sampled[index_group], short_dz[index_group]
        )
        back_cols = jnp.dot(first_mat, dz_first, preferred_element_type=jnp.float32)
        back_short = jnp.dot(
            weight_short, short_dz[index_group], preferred_element_type=jnp.float32
        )
        flat_input = untaps_strided(
            back_cols, back_short, chan_in, image_counts[index_group], extents[index_group]
        )
        partial_inputs.append(flat_input.reshape(chan_in, 1, lax.axis_size("chan"), -1))
    arrived_a, arrived_b = (
        lax.all_to_all(
            partial_inputs[0].astype(jnp.bfloat16), "dp", split_axis=0, concat_axis=1, tiled=True
        ).astype(jnp.float32),
        lax.all_to_all(
            partial_inputs[1].astype(jnp.bfloat16), "dp", split_axis=0, concat_axis=1, tiled=True
        ).astype(jnp.float32),
    )
    summed_a, summed_b = (
        lax.psum_scatter(
            arrived_a.astype(jnp.bfloat16), "chan", scatter_dimension=2, tiled=True
        ).astype(jnp.float32),
        lax.psum_scatter(
            arrived_b.astype(jnp.bfloat16), "chan", scatter_dimension=2, tiled=True
        ).astype(jnp.float32),
    )
    grad_input_a = summed_a.astype(jnp.bfloat16)
    grad_input_b = summed_b.astype(jnp.bfloat16)
    grad_first_local = grad_first_local.reshape(9, chan_in, chan_part)
    grad_second_local = grad_second_local.reshape(9, chan_full, chan_part)
    total_first, total_second, total_short = lax.psum(
        (grad_first_local, grad_second_local, grad_short_local), "dp"
    )
    position = lax.axis_index("dp")
    rows_first = chan_in // image_groups
    rows_second = chan_full // image_groups
    grad_first = lax.dynamic_slice_in_dim(total_first, position * rows_first, rows_first, 1)
    grad_second = lax.dynamic_slice_in_dim(total_second, position * rows_second, rows_second, 1)
    grad_short = lax.dynamic_slice_in_dim(total_short, position * rows_first, rows_first, 0)
    return (
        outputs[0],
        outputs[1],
        grad_input_a,
        grad_input_b,
        grad_first,
        grad_second,
        grad_short,
        gain_head,
        shift_head,
        gain_tail,
        shift_tail,
        gain_side,
        shift_tail,
    )


MESH = pl.DeviceIdType.MESH
TAPS = tuple((a, b) for a in range(3) for b in range(3))
PLANE_TAPS = (
    ((1, 1),),
    ((1, 0), (1, 2)),
    ((0, 1), (2, 1)),
    ((0, 0), (0, 2), (2, 0), (2, 2)),
)
ORDER = [tap for taps in PLANE_TAPS for tap in taps]
LANES = 128


class Links:
    def __init__(self, send_sems, recv_sems):
        self.send_sems, self.recv_sems = send_sems, recv_sems
        self.sends = self.slots = 0
        self.open = []

    def slot(self, count=1):
        first = self.slots
        self.slots += count
        return first

    def send(self, source, target, slot, where):
        copy = pltpu.make_async_remote_copy(
            source, target, self.send_sems.at[self.sends], self.recv_sems.at[slot],
            device_id=where, device_id_type=MESH,
        )
        self.sends += 1
        copy.start()
        self.open.append(copy)

    def arrived(self, target, slot, where):
        pltpu.make_async_remote_copy(
            target, target, self.send_sems.at[0], self.recv_sems.at[slot],
            device_id=where, device_id_type=MESH,
        ).wait_recv()

    def drain(self):
        for copy in self.open:
            copy.wait_send()


def mm(a, b, ca, cb):
    return lax.dot_general(a, b, (((ca,), (cb,)), ((), ())), preferred_element_type=jnp.float32)


def lanes_cat(parts):
    return jnp.concatenate(parts, axis=1) if len(parts) > 1 else parts[0]


def quarter_matrices(images, sides, segments, seg_lane, seg_row, q_rows, lanes):
    def lane(g, image, row, col):
        for (seg_g, r0, r1), first in zip(segments, seg_lane):
            if seg_g == g and 2 * r0 <= row < 2 * r1:
                return first + (image * 2 * (r1 - r0) + row - 2 * r0) * sides[g] + col

    taps = np.zeros((9, q_rows, lanes), np.float32)
    for (g, r0, r1), first in zip(segments, seg_row):
        half = sides[g] // 2
        for r in range(r0, r1):
            for s in range(half):
                for image in range(images[g]):
                    target = first + ((r - r0) * half + s) * images[g] + image
                    for t, (a, b) in enumerate(TAPS):
                        row, col = 2 * r + a - 1, 2 * s + b - 1
                        if row >= 0 and col >= 0:
                            taps[t, target, lane(g, image, row, col)] = 1.0
    sizes = [n * side * side for n, side in zip(images, sides)]
    cells = np.zeros((sum(sizes), lanes), np.float32)
    for g, (n, side) in enumerate(zip(images, sides)):
        for image in range(n):
            for row in range(side):
                for col in range(side):
                    cell = (row // 2) * (side // 2) + col // 2
                    target = g * sizes[0] + (cell * 4 + 2 * (row % 2) + col % 2) * n + image
                    cells[target, lane(g, image, row, col)] = 1.0
    return taps, cells


def regroup(value, runs):
    return jnp.concatenate([value[:, a:b] for a, b in runs], axis=1)


def sigma(v):
    return 0.5 * jnp.tanh(0.5 * v) + 0.5


class Reduce:
    def __init__(self, net, i, k, part, bufs, windows, b4=None):
        self.b4 = b4
        self.net, self.part, self.windows = net, part, windows
        self.b1, self.s1, self.b2, self.s2, self.b3 = bufs
        self.ix, self.pz, self.hz = i % 2, (i // 2) % 2, i // 4
        self.peers = (
            (i + 1 - 2 * self.ix, k),
            (i + 2 - 4 * self.pz, k),
            (i + 4 - 8 * self.hz, k),
        )
        self.slots = [net.slot(3) for _ in windows]

    def first(self, w):
        cols = self.windows[w]
        self.net.send(
            self.part.at[:, :, 1 - self.ix, :, cols], self.b1.at[:, :, :, cols],
            self.slots[w], self.peers[0],
        )

    def second(self, w):
        cols = self.windows[w]
        self.net.arrived(self.b1.at[:, :, :, cols], self.slots[w], self.peers[0])
        for h in range(2):
            for p in range(2):
                value = self.part[h, p, self.ix, :, cols].astype(jnp.float32)
                value = value + self.b1[h, p, :, cols].astype(jnp.float32)
                self.s1[h, p, :, cols] = value.astype(jnp.bfloat16)
        self.net.send(
            self.s1.at[:, 1 - self.pz, :, cols], self.b2.at[:, :, cols],
            self.slots[w] + 1, self.peers[1],
        )

    def second_of(self, w, value):
        cols = self.windows[w]
        self.s1[:, :, :, cols] = value.reshape(2, 2, -1, value.shape[1])
        self.net.send(
            self.s1.at[:, 1 - self.pz, :, cols], self.b2.at[:, :, cols],
            self.slots[w] + 1, self.peers[1],
        )

    def spread_of(self, w, value):
        cols = self.windows[w]
        self.s1[:, :, :, cols] = value.reshape(2, 2, -1, value.shape[1])
        z = 2 * self.hz + self.pz
        self.direct = self.net.slot(4)
        for d in range(1, 4):
            to = (z + d) % 4
            self.net.send(
                self.s1.at[to // 2, to % 2, :, cols], self.b4.at[z],
                self.direct + z, (2 * to + self.ix, self.peers[0][1]),
            )

    def spread_last(self, w):
        cols = self.windows[w]
        z = 2 * self.hz + self.pz
        value = self.s1[self.hz, self.pz, :, cols].astype(jnp.float32)
        for d in range(1, 4):
            to = (z + d) % 4
            self.net.arrived(self.b4.at[to], self.direct + to, (2 * to + self.ix, self.peers[0][1]))
            value = value + self.b4[to].astype(jnp.float32)
        return value

    def third(self, w):
        cols = self.windows[w]
        self.net.arrived(self.b2.at[:, :, cols], self.slots[w] + 1, self.peers[1])
        for h in range(2):
            value = self.s1[h, self.pz, :, cols].astype(jnp.float32)
            value = value + self.b2[h, :, cols].astype(jnp.float32)
            self.s2[h, :, cols] = value.astype(jnp.bfloat16)
        self.net.send(
            self.s2.at[1 - self.hz, :, cols], self.b3.at[:, cols],
            self.slots[w] + 2, self.peers[2],
        )

    def last(self, w):
        cols = self.windows[w]
        self.net.arrived(self.b3.at[:, cols], self.slots[w] + 2, self.peers[2])
        return self.s2[self.hz, :, cols].astype(jnp.float32) + self.b3[:, cols].astype(jnp.float32)


def make_fused(n_dp, in_local, images, sides, chan_in, chan_part, stop):
    f32, bf16 = jnp.float32, jnp.bfloat16
    halves = tuple(side // 2 for side in sides)
    sizes = tuple(h * h * n for h, n in zip(halves, images))
    rows = sum(sizes)
    quarter = tuple(n // 4 for n in images)
    qlanes = tuple(q * side * side for q, side in zip(quarter, sides))
    slab_lanes = -(-sum(qlanes) // LANES) * LANES
    chan_full = 4 * chan_part
    out_rows = chan_full // n_dp
    starts = (0, sizes[0])
    widths = tuple(h * n for h, n in zip(halves, images))
    chunks = [(g, r, starts[g] + r * widths[g], widths[g]) for g in range(2) for r in range(halves[g])]
    win = [-(-q // LANES) * LANES for q in qlanes]
    b_tile = qlanes[0] // LANES * LANES
    b_skip = qlanes[0] - b_tile
    rs = halves[0] // 2
    segments = [(1, 0, halves[1]), (0, 0, rs), (0, rs, halves[0])]
    seg_lane, runs = [], []
    lane_of = 0
    for g, r0, r1 in segments:
        side, base = sides[g], (0, qlanes[0])[g]
        seg_lane.append(lane_of)
        lane_of += quarter[g] * 2 * (r1 - r0) * side
        runs += [
            (base + (image * side + 2 * r0) * side, base + (image * side + 2 * r1) * side)
            for image in range(quarter[g])
        ]
    runs.append((sum(qlanes), slab_lanes))
    at, order = 0, []
    for a, b in runs:
        order.append((a, at, at + b - a))
        at += b - a
    back_runs = [(a, b) for _, a, b in sorted(order)]
    cut_lane = -(-seg_lane[2] // LANES) * LANES
    lane_parts = (slice(0, cut_lane), slice(cut_lane, slab_lanes))
    seg_cells = [(r1 - r0) * halves[g] for g, r0, r1 in segments]
    seg_rows = [cells * quarter[seg[0]] for cells, seg in zip(seg_cells, segments)]
    top = -(-(seg_rows[0] + seg_rows[1]) // 16) * 16
    seg_row = [0, seg_rows[0], top]
    q_rows = top + -(-seg_rows[2] // 16) * 16
    row_parts = (slice(0, top), slice(top, q_rows))
    patch_win = (slice(0, cut_lane), slice(seg_lane[1] // LANES * LANES, slab_lanes))
    patch_m, cells_m = quarter_matrices(
        quarter, sides, segments, seg_lane, seg_row, q_rows, slab_lanes
    )
    patch_ms = [
        np.concatenate([m[rows_, lanes_] for m in patch_m], axis=0)
        for rows_, lanes_ in zip(row_parts, patch_win)
    ]
    spans = [
        (starts[g] + r0 * widths[g], starts[g] + r1 * widths[g])
        for g, r0, r1 in (segments[0], segments[2], segments[1])
    ]
    pieces = [[segments[0]], [segments[2]], [segments[1]]]
    part_chunks = [
        [ch for ch in chunks if ch[0] == p[0][0] and p[0][1] <= ch[1] < p[0][2]] for p in pieces
    ]
    low_lane = seg_lane[1] // LANES * LANES
    out_lanes = [slice(0, low_lane), slice(cut_lane, slab_lanes), slice(low_lane, cut_lane)]
    out_win = [spans[0], spans[1], (0, rows)]
    n_parts = 3
    mid = (rows // 32 + 1) * 16
    row_halves = (slice(0, mid), slice(mid, rows))
    cols2 = (slice(0, 5 * LANES), slice(5 * LANES, 9 * LANES))
    cols1 = (slice(6 * LANES, 10 * LANES), slice(0, 6 * LANES))

    def kernel(*refs):
        (xa_h, xb_h, bxa_h, bxb_h, w1_h, w2_h, ws_h, g1_h, b1_h, g2_h, b2_h, gs_h, bs_h, ua_h, ub_h,
         pm0_h, pm1_h, cells_h,
         turn_h,
         oa, ob, gr, gw1, gws, gw2, vecs, turn,
         xa, xb, bxa, bxb, w1g, w2, wsg, vg, g2, b2, gs, bs, ua, ub, pm0, pm1, cells,
         xs, xt, xr, zb, zsq, zsr, zg, zpa, zpb, valid, vq, hat, mask, zs, a1a, a1b,
         cslots, slots, stat, up, outr, gv, dza, dzb, dzma, dzmb, apk, arx, gacc, dzsr,
         dd, hp, hr1, hs, hr2, gu, d1a, d1b,
         p22, p23, p24, p25, p26, wg1, p11, p12, p13, p14, p15,
         gp, gr1, gsum, gr2, zt, gt, lsem, ssem, rsem) = refs
        i, k = lax.axis_index("dp"), lax.axis_index("chan")
        k1 = k + 1 - 2 * (k % 2)
        k2 = (k + 2) % 4
        k3 = (k1 + 2) % 4
        ix = i % 2
        mate = (i + 1 - 2 * ix, k)
        net = Links(ssem, rsem)
        zp, a1, dz, d1 = (zpa, zpb), (a1a, a1b), (dza, dzb), (d1a, d1b)
        dzm = (dzma, dzmb)

        def flat(value):
            return value.reshape(-1, value.shape[-1])

        def zeros(count):
            return [jnp.zeros((8, LANES), f32)] * count

        loads = {}
        pairs_of = (
            ("xa", xa_h, xa), ("xb", xb_h, xb),
            ("w1", w1_h, w1g.at[k]), ("ws", ws_h, wsg.at[k]), ("g1", g1_h, vg.at[k, 0]), ("b1", b1_h, vg.at[k, 1]),
            ("bxa", bxa_h, bxa), ("bxb", bxb_h, bxb), ("pm0", pm0_h, pm0), ("pm1", pm1_h, pm1),
            ("ua", ua_h, ua), ("ub", ub_h, ub), ("g2", g2_h, g2),
            ("b2", b2_h, b2), ("gs", gs_h, gs), ("bs", bs_h, bs), ("w2", w2_h, w2), ("cells", cells_h, cells),
            ("turn", turn_h, turn),
        )
        for index, (name, source, target) in enumerate(pairs_of):
            loads[name] = pltpu.make_async_copy(source, target, lsem.at[index])
        loads["xa"].start()
        loads["xb"].start()

        def need(*names):
            for name in names:
                loads.pop(name).wait()

        barrier = pltpu.get_barrier_semaphore()
        for d in range(1, n_dp):
            pl.semaphore_signal(barrier, inc=1, device_id=((i + d) % n_dp, k), device_id_type=MESH)
        for where in (k1, k2, k3):
            pl.semaphore_signal(barrier, inc=1, device_id=(i, where), device_id_type=MESH)

        need("xa", "xb")
        for copy in loads.values():
            copy.start()
        lane = lax.broadcasted_iota(jnp.int32, (in_local, LANES), 1)
        for d in range(n_dp):
            j = (i + d) % n_dp
            begin = 4 * qlanes[0] * j + qlanes[0] * k
            tile = begin // LANES
            part_a = xa[:, pl.ds(pl.multiple_of(tile * LANES, LANES), win[0])].astype(f32)
            part_a = pltpu.roll(part_a, (win[0] - (begin - tile * LANES)) % win[0], 1)
            begin = 4 * qlanes[1] * j + qlanes[1] * k
            tile = begin // LANES
            part_b = xb[:, pl.ds(pl.multiple_of(tile * LANES, LANES), win[1])].astype(f32)
            part_b = jnp.concatenate([part_b, jnp.zeros((in_local, LANES), f32)], axis=1)
            wide = win[1] + LANES
            part_b = pltpu.roll(part_b, (wide + b_skip - (begin - tile * LANES)) % wide, 1)
            seam = jnp.where(lane < b_skip, part_a[:, b_tile : b_tile + LANES], part_b[:, :LANES])
            xs[d * in_local : (d + 1) * in_local, :] = jnp.concatenate(
                [part_a[:, :b_tile], seam, part_b[:, LANES : slab_lanes - b_tile]], axis=1
            ).astype(bf16)
        slot_x = [net.slot(n_dp) for _ in lane_parts]
        w_taps = (slice(0, 3), slice(3, 6), slice(6, 9))
        slot_w = [net.slot(4) for _ in range(len(w_taps) + 2)]

        def weight_refs(q):
            return [w1g.at[q, taps] for taps in w_taps] + [wsg.at[q], vg.at[q]]

        ordered = regroup(xs[...], runs)
        for c, cols in enumerate(lane_parts):
            moved = ordered[:, cols]
            xt[:, :, cols] = moved.reshape(n_dp, in_local, moved.shape[1])
            xr[i, :, cols] = moved[:in_local]
            if c == 0:
                pl.semaphore_wait(barrier, n_dp + 2)
            for d in range(1, n_dp):
                net.send(xt.at[d, :, cols], xr.at[i, :, cols], slot_x[c] + i, ((i + d) % n_dp, k))
            if c == 0:
                need("w1", "ws", "g1", "b1")
                for where in (k2, k1):
                    for ref, slot in zip(weight_refs(k), slot_w):
                        net.send(ref, ref, slot + k, (i, where))

        def weights_on(n):
            ref = weight_refs(k2)[n]
            net.arrived(ref, slot_w[n] + k2, (i, k2))
            net.send(ref, ref, slot_w[n] + k2, (i, k1))

        def weights_in():
            for q in (k1, k3):
                for ref, slot in zip(weight_refs(q), slot_w):
                    net.arrived(ref, slot + q, (i, k1))

        for buf in (zpa, zpb, a1a, a1b, dza, dzb, dzma, dzmb, d1a, d1b):
            side = buf.shape[1] if len(buf.shape) == 5 else buf.shape[0]
            lead = (slice(None),) if len(buf.shape) == 5 else ()
            for edge in (0, side - 1):
                for index in (lead + (edge,), lead + (slice(None), edge)):
                    region = buf.at[index]
                    region[...] = jnp.zeros(region.shape, buf.dtype)
        need("bxa", "bxb", "ua", "ub")
        population = zeros(1)[0]
        low = lax.broadcasted_iota(jnp.int32, (8, LANES), 0) < 4
        for g, box in enumerate((bxa, bxb)):
            n, half, count = images[g], halves[g], quarter[g]
            diag = lax.broadcasted_iota(jnp.int32, (n, n), 0) == lax.broadcasted_iota(jnp.int32, (n, n), 1)
            ends = [
                jnp.sum(jnp.where(diag, box[q : q + 1, :].astype(f32), 0.0), axis=1, keepdims=True)
                for q in range(4)
            ]
            ends = [jnp.broadcast_to(e, (n, LANES)) for e in ends]
            ends[2], ends[3] = ends[0] + ends[2], ends[1] + ends[3]

            def inside(ends, r, s):
                both = (r >= ends[0]) & (r < ends[2]) & (s >= ends[1]) & (s < ends[3])
                return both.astype(f32)

            for r in range(half):
                for s in range(half):
                    cell = inside(ends, r, s)
                    begin = starts[g] + (r * half + s) * n
                    valid[begin : begin + n, :] = cell
                    population = population + jnp.sum(cell.reshape(n // 8, 8, LANES), axis=0)
            mine = [pltpu.roll(e, (n - count * k) % n, 0)[:8] for e in ends]
            if count < 8:
                mine = [jnp.where(low, e, pltpu.roll(e, 4, 0)) for e in mine]
            for (seg_g, r0, r1), first, cells_n in zip(segments, seg_row, seg_cells):
                if seg_g != g:
                    continue
                per = 8 // count
                for t in range(-(-cells_n // per)):
                    spots = [divmod(min(per * t + e, cells_n - 1), half) for e in range(per)]
                    spots = [(float(r0 + r), float(s)) for r, s in spots]
                    if per == 2:
                        r, s = (jnp.where(low, spots[0][e], spots[1][e]) for e in range(2))
                    else:
                        r, s = spots[0]
                    cell = inside(mine, r, s)
                    if per == 2 and per * t + 1 >= cells_n:
                        cell = jnp.where(low, cell, 0.0)
                    vq[first + 8 * t : first + 8 * t + 8, :] = cell
        population = jnp.broadcast_to(jnp.sum(population, axis=0, keepdims=True), (8, LANES))
        for g, source in enumerate((ua, ub)):
            n, count = images[g], halves[g] ** 2
            gu[starts[g] : starts[g] + sizes[g], :] = source[...].astype(f32)
            for cell in range(count):
                up[starts[g] + cell * n : starts[g] + (cell + 1) * n, :] = gu[
                    pl.ds(starts[g] + cell, n, stride=count), :
                ]

        def rowsum(value):
            return jnp.sum(value.reshape(-1, 8, value.shape[-1]), axis=0)

        def message(sums):
            parts = [jnp.sum(v, axis=0, keepdims=True) if v.shape[0] > 1 else v for v in sums]
            if len(parts) % 8:
                parts.append(jnp.zeros((8 - len(parts) % 8, LANES), f32))
            return jnp.concatenate(parts, axis=0)

        def by_chan(value):
            return [value[:, q * LANES : (q + 1) * LANES] for q in range(4)]

        def share(rnd, value):
            mine = slots.at[rnd, i, : value.shape[0]]
            mine[...] = value
            first = net.slot(n_dp)
            for d in range(1, n_dp):
                net.send(mine, mine, first + i, ((i + d) % n_dp, k))
            return first

        def total(rnd, first, count=8):
            for d in range(1, n_dp):
                j = (i + d) % n_dp
                net.arrived(slots.at[rnd, j, :count], first + j, (j, k))
            return jnp.sum(slots[rnd, :, :count], axis=0)

        def chan_share(rnd, value):
            mine = cslots.at[rnd, k, : value.shape[0]]
            mine[...] = value
            first = net.slot(4)
            for where in (k2, k3, k1):
                net.send(mine, mine, first + k, (i, where))
            return first

        def chan_total(rnd, first, count=8):
            for where in (k1, k2, k3):
                net.arrived(cslots.at[rnd, where, :count], first + where, (i, where))
            return jnp.sum(cslots[rnd, :, :count], axis=0)

        pop_first = share(4, population)

        def quarter_in(c):
            for d in range(1, n_dp):
                j = (i + d) % n_dp
                net.arrived(xr.at[j, :, lane_parts[c]], slot_x[c] + j, (j, k))

        def patches(c):
            whole = jnp.concatenate([xr[q, :, patch_win[c]] for q in range(n_dp)], axis=0)
            value = mm((pm0, pm1)[c][...], whole, 1, 1).astype(bf16)
            count = value.shape[0] // 9
            return [value[t * count : (t + 1) * count] for t in range(9)]

        slot_z = [net.slot(4) for _ in row_parts]
        slot_s = net.slot(4)

        def first_conv(c, taps, acc):
            part = row_parts[c]
            weights = lanes_cat([w1g[q].reshape(9 * chan_in, chan_part) for q in range(4)])
            value = mm(lanes_cat(taps), weights, 1, 0).astype(bf16)
            zb[k, part, :] = value
            for where in (k2, k1):
                net.send(zb.at[k, part], zb.at[k, part], slot_z[c] + k, (i, where))
            side = mm(taps[4], lanes_cat([wsg[q] for q in range(4)]), 1, 0).astype(bf16)
            ok = lanes_cat([vq[part, :]] * 4)
            for n, z in enumerate((value, side)):
                z = z.astype(f32)
                u = z * ok
                acc[2 * n] = acc[2 * n] + rowsum(u)
                acc[2 * n + 1] = acc[2 * n + 1] + rowsum(u * z)
            for q, z in enumerate(by_chan(side)):
                zsq[q, part, :] = z
            return acc

        def act_on(c):
            part = row_parts[c]
            net.arrived(zb.at[k2, part], slot_z[c] + k2, (i, k2))
            net.send(zb.at[k2, part], zb.at[k2, part], slot_z[c] + k2, (i, k1))

        def act_in(c):
            part = row_parts[c]
            net.arrived(zb.at[k1, part], slot_z[c] + k1, (i, k1))
            net.arrived(zb.at[k3, part], slot_z[c] + k3, (i, k1))

        acc = [jnp.zeros((8, chan_full), f32)] * 4
        need("pm0", "pm1")
        weights_on(0)
        weights_on(1)
        quarter_in(0)
        taps = patches(0)
        for n in range(2, 5):
            weights_on(n)
        weights_in()
        acc = first_conv(0, taps, acc)
        quarter_in(1)
        acc = first_conv(1, patches(1), acc)
        acc = [jnp.sum(v, axis=0, keepdims=True) for v in acc]
        first = share(0, message(sum((by_chan(v) for v in acc), [])))
        act_on(0)
        need(*list(loads))
        inv_pop = 1.0 / total(4, pop_first)[0:1]
        first = chan_share(0, total(0, first, 16))
        for where in (k2, k3, k1):
            net.send(zsq.at[where], zsr.at[k], slot_s + k, (i, where))
        zsr[k] = zsq[k]
        act_on(1)
        act_in(0)
        tot = chan_total(0, first, 16)
        stat[...] = tot
        tot_first = (stat[pl.ds(k, 1), :], stat[pl.ds(4 + k, 1), :])
        if stop == 3:
            act_in(1)
            for where in (k2, k3, k1):
                net.arrived(zsr.at[where], slot_s + where, (i, where))
            valid[0:1, :] = inv_pop
            return net.drain()

        def moments(total_, square):
            mean = total_ * inv_pop
            return mean, lax.rsqrt(square * inv_pop - mean * mean + epsilon)

        mean1, sc1 = moments(tot[0:4], tot[4:8])
        mean1, sc1 = (lanes_cat([v[q : q + 1] for q in range(4)]) for v in (mean1, sc1))
        gain1, shift1 = (lanes_cat([vg[q, e] for q in range(4)]) for e in range(2))

        turn_low = lax.broadcasted_iota(jnp.int32, (8, 1), 0) < 4

        def whole_cells(read, c):
            for begin in range(row_parts[c].start, row_parts[c].stop, 16):
                blocks = [read(q, slice(begin, begin + 16)).astype(f32) for q in range(4)]
                for at in (begin, begin + 8):
                    seg = max(e for e in range(3) if seg_row[e] <= at)
                    g, r0, r1 = segments[seg]
                    per = 8 // quarter[g]
                    v = [block[at - begin : at - begin + 8] for block in blocks]
                    cell = (at - seg_row[seg]) // 8 * per
                    if per == 1:
                        found = [jnp.concatenate(v, axis=0)]
                    else:
                        t = [pltpu.roll(e, 4, 0) for e in v]
                        found = [
                            jnp.concatenate(
                                [jnp.where(turn_low, v[0], t[1]), jnp.where(turn_low, v[2], t[3])], axis=0
                            ),
                            jnp.concatenate(
                                [jnp.where(turn_low, t[0], v[1]), jnp.where(turn_low, t[2], v[3])], axis=0
                            ),
                        ]
                    for e, value in enumerate(found):
                        if cell + e < seg_cells[seg]:
                            r, s = divmod(cell + e, halves[g])
                            yield g, r0 + r, s, value

        def activate(c):
            for g, r, s, z in whole_cells(lambda q, span: zb[q, span, :], c):
                begin = starts[g] + (r * halves[g] + s) * images[g]
                span = slice(begin, begin + images[g])
                h = (z - mean1) * sc1
                hat[span, :] = h
                v = h * gain1 + shift1
                act = v * sigma(v) * lanes_cat([valid[span, :]] * 4)
                a1[g][1 + r, 1 + s] = act.astype(bf16)

        def second_conv(parts, acc):
            value = None
            for a, b in TAPS:
                patch = jnp.concatenate(
                    [flat(a1[g][r0 + a : r1 + a, b : b + halves[g]]) for g, r0, r1 in parts], axis=0
                )
                part = mm(patch, w2[3 * a + b], 1, 0)
                value = part if value is None else value + part
            at = 0
            for g, r0, r1 in parts:
                for r in range(r0, r1):
                    begin = starts[g] + r * widths[g]
                    span = slice(begin, begin + widths[g])
                    u = value[at : at + widths[g]]
                    at += widths[g]
                    gv[span, :] = u
                    uv = u * valid[span, :]
                    acc = [acc[0] + rowsum(uv), acc[1] + rowsum(uv * u)]
            return acc

        left = lax.broadcasted_iota(jnp.int32, (1, LANES), 1) < out_rows

        def pack(g, r0, r1):
            for r in range(r0, r1):
                v = by_chan(flat(a1[g][1 + r, 1 : 1 + halves[g]]).astype(f32))
                t = [pltpu.roll(e, out_rows, 1) for e in v]
                begin = starts[g] + r * widths[g]
                span = slice(begin, begin + widths[g])
                for p in range(2):
                    cols = slice(p * LANES, (p + 1) * LANES)
                    apk[0, span, cols] = jnp.where(left, v[2 * p], t[2 * p + 1]).astype(bf16)
                    apk[1, span, cols] = jnp.where(left, t[2 * p], v[2 * p + 1]).astype(bf16)

        early = starts[1] + sizes[1] * 3 // 64 * 16
        third_cut = rs * widths[0] + (sizes[0] - rs * widths[0]) * 4 // 80 * 16
        pack_spans = [
            [slice(starts[1], early)],
            [slice(early, rows), slice(0, rs * widths[0])],
            [slice(rs * widths[0], third_cut)],
            [slice(third_cut, sizes[0])],
        ]
        slot_p = [[net.slot() for _ in spans_] for spans_ in pack_spans]

        def pack_send(n):
            for span, slot in zip(pack_spans[n], slot_p[n]):
                net.send(apk.at[1 - ix, span], arx.at[span], slot, mate)

        act_in(1)
        activate(0)
        pack(1, 0, halves[1])
        pack(0, 0, rs)
        acc = second_conv([(1, 0, halves[1]), (0, 0, rs - 1)], zeros(2))
        pack_send(0)
        activate(1)
        pack(0, rs, halves[0])
        acc = second_conv([(0, rs - 1, halves[0])], acc)
        first = share(1, message(acc))
        pack_send(1)

        for where in (k2, k3, k1):
            net.arrived(zsr.at[where], slot_s + where, (i, where))
        means, scs = moments(stat[pl.ds(8 + k, 1), :], stat[pl.ds(12 + k, 1), :])
        for c in range(2):
            for g, r, s, z in whole_cells(lambda q, span: zsr[q, span, :], c):
                begin = starts[g] + (r * halves[g] + s) * images[g]
                zs[begin : begin + images[g], :] = (z - means) * scs
        row_cuts = (slice(0, rows // 32 * 16), slice(rows // 32 * 16, rows))
        slot_g0 = [net.slot(4) for _ in row_cuts]
        whole = jnp.concatenate([xr[q] for q in range(n_dp)], axis=0)
        for span, slot in zip(row_cuts, slot_g0):
            zg[k, span, :] = mm(cells[span, :], whole, 1, 1).astype(bf16)
            for where in (k2, k1):
                net.send(zg.at[k, span], zg.at[k, span], slot + k, (i, where))

        def slab_on(n):
            span, slot = row_cuts[n], slot_g0[n]
            net.arrived(zg.at[k2, span], slot + k2, (i, k2))
            net.send(zg.at[k2, span], zg.at[k2, span], slot + k2, (i, k1))

        def slab_in(n):
            span, slot = row_cuts[n], slot_g0[n]
            net.arrived(zg.at[k1, span], slot + k1, (i, k1))
            net.arrived(zg.at[k3, span], slot + k3, (i, k1))

        def planes_of(quarters, g):
            count = quarter[g]
            if count % 8 == 0:
                return [
                    jnp.concatenate([v[:, count * p : count * (p + 1)] for v in quarters], axis=1)
                    for p in range(4)
                ]
            low = lax.broadcasted_iota(jnp.int32, (1, 8, 1), 1) < 4
            parts = [[v[:, 8 * h : 8 * h + 8] for v in quarters] for h in range(2)]
            turned = [[pltpu.roll(v, 4, 1) for v in side] for side in parts]
            result = []
            for p in range(4):
                v, t = parts[p // 2], turned[p // 2]
                if p % 2 == 0:
                    both = [jnp.where(low, v[0], t[1]), jnp.where(low, v[2], t[3])]
                else:
                    both = [jnp.where(low, t[0], v[1]), jnp.where(low, t[2], v[3])]
                result.append(jnp.concatenate(both, axis=1))
            return result

        def make_planes():
            for g, r, begin, count in chunks:
                quarters = [
                    zg[q, begin : begin + count, :].astype(f32).reshape(halves[g], images[g], chan_in)
                    for q in range(4)
                ]
                for p, value in enumerate(planes_of(quarters, g)):
                    zp[g][p, 1 + r, 1 : 1 + halves[g]] = value.astype(bf16)

        tot = total(1, first)
        mean2, sc2 = moments(tot[0:1], tot[1:2])
        if stop == 5:
            valid[0:1, :] = sc2
            for n in range(2):
                slab_on(n)
            for n in range(2):
                slab_in(n)
            return net.drain()
        gain2, gains = g2[...], gs[...]
        shifts = b2[...] + bs[...]
        acc = zeros(3)
        for g, r, begin, count in chunks:
            span = slice(begin, begin + count)
            ok = valid[span, :]
            hat2 = (gv[span, :] - mean2) * sc2
            hats = zs[span, :]
            v = hat2 * gain2 + hats * gains + shifts
            sig = sigma(v)
            outr[span, :] = v * sig * ok
            grad = up[span, :] * ok * (sig * (1.0 + v * (1.0 - sig)))
            up[span, :] = grad
            gv[span, :] = hat2
            acc = [acc[0] + rowsum(grad), acc[1] + rowsum(grad * hat2), acc[2] + rowsum(grad * hats)]
        first = share(2, message(acc))
        pack_send(2)
        for g, target in enumerate((oa, ob)):
            n, count = images[g], halves[g] ** 2
            for cell in range(count):
                gu[pl.ds(starts[g] + cell, n, stride=count), :] = outr[
                    starts[g] + cell * n : starts[g] + (cell + 1) * n, :
                ]
            target[...] = gu[starts[g] : starts[g] + sizes[g], :].astype(bf16)
        for begin in range(0, rows, 16):
            span = slice(begin, begin + 16)
            v = hat[span, :] * gain1 + shift1
            sig = sigma(v)
            mask[span, :] = sig * (1.0 + v * (1.0 - sig)) * lanes_cat([valid[span, :]] * 4)
        tot = total(2, first)
        sum_tail, sum_gain2, sum_gains = tot[0:1], tot[1:2], tot[2:3]
        if stop == 6:
            valid[0:1, :] = sum_tail
            for n in range(2):
                slab_on(n)
            for n in range(2):
                slab_in(n)
            return net.drain()

        k2g, ksg = gain2 * sc2, gains * scs
        db, dg2, dgs = sum_tail * inv_pop, sum_gain2 * inv_pop, sum_gains * inv_pop
        for g, r, begin, count in chunks:
            span = slice(begin, begin + count)
            value = k2g * (up[span, :] - valid[span, :] * (db + gv[span, :] * dg2))
            dz[g][1 + r, 1 : 1 + halves[g]] = value.astype(bf16).reshape(halves[g], images[g], chan_part)
        slot_d = net.slot(2)

        def dz_inner(buf, g):
            return buf[g].at[1 : 1 + halves[g], 1 : 1 + halves[g]]

        pack_send(3)
        for g in range(2):
            net.send(dz_inner(dz, g), dz_inner(dzm, g), slot_d + g, mate)

        def columns(buf):
            for g in range(2):
                for t, (a, b) in enumerate(TAPS):
                    dd[starts[g] : starts[g] + sizes[g], t * LANES : (t + 1) * LANES] = flat(
                        buf[g][2 - a : 2 - a + halves[g], 2 - b : 2 - b + halves[g]]
                    )

        columns(dz)

        def back_second(first, span):
            begin = pl.multiple_of(first * chan_part, LANES)
            weights = lanes_cat([w2[t, pl.ds(begin, 2 * chan_part), :] for t in range(9)])
            value = mm(dd[span, :], weights, 1, 1).astype(bf16)
            hp[first, span, :] = value[:, :chan_part]
            hp[first + 1, span, :] = value[:, chan_part:]

        slot_h = [net.slot(3) for _ in row_halves]
        for span, slot in zip(row_halves, slot_h):
            back_second(2 * (k2 // 2), span)
            net.send(hp.at[k3, span], hr1.at[1, span], slot + 1, (i, k1))
        for span, slot in zip(row_halves, slot_h):
            net.arrived(hr1.at[1, span], slot + 1, (i, k1))
            hs[span, :] = (hp[k2, span, :].astype(f32) + hr1[1, span, :].astype(f32)).astype(bf16)
            net.send(hs.at[span], hr2.at[span], slot + 2, (i, k2))
        back_second(2 * (k // 2), slice(0, rows))
        for span, slot in zip(row_halves, slot_h):
            net.send(hp.at[k1, span], hr1.at[0, span], slot, (i, k1))

        acc = [jnp.zeros((8, chan_full), f32)] * 2
        for begin in range(0, rows, 16):
            span = slice(begin, begin + 16)
            part = lanes_cat([hp[q, span, :] for q in range(4)]).astype(f32) * mask[span, :]
            acc = [acc[0] + rowsum(part), acc[1] + rowsum(part * hat[span, :])]
        acc = [jnp.sum(v, axis=0, keepdims=True) for v in acc]
        first = share(3, message(sum((by_chan(v) for v in acc), [])))

        sum2 = Reduce(net, i, k, None, (None, p22, p23, p24, p25), cols2, p26)
        gacc[...] = mm(apk[ix], dd[...], 0, 0)
        first = chan_share(1, total(3, first))
        for g, r, begin, count in chunks:
            span = slice(begin, begin + count)
            value = ksg * (up[span, :] - valid[span, :] * (db + zs[span, :] * dgs))
            dzsr[span, :] = value.astype(bf16)
        for n in range(2):
            slab_on(n)
        for spans_, slots_ in zip(pack_spans, slot_p):
            for span, slot in zip(spans_, slots_):
                net.arrived(arx.at[span], slot, mate)
        for g in range(2):
            net.arrived(dz_inner(dzm, g), slot_d + g, mate)
        columns(dzm)
        for w, cols in enumerate(cols2):
            value = (gacc[:, cols] + mm(arx[...], dd[:, cols], 0, 0)).astype(bf16)
            (sum2.spread_of, sum2.second_of)[w](w, value)
        tot = chan_total(1, first)
        stat[0:8, :] = tot
        sum_head, sum_gain1 = stat[pl.ds(k, 1), :], stat[pl.ds(4 + k, 1), :]

        def close_second():
            for w, cols in enumerate(cols2):
                value = (sum2.spread_last, sum2.last)[w](w)
                for t in range(cols.start // LANES, cols.stop // LANES):
                    gw2[t] = value[:, t * LANES - cols.start : (t + 1) * LANES - cols.start]

        own = pl.ds(pl.multiple_of(k * chan_part, LANES), chan_part)
        mean1, sc1 = moments(tot_first[0], tot_first[1])
        k1g = vg[k, 0] * sc1
        db, dg1 = sum_head * inv_pop, sum_gain1 * inv_pop
        per_cell = [(g, r, s) for g in range(2) for r in range(halves[g]) for s in range(halves[g])]
        waiting = list(zip(row_halves, slot_h))
        for g, r, s in per_cell:
            begin = starts[g] + (r * halves[g] + s) * images[g]
            part = slice(begin, begin + images[g])
            while waiting and waiting[0][0].start < part.stop:
                span, slot = waiting.pop(0)
                net.arrived(hr1.at[0, span], slot, (i, k1))
                net.arrived(hr2.at[span], slot + 2, (i, k2))
            grad = hp[k, part, :].astype(f32) + hr1[0, part, :].astype(f32) + hr2[part, :].astype(f32)
            grad = grad * mask[part, own]
            value = k1g * (grad - valid[part, :] * (db + hat[part, own] * dg1))
            d1[g][r, s] = value.astype(bf16)
        if stop == 8:
            valid[0:1, :] = sum_head
            sum2.third(1)
            close_second()
            for n in range(2):
                slab_in(n)
            return net.drain()

        def back_patch(pieces, p):
            parts = []
            for g, r0, r1 in pieces:
                width = halves[g] * images[g]
                taps = [
                    flat(d1[g][r0 + (a == 0) : r1 + (a == 0), (b == 0) : (b == 0) + halves[g]])
                    for a, b in PLANE_TAPS[p]
                ]
                if p == 0:
                    taps.append(dzsr[starts[g] + r0 * width : starts[g] + r1 * width, :])
                parts.append(lanes_cat(taps))
            return jnp.concatenate(parts, axis=0) if len(parts) > 1 else parts[0]

        slot_g = [net.slot(3) for _ in range(n_parts)]

        def back_first(c):
            a, b = spans[c]
            planes = []
            for p in range(4):
                weights = [w1g[k, 3 * ta + tb] for ta, tb in PLANE_TAPS[p]]
                if p == 0:
                    weights.append(wsg[k])
                planes.append(mm(back_patch(pieces[c], p), lanes_cat(weights), 1, 1))
            for g, r, begin, count in part_chunks[c]:
                values = [
                    v[begin - a : begin - a + count].reshape(halves[g], images[g], chan_in)
                    for v in planes
                ]
                for q, value in enumerate(planes_of(values, g)):
                    gp[q, begin : begin + count, :] = flat(value).astype(bf16)
            net.send(gp.at[k3, a:b], gr1.at[1, a:b], slot_g[c] + 1, (i, k1))

        def back_cross(c):
            a, b = spans[c]
            net.arrived(gr1.at[1, a:b], slot_g[c] + 1, (i, k1))
            for begin in range(a, b, 16):
                span = slice(begin, begin + 16)
                value = gp[k2, span, :].astype(f32) + gr1[1, span, :].astype(f32)
                gsum[span, :] = value.astype(bf16)
            net.send(gsum.at[a:b], gr2.at[a:b], slot_g[c] + 2, (i, k2))
            net.send(gp.at[k1, a:b], gr1.at[0, a:b], slot_g[c], (i, k1))

        slot_o = [net.slot(n_dp) for _ in range(n_parts)]

        def back_out(c):
            a, b = spans[c]
            net.arrived(gr1.at[0, a:b], slot_g[c], (i, k1))
            net.arrived(gr2.at[a:b], slot_g[c] + 2, (i, k2))
            for begin in range(a, b, 16):
                span = slice(begin, begin + 16)
                value = gp[k, span, :].astype(f32) + gr1[0, span, :].astype(f32)
                zt[span, :] = (value + gr2[span, :].astype(f32)).astype(bf16)
            cols = out_lanes[c]
            a, b = out_win[c]
            value = mm(zt[a:b, :], cells[a:b, cols], 0, 0).astype(bf16)
            gt[:, :, cols] = value.reshape(n_dp, in_local, value.shape[1])
            for d in range(1, n_dp):
                j = (i + d) % n_dp
                net.send(gt.at[j, :, cols], gr.at[i, :, cols], slot_o[c] + i, (j, k))

        sum1 = Reduce(net, i, k, wg1, (p11, p12, p13, p14, p15), cols1)

        def weight_first(w):
            cols = cols1[w]
            blocks = []
            for p in ((3,), (0, 1, 2))[w]:
                value = 0.0
                for g, r0, r1 in ((0, 0, halves[0]), (1, 0, halves[1])):
                    cell = flat(zp[g][p, 1 : 1 + halves[g], 1 : 1 + halves[g]])
                    value = value + mm(cell, back_patch([(g, r0, r1)], p), 0, 0)
                blocks.append(value.astype(bf16))
            wg1[:, :, :, :, cols] = lanes_cat(blocks).reshape(2, 2, 2, in_local, cols.stop - cols.start)
            sum1.first(w)

        back_first(0)
        for n in range(2):
            slab_in(n)
        make_planes()
        weight_first(0)
        back_cross(0)
        weight_first(1)
        back_first(1)
        back_first(2)
        back_cross(1)
        back_cross(2)
        back_out(0)
        sum2.third(1)
        sum1.second(0)
        sum1.second(1)
        back_out(1)
        sum1.third(0)
        back_out(2)
        sum1.third(1)
        gr[i] = gt[i]
        close_second()
        for w, cols in enumerate(cols1):
            value = sum1.last(w)
            for t, tap in enumerate(TAPS):
                place = ORDER.index(tap)
                place = (place + (place > 0)) * LANES
                if cols.start <= place < cols.stop:
                    gw1[t] = value[:, place - cols.start : place - cols.start + LANES]
            if cols.start <= LANES < cols.stop:
                gws[...] = value[:, LANES - cols.start : 2 * LANES - cols.start]
        vecs[...] = message([sum_gain1, sum_head, sum_gain2, sum_tail, sum_gains])
        for c in range(n_parts):
            cols = out_lanes[c]
            for d in range(1, n_dp):
                j = (i + d) % n_dp
                net.arrived(gr.at[j, :, cols], slot_o[c] + j, (j, k))
        net.drain()

    V = pltpu.VMEM
    pads = [(h + 2, h + 2, n, chan_part) for h, n in zip(halves, images)]
    half_pads = [(h + 1, h + 1, n) for h, n in zip(halves, images)]

    def ladder(count, width):
        return [
            V((2, 2, 2, count, width), bf16), V((2, 2, count, width), bf16), V((2, 2, count, width), bf16),
            V((2, count, width), bf16), V((2, count, width), bf16), V((count, width), bf16),
        ]

    inputs = [
        V((in_local, n_dp * 4 * qlanes[0]), bf16), V((in_local, n_dp * 4 * qlanes[1]), bf16),
        V((4, images[0]), jnp.int32), V((4, images[1]), jnp.int32),
        V((4, 9, chan_in, chan_part), bf16), V((9, chan_full, chan_part), bf16),
        V((4, chan_in, chan_part), bf16), V((4, 2, 1, chan_part), f32),
    ] + [V((1, chan_part), f32)] * 4 + [
        V((sizes[0], chan_part), bf16), V((sizes[1], chan_part), bf16),
    ] + [V(m.shape, bf16) for m in patch_ms] + [V((rows, slab_lanes), bf16)]
    scratch = inputs + [
        V((n_dp * in_local, slab_lanes), bf16),
        V((n_dp, in_local, slab_lanes), bf16),
        V((n_dp, in_local, slab_lanes), bf16),
        V((4, q_rows, chan_full), bf16),
        V((4, q_rows, chan_part), bf16),
        V((4, q_rows, chan_part), bf16),
        V((4, rows, chan_in), bf16),
        V((4,) + half_pads[0] + (chan_in,), bf16),
        V((4,) + half_pads[1] + (chan_in,), bf16),
        V((rows, LANES), f32),
        V((q_rows, LANES), f32),
        V((rows, chan_full), f32),
        V((rows, chan_full), f32),
        V((rows, chan_part), f32),
        V(pads[0][:3] + (chan_full,), bf16),
        V(pads[1][:3] + (chan_full,), bf16),
        V((2, 4, 16, LANES), f32),
        V((5, n_dp, 16, LANES), f32),
        V((16, LANES), f32),
        V((rows, chan_part), f32),
        V((rows, chan_part), f32),
        V((rows, chan_part), f32),
        V(pads[0], bf16),
        V(pads[1], bf16),
        V(pads[0], bf16),
        V(pads[1], bf16),
        V((2, rows, chan_full // 2), bf16),
        V((rows, chan_full // 2), bf16),
        V((chan_full // 2, 9 * chan_part), f32),
        V((rows, chan_part), bf16),
        V((rows, 9 * chan_part), bf16),
        V((4, rows, chan_part), bf16),
        V((2, rows, chan_part), bf16),
        V((rows, chan_part), bf16),
        V((rows, chan_part), bf16),
        V((rows, chan_part), f32),
        V(half_pads[0] + (chan_part,), bf16),
        V(half_pads[1] + (chan_part,), bf16),
    ]
    scratch += ladder(out_rows, 9 * LANES)[2:]
    scratch += [V((n_dp // 2, out_rows, cols2[0].stop), bf16)] + ladder(in_local, 10 * LANES)
    scratch += [
        V((4, rows, chan_in), bf16),
        V((2, rows, chan_in), bf16),
        V((rows, chan_in), bf16),
        V((rows, chan_in), bf16),
        V((rows, chan_in), bf16),
        V((n_dp, in_local, slab_lanes), bf16),
        pltpu.SemaphoreType.DMA((20,)),
        pltpu.SemaphoreType.DMA((192,)),
        pltpu.SemaphoreType.DMA((192,)),
    ]
    mid_outs = [
        V((sizes[0], chan_part), bf16),
        V((sizes[1], chan_part), bf16),
        V((n_dp, in_local, slab_lanes), bf16),
        V((9, in_local, LANES), f32),
        V((in_local, LANES), f32),
        V((9, out_rows, LANES), f32),
        V((8, LANES), f32),
        V((n_dp * in_local, n_dp * in_local), bf16),
    ]
    vmem = pl.BlockSpec(memory_space=pltpu.VMEM)
    hbm = pl.BlockSpec(memory_space=pl.ANY)
    main = pl.pallas_call(
        kernel,
        out_shape=mid_outs,
        in_specs=[hbm] * 19,
        out_specs=[vmem] * len(mid_outs),
        scratch_shapes=scratch,
        compiler_params=pltpu.CompilerParams(
            collective_id=1, has_side_effects=True, vmem_limit_bytes=58 * 2**20
        ),
        name="block",
    )

    def closing(oa, ob, gr, gw1, gws, gw2, vecs, turn,
                fa, fb, ia, ib, f1, f2, fs, c1, h1, c2, h2, cs, hs, sems):
        outs = [
            pltpu.make_async_copy(source, target, sems.at[index])
            for index, (source, target) in enumerate(
                ((gw2, f2), (gw1, f1), (oa, fa), (ob, fb), (gws, fs))
            )
        ]
        for out in outs:
            out.start()
        moved = mm(turn[...], gr[...].reshape(n_dp * in_local, slab_lanes), 1, 0)
        natural = regroup(moved, back_runs)
        ia[...] = natural[:, : qlanes[0]].reshape(in_local, n_dp, qlanes[0]).astype(bf16)
        tail = natural[:, qlanes[0] : qlanes[0] + qlanes[1]]
        ib[...] = tail.reshape(in_local, n_dp, qlanes[1]).astype(bf16)
        for ref, row in ((c1, 0), (h1, 1), (c2, 2), (h2, 3), (cs, 4), (hs, 3)):
            ref[...] = vecs[row : row + 1, :]
        for out in outs:
            out.wait()

    last = pl.pallas_call(
        closing,
        out_shape=[
            jax.ShapeDtypeStruct((sizes[0], chan_part), bf16),
            jax.ShapeDtypeStruct((sizes[1], chan_part), bf16),
            jax.ShapeDtypeStruct((in_local, n_dp, qlanes[0]), bf16),
            jax.ShapeDtypeStruct((in_local, n_dp, qlanes[1]), bf16),
            jax.ShapeDtypeStruct((9, in_local, LANES), f32),
            jax.ShapeDtypeStruct((9, out_rows, LANES), f32),
            jax.ShapeDtypeStruct((in_local, LANES), f32),
        ]
        + [jax.ShapeDtypeStruct((1, LANES), f32)] * 6,
        in_specs=[vmem] * 8,
        out_specs=[hbm, hbm, vmem, vmem, hbm, hbm, hbm] + [vmem] * 6,
        scratch_shapes=[pltpu.SemaphoreType.DMA((5,))],
        compiler_params=pltpu.CompilerParams(vmem_limit_bytes=32 * 2**20),
        name="closing",
    )
    total_rows = n_dp * in_local
    turn = np.zeros((total_rows, total_rows), np.float32)
    for c in range(in_local):
        for j in range(n_dp):
            turn[c * n_dp + j, j * in_local + c] = 1.0
    return (main, last) + tuple(m.astype(jnp.bfloat16) for m in (*patch_ms, cells_m, turn))


STOP = 99


def fused_body(
    input_a, input_b, boxes_a, boxes_b, weight_first, weight_second, weight_short,
    gain_first, shift_first, gain_second, shift_second, gain_short, shift_short,
    upstream_a, upstream_b,
):
    n_dp = lax.axis_size("dp")
    chan_part = weight_first.shape[2]
    in_local = input_a.shape[0]
    main, last, *matrices = make_fused(
        n_dp, in_local, (boxes_a.shape[0], boxes_b.shape[0]), (SA, SB),
        weight_first.shape[1], chan_part, STOP,
    )
    vectors = [
        v.reshape(1, chan_part)
        for v in (gain_first, shift_first, gain_second, shift_second, gain_short, shift_short)
    ]
    mid = main(
        input_a, input_b, boxes_a.T, boxes_b.T, weight_first, weight_second, weight_short,
        *vectors, upstream_a.T, upstream_b.T, *matrices,
    )
    res = last(*mid)
    return (
        res[0].T, res[1].T,
        res[2].reshape(in_local, n_dp, 1, -1), res[3].reshape(in_local, n_dp, 1, -1),
        res[4], res[5], res[6],
    ) + tuple(v.reshape(chan_part) for v in res[7:])


def choose_body(mesh):
    return fused_body if mesh.shape["dp"] == 8 and mesh.shape["chan"] == 4 else plain_body


def solution(mesh):
    placed = (
        P("dp", None),
        P("dp", None),
        P("dp", None),
        P("dp", None),
        P(None, None, "chan"),
        P(None, None, "chan"),
        P(None, "chan"),
        P("chan"),
        P("chan"),
        P("chan"),
        P("chan"),
        P("chan"),
        P("chan"),
        P("chan", "dp"),
        P("chan", "dp"),
    )
    return jax.shard_map(
        choose_body(mesh),
        mesh=mesh,
        in_specs=placed,
        out_specs=(
            P("chan", "dp"),
            P("chan", "dp"),
            P("dp", None, "chan", None),
            P("dp", None, "chan", None),
            P(None, "dp", "chan"),
            P(None, "dp", "chan"),
            P("dp", "chan"),
            P("chan"),
            P("chan"),
            P("chan"),
            P("chan"),
            P("chan"),
            P("chan"),
        ),
        check_vma=False,
    )
```

```python
import jax
import jax.numpy as jnp
from jax import lax
import numpy as np
from jax.experimental import pallas as pl
from jax.experimental.pallas import tpu as pltpu
from jax.sharding import PartitionSpec as P

SA = 14
SB = 6


epsilon = 1e-05


def box_mask(box_rows, extent):
    positions = jnp.arange(extent, dtype=jnp.int32)[None, :]
    row_inside = (positions >= box_rows[:, 0:1]) & (positions < box_rows[:, 0:1] + box_rows[:, 2:3])
    col_inside = (positions >= box_rows[:, 1:2]) & (positions < box_rows[:, 1:2] + box_rows[:, 3:4])
    return (row_inside[:, :, None] & col_inside[:, None, :]).astype(jnp.float32)


def taps_strided(feature, image_count, extent):
    channels = feature.shape[0]
    output_side = extent // 2
    padded = jnp.pad(
        feature.reshape(channels, image_count, extent, extent), ((0, 0), (0, 0), (1, 1), (1, 1))
    )
    pieces = [
        padded[:, :, tap_row : tap_row + extent : 2, tap_col : tap_col + extent : 2]
        for tap_row in range(3)
        for tap_col in range(3)
    ]
    return jnp.stack(pieces, axis=0).reshape(9 * channels, image_count * output_side * output_side)


def taps_plain(feature, image_count, extent):
    channels = feature.shape[0]
    padded = jnp.pad(
        feature.reshape(channels, image_count, extent, extent), ((0, 0), (0, 0), (1, 1), (1, 1))
    )
    pieces = [
        padded[:, :, tap_row : tap_row + extent, tap_col : tap_col + extent]
        for tap_row in range(3)
        for tap_col in range(3)
    ]
    return jnp.stack(pieces, axis=0).reshape(9 * channels, image_count * extent * extent)


def untaps_plain(columns, channels, image_count, extent):
    pieces = columns.reshape(9, channels, image_count, extent, extent)
    running = jnp.zeros((channels, image_count, extent + 2, extent + 2), jnp.float32)
    for tap_row in range(3):
        for tap_col in range(3):
            running = running + jnp.pad(
                pieces[3 * tap_row + tap_col],
                ((0, 0), (0, 0), (tap_row, 2 - tap_row), (tap_col, 2 - tap_col)),
            )
    return running[:, :, 1:-1, 1:-1].reshape(channels, image_count * extent * extent)


def untaps_strided(columns, shortcut, channels, image_count, extent):
    output_side = extent // 2
    pieces = columns.reshape(9, channels, image_count, output_side, output_side)
    parity_sums = {}
    for tap_row in range(3):
        for tap_col in range(3):
            block_row = tap_row // 2
            block_col = tap_col // 2
            placed = jnp.pad(
                pieces[3 * tap_row + tap_col],
                ((0, 0), (0, 0), (block_row, 1 - block_row), (block_col, 1 - block_col)),
            )
            parity = (tap_row % 2, tap_col % 2)
            parity_sums[parity] = (
                placed if parity not in parity_sums else parity_sums[parity] + placed
            )
    direct = jnp.pad(
        shortcut.reshape(channels, image_count, output_side, output_side),
        ((0, 0), (0, 0), (0, 1), (0, 1)),
    )
    parity_sums[1, 1] = parity_sums[1, 1] + direct
    rows_even = jnp.stack([parity_sums[0, 0], parity_sums[0, 1]], axis=-1)
    rows_odd = jnp.stack([parity_sums[1, 0], parity_sums[1, 1]], axis=-1)
    padded = jnp.stack([rows_even, rows_odd], axis=3).reshape(
        channels, image_count, extent + 2, extent + 2
    )
    return padded[:, :, 1:-1, 1:-1].reshape(channels, image_count * extent * extent)


def contract_first(weights, columns):
    return lax.dot_general(
        weights, columns, (((0,), (0,)), ((), ())), preferred_element_type=jnp.float32
    )


def weight_product(columns, gradient):
    return lax.dot_general(
        columns, gradient, (((1,), (1,)), ((), ())), preferred_element_type=jnp.float32
    )


def swish_slope(values):
    logistic = jax.nn.sigmoid(values)
    return logistic * (1.0 + values * (1.0 - logistic))


def moments(values, valid_list):
    running = 0.0
    squares = 0.0
    for tensor, valid in zip(values, valid_list):
        widened = tensor.astype(jnp.float32)
        running = running + jnp.sum(widened * valid, axis=1)
        squares = squares + jnp.sum(widened * widened * valid, axis=1)
    return (running, squares)


def standardize(values, running, squares, population):
    mean_value = running / population
    variance = squares / population - mean_value * mean_value
    scaling = lax.rsqrt(variance + epsilon)
    return (
        [
            (tensor.astype(jnp.float32) - mean_value[:, None]) * scaling[:, None]
            for tensor in values
        ],
        scaling,
    )


def norm_back(gradient, normed, valid, scaling, gain_values, shift_sum, gain_sum, population):
    return (gain_values * scaling)[:, None] * (
        gradient - valid * (shift_sum[:, None] + normed * gain_sum[:, None]) / population
    )


def plain_body(
    input_a,
    input_b,
    boxes_a,
    boxes_b,
    weight_first,
    weight_second,
    weight_short,
    gain_first,
    shift_first,
    gain_second,
    shift_second,
    gain_short,
    shift_short,
    upstream_a,
    upstream_b,
):
    image_groups = lax.axis_size("dp")
    in_local = input_a.shape[0]
    chan_in = weight_first.shape[1]
    chan_part = weight_first.shape[2]
    chan_full = weight_second.shape[1]
    image_counts = (boxes_a.shape[0], boxes_b.shape[0])
    extents = (SA, SB)
    whole_a, whole_b = (
        lax.all_to_all(
            input_a.reshape(in_local, image_groups, -1),
            "dp",
            split_axis=1,
            concat_axis=0,
            tiled=True,
        ),
        lax.all_to_all(
            input_b.reshape(in_local, image_groups, -1),
            "dp",
            split_axis=1,
            concat_axis=0,
            tiled=True,
        ),
    )
    features = (whole_a.reshape(chan_in, -1), whole_b.reshape(chan_in, -1))
    valid_list = (
        box_mask(boxes_a, SA // 2).reshape(1, -1),
        box_mask(boxes_b, SB // 2).reshape(1, -1),
    )
    first_mat = weight_first.reshape(9 * chan_in, chan_part)
    second_mat = weight_second.reshape(9 * chan_full, chan_part)
    first_cols = []
    sampled = []
    first_z = []
    short_z = []
    for feature, image_count, extent in zip(features, image_counts, extents):
        columns = taps_strided(feature, image_count, extent)
        picked = feature.reshape(chan_in, image_count, extent, extent)[:, :, ::2, ::2].reshape(
            chan_in, -1
        )
        first_cols.append(columns)
        sampled.append(picked)
        first_z.append(contract_first(first_mat, columns).astype(jnp.bfloat16))
        short_z.append(contract_first(weight_short, picked).astype(jnp.bfloat16))
    sum_first, square_first = moments(first_z, valid_list)
    sum_short, square_short = moments(short_z, valid_list)
    population = jnp.sum(valid_list[0]) + jnp.sum(valid_list[1])
    sum_first, square_first, sum_short, square_short, population = lax.psum(
        (sum_first, square_first, sum_short, square_short, population), "dp"
    )
    normed_first, scaling_first = standardize(first_z, sum_first, square_first, population)
    normed_short, scaling_short = standardize(short_z, sum_short, square_short, population)
    before_first = [normed * gain_first[:, None] + shift_first[:, None] for normed in normed_first]
    outgoing_a = (jax.nn.silu(before_first[0]) * valid_list[0]).astype(jnp.bfloat16)
    outgoing_b = (jax.nn.silu(before_first[1]) * valid_list[1]).astype(jnp.bfloat16)
    gathered_a, gathered_b = (
        lax.all_gather(outgoing_a, "chan", axis=0, tiled=True),
        lax.all_gather(outgoing_b, "chan", axis=0, tiled=True),
    )
    second_cols = []
    second_z = []
    for gathered, image_count, extent in zip((gathered_a, gathered_b), image_counts, extents):
        columns = taps_plain(gathered, image_count, extent // 2)
        second_cols.append(columns)
        second_z.append(contract_first(second_mat, columns).astype(jnp.bfloat16))
    sum_second, square_second = moments(second_z, valid_list)
    sum_second, square_second = lax.psum((sum_second, square_second), "dp")
    normed_second, scaling_second = standardize(second_z, sum_second, square_second, population)
    summed_pre = [
        main_part * gain_second[:, None]
        + shift_second[:, None]
        + side_part * gain_short[:, None]
        + shift_short[:, None]
        for main_part, side_part in zip(normed_second, normed_short)
    ]
    outputs = [
        (jax.nn.silu(tensor) * valid).astype(jnp.bfloat16)
        for tensor, valid in zip(summed_pre, valid_list)
    ]
    tail_grads = [
        upstream.astype(jnp.float32) * valid * swish_slope(tensor)
        for upstream, valid, tensor in zip((upstream_a, upstream_b), valid_list, summed_pre)
    ]
    shift_tail = sum((jnp.sum(gradient, axis=1) for gradient in tail_grads))
    gain_tail = sum(
        (jnp.sum(gradient * normed, axis=1) for gradient, normed in zip(tail_grads, normed_second))
    )
    gain_side = sum(
        (jnp.sum(gradient * normed, axis=1) for gradient, normed in zip(tail_grads, normed_short))
    )
    shift_tail, gain_tail, gain_side = lax.psum((shift_tail, gain_tail, gain_side), "dp")
    grad_second_local = 0.0
    partial_hidden = []
    short_dz = []
    for index_group in range(2):
        valid = valid_list[index_group]
        dz_second = norm_back(
            tail_grads[index_group],
            normed_second[index_group],
            valid,
            scaling_second,
            gain_second,
            shift_tail,
            gain_tail,
            population,
        ).astype(jnp.bfloat16)
        dz_short = norm_back(
            tail_grads[index_group],
            normed_short[index_group],
            valid,
            scaling_short,
            gain_short,
            shift_tail,
            gain_side,
            population,
        ).astype(jnp.bfloat16)
        short_dz.append(dz_short)
        grad_second_local = grad_second_local + weight_product(second_cols[index_group], dz_second)
        back_cols = jnp.dot(second_mat, dz_second, preferred_element_type=jnp.float32)
        partial_hidden.append(
            untaps_plain(back_cols, chan_full, image_counts[index_group], extents[index_group] // 2)
        )
    hidden_a, hidden_b = (
        lax.psum_scatter(
            partial_hidden[0].astype(jnp.bfloat16), "chan", scatter_dimension=0, tiled=True
        ).astype(jnp.float32),
        lax.psum_scatter(
            partial_hidden[1].astype(jnp.bfloat16), "chan", scatter_dimension=0, tiled=True
        ).astype(jnp.float32),
    )
    head_grads = [
        hidden * valid * swish_slope(tensor)
        for hidden, valid, tensor in zip((hidden_a, hidden_b), valid_list, before_first)
    ]
    shift_head = sum((jnp.sum(gradient, axis=1) for gradient in head_grads))
    gain_head = sum(
        (jnp.sum(gradient * normed, axis=1) for gradient, normed in zip(head_grads, normed_first))
    )
    shift_head, gain_head = lax.psum((shift_head, gain_head), "dp")
    grad_first_local = 0.0
    grad_short_local = 0.0
    partial_inputs = []
    for index_group in range(2):
        valid = valid_list[index_group]
        dz_first = norm_back(
            head_grads[index_group],
            normed_first[index_group],
            valid,
            scaling_first,
            gain_first,
            shift_head,
            gain_head,
            population,
        ).astype(jnp.bfloat16)
        grad_first_local = grad_first_local + weight_product(first_cols[index_group], dz_first)
        grad_short_local = grad_short_local + weight_product(
            sampled[index_group], short_dz[index_group]
        )
        back_cols = jnp.dot(first_mat, dz_first, preferred_element_type=jnp.float32)
        back_short = jnp.dot(
            weight_short, short_dz[index_group], preferred_element_type=jnp.float32
        )
        flat_input = untaps_strided(
            back_cols, back_short, chan_in, image_counts[index_group], extents[index_group]
        )
        partial_inputs.append(flat_input.reshape(chan_in, 1, lax.axis_size("chan"), -1))
    arrived_a, arrived_b = (
        lax.all_to_all(
            partial_inputs[0].astype(jnp.bfloat16), "dp", split_axis=0, concat_axis=1, tiled=True
        ).astype(jnp.float32),
        lax.all_to_all(
            partial_inputs[1].astype(jnp.bfloat16), "dp", split_axis=0, concat_axis=1, tiled=True
        ).astype(jnp.float32),
    )
    summed_a, summed_b = (
        lax.psum_scatter(
            arrived_a.astype(jnp.bfloat16), "chan", scatter_dimension=2, tiled=True
        ).astype(jnp.float32),
        lax.psum_scatter(
            arrived_b.astype(jnp.bfloat16), "chan", scatter_dimension=2, tiled=True
        ).astype(jnp.float32),
    )
    grad_input_a = summed_a.astype(jnp.bfloat16)
    grad_input_b = summed_b.astype(jnp.bfloat16)
    grad_first_local = grad_first_local.reshape(9, chan_in, chan_part)
    grad_second_local = grad_second_local.reshape(9, chan_full, chan_part)
    total_first, total_second, total_short = lax.psum(
        (grad_first_local, grad_second_local, grad_short_local), "dp"
    )
    position = lax.axis_index("dp")
    rows_first = chan_in // image_groups
    rows_second = chan_full // image_groups
    grad_first = lax.dynamic_slice_in_dim(total_first, position * rows_first, rows_first, 1)
    grad_second = lax.dynamic_slice_in_dim(total_second, position * rows_second, rows_second, 1)
    grad_short = lax.dynamic_slice_in_dim(total_short, position * rows_first, rows_first, 0)
    return (
        outputs[0],
        outputs[1],
        grad_input_a,
        grad_input_b,
        grad_first,
        grad_second,
        grad_short,
        gain_head,
        shift_head,
        gain_tail,
        shift_tail,
        gain_side,
        shift_tail,
    )


MESH = pl.DeviceIdType.MESH
TAPS = tuple((a, b) for a in range(3) for b in range(3))
PLANE_TAPS = (
    ((1, 1),),
    ((1, 0), (1, 2)),
    ((0, 1), (2, 1)),
    ((0, 0), (0, 2), (2, 0), (2, 2)),
)
ORDER = [tap for taps in PLANE_TAPS for tap in taps]
LANES = 128


class Links:
    def __init__(self, send_sems, recv_sems):
        self.send_sems, self.recv_sems = send_sems, recv_sems
        self.sends = self.slots = 0
        self.open = []

    def slot(self, count=1):
        first = self.slots
        self.slots += count
        return first

    def send(self, source, target, slot, where):
        copy = pltpu.make_async_remote_copy(
            source, target, self.send_sems.at[self.sends], self.recv_sems.at[slot],
            device_id=where, device_id_type=MESH,
        )
        self.sends += 1
        copy.start()
        self.open.append(copy)

    def arrived(self, target, slot, where):
        pltpu.make_async_remote_copy(
            target, target, self.send_sems.at[0], self.recv_sems.at[slot],
            device_id=where, device_id_type=MESH,
        ).wait_recv()

    def drain(self):
        for copy in self.open:
            copy.wait_send()


def mm(a, b, ca, cb):
    return lax.dot_general(a, b, (((ca,), (cb,)), ((), ())), preferred_element_type=jnp.float32)


def lanes_cat(parts):
    return jnp.concatenate(parts, axis=1) if len(parts) > 1 else parts[0]


def quarter_matrices(images, sides, segments, seg_lane, seg_row, q_rows, lanes):
    def lane(g, image, row, col):
        for (seg_g, r0, r1), first in zip(segments, seg_lane):
            if seg_g == g and 2 * r0 <= row < 2 * r1:
                return first + (image * 2 * (r1 - r0) + row - 2 * r0) * sides[g] + col

    taps = np.zeros((9, q_rows, lanes), np.float32)
    for (g, r0, r1), first in zip(segments, seg_row):
        half = sides[g] // 2
        for r in range(r0, r1):
            for s in range(half):
                for image in range(images[g]):
                    target = first + ((r - r0) * half + s) * images[g] + image
                    for t, (a, b) in enumerate(TAPS):
                        row, col = 2 * r + a - 1, 2 * s + b - 1
                        if row >= 0 and col >= 0:
                            taps[t, target, lane(g, image, row, col)] = 1.0
    sizes = [n * side * side for n, side in zip(images, sides)]
    cells = np.zeros((sum(sizes), lanes), np.float32)
    for g, (n, side) in enumerate(zip(images, sides)):
        for image in range(n):
            for row in range(side):
                for col in range(side):
                    cell = (row // 2) * (side // 2) + col // 2
                    target = g * sizes[0] + (cell * 4 + 2 * (row % 2) + col % 2) * n + image
                    cells[target, lane(g, image, row, col)] = 1.0
    return taps, cells


def regroup(value, runs):
    return jnp.concatenate([value[:, a:b] for a, b in runs], axis=1)


def sigma(v):
    return 0.5 * jnp.tanh(0.5 * v) + 0.5


class Reduce:
    def __init__(self, net, i, k, part, bufs, windows, b4=None):
        self.b4 = b4
        self.net, self.part, self.windows = net, part, windows
        self.b1, self.s1, self.b2, self.s2, self.b3 = bufs
        self.ix, self.pz, self.hz = i % 2, (i // 2) % 2, i // 4
        self.peers = (
            (i + 1 - 2 * self.ix, k),
            (i + 2 - 4 * self.pz, k),
            (i + 4 - 8 * self.hz, k),
        )
        self.slots = [net.slot(3) for _ in windows]

    def first(self, w):
        cols = self.windows[w]
        self.net.send(
            self.part.at[:, :, 1 - self.ix, :, cols], self.b1.at[:, :, :, cols],
            self.slots[w], self.peers[0],
        )

    def second(self, w):
        cols = self.windows[w]
        self.net.arrived(self.b1.at[:, :, :, cols], self.slots[w], self.peers[0])
        for h in range(2):
            for p in range(2):
                value = self.part[h, p, self.ix, :, cols].astype(jnp.float32)
                value = value + self.b1[h, p, :, cols].astype(jnp.float32)
                self.s1[h, p, :, cols] = value.astype(jnp.bfloat16)
        self.net.send(
            self.s1.at[:, 1 - self.pz, :, cols], self.b2.at[:, :, cols],
            self.slots[w] + 1, self.peers[1],
        )

    def second_of(self, w, value):
        cols = self.windows[w]
        self.s1[:, :, :, cols] = value.reshape(2, 2, -1, value.shape[1])
        self.net.send(
            self.s1.at[:, 1 - self.pz, :, cols], self.b2.at[:, :, cols],
            self.slots[w] + 1, self.peers[1],
        )

    def spread_of(self, w, value):
        cols = self.windows[w]
        self.s1[:, :, :, cols] = value.reshape(2, 2, -1, value.shape[1])
        z = 2 * self.hz + self.pz
        self.direct = self.net.slot(4)
        for d in range(1, 4):
            to = (z + d) % 4
            self.net.send(
                self.s1.at[to // 2, to % 2, :, cols], self.b4.at[z],
                self.direct + z, (2 * to + self.ix, self.peers[0][1]),
            )

    def spread_last(self, w):
        cols = self.windows[w]
        z = 2 * self.hz + self.pz
        value = self.s1[self.hz, self.pz, :, cols].astype(jnp.float32)
        for d in range(1, 4):
            to = (z + d) % 4
            self.net.arrived(self.b4.at[to], self.direct + to, (2 * to + self.ix, self.peers[0][1]))
            value = value + self.b4[to].astype(jnp.float32)
        return value

    def third(self, w):
        cols = self.windows[w]
        self.net.arrived(self.b2.at[:, :, cols], self.slots[w] + 1, self.peers[1])
        for h in range(2):
            value = self.s1[h, self.pz, :, cols].astype(jnp.float32)
            value = value + self.b2[h, :, cols].astype(jnp.float32)
            self.s2[h, :, cols] = value.astype(jnp.bfloat16)
        self.net.send(
            self.s2.at[1 - self.hz, :, cols], self.b3.at[:, cols],
            self.slots[w] + 2, self.peers[2],
        )

    def last(self, w):
        cols = self.windows[w]
        self.net.arrived(self.b3.at[:, cols], self.slots[w] + 2, self.peers[2])
        return self.s2[self.hz, :, cols].astype(jnp.float32) + self.b3[:, cols].astype(jnp.float32)


def make_fused(n_dp, in_local, images, sides, chan_in, chan_part, stop):
    f32, bf16 = jnp.float32, jnp.bfloat16
    halves = tuple(side // 2 for side in sides)
    sizes = tuple(h * h * n for h, n in zip(halves, images))
    rows = sum(sizes)
    quarter = tuple(n // 4 for n in images)
    qlanes = tuple(q * side * side for q, side in zip(quarter, sides))
    slab_lanes = -(-sum(qlanes) // LANES) * LANES
    chan_full = 4 * chan_part
    out_rows = chan_full // n_dp
    starts = (0, sizes[0])
    widths = tuple(h * n for h, n in zip(halves, images))
    chunks = [(g, r, starts[g] + r * widths[g], widths[g]) for g in range(2) for r in range(halves[g])]
    win = [-(-q // LANES) * LANES for q in qlanes]
    b_tile = qlanes[0] // LANES * LANES
    b_skip = qlanes[0] - b_tile
    rs = halves[0] // 2
    segments = [(1, 0, halves[1]), (0, 0, rs), (0, rs, halves[0])]
    seg_lane, runs = [], []
    lane_of = 0
    for g, r0, r1 in segments:
        side, base = sides[g], (0, qlanes[0])[g]
        seg_lane.append(lane_of)
        lane_of += quarter[g] * 2 * (r1 - r0) * side
        runs += [
            (base + (image * side + 2 * r0) * side, base + (image * side + 2 * r1) * side)
            for image in range(quarter[g])
        ]
    runs.append((sum(qlanes), slab_lanes))
    at, order = 0, []
    for a, b in runs:
        order.append((a, at, at + b - a))
        at += b - a
    back_runs = [(a, b) for _, a, b in sorted(order)]
    cut_lane = -(-seg_lane[2] // LANES) * LANES
    lane_parts = (slice(0, cut_lane), slice(cut_lane, slab_lanes))
    seg_cells = [(r1 - r0) * halves[g] for g, r0, r1 in segments]
    seg_rows = [cells * quarter[seg[0]] for cells, seg in zip(seg_cells, segments)]
    top = -(-(seg_rows[0] + seg_rows[1]) // 16) * 16
    seg_row = [0, seg_rows[0], top]
    q_rows = top + -(-seg_rows[2] // 16) * 16
    row_parts = (slice(0, top), slice(top, q_rows))
    patch_win = (slice(0, cut_lane), slice(seg_lane[1] // LANES * LANES, slab_lanes))
    patch_m, cells_m = quarter_matrices(
        quarter, sides, segments, seg_lane, seg_row, q_rows, slab_lanes
    )
    patch_ms = [
        np.concatenate([m[rows_, lanes_] for m in patch_m], axis=0)
        for rows_, lanes_ in zip(row_parts, patch_win)
    ]
    spans = [
        (starts[g] + r0 * widths[g], starts[g] + r1 * widths[g])
        for g, r0, r1 in (segments[0], segments[2], segments[1])
    ]
    pieces = [[segments[0]], [segments[2]], [segments[1]]]
    part_chunks = [
        [ch for ch in chunks if ch[0] == p[0][0] and p[0][1] <= ch[1] < p[0][2]] for p in pieces
    ]
    low_lane = seg_lane[1] // LANES * LANES
    out_lanes = [slice(0, low_lane), slice(cut_lane, slab_lanes), slice(low_lane, cut_lane)]
    out_win = [spans[0], spans[1], (0, rows)]
    n_parts = 3
    back_pieces = (((0, 0, 2),), ((0, 2, halves[0] - 1),), ((0, halves[0] - 1, halves[0]), (1, 0, halves[1])))
    row_halves = [
        slice(starts[p[0][0]] + p[0][1] * widths[p[0][0]], starts[p[-1][0]] + p[-1][2] * widths[p[-1][0]])
        for p in back_pieces
    ]
    cols2 = (slice(0, 6 * LANES), slice(6 * LANES, 9 * LANES))
    cols1 = (slice(6 * LANES, 10 * LANES), slice(0, 6 * LANES))

    def kernel(*refs):
        (xa_h, xb_h, bxa_h, bxb_h, w1_h, w2_h, ws_h, g1_h, b1_h, g2_h, b2_h, gs_h, bs_h, ua_h, ub_h,
         pm0_h, pm1_h, cells_h,
         turn_h,
         oa, ob, gr, gw1, gws, gw2, vecs, turn,
         xa, xb, bxa, bxb, w1g, w2, wsg, vg, g2, b2, gs, bs, ua, ub, pm0, pm1, cells,
         xs, xt, xr, zb, zsq, zsr, zg, zpa, zpb, valid, vq, hat, mask, zs, a1a, a1b,
         cslots, slots, stat, up, outr, gv, dza, dzb, dzma, dzmb, apk, arx, gacc, dzsr,
         dd, hp, hr1, hs, hr2, gu, d1a, d1b,
         p22, p23, p24, p25, p26, wg1, p11, p12, p13, p14, p15,
         gp, gr1, gsum, gr2, zt, gt, lsem, ssem, rsem) = refs
        i, k = lax.axis_index("dp"), lax.axis_index("chan")
        k1 = k + 1 - 2 * (k % 2)
        k2 = (k + 2) % 4
        k3 = (k1 + 2) % 4
        ix = i % 2
        mate = (i + 1 - 2 * ix, k)
        net = Links(ssem, rsem)
        bits = n_dp.bit_length() - 1

        def flip(d):
            j = i
            for b in range(bits):
                if d >> b & 1:
                    j = j + (1 << b) * (1 - 2 * ((i // (1 << b)) % 2))
            return j

        peers = [flip(d) for d in sorted(range(n_dp), key=lambda d: (d == 0, -(d >> 1), d & 1))]
        peers, home = peers[:-1], peers[-1]
        zp, a1, dz, d1 = (zpa, zpb), (a1a, a1b), (dza, dzb), (d1a, d1b)
        dzm = (dzma, dzmb)

        def flat(value):
            return value.reshape(-1, value.shape[-1])

        def zeros(count):
            return [jnp.zeros((8, LANES), f32)] * count

        loads = {}
        pairs_of = (
            ("xa", xa_h, xa), ("xb", xb_h, xb),
            ("w1", w1_h, w1g.at[k]), ("ws", ws_h, wsg.at[k]), ("g1", g1_h, vg.at[k, 0]), ("b1", b1_h, vg.at[k, 1]),
            ("bxa", bxa_h, bxa), ("bxb", bxb_h, bxb), ("pm0", pm0_h, pm0), ("pm1", pm1_h, pm1),
            ("ua", ua_h, ua), ("ub", ub_h, ub), ("g2", g2_h, g2),
            ("b2", b2_h, b2), ("gs", gs_h, gs), ("bs", bs_h, bs), ("w2", w2_h, w2), ("cells", cells_h, cells),
            ("turn", turn_h, turn),
        )
        for index, (name, source, target) in enumerate(pairs_of):
            loads[name] = pltpu.make_async_copy(source, target, lsem.at[index])
        loads["xa"].start()
        loads["xb"].start()

        def need(*names):
            for name in names:
                loads.pop(name).wait()

        barrier = pltpu.get_barrier_semaphore()
        for j in peers:
            pl.semaphore_signal(barrier, inc=1, device_id=(j, k), device_id_type=MESH)
        for where in (k1, k2, k3):
            pl.semaphore_signal(barrier, inc=1, device_id=(i, where), device_id_type=MESH)

        need("xa", "xb")
        for copy in loads.values():
            copy.start()
        lane = lax.broadcasted_iota(jnp.int32, (in_local, LANES), 1)
        for d, j in enumerate(peers + [home]):
            begin = 4 * qlanes[0] * j + qlanes[0] * k
            tile = begin // LANES
            part_a = xa[:, pl.ds(pl.multiple_of(tile * LANES, LANES), win[0])].astype(f32)
            part_a = pltpu.roll(part_a, (win[0] - (begin - tile * LANES)) % win[0], 1)
            begin = 4 * qlanes[1] * j + qlanes[1] * k
            tile = begin // LANES
            part_b = xb[:, pl.ds(pl.multiple_of(tile * LANES, LANES), win[1])].astype(f32)
            part_b = jnp.concatenate([part_b, jnp.zeros((in_local, LANES), f32)], axis=1)
            wide = win[1] + LANES
            part_b = pltpu.roll(part_b, (wide + b_skip - (begin - tile * LANES)) % wide, 1)
            seam = jnp.where(lane < b_skip, part_a[:, b_tile : b_tile + LANES], part_b[:, :LANES])
            xs[d * in_local : (d + 1) * in_local, :] = jnp.concatenate(
                [part_a[:, :b_tile], seam, part_b[:, LANES : slab_lanes - b_tile]], axis=1
            ).astype(bf16)
        slot_x = [net.slot(n_dp) for _ in lane_parts]
        n_via = 2
        via = [pl.ds((9 - n_via) * e, n_via) for e in (ix, 1 - ix)]
        w_taps = [via[0], slice(n_via, 5), slice(5, 9 - n_via)]
        slot_w = [net.slot(4) for _ in range(6)]

        def weight_refs(q):
            return [w1g.at[q, taps] for taps in w_taps] + [wsg.at[q], vg.at[q], w1g.at[q, via[1]]]

        ordered = regroup(xs[...], runs)
        for c, cols in enumerate(lane_parts):
            moved = ordered[:, cols]
            xt[:, :, cols] = moved.reshape(n_dp, in_local, moved.shape[1])
            xr[i, :, cols] = moved[-in_local:]
            if c == 0:
                pl.semaphore_wait(barrier, n_dp + 2)
            for d, j in enumerate(peers):
                net.send(xt.at[d, :, cols], xr.at[i, :, cols], slot_x[c] + i, (j, k))
            if c == 0:
                need("w1", "ws", "g1", "b1")
                for ref, slot in zip(weight_refs(k)[:5], slot_w):
                    net.send(ref, ref, slot + k, (i, k2))
                for ref, slot in zip(weight_refs(k), slot_w):
                    net.send(ref, ref, slot + k, (i, k1))

        def weights_on(n):
            ref = weight_refs(k2)[n]
            net.arrived(ref, slot_w[n] + k2, mate if n == 5 else (i, k2))
            net.send(ref, ref, slot_w[n] + k2, (i, k1))
            if n == 0:
                net.send(ref, ref, slot_w[5] + k2, mate)

        def weights_in(parts):
            for q in (k1, k3):
                for n in parts:
                    net.arrived(weight_refs(q)[n], slot_w[n] + q, (i, k1))

        for buf in (zpa, zpb, a1a, a1b, dza, dzb, dzma, dzmb, d1a, d1b):
            side = buf.shape[1] if len(buf.shape) == 5 else buf.shape[0]
            lead = (slice(None),) if len(buf.shape) == 5 else ()
            for edge in (0, side - 1):
                for index in (lead + (edge,), lead + (slice(None), edge)):
                    region = buf.at[index]
                    region[...] = jnp.zeros(region.shape, buf.dtype)
        need("bxa", "bxb", "ua", "ub")
        population = zeros(1)[0]
        low = lax.broadcasted_iota(jnp.int32, (8, LANES), 0) < 4
        for g, box in enumerate((bxa, bxb)):
            n, half, count = images[g], halves[g], quarter[g]
            diag = lax.broadcasted_iota(jnp.int32, (n, n), 0) == lax.broadcasted_iota(jnp.int32, (n, n), 1)
            ends = [
                jnp.sum(jnp.where(diag, box[q : q + 1, :].astype(f32), 0.0), axis=1, keepdims=True)
                for q in range(4)
            ]
            ends = [jnp.broadcast_to(e, (n, LANES)) for e in ends]
            ends[2], ends[3] = ends[0] + ends[2], ends[1] + ends[3]

            def inside(ends, r, s):
                both = (r >= ends[0]) & (r < ends[2]) & (s >= ends[1]) & (s < ends[3])
                return both.astype(f32)

            for r in range(half):
                for s in range(half):
                    cell = inside(ends, r, s)
                    begin = starts[g] + (r * half + s) * n
                    valid[begin : begin + n, :] = cell
                    population = population + jnp.sum(cell.reshape(n // 8, 8, LANES), axis=0)
            mine = [pltpu.roll(e, (n - count * k) % n, 0)[:8] for e in ends]
            if count < 8:
                mine = [jnp.where(low, e, pltpu.roll(e, 4, 0)) for e in mine]
            for (seg_g, r0, r1), first, cells_n in zip(segments, seg_row, seg_cells):
                if seg_g != g:
                    continue
                per = 8 // count
                for t in range(-(-cells_n // per)):
                    spots = [divmod(min(per * t + e, cells_n - 1), half) for e in range(per)]
                    spots = [(float(r0 + r), float(s)) for r, s in spots]
                    if per == 2:
                        r, s = (jnp.where(low, spots[0][e], spots[1][e]) for e in range(2))
                    else:
                        r, s = spots[0]
                    cell = inside(mine, r, s)
                    if per == 2 and per * t + 1 >= cells_n:
                        cell = jnp.where(low, cell, 0.0)
                    vq[first + 8 * t : first + 8 * t + 8, :] = cell
        population = jnp.broadcast_to(jnp.sum(population, axis=0, keepdims=True), (8, LANES))
        for g, source in enumerate((ua, ub)):
            n, count = images[g], halves[g] ** 2
            gu[starts[g] : starts[g] + sizes[g], :] = source[...].astype(f32)
            for cell in range(count):
                up[starts[g] + cell * n : starts[g] + (cell + 1) * n, :] = gu[
                    pl.ds(starts[g] + cell, n, stride=count), :
                ]

        def rowsum(value):
            return jnp.sum(value.reshape(-1, 8, value.shape[-1]), axis=0)

        def message(sums):
            parts = [jnp.sum(v, axis=0, keepdims=True) if v.shape[0] > 1 else v for v in sums]
            if len(parts) % 8:
                parts.append(jnp.zeros((8 - len(parts) % 8, LANES), f32))
            return jnp.concatenate(parts, axis=0)

        def by_chan(value):
            return [value[:, q * LANES : (q + 1) * LANES] for q in range(4)]

        def share(rnd, value):
            mine = slots.at[rnd, i, : value.shape[0]]
            mine[...] = value
            first = net.slot(n_dp)
            for j in peers:
                net.send(mine, mine, first + i, (j, k))
            return first

        def total(rnd, first, count=8):
            for j in peers:
                net.arrived(slots.at[rnd, j, :count], first + j, (j, k))
            return jnp.sum(slots[rnd, :, :count], axis=0)

        def chan_share(rnd, value):
            mine = cslots.at[rnd, k, : value.shape[0]]
            mine[...] = value
            first = net.slot(4)
            for where in (k2, k3, k1):
                net.send(mine, mine, first + k, (i, where))
            return first

        def chan_total(rnd, first, count=8):
            for where in (k1, k2, k3):
                net.arrived(cslots.at[rnd, where, :count], first + where, (i, where))
            return jnp.sum(cslots[rnd, :, :count], axis=0)

        pop_first = share(4, population)

        def quarter_in(c):
            for j in peers:
                net.arrived(xr.at[j, :, lane_parts[c]], slot_x[c] + j, (j, k))

        def patches(c):
            whole = jnp.concatenate([xr[q, :, patch_win[c]] for q in range(n_dp)], axis=0)
            value = mm((pm0, pm1)[c][...], whole, 1, 1).astype(bf16)
            count = value.shape[0] // 9
            return [value[t * count : (t + 1) * count] for t in range(9)]

        slot_s = net.slot(4)

        z_cuts = (slice(0, top * 3 // 80 * 16), slice(top * 3 // 80 * 16, top), slice(top, q_rows))
        slot_z = [net.slot(4) for _ in z_cuts]

        def z_send(n):
            for where in (k2, k1):
                net.send(zb.at[k, z_cuts[n]], zb.at[k, z_cuts[n]], slot_z[n] + k, (i, where))

        def first_conv(c, taps, acc):
            part = row_parts[c]
            weights = lanes_cat([w1g[q].reshape(9 * chan_in, chan_part) for q in range(4)])
            value = mm(lanes_cat(taps), weights, 1, 0).astype(bf16)
            zb[k, part, :] = value
            if c == 0:
                z_send(0)
            z = value.astype(f32)
            u = z * lanes_cat([vq[part, :]] * 4)
            return [acc[0] + rowsum(u), acc[1] + rowsum(u * z)]

        def projection(c, patch):
            side = mm(patch, lanes_cat([wsg[q] for q in range(4)]), 1, 0).astype(bf16)
            for q, z in enumerate(by_chan(side)):
                zsq[q, row_parts[c], :] = z

        def act_on(n):
            part = zb.at[k2, z_cuts[n]]
            net.arrived(part, slot_z[n] + k2, (i, k2))
            net.send(part, part, slot_z[n] + k2, (i, k1))

        def act_in(n):
            net.arrived(zb.at[k1, z_cuts[n]], slot_z[n] + k1, (i, k1))
            net.arrived(zb.at[k3, z_cuts[n]], slot_z[n] + k3, (i, k1))

        acc = [jnp.zeros((8, chan_full), f32)] * 2
        need("pm0", "pm1")
        for n in (0, 1, 5, 2):
            weights_on(n)
        quarter_in(0)
        taps = patches(0)
        center = [taps[4]]
        weights_on(3)
        weights_on(4)
        weights_in((0, 1, 2, 5))
        acc = first_conv(0, taps, acc)
        quarter_in(1)
        taps = patches(1)
        center.append(taps[4])
        acc = first_conv(1, taps, acc)
        acc = [jnp.sum(v, axis=0, keepdims=True) for v in acc]
        first = chan_share(0, message(sum((by_chan(v) for v in acc), [])))
        z_send(1)
        z_send(2)
        weights_in((3, 4))
        for c in range(2):
            projection(c, center[c])
        zsr[k] = zsq[k]

        need(*list(loads))
        row_cuts = (slice(0, rows // 32 * 16), slice(rows // 32 * 16, rows))
        slot_g0 = [net.slot(4) for _ in row_cuts]
        whole = jnp.concatenate([xr[q] for q in range(n_dp)], axis=0)
        for span in row_cuts:
            zg[k, span, :] = mm(cells[span, :], whole, 1, 1).astype(bf16)
        first = share(0, chan_total(0, first))
        for where in (k2, k3, k1):
            net.send(zsq.at[where], zsr.at[k], slot_s + k, (i, where))
        act_on(0)
        for span, slot in zip(row_cuts, slot_g0):
            for where in (k2, k1):
                net.send(zg.at[k, span], zg.at[k, span], slot + k, (i, where))
        act_on(1)
        act_on(2)

        def slab_on(n):
            span, slot = row_cuts[n], slot_g0[n]
            net.arrived(zg.at[k2, span], slot + k2, (i, k2))
            net.send(zg.at[k2, span], zg.at[k2, span], slot + k2, (i, k1))

        def slab_in(n):
            span, slot = row_cuts[n], slot_g0[n]
            net.arrived(zg.at[k1, span], slot + k1, (i, k1))
            net.arrived(zg.at[k3, span], slot + k3, (i, k1))

        inv_pop = 1.0 / total(4, pop_first)[0:1]
        for n in range(3):
            act_in(n)
        tot = total(0, first)
        stat[0:8, :] = tot
        tot_first = (stat[pl.ds(k, 1), :], stat[pl.ds(4 + k, 1), :])
        def moments(total_, square):
            mean = total_ * inv_pop
            return mean, lax.rsqrt(square * inv_pop - mean * mean + epsilon)

        mean1, sc1 = moments(tot[0:4], tot[4:8])
        mean1, sc1 = (lanes_cat([v[q : q + 1] for q in range(4)]) for v in (mean1, sc1))
        gain1, shift1 = (lanes_cat([vg[q, e] for q in range(4)]) for e in range(2))

        turn_low = lax.broadcasted_iota(jnp.int32, (8, 1), 0) < 4

        def whole_cells(read, c):
            for begin in range(row_parts[c].start, row_parts[c].stop, 16):
                blocks = [read(q, slice(begin, begin + 16)).astype(f32) for q in range(4)]
                for at in (begin, begin + 8):
                    seg = max(e for e in range(3) if seg_row[e] <= at)
                    g, r0, r1 = segments[seg]
                    per = 8 // quarter[g]
                    v = [block[at - begin : at - begin + 8] for block in blocks]
                    cell = (at - seg_row[seg]) // 8 * per
                    if per == 1:
                        found = [jnp.concatenate(v, axis=0)]
                    else:
                        t = [pltpu.roll(e, 4, 0) for e in v]
                        found = [
                            jnp.concatenate(
                                [jnp.where(turn_low, v[0], t[1]), jnp.where(turn_low, v[2], t[3])], axis=0
                            ),
                            jnp.concatenate(
                                [jnp.where(turn_low, t[0], v[1]), jnp.where(turn_low, t[2], v[3])], axis=0
                            ),
                        ]
                    for e, value in enumerate(found):
                        if cell + e < seg_cells[seg]:
                            r, s = divmod(cell + e, halves[g])
                            yield g, r0 + r, s, value

        def activate(c):
            for g, r, s, z in whole_cells(lambda q, span: zb[q, span, :], c):
                begin = starts[g] + (r * halves[g] + s) * images[g]
                span = slice(begin, begin + images[g])
                h = (z - mean1) * sc1
                hat[span, :] = h
                v = h * gain1 + shift1
                act = v * sigma(v) * lanes_cat([valid[span, :]] * 4)
                a1[g][1 + r, 1 + s] = act.astype(bf16)

        def second_conv(parts, acc):
            value = None
            for a, b in TAPS:
                patch = jnp.concatenate(
                    [flat(a1[g][r0 + a : r1 + a, b : b + halves[g]]) for g, r0, r1 in parts], axis=0
                )
                part = mm(patch, w2[3 * a + b], 1, 0)
                value = part if value is None else value + part
            at = 0
            for g, r0, r1 in parts:
                for r in range(r0, r1):
                    begin = starts[g] + r * widths[g]
                    span = slice(begin, begin + widths[g])
                    u = value[at : at + widths[g]]
                    at += widths[g]
                    gv[span, :] = u
                    uv = u * valid[span, :]
                    acc = [acc[0] + rowsum(uv), acc[1] + rowsum(uv * u)]
            return acc

        left = lax.broadcasted_iota(jnp.int32, (1, LANES), 1) < out_rows

        def pack(g, r0, r1):
            for r in range(r0, r1):
                v = by_chan(flat(a1[g][1 + r, 1 : 1 + halves[g]]).astype(f32))
                t = [pltpu.roll(e, out_rows, 1) for e in v]
                begin = starts[g] + r * widths[g]
                span = slice(begin, begin + widths[g])
                for p in range(2):
                    cols = slice(p * LANES, (p + 1) * LANES)
                    apk[0, span, cols] = jnp.where(left, v[2 * p], t[2 * p + 1]).astype(bf16)
                    apk[1, span, cols] = jnp.where(left, t[2 * p], v[2 * p + 1]).astype(bf16)

        near = sizes[1] - sizes[1] // 6 // 16 * 16
        far = sizes[0] * 17 // 32 // 16 * 16
        pack_spans = [
            [slice(starts[1], starts[1] + near)],
            [slice(starts[1] + near, rows), slice(0, far)],
            [slice(far, sizes[0])],
        ]
        slot_p = [[net.slot() for _ in spans_] for spans_ in pack_spans]

        def pack_send(n):
            for span, slot in zip(pack_spans[n], slot_p[n]):
                net.send(apk.at[1 - ix, span], arx.at[span], slot, mate)

        activate(0)
        pack(1, 0, halves[1])
        pack(0, 0, rs)
        pack_send(0)
        for where in (k2, k3, k1):
            net.arrived(zsr.at[where], slot_s + where, (i, where))
        side_acc = zeros(2)
        for c in range(2):
            for g, r, s, z in whole_cells(lambda q, span: zsr[q, span, :], c):
                begin = starts[g] + (r * halves[g] + s) * images[g]
                span = slice(begin, begin + images[g])
                zs[span, :] = z
                u = z * valid[span, :]
                side_acc = [side_acc[0] + rowsum(u), side_acc[1] + rowsum(u * z)]
        acc = second_conv([(1, 0, halves[1]), (0, 0, rs - 1)], zeros(2))
        activate(1)
        pack(0, rs, halves[0])
        acc = second_conv([(0, rs - 1, halves[0])], acc)
        first = share(1, message(acc + side_acc))
        pack_send(1)

        def planes_of(quarters, g):
            count = quarter[g]
            if count % 8 == 0:
                return [
                    jnp.concatenate([v[:, count * p : count * (p + 1)] for v in quarters], axis=1)
                    for p in range(4)
                ]
            low = lax.broadcasted_iota(jnp.int32, (1, 8, 1), 1) < 4
            parts = [[v[:, 8 * h : 8 * h + 8] for v in quarters] for h in range(2)]
            turned = [[pltpu.roll(v, 4, 1) for v in side] for side in parts]
            result = []
            for p in range(4):
                v, t = parts[p // 2], turned[p // 2]
                if p % 2 == 0:
                    both = [jnp.where(low, v[0], t[1]), jnp.where(low, v[2], t[3])]
                else:
                    both = [jnp.where(low, t[0], v[1]), jnp.where(low, t[2], v[3])]
                result.append(jnp.concatenate(both, axis=1))
            return result

        def make_planes():
            for g, r, begin, count in chunks:
                quarters = [
                    zg[q, begin : begin + count, :].astype(f32).reshape(halves[g], images[g], chan_in)
                    for q in range(4)
                ]
                for p, value in enumerate(planes_of(quarters, g)):
                    zp[g][p, 1 + r, 1 : 1 + halves[g]] = value.astype(bf16)

        tot = total(1, first)
        mean2, sc2 = moments(tot[0:1], tot[1:2])
        means, scs = moments(tot[2:3], tot[3:4])
        gain2, gains = g2[...], gs[...]
        shifts = b2[...] + bs[...]
        acc = zeros(3)
        for g, r, begin, count in chunks:
            span = slice(begin, begin + count)
            ok = valid[span, :]
            hat2 = (gv[span, :] - mean2) * sc2
            hats = (zs[span, :] - means) * scs
            v = hat2 * gain2 + hats * gains + shifts
            sig = sigma(v)
            outr[span, :] = v * sig * ok
            grad = up[span, :] * ok * (sig * (1.0 + v * (1.0 - sig)))
            up[span, :] = grad
            gv[span, :] = hat2
            zs[span, :] = hats
            acc = [acc[0] + rowsum(grad), acc[1] + rowsum(grad * hat2), acc[2] + rowsum(grad * hats)]
        first = share(2, message(acc))
        pack_send(2)
        for g, target in enumerate((oa, ob)):
            n, count = images[g], halves[g] ** 2
            for cell in range(count):
                gu[pl.ds(starts[g] + cell, n, stride=count), :] = outr[
                    starts[g] + cell * n : starts[g] + (cell + 1) * n, :
                ]
            target[...] = gu[starts[g] : starts[g] + sizes[g], :].astype(bf16)
        for begin in range(0, rows, 16):
            span = slice(begin, begin + 16)
            v = hat[span, :] * gain1 + shift1
            sig = sigma(v)
            mask[span, :] = sig * (1.0 + v * (1.0 - sig)) * lanes_cat([valid[span, :]] * 4)
        tot = total(2, first)
        sum_tail, sum_gain2, sum_gains = tot[0:1], tot[1:2], tot[2:3]
        k2g, ksg = gain2 * sc2, gains * scs
        db, dg2, dgs = sum_tail * inv_pop, sum_gain2 * inv_pop, sum_gains * inv_pop
        for g, r, begin, count in chunks:
            span = slice(begin, begin + count)
            value = k2g * (up[span, :] - valid[span, :] * (db + gv[span, :] * dg2))
            dz[g][1 + r, 1 : 1 + halves[g]] = value.astype(bf16).reshape(halves[g], images[g], chan_part)
        slot_d = net.slot(2)

        def dz_inner(buf, g):
            return buf[g].at[1 : 1 + halves[g], 1 : 1 + halves[g]]

        for g in range(2):
            net.send(dz_inner(dz, g), dz_inner(dzm, g), slot_d + g, mate)

        def columns(buf, piece):
            for g, r0, r1 in piece:
                for t, (a, b) in enumerate(TAPS):
                    dd[
                        starts[g] + r0 * widths[g] : starts[g] + r1 * widths[g],
                        t * LANES : (t + 1) * LANES,
                    ] = flat(buf[g][r0 + 2 - a : r1 + 2 - a, 2 - b : 2 - b + halves[g]])

        def back_second(first, span):
            begin = pl.multiple_of(first * chan_part, LANES)
            weights = lanes_cat([w2[t, pl.ds(begin, 2 * chan_part), :] for t in range(9)])
            value = mm(dd[span, :], weights, 1, 1).astype(bf16)
            hp[first, span, :] = value[:, :chan_part]
            hp[first + 1, span, :] = value[:, chan_part:]

        slot_h = [net.slot(3) for _ in row_halves]
        for span, slot, piece in zip(row_halves, slot_h, back_pieces):
            columns(dz, piece)
            back_second(2 * (k2 // 2), span)
            net.send(hp.at[k3, span], hr1.at[1, span], slot + 1, (i, k1))
        for span, slot in zip(row_halves, slot_h):
            net.arrived(hr1.at[1, span], slot + 1, (i, k1))
            hs[span, :] = (hp[k2, span, :].astype(f32) + hr1[1, span, :].astype(f32)).astype(bf16)
            net.send(hs.at[span], hr2.at[span], slot + 2, (i, k2))
        back_second(2 * (k // 2), slice(0, rows))
        for span, slot in zip(row_halves, slot_h):
            net.send(hp.at[k1, span], hr1.at[0, span], slot, (i, k1))

        acc = [jnp.zeros((8, chan_full), f32)] * 2
        for begin in range(0, rows, 16):
            span = slice(begin, begin + 16)
            part = lanes_cat([hp[q, span, :] for q in range(4)]).astype(f32) * mask[span, :]
            acc = [acc[0] + rowsum(part), acc[1] + rowsum(part * hat[span, :])]
        acc = [jnp.sum(v, axis=0, keepdims=True) for v in acc]
        first = share(3, message(sum((by_chan(v) for v in acc), [])))

        sum2 = Reduce(net, i, k, None, (None, p22, p23, p24, p25), cols2, p26)
        gacc[...] = mm(apk[ix], dd[...], 0, 0)
        first = chan_share(1, total(3, first))
        for g, r, begin, count in chunks:
            span = slice(begin, begin + count)
            value = ksg * (up[span, :] - valid[span, :] * (db + zs[span, :] * dgs))
            dzsr[span, :] = value.astype(bf16)
        for n in range(2):
            slab_on(n)
        for spans_, slots_ in zip(pack_spans, slot_p):
            for span, slot in zip(spans_, slots_):
                net.arrived(arx.at[span], slot, mate)
        for g in range(2):
            net.arrived(dz_inner(dzm, g), slot_d + g, mate)
        for piece in back_pieces:
            columns(dzm, piece)
        for w, cols in enumerate(cols2):
            value = (gacc[:, cols] + mm(arx[...], dd[:, cols], 0, 0)).astype(bf16)
            (sum2.spread_of, sum2.second_of)[w](w, value)
        tot = chan_total(1, first)
        stat[0:8, :] = tot
        sum_head, sum_gain1 = stat[pl.ds(k, 1), :], stat[pl.ds(4 + k, 1), :]

        def close_second():
            for w, cols in enumerate(cols2):
                value = (sum2.spread_last, sum2.last)[w](w)
                for t in range(cols.start // LANES, cols.stop // LANES):
                    gw2[t] = value[:, t * LANES - cols.start : (t + 1) * LANES - cols.start]

        own = pl.ds(pl.multiple_of(k * chan_part, LANES), chan_part)
        mean1, sc1 = moments(tot_first[0], tot_first[1])
        k1g = vg[k, 0] * sc1
        db, dg1 = sum_head * inv_pop, sum_gain1 * inv_pop
        per_cell = [(g, r, s) for g in range(2) for r in range(halves[g]) for s in range(halves[g])]
        waiting = list(zip(row_halves, slot_h))
        for g, r, s in per_cell:
            begin = starts[g] + (r * halves[g] + s) * images[g]
            part = slice(begin, begin + images[g])
            while waiting and waiting[0][0].start < part.stop:
                span, slot = waiting.pop(0)
                net.arrived(hr1.at[0, span], slot, (i, k1))
                net.arrived(hr2.at[span], slot + 2, (i, k2))
            grad = hp[k, part, :].astype(f32) + hr1[0, part, :].astype(f32) + hr2[part, :].astype(f32)
            grad = grad * mask[part, own]
            value = k1g * (grad - valid[part, :] * (db + hat[part, own] * dg1))
            d1[g][r, s] = value.astype(bf16)
        def back_patch(pieces, p):
            parts = []
            for g, r0, r1 in pieces:
                width = halves[g] * images[g]
                taps = [
                    flat(d1[g][r0 + (a == 0) : r1 + (a == 0), (b == 0) : (b == 0) + halves[g]])
                    for a, b in PLANE_TAPS[p]
                ]
                if p == 0:
                    taps.append(dzsr[starts[g] + r0 * width : starts[g] + r1 * width, :])
                parts.append(lanes_cat(taps))
            return jnp.concatenate(parts, axis=0) if len(parts) > 1 else parts[0]

        slot_g = [net.slot(3) for _ in range(n_parts)]

        def back_first(c):
            a, b = spans[c]
            planes = []
            for p in range(4):
                weights = [w1g[k, 3 * ta + tb] for ta, tb in PLANE_TAPS[p]]
                if p == 0:
                    weights.append(wsg[k])
                planes.append(mm(back_patch(pieces[c], p), lanes_cat(weights), 1, 1))
            for g, r, begin, count in part_chunks[c]:
                values = [
                    v[begin - a : begin - a + count].reshape(halves[g], images[g], chan_in)
                    for v in planes
                ]
                for q, value in enumerate(planes_of(values, g)):
                    gp[q, begin : begin + count, :] = flat(value).astype(bf16)
            net.send(gp.at[k3, a:b], gr1.at[1, a:b], slot_g[c] + 1, (i, k1))

        def back_cross(c):
            a, b = spans[c]
            net.arrived(gr1.at[1, a:b], slot_g[c] + 1, (i, k1))
            for begin in range(a, b, 16):
                span = slice(begin, begin + 16)
                value = gp[k2, span, :].astype(f32) + gr1[1, span, :].astype(f32)
                gsum[span, :] = value.astype(bf16)
            net.send(gsum.at[a:b], gr2.at[a:b], slot_g[c] + 2, (i, k2))
            net.send(gp.at[k1, a:b], gr1.at[0, a:b], slot_g[c], (i, k1))

        slot_o = [net.slot(n_dp) for _ in range(n_parts)]

        def back_out(c):
            a, b = spans[c]
            net.arrived(gr1.at[0, a:b], slot_g[c], (i, k1))
            net.arrived(gr2.at[a:b], slot_g[c] + 2, (i, k2))
            for begin in range(a, b, 16):
                span = slice(begin, begin + 16)
                value = gp[k, span, :].astype(f32) + gr1[0, span, :].astype(f32)
                zt[span, :] = (value + gr2[span, :].astype(f32)).astype(bf16)
            cols = out_lanes[c]
            a, b = out_win[c]
            value = mm(zt[a:b, :], cells[a:b, cols], 0, 0).astype(bf16)
            gt[:, :, cols] = value.reshape(n_dp, in_local, value.shape[1])
            for j in peers:
                net.send(gt.at[j, :, cols], gr.at[i, :, cols], slot_o[c] + i, (j, k))

        sum1 = Reduce(net, i, k, wg1, (p11, p12, p13, p14, p15), cols1)

        def weight_first(w):
            cols = cols1[w]
            blocks = []
            for p in ((3,), (0, 1, 2))[w]:
                value = 0.0
                for g, r0, r1 in ((0, 0, halves[0]), (1, 0, halves[1])):
                    cell = flat(zp[g][p, 1 : 1 + halves[g], 1 : 1 + halves[g]])
                    value = value + mm(cell, back_patch([(g, r0, r1)], p), 0, 0)
                blocks.append(value.astype(bf16))
            wg1[:, :, :, :, cols] = lanes_cat(blocks).reshape(2, 2, 2, in_local, cols.stop - cols.start)
            sum1.first(w)

        back_first(0)
        for n in range(2):
            slab_in(n)
        make_planes()
        weight_first(0)
        back_cross(0)
        weight_first(1)
        back_first(1)
        back_first(2)
        back_cross(1)
        back_cross(2)
        back_out(0)
        sum2.third(1)
        sum1.second(0)
        sum1.second(1)
        back_out(1)
        sum1.third(0)
        back_out(2)
        sum1.third(1)
        gr[i] = gt[i]
        close_second()
        for w, cols in enumerate(cols1):
            value = sum1.last(w)
            for t, tap in enumerate(TAPS):
                place = ORDER.index(tap)
                place = (place + (place > 0)) * LANES
                if cols.start <= place < cols.stop:
                    gw1[t] = value[:, place - cols.start : place - cols.start + LANES]
            if cols.start <= LANES < cols.stop:
                gws[...] = value[:, LANES - cols.start : 2 * LANES - cols.start]
        vecs[...] = message([sum_gain1, sum_head, sum_gain2, sum_tail, sum_gains])
        for c in range(n_parts):
            cols = out_lanes[c]
            for j in peers:
                net.arrived(gr.at[j, :, cols], slot_o[c] + j, (j, k))
        net.drain()

    V = pltpu.VMEM
    pads = [(h + 2, h + 2, n, chan_part) for h, n in zip(halves, images)]
    half_pads = [(h + 1, h + 1, n) for h, n in zip(halves, images)]

    def ladder(count, width):
        return [
            V((2, 2, 2, count, width), bf16), V((2, 2, count, width), bf16), V((2, 2, count, width), bf16),
            V((2, count, width), bf16), V((2, count, width), bf16), V((count, width), bf16),
        ]

    inputs = [
        V((in_local, n_dp * 4 * qlanes[0]), bf16), V((in_local, n_dp * 4 * qlanes[1]), bf16),
        V((4, images[0]), jnp.int32), V((4, images[1]), jnp.int32),
        V((4, 9, chan_in, chan_part), bf16), V((9, chan_full, chan_part), bf16),
        V((4, chan_in, chan_part), bf16), V((4, 2, 1, chan_part), f32),
    ] + [V((1, chan_part), f32)] * 4 + [
        V((sizes[0], chan_part), bf16), V((sizes[1], chan_part), bf16),
    ] + [V(m.shape, bf16) for m in patch_ms] + [V((rows, slab_lanes), bf16)]
    scratch = inputs + [
        V((n_dp * in_local, slab_lanes), bf16),
        V((n_dp, in_local, slab_lanes), bf16),
        V((n_dp, in_local, slab_lanes), bf16),
        V((4, q_rows, chan_full), bf16),
        V((4, q_rows, chan_part), bf16),
        V((4, q_rows, chan_part), bf16),
        V((4, rows, chan_in), bf16),
        V((4,) + half_pads[0] + (chan_in,), bf16),
        V((4,) + half_pads[1] + (chan_in,), bf16),
        V((rows, LANES), f32),
        V((q_rows, LANES), f32),
        V((rows, chan_full), f32),
        V((rows, chan_full), f32),
        V((rows, chan_part), f32),
        V(pads[0][:3] + (chan_full,), bf16),
        V(pads[1][:3] + (chan_full,), bf16),
        V((2, 4, 16, LANES), f32),
        V((5, n_dp, 16, LANES), f32),
        V((16, LANES), f32),
        V((rows, chan_part), f32),
        V((rows, chan_part), f32),
        V((rows, chan_part), f32),
        V(pads[0], bf16),
        V(pads[1], bf16),
        V(pads[0], bf16),
        V(pads[1], bf16),
        V((2, rows, chan_full // 2), bf16),
        V((rows, chan_full // 2), bf16),
        V((chan_full // 2, 9 * chan_part), f32),
        V((rows, chan_part), bf16),
        V((rows, 9 * chan_part), bf16),
        V((4, rows, chan_part), bf16),
        V((2, rows, chan_part), bf16),
        V((rows, chan_part), bf16),
        V((rows, chan_part), bf16),
        V((rows, chan_part), f32),
        V(half_pads[0] + (chan_part,), bf16),
        V(half_pads[1] + (chan_part,), bf16),
    ]
    scratch += ladder(out_rows, 9 * LANES)[2:]
    scratch += [V((n_dp // 2, out_rows, cols2[0].stop), bf16)] + ladder(in_local, 10 * LANES)
    scratch += [
        V((4, rows, chan_in), bf16),
        V((2, rows, chan_in), bf16),
        V((rows, chan_in), bf16),
        V((rows, chan_in), bf16),
        V((rows, chan_in), bf16),
        V((n_dp, in_local, slab_lanes), bf16),
        pltpu.SemaphoreType.DMA((20,)),
        pltpu.SemaphoreType.DMA((192,)),
        pltpu.SemaphoreType.DMA((192,)),
    ]
    mid_outs = [
        V((sizes[0], chan_part), bf16),
        V((sizes[1], chan_part), bf16),
        V((n_dp, in_local, slab_lanes), bf16),
        V((9, in_local, LANES), f32),
        V((in_local, LANES), f32),
        V((9, out_rows, LANES), f32),
        V((8, LANES), f32),
        V((n_dp * in_local, n_dp * in_local), bf16),
    ]
    vmem = pl.BlockSpec(memory_space=pltpu.VMEM)
    hbm = pl.BlockSpec(memory_space=pl.ANY)
    main = pl.pallas_call(
        kernel,
        out_shape=mid_outs,
        in_specs=[hbm] * 19,
        out_specs=[vmem] * len(mid_outs),
        scratch_shapes=scratch,
        compiler_params=pltpu.CompilerParams(
            collective_id=1, has_side_effects=True, vmem_limit_bytes=58 * 2**20
        ),
        name="block",
    )

    def closing(oa, ob, gr, gw1, gws, gw2, vecs, turn,
                fa, fb, ia, ib, f1, f2, fs, c1, h1, c2, h2, cs, hs, sems):
        outs = [
            pltpu.make_async_copy(source, target, sems.at[index])
            for index, (source, target) in enumerate(
                ((gw2, f2), (gw1, f1), (oa, fa), (ob, fb), (gws, fs))
            )
        ]
        for out in outs:
            out.start()
        moved = mm(turn[...], gr[...].reshape(n_dp * in_local, slab_lanes), 1, 0)
        natural = regroup(moved, back_runs)
        ia[...] = natural[:, : qlanes[0]].reshape(in_local, n_dp, qlanes[0]).astype(bf16)
        tail = natural[:, qlanes[0] : qlanes[0] + qlanes[1]]
        ib[...] = tail.reshape(in_local, n_dp, qlanes[1]).astype(bf16)
        for ref, row in ((c1, 0), (h1, 1), (c2, 2), (h2, 3), (cs, 4), (hs, 3)):
            ref[...] = vecs[row : row + 1, :]
        for out in outs:
            out.wait()

    last = pl.pallas_call(
        closing,
        out_shape=[
            jax.ShapeDtypeStruct((sizes[0], chan_part), bf16),
            jax.ShapeDtypeStruct((sizes[1], chan_part), bf16),
            jax.ShapeDtypeStruct((in_local, n_dp, qlanes[0]), bf16),
            jax.ShapeDtypeStruct((in_local, n_dp, qlanes[1]), bf16),
            jax.ShapeDtypeStruct((9, in_local, LANES), f32),
            jax.ShapeDtypeStruct((9, out_rows, LANES), f32),
            jax.ShapeDtypeStruct((in_local, LANES), f32),
        ]
        + [jax.ShapeDtypeStruct((1, LANES), f32)] * 6,
        in_specs=[vmem] * 8,
        out_specs=[hbm, hbm, vmem, vmem, hbm, hbm, hbm] + [vmem] * 6,
        scratch_shapes=[pltpu.SemaphoreType.DMA((5,))],
        compiler_params=pltpu.CompilerParams(vmem_limit_bytes=32 * 2**20),
        name="closing",
    )
    total_rows = n_dp * in_local
    turn = np.zeros((total_rows, total_rows), np.float32)
    for c in range(in_local):
        for j in range(n_dp):
            turn[c * n_dp + j, j * in_local + c] = 1.0
    return (main, last) + tuple(m.astype(jnp.bfloat16) for m in (*patch_ms, cells_m, turn))


STOP = 99


def fused_body(
    input_a, input_b, boxes_a, boxes_b, weight_first, weight_second, weight_short,
    gain_first, shift_first, gain_second, shift_second, gain_short, shift_short,
    upstream_a, upstream_b,
):
    n_dp = lax.axis_size("dp")
    chan_part = weight_first.shape[2]
    in_local = input_a.shape[0]
    main, last, *matrices = make_fused(
        n_dp, in_local, (boxes_a.shape[0], boxes_b.shape[0]), (SA, SB),
        weight_first.shape[1], chan_part, STOP,
    )
    vectors = [
        v.reshape(1, chan_part)
        for v in (gain_first, shift_first, gain_second, shift_second, gain_short, shift_short)
    ]
    mid = main(
        input_a, input_b, boxes_a.T, boxes_b.T, weight_first, weight_second, weight_short,
        *vectors, upstream_a.T, upstream_b.T, *matrices,
    )
    res = last(*mid)
    return (
        res[0].T, res[1].T,
        res[2].reshape(in_local, n_dp, 1, -1), res[3].reshape(in_local, n_dp, 1, -1),
        res[4], res[5], res[6],
    ) + tuple(v.reshape(chan_part) for v in res[7:])


def choose_body(mesh):
    return fused_body if mesh.shape["dp"] == 8 and mesh.shape["chan"] == 4 else plain_body


def solution(mesh):
    placed = (
        P("dp", None),
        P("dp", None),
        P("dp", None),
        P("dp", None),
        P(None, None, "chan"),
        P(None, None, "chan"),
        P(None, "chan"),
        P("chan"),
        P("chan"),
        P("chan"),
        P("chan"),
        P("chan"),
        P("chan"),
        P("chan", "dp"),
        P("chan", "dp"),
    )
    return jax.shard_map(
        choose_body(mesh),
        mesh=mesh,
        in_specs=placed,
        out_specs=(
            P("chan", "dp"),
            P("chan", "dp"),
            P("dp", None, "chan", None),
            P("dp", None, "chan", None),
            P(None, "dp", "chan"),
            P(None, "dp", "chan"),
            P("dp", "chan"),
            P("chan"),
            P("chan"),
            P("chan"),
            P("chan"),
            P("chan"),
            P("chan"),
        ),
        check_vma=False,
    )
```

```python
import jax
import jax.numpy as jnp
from jax import lax
import numpy as np
from jax.experimental import pallas as pl
from jax.experimental.pallas import tpu as pltpu
from jax.sharding import PartitionSpec as P

SA = 14
SB = 6


epsilon = 1e-05


def box_mask(box_rows, extent):
    positions = jnp.arange(extent, dtype=jnp.int32)[None, :]
    row_inside = (positions >= box_rows[:, 0:1]) & (positions < box_rows[:, 0:1] + box_rows[:, 2:3])
    col_inside = (positions >= box_rows[:, 1:2]) & (positions < box_rows[:, 1:2] + box_rows[:, 3:4])
    return (row_inside[:, :, None] & col_inside[:, None, :]).astype(jnp.float32)


def taps_strided(feature, image_count, extent):
    channels = feature.shape[0]
    output_side = extent // 2
    padded = jnp.pad(
        feature.reshape(channels, image_count, extent, extent), ((0, 0), (0, 0), (1, 1), (1, 1))
    )
    pieces = [
        padded[:, :, tap_row : tap_row + extent : 2, tap_col : tap_col + extent : 2]
        for tap_row in range(3)
        for tap_col in range(3)
    ]
    return jnp.stack(pieces, axis=0).reshape(9 * channels, image_count * output_side * output_side)


def taps_plain(feature, image_count, extent):
    channels = feature.shape[0]
    padded = jnp.pad(
        feature.reshape(channels, image_count, extent, extent), ((0, 0), (0, 0), (1, 1), (1, 1))
    )
    pieces = [
        padded[:, :, tap_row : tap_row + extent, tap_col : tap_col + extent]
        for tap_row in range(3)
        for tap_col in range(3)
    ]
    return jnp.stack(pieces, axis=0).reshape(9 * channels, image_count * extent * extent)


def untaps_plain(columns, channels, image_count, extent):
    pieces = columns.reshape(9, channels, image_count, extent, extent)
    running = jnp.zeros((channels, image_count, extent + 2, extent + 2), jnp.float32)
    for tap_row in range(3):
        for tap_col in range(3):
            running = running + jnp.pad(
                pieces[3 * tap_row + tap_col],
                ((0, 0), (0, 0), (tap_row, 2 - tap_row), (tap_col, 2 - tap_col)),
            )
    return running[:, :, 1:-1, 1:-1].reshape(channels, image_count * extent * extent)


def untaps_strided(columns, shortcut, channels, image_count, extent):
    output_side = extent // 2
    pieces = columns.reshape(9, channels, image_count, output_side, output_side)
    parity_sums = {}
    for tap_row in range(3):
        for tap_col in range(3):
            block_row = tap_row // 2
            block_col = tap_col // 2
            placed = jnp.pad(
                pieces[3 * tap_row + tap_col],
                ((0, 0), (0, 0), (block_row, 1 - block_row), (block_col, 1 - block_col)),
            )
            parity = (tap_row % 2, tap_col % 2)
            parity_sums[parity] = (
                placed if parity not in parity_sums else parity_sums[parity] + placed
            )
    direct = jnp.pad(
        shortcut.reshape(channels, image_count, output_side, output_side),
        ((0, 0), (0, 0), (0, 1), (0, 1)),
    )
    parity_sums[1, 1] = parity_sums[1, 1] + direct
    rows_even = jnp.stack([parity_sums[0, 0], parity_sums[0, 1]], axis=-1)
    rows_odd = jnp.stack([parity_sums[1, 0], parity_sums[1, 1]], axis=-1)
    padded = jnp.stack([rows_even, rows_odd], axis=3).reshape(
        channels, image_count, extent + 2, extent + 2
    )
    return padded[:, :, 1:-1, 1:-1].reshape(channels, image_count * extent * extent)


def contract_first(weights, columns):
    return lax.dot_general(
        weights, columns, (((0,), (0,)), ((), ())), preferred_element_type=jnp.float32
    )


def weight_product(columns, gradient):
    return lax.dot_general(
        columns, gradient, (((1,), (1,)), ((), ())), preferred_element_type=jnp.float32
    )


def swish_slope(values):
    logistic = jax.nn.sigmoid(values)
    return logistic * (1.0 + values * (1.0 - logistic))


def moments(values, valid_list):
    running = 0.0
    squares = 0.0
    for tensor, valid in zip(values, valid_list):
        widened = tensor.astype(jnp.float32)
        running = running + jnp.sum(widened * valid, axis=1)
        squares = squares + jnp.sum(widened * widened * valid, axis=1)
    return (running, squares)


def standardize(values, running, squares, population):
    mean_value = running / population
    variance = squares / population - mean_value * mean_value
    scaling = lax.rsqrt(variance + epsilon)
    return (
        [
            (tensor.astype(jnp.float32) - mean_value[:, None]) * scaling[:, None]
            for tensor in values
        ],
        scaling,
    )


def norm_back(gradient, normed, valid, scaling, gain_values, shift_sum, gain_sum, population):
    return (gain_values * scaling)[:, None] * (
        gradient - valid * (shift_sum[:, None] + normed * gain_sum[:, None]) / population
    )


def plain_body(
    input_a,
    input_b,
    boxes_a,
    boxes_b,
    weight_first,
    weight_second,
    weight_short,
    gain_first,
    shift_first,
    gain_second,
    shift_second,
    gain_short,
    shift_short,
    upstream_a,
    upstream_b,
):
    image_groups = lax.axis_size("dp")
    in_local = input_a.shape[0]
    chan_in = weight_first.shape[1]
    chan_part = weight_first.shape[2]
    chan_full = weight_second.shape[1]
    image_counts = (boxes_a.shape[0], boxes_b.shape[0])
    extents = (SA, SB)
    whole_a, whole_b = (
        lax.all_to_all(
            input_a.reshape(in_local, image_groups, -1),
            "dp",
            split_axis=1,
            concat_axis=0,
            tiled=True,
        ),
        lax.all_to_all(
            input_b.reshape(in_local, image_groups, -1),
            "dp",
            split_axis=1,
            concat_axis=0,
            tiled=True,
        ),
    )
    features = (whole_a.reshape(chan_in, -1), whole_b.reshape(chan_in, -1))
    valid_list = (
        box_mask(boxes_a, SA // 2).reshape(1, -1),
        box_mask(boxes_b, SB // 2).reshape(1, -1),
    )
    first_mat = weight_first.reshape(9 * chan_in, chan_part)
    second_mat = weight_second.reshape(9 * chan_full, chan_part)
    first_cols = []
    sampled = []
    first_z = []
    short_z = []
    for feature, image_count, extent in zip(features, image_counts, extents):
        columns = taps_strided(feature, image_count, extent)
        picked = feature.reshape(chan_in, image_count, extent, extent)[:, :, ::2, ::2].reshape(
            chan_in, -1
        )
        first_cols.append(columns)
        sampled.append(picked)
        first_z.append(contract_first(first_mat, columns).astype(jnp.bfloat16))
        short_z.append(contract_first(weight_short, picked).astype(jnp.bfloat16))
    sum_first, square_first = moments(first_z, valid_list)
    sum_short, square_short = moments(short_z, valid_list)
    population = jnp.sum(valid_list[0]) + jnp.sum(valid_list[1])
    sum_first, square_first, sum_short, square_short, population = lax.psum(
        (sum_first, square_first, sum_short, square_short, population), "dp"
    )
    normed_first, scaling_first = standardize(first_z, sum_first, square_first, population)
    normed_short, scaling_short = standardize(short_z, sum_short, square_short, population)
    before_first = [normed * gain_first[:, None] + shift_first[:, None] for normed in normed_first]
    outgoing_a = (jax.nn.silu(before_first[0]) * valid_list[0]).astype(jnp.bfloat16)
    outgoing_b = (jax.nn.silu(before_first[1]) * valid_list[1]).astype(jnp.bfloat16)
    gathered_a, gathered_b = (
        lax.all_gather(outgoing_a, "chan", axis=0, tiled=True),
        lax.all_gather(outgoing_b, "chan", axis=0, tiled=True),
    )
    second_cols = []
    second_z = []
    for gathered, image_count, extent in zip((gathered_a, gathered_b), image_counts, extents):
        columns = taps_plain(gathered, image_count, extent // 2)
        second_cols.append(columns)
        second_z.append(contract_first(second_mat, columns).astype(jnp.bfloat16))
    sum_second, square_second = moments(second_z, valid_list)
    sum_second, square_second = lax.psum((sum_second, square_second), "dp")
    normed_second, scaling_second = standardize(second_z, sum_second, square_second, population)
    summed_pre = [
        main_part * gain_second[:, None]
        + shift_second[:, None]
        + side_part * gain_short[:, None]
        + shift_short[:, None]
        for main_part, side_part in zip(normed_second, normed_short)
    ]
    outputs = [
        (jax.nn.silu(tensor) * valid).astype(jnp.bfloat16)
        for tensor, valid in zip(summed_pre, valid_list)
    ]
    tail_grads = [
        upstream.astype(jnp.float32) * valid * swish_slope(tensor)
        for upstream, valid, tensor in zip((upstream_a, upstream_b), valid_list, summed_pre)
    ]
    shift_tail = sum((jnp.sum(gradient, axis=1) for gradient in tail_grads))
    gain_tail = sum(
        (jnp.sum(gradient * normed, axis=1) for gradient, normed in zip(tail_grads, normed_second))
    )
    gain_side = sum(
        (jnp.sum(gradient * normed, axis=1) for gradient, normed in zip(tail_grads, normed_short))
    )
    shift_tail, gain_tail, gain_side = lax.psum((shift_tail, gain_tail, gain_side), "dp")
    grad_second_local = 0.0
    partial_hidden = []
    short_dz = []
    for index_group in range(2):
        valid = valid_list[index_group]
        dz_second = norm_back(
            tail_grads[index_group],
            normed_second[index_group],
            valid,
            scaling_second,
            gain_second,
            shift_tail,
            gain_tail,
            population,
        ).astype(jnp.bfloat16)
        dz_short = norm_back(
            tail_grads[index_group],
            normed_short[index_group],
            valid,
            scaling_short,
            gain_short,
            shift_tail,
            gain_side,
            population,
        ).astype(jnp.bfloat16)
        short_dz.append(dz_short)
        grad_second_local = grad_second_local + weight_product(second_cols[index_group], dz_second)
        back_cols = jnp.dot(second_mat, dz_second, preferred_element_type=jnp.float32)
        partial_hidden.append(
            untaps_plain(back_cols, chan_full, image_counts[index_group], extents[index_group] // 2)
        )
    hidden_a, hidden_b = (
        lax.psum_scatter(
            partial_hidden[0].astype(jnp.bfloat16), "chan", scatter_dimension=0, tiled=True
        ).astype(jnp.float32),
        lax.psum_scatter(
            partial_hidden[1].astype(jnp.bfloat16), "chan", scatter_dimension=0, tiled=True
        ).astype(jnp.float32),
    )
    head_grads = [
        hidden * valid * swish_slope(tensor)
        for hidden, valid, tensor in zip((hidden_a, hidden_b), valid_list, before_first)
    ]
    shift_head = sum((jnp.sum(gradient, axis=1) for gradient in head_grads))
    gain_head = sum(
        (jnp.sum(gradient * normed, axis=1) for gradient, normed in zip(head_grads, normed_first))
    )
    shift_head, gain_head = lax.psum((shift_head, gain_head), "dp")
    grad_first_local = 0.0
    grad_short_local = 0.0
    partial_inputs = []
    for index_group in range(2):
        valid = valid_list[index_group]
        dz_first = norm_back(
            head_grads[index_group],
            normed_first[index_group],
            valid,
            scaling_first,
            gain_first,
            shift_head,
            gain_head,
            population,
        ).astype(jnp.bfloat16)
        grad_first_local = grad_first_local + weight_product(first_cols[index_group], dz_first)
        grad_short_local = grad_short_local + weight_product(
            sampled[index_group], short_dz[index_group]
        )
        back_cols = jnp.dot(first_mat, dz_first, preferred_element_type=jnp.float32)
        back_short = jnp.dot(
            weight_short, short_dz[index_group], preferred_element_type=jnp.float32
        )
        flat_input = untaps_strided(
            back_cols, back_short, chan_in, image_counts[index_group], extents[index_group]
        )
        partial_inputs.append(flat_input.reshape(chan_in, 1, lax.axis_size("chan"), -1))
    arrived_a, arrived_b = (
        lax.all_to_all(
            partial_inputs[0].astype(jnp.bfloat16), "dp", split_axis=0, concat_axis=1, tiled=True
        ).astype(jnp.float32),
        lax.all_to_all(
            partial_inputs[1].astype(jnp.bfloat16), "dp", split_axis=0, concat_axis=1, tiled=True
        ).astype(jnp.float32),
    )
    summed_a, summed_b = (
        lax.psum_scatter(
            arrived_a.astype(jnp.bfloat16), "chan", scatter_dimension=2, tiled=True
        ).astype(jnp.float32),
        lax.psum_scatter(
            arrived_b.astype(jnp.bfloat16), "chan", scatter_dimension=2, tiled=True
        ).astype(jnp.float32),
    )
    grad_input_a = summed_a.astype(jnp.bfloat16)
    grad_input_b = summed_b.astype(jnp.bfloat16)
    grad_first_local = grad_first_local.reshape(9, chan_in, chan_part)
    grad_second_local = grad_second_local.reshape(9, chan_full, chan_part)
    total_first, total_second, total_short = lax.psum(
        (grad_first_local, grad_second_local, grad_short_local), "dp"
    )
    position = lax.axis_index("dp")
    rows_first = chan_in // image_groups
    rows_second = chan_full // image_groups
    grad_first = lax.dynamic_slice_in_dim(total_first, position * rows_first, rows_first, 1)
    grad_second = lax.dynamic_slice_in_dim(total_second, position * rows_second, rows_second, 1)
    grad_short = lax.dynamic_slice_in_dim(total_short, position * rows_first, rows_first, 0)
    return (
        outputs[0],
        outputs[1],
        grad_input_a,
        grad_input_b,
        grad_first,
        grad_second,
        grad_short,
        gain_head,
        shift_head,
        gain_tail,
        shift_tail,
        gain_side,
        shift_tail,
    )


MESH = pl.DeviceIdType.MESH
TAPS = tuple((a, b) for a in range(3) for b in range(3))
PLANE_TAPS = (
    ((1, 1),),
    ((1, 0), (1, 2)),
    ((0, 1), (2, 1)),
    ((0, 0), (0, 2), (2, 0), (2, 2)),
)
ORDER = [tap for taps in PLANE_TAPS for tap in taps]
LANES = 128


class Links:
    def __init__(self, send_sems, recv_sems):
        self.send_sems, self.recv_sems = send_sems, recv_sems
        self.sends = self.slots = 0
        self.open = []

    def slot(self, count=1):
        first = self.slots
        self.slots += count
        return first

    def send(self, source, target, slot, where):
        copy = pltpu.make_async_remote_copy(
            source, target, self.send_sems.at[self.sends], self.recv_sems.at[slot],
            device_id=where, device_id_type=MESH,
        )
        self.sends += 1
        copy.start()
        self.open.append(copy)

    def arrived(self, target, slot, where):
        pltpu.make_async_remote_copy(
            target, target, self.send_sems.at[0], self.recv_sems.at[slot],
            device_id=where, device_id_type=MESH,
        ).wait_recv()

    def drain(self):
        for copy in self.open:
            copy.wait_send()


def mm(a, b, ca, cb):
    return lax.dot_general(a, b, (((ca,), (cb,)), ((), ())), preferred_element_type=jnp.float32)


def lanes_cat(parts):
    return jnp.concatenate(parts, axis=1) if len(parts) > 1 else parts[0]


def quarter_matrices(images, sides, segments, seg_lane, seg_row, q_rows, lanes):
    def lane(g, image, row, col):
        for (seg_g, r0, r1), first in zip(segments, seg_lane):
            if seg_g == g and 2 * r0 <= row < 2 * r1:
                return first + (image * 2 * (r1 - r0) + row - 2 * r0) * sides[g] + col

    taps = np.zeros((9, q_rows, lanes), np.float32)
    for (g, r0, r1), first in zip(segments, seg_row):
        half = sides[g] // 2
        for r in range(r0, r1):
            for s in range(half):
                for image in range(images[g]):
                    target = first + ((r - r0) * half + s) * images[g] + image
                    for t, (a, b) in enumerate(TAPS):
                        row, col = 2 * r + a - 1, 2 * s + b - 1
                        if row >= 0 and col >= 0:
                            taps[t, target, lane(g, image, row, col)] = 1.0
    sizes = [n * side * side for n, side in zip(images, sides)]
    cells = np.zeros((sum(sizes), lanes), np.float32)
    for g, (n, side) in enumerate(zip(images, sides)):
        for image in range(n):
            for row in range(side):
                for col in range(side):
                    cell = (row // 2) * (side // 2) + col // 2
                    target = g * sizes[0] + (cell * 4 + 2 * (row % 2) + col % 2) * n + image
                    cells[target, lane(g, image, row, col)] = 1.0
    return taps, cells


def regroup(value, runs):
    return jnp.concatenate([value[:, a:b] for a, b in runs], axis=1)


def sigma(v):
    return 0.5 * jnp.tanh(0.5 * v) + 0.5


class Reduce:
    def __init__(self, net, i, k, part, bufs, windows, b4=None):
        self.b4 = b4
        self.net, self.part, self.windows = net, part, windows
        self.b1, self.s1, self.b2, self.s2, self.b3 = bufs
        self.ix, self.pz, self.hz = i % 2, (i // 2) % 2, i // 4
        self.peers = (
            (i + 1 - 2 * self.ix, k),
            (i + 2 - 4 * self.pz, k),
            (i + 4 - 8 * self.hz, k),
        )
        self.slots = [net.slot(3) for _ in windows]

    def first(self, w):
        cols = self.windows[w]
        self.net.send(
            self.part.at[:, :, 1 - self.ix, :, cols], self.b1.at[:, :, :, cols],
            self.slots[w], self.peers[0],
        )

    def second(self, w):
        cols = self.windows[w]
        self.net.arrived(self.b1.at[:, :, :, cols], self.slots[w], self.peers[0])
        for h in range(2):
            for p in range(2):
                value = self.part[h, p, self.ix, :, cols].astype(jnp.float32)
                value = value + self.b1[h, p, :, cols].astype(jnp.float32)
                self.s1[h, p, :, cols] = value.astype(jnp.bfloat16)
        self.net.send(
            self.s1.at[:, 1 - self.pz, :, cols], self.b2.at[:, :, cols],
            self.slots[w] + 1, self.peers[1],
        )

    def second_of(self, w, value):
        cols = self.windows[w]
        self.s1[:, :, :, cols] = value.reshape(2, 2, -1, value.shape[1])
        self.net.send(
            self.s1.at[:, 1 - self.pz, :, cols], self.b2.at[:, :, cols],
            self.slots[w] + 1, self.peers[1],
        )

    def spread_of(self, w, value):
        cols = self.windows[w]
        self.s1[:, :, :, cols] = value.reshape(2, 2, -1, value.shape[1])
        z = 2 * self.hz + self.pz
        self.direct = self.net.slot(4)
        for d in range(1, 4):
            to = (z + d) % 4
            self.net.send(
                self.s1.at[to // 2, to % 2, :, cols], self.b4.at[z],
                self.direct + z, (2 * to + self.ix, self.peers[0][1]),
            )

    def spread_last(self, w):
        cols = self.windows[w]
        z = 2 * self.hz + self.pz
        value = self.s1[self.hz, self.pz, :, cols].astype(jnp.float32)
        for d in range(1, 4):
            to = (z + d) % 4
            self.net.arrived(self.b4.at[to], self.direct + to, (2 * to + self.ix, self.peers[0][1]))
            value = value + self.b4[to].astype(jnp.float32)
        return value

    def third(self, w):
        cols = self.windows[w]
        self.net.arrived(self.b2.at[:, :, cols], self.slots[w] + 1, self.peers[1])
        for h in range(2):
            value = self.s1[h, self.pz, :, cols].astype(jnp.float32)
            value = value + self.b2[h, :, cols].astype(jnp.float32)
            self.s2[h, :, cols] = value.astype(jnp.bfloat16)
        self.net.send(
            self.s2.at[1 - self.hz, :, cols], self.b3.at[:, cols],
            self.slots[w] + 2, self.peers[2],
        )

    def last(self, w):
        cols = self.windows[w]
        self.net.arrived(self.b3.at[:, cols], self.slots[w] + 2, self.peers[2])
        return self.s2[self.hz, :, cols].astype(jnp.float32) + self.b3[:, cols].astype(jnp.float32)


def make_fused(n_dp, in_local, images, sides, chan_in, chan_part, stop):
    f32, bf16 = jnp.float32, jnp.bfloat16
    halves = tuple(side // 2 for side in sides)
    sizes = tuple(h * h * n for h, n in zip(halves, images))
    rows = sum(sizes)
    quarter = tuple(n // 4 for n in images)
    qlanes = tuple(q * side * side for q, side in zip(quarter, sides))
    slab_lanes = -(-sum(qlanes) // LANES) * LANES
    chan_full = 4 * chan_part
    out_rows = chan_full // n_dp
    starts = (0, sizes[0])
    widths = tuple(h * n for h, n in zip(halves, images))
    chunks = [(g, r, starts[g] + r * widths[g], widths[g]) for g in range(2) for r in range(halves[g])]
    win = [-(-q // LANES) * LANES for q in qlanes]
    b_tile = qlanes[0] // LANES * LANES
    b_skip = qlanes[0] - b_tile
    rs = halves[0] // 2
    segments = [(1, 0, halves[1]), (0, 0, rs), (0, rs, halves[0])]
    seg_lane, runs = [], []
    lane_of = 0
    for g, r0, r1 in segments:
        side, base = sides[g], (0, qlanes[0])[g]
        seg_lane.append(lane_of)
        lane_of += quarter[g] * 2 * (r1 - r0) * side
        runs += [
            (base + (image * side + 2 * r0) * side, base + (image * side + 2 * r1) * side)
            for image in range(quarter[g])
        ]
    runs.append((sum(qlanes), slab_lanes))
    at, order = 0, []
    for a, b in runs:
        order.append((a, at, at + b - a))
        at += b - a
    back_runs = [(a, b) for _, a, b in sorted(order)]
    cut_lane = -(-seg_lane[2] // LANES) * LANES
    lane_parts = (slice(0, cut_lane), slice(cut_lane, slab_lanes))
    seg_cells = [(r1 - r0) * halves[g] for g, r0, r1 in segments]
    seg_rows = [cells * quarter[seg[0]] for cells, seg in zip(seg_cells, segments)]
    top = -(-(seg_rows[0] + seg_rows[1]) // 16) * 16
    seg_row = [0, seg_rows[0], top]
    q_rows = top + -(-seg_rows[2] // 16) * 16
    row_parts = (slice(0, top), slice(top, q_rows))
    patch_win = (slice(0, cut_lane), slice(seg_lane[1] // LANES * LANES, slab_lanes))
    patch_m, cells_m = quarter_matrices(
        quarter, sides, segments, seg_lane, seg_row, q_rows, slab_lanes
    )
    patch_ms = [
        np.concatenate([m[rows_, lanes_] for m in patch_m], axis=0)
        for rows_, lanes_ in zip(row_parts, patch_win)
    ]
    low_lane = seg_lane[1] // LANES * LANES
    out_lanes = [slice(cut_lane, slab_lanes), slice(0, low_lane), slice(low_lane, cut_lane)]
    back_pieces = (((0, 0, 2),), ((0, 2, halves[0] - 1),), ((0, halves[0] - 1, halves[0]), (1, 0, halves[1])))
    row_halves = [
        slice(starts[p[0][0]] + p[0][1] * widths[p[0][0]], starts[p[-1][0]] + p[-1][2] * widths[p[-1][0]])
        for p in back_pieces
    ]
    cols2 = (slice(0, 4 * LANES), slice(4 * LANES, 9 * LANES))
    cols1 = (slice(6 * LANES, 10 * LANES), slice(0, 6 * LANES))

    def kernel(*refs):
        (xa_h, xb_h, bxa_h, bxb_h, w1_h, w2_h, ws_h, g1_h, b1_h, g2_h, b2_h, gs_h, bs_h, ua_h, ub_h,
         pm0_h, pm1_h, cells_h,
         turn_h,
         oa, ob, gr, gw1, gws, gw2, vecs, turn,
         xa, xb, bxa, bxb, w1g, w2, wsg, vg, g2, b2, gs, bs, ua, ub, pm0, pm1, cells,
         xs, xt, xr, zb, zsq, zsr, zg, zpa, zpb, valid, vq, hat, mask, zs, a1a, a1b,
         cslots, slots, stat, up, outr, gv, dza, dzb, dzma, dzmb, apk, arx, gacc, dzsr,
         dd, hp, hr1, hs, hr2, gu, d1a, d1b,
         p22, p23, p24, p25, p26, wg1, p11, p12, p13, p14, p15,
         sq, si, dq, di, gt, lsem, ssem, rsem) = refs
        i, k = lax.axis_index("dp"), lax.axis_index("chan")
        k1 = k + 1 - 2 * (k % 2)
        k2 = (k + 2) % 4
        k3 = (k1 + 2) % 4
        ix = i % 2
        mate = (i + 1 - 2 * ix, k)
        net = Links(ssem, rsem)
        bits = n_dp.bit_length() - 1

        def flip(d):
            j = i
            for b in range(bits):
                if d >> b & 1:
                    j = j + (1 << b) * (1 - 2 * ((i // (1 << b)) % 2))
            return j

        peers = [flip(d) for d in sorted(range(n_dp), key=lambda d: (d == 0, -(d >> 1), d & 1))]
        peers, home = peers[:-1], peers[-1]
        zp, a1, dz, d1 = (zpa, zpb), (a1a, a1b), (dza, dzb), (d1a, d1b)
        dzm = (dzma, dzmb)

        def flat(value):
            return value.reshape(-1, value.shape[-1])

        def zeros(count):
            return [jnp.zeros((8, LANES), f32)] * count

        loads = {}
        pairs_of = (
            ("xa", xa_h, xa), ("xb", xb_h, xb),
            ("w1", w1_h, w1g.at[k]), ("ws", ws_h, wsg.at[k]), ("g1", g1_h, vg.at[k, 0]), ("b1", b1_h, vg.at[k, 1]),
            ("bxa", bxa_h, bxa), ("bxb", bxb_h, bxb), ("pm0", pm0_h, pm0), ("pm1", pm1_h, pm1),
            ("ua", ua_h, ua), ("ub", ub_h, ub), ("g2", g2_h, g2),
            ("b2", b2_h, b2), ("gs", gs_h, gs), ("bs", bs_h, bs), ("w2", w2_h, w2), ("cells", cells_h, cells),
            ("turn", turn_h, turn),
        )
        for index, (name, source, target) in enumerate(pairs_of):
            loads[name] = pltpu.make_async_copy(source, target, lsem.at[index])
        loads["xa"].start()
        loads["xb"].start()

        def need(*names):
            for name in names:
                loads.pop(name).wait()

        barrier = pltpu.get_barrier_semaphore()
        for j in peers:
            pl.semaphore_signal(barrier, inc=1, device_id=(j, k), device_id_type=MESH)
        for where in (k1, k2, k3):
            pl.semaphore_signal(barrier, inc=1, device_id=(i, where), device_id_type=MESH)

        need("xa", "xb")
        for copy in loads.values():
            copy.start()
        lane = lax.broadcasted_iota(jnp.int32, (in_local, LANES), 1)
        for d, j in enumerate(peers + [home]):
            begin = 4 * qlanes[0] * j + qlanes[0] * k
            tile = begin // LANES
            part_a = xa[:, pl.ds(pl.multiple_of(tile * LANES, LANES), win[0])].astype(f32)
            part_a = pltpu.roll(part_a, (win[0] - (begin - tile * LANES)) % win[0], 1)
            begin = 4 * qlanes[1] * j + qlanes[1] * k
            tile = begin // LANES
            part_b = xb[:, pl.ds(pl.multiple_of(tile * LANES, LANES), win[1])].astype(f32)
            part_b = jnp.concatenate([part_b, jnp.zeros((in_local, LANES), f32)], axis=1)
            wide = win[1] + LANES
            part_b = pltpu.roll(part_b, (wide + b_skip - (begin - tile * LANES)) % wide, 1)
            seam = jnp.where(lane < b_skip, part_a[:, b_tile : b_tile + LANES], part_b[:, :LANES])
            xs[d * in_local : (d + 1) * in_local, :] = jnp.concatenate(
                [part_a[:, :b_tile], seam, part_b[:, LANES : slab_lanes - b_tile]], axis=1
            ).astype(bf16)
        slot_x = [net.slot(n_dp) for _ in lane_parts]
        n_via = 2
        via = [pl.ds((9 - n_via) * e, n_via) for e in (ix, 1 - ix)]
        w_taps = [via[0], slice(n_via, 5), slice(5, 9 - n_via)]
        slot_w = [net.slot(4) for _ in range(6)]

        def weight_refs(q):
            return [w1g.at[q, taps] for taps in w_taps] + [wsg.at[q], vg.at[q], w1g.at[q, via[1]]]

        ordered = regroup(xs[...], runs)
        for c, cols in enumerate(lane_parts):
            moved = ordered[:, cols]
            xt[:, :, cols] = moved.reshape(n_dp, in_local, moved.shape[1])
            xr[i, :, cols] = moved[-in_local:]
            if c == 0:
                pl.semaphore_wait(barrier, n_dp + 2)
            for d, j in enumerate(peers):
                net.send(xt.at[d, :, cols], xr.at[i, :, cols], slot_x[c] + i, (j, k))
            if c == 0:
                need("w1", "ws", "g1", "b1")
                for ref, slot in zip(weight_refs(k)[:5], slot_w):
                    net.send(ref, ref, slot + k, (i, k2))
                for ref, slot in zip(weight_refs(k), slot_w):
                    net.send(ref, ref, slot + k, (i, k1))

        def weights_on(n):
            ref = weight_refs(k2)[n]
            net.arrived(ref, slot_w[n] + k2, mate if n == 5 else (i, k2))
            net.send(ref, ref, slot_w[n] + k2, (i, k1))
            if n == 0:
                net.send(ref, ref, slot_w[5] + k2, mate)

        def weights_in(parts):
            for q in (k1, k3):
                for n in parts:
                    net.arrived(weight_refs(q)[n], slot_w[n] + q, (i, k1))

        for buf in (zpa, zpb, a1a, a1b, dza, dzb, dzma, dzmb, d1a, d1b):
            side = buf.shape[1] if len(buf.shape) == 5 else buf.shape[0]
            lead = (slice(None),) if len(buf.shape) == 5 else ()
            for edge in (0, side - 1):
                for index in (lead + (edge,), lead + (slice(None), edge)):
                    region = buf.at[index]
                    region[...] = jnp.zeros(region.shape, buf.dtype)
        need("bxa", "bxb", "ua", "ub")
        population = zeros(1)[0]
        low = lax.broadcasted_iota(jnp.int32, (8, LANES), 0) < 4
        for g, box in enumerate((bxa, bxb)):
            n, half, count = images[g], halves[g], quarter[g]
            diag = lax.broadcasted_iota(jnp.int32, (n, n), 0) == lax.broadcasted_iota(jnp.int32, (n, n), 1)
            ends = [
                jnp.sum(jnp.where(diag, box[q : q + 1, :].astype(f32), 0.0), axis=1, keepdims=True)
                for q in range(4)
            ]
            ends = [jnp.broadcast_to(e, (n, LANES)) for e in ends]
            ends[2], ends[3] = ends[0] + ends[2], ends[1] + ends[3]

            def inside(ends, r, s):
                both = (r >= ends[0]) & (r < ends[2]) & (s >= ends[1]) & (s < ends[3])
                return both.astype(f32)

            for r in range(half):
                for s in range(half):
                    cell = inside(ends, r, s)
                    begin = starts[g] + (r * half + s) * n
                    valid[begin : begin + n, :] = cell
                    population = population + jnp.sum(cell.reshape(n // 8, 8, LANES), axis=0)
            mine = [pltpu.roll(e, (n - count * k) % n, 0)[:8] for e in ends]
            if count < 8:
                mine = [jnp.where(low, e, pltpu.roll(e, 4, 0)) for e in mine]
            for (seg_g, r0, r1), first, cells_n in zip(segments, seg_row, seg_cells):
                if seg_g != g:
                    continue
                per = 8 // count
                for t in range(-(-cells_n // per)):
                    spots = [divmod(min(per * t + e, cells_n - 1), half) for e in range(per)]
                    spots = [(float(r0 + r), float(s)) for r, s in spots]
                    if per == 2:
                        r, s = (jnp.where(low, spots[0][e], spots[1][e]) for e in range(2))
                    else:
                        r, s = spots[0]
                    cell = inside(mine, r, s)
                    if per == 2 and per * t + 1 >= cells_n:
                        cell = jnp.where(low, cell, 0.0)
                    vq[first + 8 * t : first + 8 * t + 8, :] = cell
        population = jnp.broadcast_to(jnp.sum(population, axis=0, keepdims=True), (8, LANES))
        for g, source in enumerate((ua, ub)):
            n, count = images[g], halves[g] ** 2
            gu[starts[g] : starts[g] + sizes[g], :] = source[...].astype(f32)
            for cell in range(count):
                up[starts[g] + cell * n : starts[g] + (cell + 1) * n, :] = gu[
                    pl.ds(starts[g] + cell, n, stride=count), :
                ]

        def rowsum(value):
            return jnp.sum(value.reshape(-1, 8, value.shape[-1]), axis=0)

        def message(sums):
            parts = [jnp.sum(v, axis=0, keepdims=True) if v.shape[0] > 1 else v for v in sums]
            if len(parts) % 8:
                parts.append(jnp.zeros((8 - len(parts) % 8, LANES), f32))
            return jnp.concatenate(parts, axis=0)

        def by_chan(value):
            return [value[:, q * LANES : (q + 1) * LANES] for q in range(4)]

        def share(rnd, value):
            mine = slots.at[rnd, i, : value.shape[0]]
            mine[...] = value
            first = net.slot(n_dp)
            for j in peers:
                net.send(mine, mine, first + i, (j, k))
            return first

        def total(rnd, first, count=8):
            for j in peers:
                net.arrived(slots.at[rnd, j, :count], first + j, (j, k))
            return jnp.sum(slots[rnd, :, :count], axis=0)

        def chan_share(rnd, value):
            mine = cslots.at[rnd, k, : value.shape[0]]
            mine[...] = value
            first = net.slot(4)
            for where in (k2, k3, k1):
                net.send(mine, mine, first + k, (i, where))
            return first

        def chan_total(rnd, first, count=8):
            for where in (k1, k2, k3):
                net.arrived(cslots.at[rnd, where, :count], first + where, (i, where))
            return jnp.sum(cslots[rnd, :, :count], axis=0)

        pop_first = share(4, population)

        def quarter_in(c):
            for j in peers:
                net.arrived(xr.at[j, :, lane_parts[c]], slot_x[c] + j, (j, k))

        def patches(c):
            whole = jnp.concatenate([xr[q, :, patch_win[c]] for q in range(n_dp)], axis=0)
            value = mm((pm0, pm1)[c][...], whole, 1, 1).astype(bf16)
            count = value.shape[0] // 9
            return [value[t * count : (t + 1) * count] for t in range(9)]

        slot_s = net.slot(4)

        z_cuts = (slice(0, top * 3 // 80 * 16), slice(top * 3 // 80 * 16, top), slice(top, q_rows))
        slot_z = [net.slot(4) for _ in z_cuts]

        def z_send(n):
            for where in (k2, k1):
                net.send(zb.at[k, z_cuts[n]], zb.at[k, z_cuts[n]], slot_z[n] + k, (i, where))

        def first_conv(c, taps, acc):
            part = row_parts[c]
            weights = lanes_cat([w1g[q].reshape(9 * chan_in, chan_part) for q in range(4)])
            value = mm(lanes_cat(taps), weights, 1, 0).astype(bf16)
            zb[k, part, :] = value
            if c == 0:
                z_send(0)
            z = value.astype(f32)
            u = z * lanes_cat([vq[part, :]] * 4)
            return [acc[0] + rowsum(u), acc[1] + rowsum(u * z)]

        def projection(c, patch, acc):
            side = mm(patch, lanes_cat([wsg[q] for q in range(4)]), 1, 0).astype(bf16)
            for q, z in enumerate(by_chan(side)):
                zsq[q, row_parts[c], :] = z
            z = side.astype(f32)
            u = z * lanes_cat([vq[row_parts[c], :]] * 4)
            return [acc[0] + rowsum(u), acc[1] + rowsum(u * z)]

        def act_on(n):
            part = zb.at[k2, z_cuts[n]]
            net.arrived(part, slot_z[n] + k2, (i, k2))
            net.send(part, part, slot_z[n] + k2, (i, k1))

        def act_in(n):
            net.arrived(zb.at[k1, z_cuts[n]], slot_z[n] + k1, (i, k1))
            net.arrived(zb.at[k3, z_cuts[n]], slot_z[n] + k3, (i, k1))

        acc = [jnp.zeros((8, chan_full), f32)] * 2
        need("pm0", "pm1")
        for n in (0, 1, 5, 2):
            weights_on(n)
        quarter_in(0)
        taps = patches(0)
        center = [taps[4]]
        weights_on(3)
        weights_on(4)
        weights_in((0, 1, 2, 5))
        acc = first_conv(0, taps, acc)
        quarter_in(1)
        taps = patches(1)
        center.append(taps[4])
        acc = first_conv(1, taps, acc)
        acc = [jnp.sum(v, axis=0, keepdims=True) for v in acc]
        first = chan_share(0, message(sum((by_chan(v) for v in acc), [])))
        z_send(1)
        z_send(2)
        weights_in((3, 4))
        acc = [jnp.zeros((8, chan_full), f32)] * 2
        for c in range(2):
            acc = projection(c, center[c], acc)
        acc = [jnp.sum(v, axis=0, keepdims=True) for v in acc]
        side_first = share(5, message(sum((by_chan(v) for v in acc), [])))
        zsr[k] = zsq[k]

        need(*list(loads))
        row_cuts = (slice(0, rows // 32 * 16), slice(rows // 32 * 16, rows))
        slot_g0 = [net.slot(4) for _ in row_cuts]
        whole = jnp.concatenate([xr[q] for q in range(n_dp)], axis=0)
        for span in row_cuts:
            zg[k, span, :] = mm(cells[span, :], whole, 1, 1).astype(bf16)
        first = share(0, chan_total(0, first))
        for where in (k2, k3, k1):
            net.send(zsq.at[where], zsr.at[k], slot_s + k, (i, where))
        act_on(0)
        act_on(1)
        act_on(2)
        side_first = chan_share(2, total(5, side_first))
        for span, slot in zip(row_cuts, slot_g0):
            for where in (k2, k1):
                net.send(zg.at[k, span], zg.at[k, span], slot + k, (i, where))

        def slab_on(n):
            span, slot = row_cuts[n], slot_g0[n]
            net.arrived(zg.at[k2, span], slot + k2, (i, k2))
            net.send(zg.at[k2, span], zg.at[k2, span], slot + k2, (i, k1))

        def slab_in(n):
            span, slot = row_cuts[n], slot_g0[n]
            net.arrived(zg.at[k1, span], slot + k1, (i, k1))
            net.arrived(zg.at[k3, span], slot + k3, (i, k1))

        inv_pop = 1.0 / total(4, pop_first)[0:1]
        turn_low = lax.broadcasted_iota(jnp.int32, (8, 1), 0) < 4

        def whole_cells(read, c):
            for begin in range(row_parts[c].start, row_parts[c].stop, 16):
                blocks = [read(q, slice(begin, begin + 16)).astype(f32) for q in range(4)]
                for at in (begin, begin + 8):
                    seg = max(e for e in range(3) if seg_row[e] <= at)
                    g, r0, r1 = segments[seg]
                    per = 8 // quarter[g]
                    v = [block[at - begin : at - begin + 8] for block in blocks]
                    cell = (at - seg_row[seg]) // 8 * per
                    if per == 1:
                        found = [jnp.concatenate(v, axis=0)]
                    else:
                        t = [pltpu.roll(e, 4, 0) for e in v]
                        found = [
                            jnp.concatenate(
                                [jnp.where(turn_low, v[0], t[1]), jnp.where(turn_low, v[2], t[3])], axis=0
                            ),
                            jnp.concatenate(
                                [jnp.where(turn_low, t[0], v[1]), jnp.where(turn_low, t[2], v[3])], axis=0
                            ),
                        ]
                    for e, value in enumerate(found):
                        if cell + e < seg_cells[seg]:
                            r, s = divmod(cell + e, halves[g])
                            yield g, r0 + r, s, value

        def gather_cells(c):
            for g, r, s, z in whole_cells(lambda q, span: zb[q, span, :], c):
                begin = starts[g] + (r * halves[g] + s) * images[g]
                hat[begin : begin + images[g], :] = z

        for n in range(2):
            act_in(n)
        gather_cells(0)
        act_in(2)
        gather_cells(1)
        tot = total(0, first)
        stat[0:8, :] = tot
        tot_first = (stat[pl.ds(k, 1), :], stat[pl.ds(4 + k, 1), :])
        def moments(total_, square):
            mean = total_ * inv_pop
            return mean, lax.rsqrt(square * inv_pop - mean * mean + epsilon)

        mean1, sc1 = moments(tot[0:4], tot[4:8])
        mean1, sc1 = (lanes_cat([v[q : q + 1] for q in range(4)]) for v in (mean1, sc1))
        gain1, shift1 = (lanes_cat([vg[q, e] for q in range(4)]) for e in range(2))

        scale1 = sc1 * gain1
        offset1 = shift1 - mean1 * scale1

        def activate(c):
            for g, r0, r1 in (segments[:2], segments[2:])[c]:
                for r in range(r0, r1):
                    for s in range(halves[g]):
                        begin = starts[g] + (r * halves[g] + s) * images[g]
                        span = slice(begin, begin + images[g])
                        v = hat[span, :] * scale1 + offset1
                        act = v * sigma(v) * lanes_cat([valid[span, :]] * 4)
                        a1[g][1 + r, 1 + s] = act.astype(bf16)

        def second_conv(parts, acc):
            value = None
            for a, b in TAPS:
                patch = jnp.concatenate(
                    [flat(a1[g][r0 + a : r1 + a, b : b + halves[g]]) for g, r0, r1 in parts], axis=0
                )
                part = mm(patch, w2[3 * a + b], 1, 0)
                value = part if value is None else value + part
            at = 0
            for g, r0, r1 in parts:
                for r in range(r0, r1):
                    begin = starts[g] + r * widths[g]
                    span = slice(begin, begin + widths[g])
                    u = value[at : at + widths[g]]
                    at += widths[g]
                    gv[span, :] = u
                    uv = u * valid[span, :]
                    acc = [acc[0] + rowsum(uv), acc[1] + rowsum(uv * u)]
            return acc

        left = lax.broadcasted_iota(jnp.int32, (1, LANES), 1) < out_rows

        def pack(g, r0, r1):
            for r in range(r0, r1):
                v = by_chan(flat(a1[g][1 + r, 1 : 1 + halves[g]]).astype(f32))
                t = [pltpu.roll(e, out_rows, 1) for e in v]
                begin = starts[g] + r * widths[g]
                span = slice(begin, begin + widths[g])
                for p in range(2):
                    cols = slice(p * LANES, (p + 1) * LANES)
                    apk[0, span, cols] = jnp.where(left, v[2 * p], t[2 * p + 1]).astype(bf16)
                    apk[1, span, cols] = jnp.where(left, t[2 * p], v[2 * p + 1]).astype(bf16)

        near = sizes[1] - sizes[1] // 6 // 16 * 16
        far = sizes[0] * 17 // 32 // 16 * 16
        pack_spans = [
            [slice(starts[1], starts[1] + near)],
            [slice(starts[1] + near, rows), slice(0, far)],
            [slice(far, sizes[0])],
        ]
        slot_p = [[net.slot() for _ in spans_] for spans_ in pack_spans]

        def pack_send(n):
            for span, slot in zip(pack_spans[n], slot_p[n]):
                net.send(apk.at[1 - ix, span], arx.at[span], slot, mate)

        activate(0)
        pack(1, 0, halves[1])
        pack(0, 0, rs)
        pack_send(0)
        acc = second_conv([(1, 0, halves[1]), (0, 0, rs - 1)], zeros(2))
        activate(1)
        pack(0, rs, halves[0])
        acc = second_conv([(0, rs - 1, halves[0])], acc)
        first = share(1, message(acc))
        pack_send(1)

        stat[0:8, :] = chan_total(2, side_first)
        means, scs = moments(stat[pl.ds(k, 1), :], stat[pl.ds(4 + k, 1), :])
        for where in (k2, k3, k1):
            net.arrived(zsr.at[where], slot_s + where, (i, where))
        for c in range(2):
            for g, r, s, z in whole_cells(lambda q, span: zsr[q, span, :], c):
                begin = starts[g] + (r * halves[g] + s) * images[g]
                zs[begin : begin + images[g], :] = (z - means) * scs

        def planes_of(quarters, g):
            count = quarter[g]
            if count % 8 == 0:
                return [
                    jnp.concatenate([v[:, count * p : count * (p + 1)] for v in quarters], axis=1)
                    for p in range(4)
                ]
            low = lax.broadcasted_iota(jnp.int32, (1, 8, 1), 1) < 4
            parts = [[v[:, 8 * h : 8 * h + 8] for v in quarters] for h in range(2)]
            turned = [[pltpu.roll(v, 4, 1) for v in side] for side in parts]
            result = []
            for p in range(4):
                v, t = parts[p // 2], turned[p // 2]
                if p % 2 == 0:
                    both = [jnp.where(low, v[0], t[1]), jnp.where(low, v[2], t[3])]
                else:
                    both = [jnp.where(low, t[0], v[1]), jnp.where(low, t[2], v[3])]
                result.append(jnp.concatenate(both, axis=1))
            return result

        def make_planes():
            for g, r, begin, count in chunks:
                quarters = [
                    zg[q, begin : begin + count, :].astype(f32).reshape(halves[g], images[g], chan_in)
                    for q in range(4)
                ]
                for p, value in enumerate(planes_of(quarters, g)):
                    zp[g][p, 1 + r, 1 : 1 + halves[g]] = value.astype(bf16)

        tot = total(1, first)
        mean2, sc2 = moments(tot[0:1], tot[1:2])
        gain2, gains = g2[...], gs[...]
        shifts = b2[...] + bs[...]
        acc = zeros(3)
        for g, r, begin, count in chunks:
            span = slice(begin, begin + count)
            ok = valid[span, :]
            hat2 = (gv[span, :] - mean2) * sc2
            hats = zs[span, :]
            v = hat2 * gain2 + hats * gains + shifts
            sig = sigma(v)
            outr[span, :] = v * sig * ok
            grad = up[span, :] * ok * (sig * (1.0 + v * (1.0 - sig)))
            up[span, :] = grad
            gv[span, :] = hat2
            acc = [acc[0] + rowsum(grad), acc[1] + rowsum(grad * hat2), acc[2] + rowsum(grad * hats)]
        first = share(2, message(acc))
        pack_send(2)
        for g, target in enumerate((oa, ob)):
            n, count = images[g], halves[g] ** 2
            for cell in range(count):
                gu[pl.ds(starts[g] + cell, n, stride=count), :] = outr[
                    starts[g] + cell * n : starts[g] + (cell + 1) * n, :
                ]
            target[...] = gu[starts[g] : starts[g] + sizes[g], :].astype(bf16)
        for begin in range(0, rows, 16):
            span = slice(begin, begin + 16)
            h = (hat[span, :] - mean1) * sc1
            hat[span, :] = h
            v = h * gain1 + shift1
            sig = sigma(v)
            mask[span, :] = sig * (1.0 + v * (1.0 - sig)) * lanes_cat([valid[span, :]] * 4)
        tot = total(2, first)
        sum_tail, sum_gain2, sum_gains = tot[0:1], tot[1:2], tot[2:3]
        k2g, ksg = gain2 * sc2, gains * scs
        db, dg2, dgs = sum_tail * inv_pop, sum_gain2 * inv_pop, sum_gains * inv_pop
        for g, r, begin, count in chunks:
            span = slice(begin, begin + count)
            value = k2g * (up[span, :] - valid[span, :] * (db + gv[span, :] * dg2))
            dz[g][1 + r, 1 : 1 + halves[g]] = value.astype(bf16).reshape(halves[g], images[g], chan_part)
        slot_d = net.slot(2)

        def dz_inner(buf, g):
            return buf[g].at[1 : 1 + halves[g], 1 : 1 + halves[g]]

        for g in range(2):
            net.send(dz_inner(dz, g), dz_inner(dzm, g), slot_d + g, mate)

        def columns(buf, piece, taps=range(9)):
            for g, r0, r1 in piece:
                for t in taps:
                    a, b = TAPS[t]
                    dd[
                        starts[g] + r0 * widths[g] : starts[g] + r1 * widths[g],
                        t * LANES : (t + 1) * LANES,
                    ] = flat(buf[g][r0 + 2 - a : r1 + 2 - a, 2 - b : 2 - b + halves[g]])

        def back_second(first, span):
            begin = pl.multiple_of(first * chan_part, LANES)
            weights = lanes_cat([w2[t, pl.ds(begin, 2 * chan_part), :] for t in range(9)])
            value = mm(dd[span, :], weights, 1, 1).astype(bf16)
            hp[first, span, :] = value[:, :chan_part]
            hp[first + 1, span, :] = value[:, chan_part:]

        slot_h = [net.slot(3) for _ in row_halves]
        def other_pair(n):
            columns(dz, back_pieces[n])
            back_second(2 * (k2 // 2), row_halves[n])
            net.send(hp.at[k3, row_halves[n]], hr1.at[1, row_halves[n]], slot_h[n] + 1, (i, k1))

        def cross_second(n):
            span = row_halves[n]
            net.arrived(hr1.at[1, span], slot_h[n] + 1, (i, k1))
            hs[span, :] = (hp[k2, span, :].astype(f32) + hr1[1, span, :].astype(f32)).astype(bf16)
            net.send(hs.at[span], hr2.at[span], slot_h[n] + 2, (i, k2))

        def pair_sums(first):
            acc = [jnp.zeros((8, 2 * chan_part), f32)] * 2
            cols = pl.ds(pl.multiple_of(first * chan_part, 2 * LANES), 2 * chan_part)
            for begin in range(0, rows, 16):
                span = slice(begin, begin + 16)
                part = lanes_cat([hp[first + e, span, :] for e in range(2)]).astype(f32) * mask[span, cols]
                acc = [acc[0] + rowsum(part), acc[1] + rowsum(part * hat[span, cols])]
            acc = [jnp.sum(v, axis=0, keepdims=True) for v in acc]
            for e in range(2):
                for n in range(2):
                    stat[pl.ds(4 * n + first + e, 1), :] = acc[n][:, e * LANES : (e + 1) * LANES]

        other_pair(0)
        other_pair(1)
        cross_second(0)
        other_pair(2)
        cross_second(1)
        back_second(2 * (k // 2), slice(0, rows))
        pair_sums(2 * (k2 // 2))
        cross_second(2)
        for span, slot in zip(row_halves, slot_h):
            net.send(hp.at[k1, span], hr1.at[0, span], slot, (i, k1))
        pair_sums(2 * (k // 2))
        first = share(3, stat[0:8, :])

        sum2 = Reduce(net, i, k, None, (None, p22, p23, p24, p25), cols2, p26)
        gacc[...] = mm(apk[ix], dd[...], 0, 0)
        first = chan_share(1, total(3, first))
        def split_cells(read, target, c):
            for begin in range(row_parts[c].start, row_parts[c].stop, 16):
                tiles = []
                for at in (begin, begin + 8):
                    seg = max(e for e in range(3) if seg_row[e] <= at)
                    g, r0, r1 = segments[seg]
                    per = 8 // quarter[g]
                    cell = (at - seg_row[seg]) // 8 * per
                    blocks = []
                    for e in range(per):
                        if cell + e < seg_cells[seg]:
                            r, s = divmod(cell + e, halves[g])
                            blocks.append(read(g, r0 + r, s))
                        else:
                            blocks.append(jnp.zeros((images[g], chan_part), f32))
                    if per == 1:
                        tiles.append([blocks[0][8 * q : 8 * q + 8] for q in range(4)])
                    else:
                        found = []
                        for h in range(2):
                            v = [block[8 * h : 8 * h + 8] for block in blocks]
                            t = [pltpu.roll(e, 4, 0) for e in v]
                            found += [jnp.where(turn_low, v[0], t[1]), jnp.where(turn_low, t[0], v[1])]
                        tiles.append(found)
                for q in range(4):
                    both = jnp.concatenate([tiles[0][q], tiles[1][q]], axis=0)
                    target[q, begin : begin + 16, :] = both.astype(bf16)

        def cell_span(g, r, s):
            begin = starts[g] + (r * halves[g] + s) * images[g]
            return slice(begin, begin + images[g])

        def short_cell(g, r, s):
            span = cell_span(g, r, s)
            value = ksg * (up[span, :] - valid[span, :] * (db + zs[span, :] * dgs))
            dzsr[span, :] = value.astype(bf16)
            return value

        slot_q = [net.slot(4) for _ in range(3)]

        def quarters_out(source, target, span, slot):
            for where in (k2, k3, k1):
                net.send(source.at[where, span], target.at[k, span], slot + k, (i, where))
            target[k, span, :] = source[k, span, :]

        def quarters_in(target, span, slot):
            for where in (k1, k2, k3):
                net.arrived(target.at[where, span], slot + where, (i, where))

        for c in range(2):
            split_cells(short_cell, sq, c)
        quarters_out(sq, si, slice(0, q_rows), slot_q[2])
        for n in range(2):
            slab_on(n)
        for spans_, slots_ in zip(pack_spans, slot_p):
            for span, slot in zip(spans_, slots_):
                net.arrived(arx.at[span], slot, mate)
        for g in range(2):
            net.arrived(dz_inner(dzm, g), slot_d + g, mate)
        for w, cols in enumerate(cols2):
            for piece in back_pieces:
                columns(dzm, piece, range(cols.start // LANES, cols.stop // LANES))
            value = (gacc[:, cols] + mm(arx[...], dd[:, cols], 0, 0)).astype(bf16)
            (sum2.spread_of, sum2.second_of)[w](w, value)
        tot = chan_total(1, first)
        stat[0:8, :] = tot
        sum_head, sum_gain1 = stat[pl.ds(k, 1), :], stat[pl.ds(4 + k, 1), :]

        def close_second():
            for w, cols in enumerate(cols2):
                value = (sum2.spread_last, sum2.last)[w](w)
                for t in range(cols.start // LANES, cols.stop // LANES):
                    gw2[t] = value[:, t * LANES - cols.start : (t + 1) * LANES - cols.start]

        own = pl.ds(pl.multiple_of(k * chan_part, LANES), chan_part)
        mean1, sc1 = moments(tot_first[0], tot_first[1])
        k1g = vg[k, 0] * sc1
        db, dg1 = sum_head * inv_pop, sum_gain1 * inv_pop
        for span, slot in zip(row_halves, slot_h):
            net.arrived(hr1.at[0, span], slot, (i, k1))
            net.arrived(hr2.at[span], slot + 2, (i, k2))

        def first_cell(g, r, s):
            span = cell_span(g, r, s)
            grad = hp[k, span, :].astype(f32) + hr1[0, span, :].astype(f32) + hr2[span, :].astype(f32)
            grad = grad * mask[span, own]
            value = k1g * (grad - valid[span, :] * (db + hat[span, own] * dg1))
            d1[g][r, s] = value.astype(bf16)
            return value

        for c in (1, 0):
            split_cells(first_cell, dq, c)
            quarters_out(dq, di, row_parts[c], slot_q[c])

        def back_patch(pieces, p):
            parts = []
            for g, r0, r1 in pieces:
                width = halves[g] * images[g]
                taps = [
                    flat(d1[g][r0 + (a == 0) : r1 + (a == 0), (b == 0) : (b == 0) + halves[g]])
                    for a, b in PLANE_TAPS[p]
                ]
                if p == 0:
                    taps.append(dzsr[starts[g] + r0 * width : starts[g] + r1 * width, :])
                parts.append(lanes_cat(taps))
            return jnp.concatenate(parts, axis=0) if len(parts) > 1 else parts[0]

        slot_o = [net.slot(n_dp) for _ in out_lanes]

        def back_taps(c):
            part = row_parts[c]
            quarters_in(di, part, slot_q[c])
            grads = lanes_cat([di[q, part, :] for q in range(4)])
            weights = lanes_cat([w1g[q].reshape(9 * chan_in, chan_part) for q in range(4)])
            value = mm(grads, weights, 1, 1)
            taps = [value[:, t * chan_in : (t + 1) * chan_in] for t in range(9)]
            side = lanes_cat([si[q, part, :] for q in range(4)])
            taps[4] = taps[4] + mm(side, lanes_cat([wsg[q] for q in range(4)]), 1, 1)
            return jnp.concatenate([tap.astype(bf16) for tap in taps], axis=0)

        def out_send(n, value):
            cols = out_lanes[n]
            gt[:, :, cols] = value.astype(bf16).reshape(n_dp, in_local, value.shape[1])
            for j in peers:
                net.send(gt.at[j, :, cols], gr.at[i, :, cols], slot_o[n] + i, (j, k))

        sum1 = Reduce(net, i, k, wg1, (p11, p12, p13, p14, p15), cols1)

        def weight_first(w):
            cols = cols1[w]
            blocks = []
            for p in ((3,), (0, 1, 2))[w]:
                value = 0.0
                for g, r0, r1 in ((0, 0, halves[0]), (1, 0, halves[1])):
                    cell = flat(zp[g][p, 1 : 1 + halves[g], 1 : 1 + halves[g]])
                    value = value + mm(cell, back_patch([(g, r0, r1)], p), 0, 0)
                blocks.append(value.astype(bf16))
            wg1[:, :, :, :, cols] = lanes_cat(blocks).reshape(2, 2, 2, in_local, cols.stop - cols.start)
            sum1.first(w)

        for n in range(2):
            slab_in(n)
        make_planes()
        weight_first(0)
        weight_first(1)
        quarters_in(si, slice(0, q_rows), slot_q[2])
        late = back_taps(1)
        edge = cut_lane - patch_win[1].start
        out_send(0, mm(late, pm1[:, edge:], 0, 0))
        early_ = back_taps(0)
        out_send(1, mm(early_, pm0[:, :low_lane], 0, 0))
        rest = mm(early_, pm0[:, low_lane:], 0, 0)
        shared = mm(late, pm1[:, low_lane - patch_win[1].start : edge], 0, 0)
        sum2.third(1)
        sum1.second(0)
        sum1.second(1)
        out_send(2, rest + shared)
        sum1.third(0)
        sum1.third(1)
        gr[i] = gt[i]
        close_second()
        for w, cols in enumerate(cols1):
            value = sum1.last(w)
            for t, tap in enumerate(TAPS):
                place = ORDER.index(tap)
                place = (place + (place > 0)) * LANES
                if cols.start <= place < cols.stop:
                    gw1[t] = value[:, place - cols.start : place - cols.start + LANES]
            if cols.start <= LANES < cols.stop:
                gws[...] = value[:, LANES - cols.start : 2 * LANES - cols.start]
        vecs[...] = message([sum_gain1, sum_head, sum_gain2, sum_tail, sum_gains])
        for c, cols in enumerate(out_lanes):
            for j in peers:
                net.arrived(gr.at[j, :, cols], slot_o[c] + j, (j, k))
        net.drain()

    V = pltpu.VMEM
    pads = [(h + 2, h + 2, n, chan_part) for h, n in zip(halves, images)]
    half_pads = [(h + 1, h + 1, n) for h, n in zip(halves, images)]

    def ladder(count, width):
        return [
            V((2, 2, 2, count, width), bf16), V((2, 2, count, width), bf16), V((2, 2, count, width), bf16),
            V((2, count, width), bf16), V((2, count, width), bf16), V((count, width), bf16),
        ]

    inputs = [
        V((in_local, n_dp * 4 * qlanes[0]), bf16), V((in_local, n_dp * 4 * qlanes[1]), bf16),
        V((4, images[0]), jnp.int32), V((4, images[1]), jnp.int32),
        V((4, 9, chan_in, chan_part), bf16), V((9, chan_full, chan_part), bf16),
        V((4, chan_in, chan_part), bf16), V((4, 2, 1, chan_part), f32),
    ] + [V((1, chan_part), f32)] * 4 + [
        V((sizes[0], chan_part), bf16), V((sizes[1], chan_part), bf16),
    ] + [V(m.shape, bf16) for m in patch_ms] + [V((rows, slab_lanes), bf16)]
    scratch = inputs + [
        V((n_dp * in_local, slab_lanes), bf16),
        V((n_dp, in_local, slab_lanes), bf16),
        V((n_dp, in_local, slab_lanes), bf16),
        V((4, q_rows, chan_full), bf16),
        V((4, q_rows, chan_part), bf16),
        V((4, q_rows, chan_part), bf16),
        V((4, rows, chan_in), bf16),
        V((4,) + half_pads[0] + (chan_in,), bf16),
        V((4,) + half_pads[1] + (chan_in,), bf16),
        V((rows, LANES), f32),
        V((q_rows, LANES), f32),
        V((rows, chan_full), f32),
        V((rows, chan_full), f32),
        V((rows, chan_part), f32),
        V(pads[0][:3] + (chan_full,), bf16),
        V(pads[1][:3] + (chan_full,), bf16),
        V((3, 4, 16, LANES), f32),
        V((6, n_dp, 16, LANES), f32),
        V((16, LANES), f32),
        V((rows, chan_part), f32),
        V((rows, chan_part), f32),
        V((rows, chan_part), f32),
        V(pads[0], bf16),
        V(pads[1], bf16),
        V(pads[0], bf16),
        V(pads[1], bf16),
        V((2, rows, chan_full // 2), bf16),
        V((rows, chan_full // 2), bf16),
        V((chan_full // 2, 9 * chan_part), f32),
        V((rows, chan_part), bf16),
        V((rows, 9 * chan_part), bf16),
        V((4, rows, chan_part), bf16),
        V((2, rows, chan_part), bf16),
        V((rows, chan_part), bf16),
        V((rows, chan_part), bf16),
        V((rows, chan_part), f32),
        V(half_pads[0] + (chan_part,), bf16),
        V(half_pads[1] + (chan_part,), bf16),
    ]
    scratch += ladder(out_rows, 9 * LANES)[2:]
    scratch += [V((n_dp // 2, out_rows, cols2[0].stop), bf16)] + ladder(in_local, 10 * LANES)
    scratch += [
        V((4, q_rows, chan_part), bf16),
        V((4, q_rows, chan_part), bf16),
        V((4, q_rows, chan_part), bf16),
        V((4, q_rows, chan_part), bf16),
        V((n_dp, in_local, slab_lanes), bf16),
        pltpu.SemaphoreType.DMA((20,)),
        pltpu.SemaphoreType.DMA((192,)),
        pltpu.SemaphoreType.DMA((192,)),
    ]
    mid_outs = [
        V((sizes[0], chan_part), bf16),
        V((sizes[1], chan_part), bf16),
        V((n_dp, in_local, slab_lanes), bf16),
        V((9, in_local, LANES), f32),
        V((in_local, LANES), f32),
        V((9, out_rows, LANES), f32),
        V((8, LANES), f32),
        V((n_dp * in_local, n_dp * in_local), bf16),
    ]
    vmem = pl.BlockSpec(memory_space=pltpu.VMEM)
    hbm = pl.BlockSpec(memory_space=pl.ANY)
    main = pl.pallas_call(
        kernel,
        out_shape=mid_outs,
        in_specs=[hbm] * 19,
        out_specs=[vmem] * len(mid_outs),
        scratch_shapes=scratch,
        compiler_params=pltpu.CompilerParams(
            collective_id=1, has_side_effects=True, vmem_limit_bytes=58 * 2**20
        ),
        name="block",
    )

    def closing(oa, ob, gr, gw1, gws, gw2, vecs, turn,
                fa, fb, ia, ib, f1, f2, fs, c1, h1, c2, h2, cs, hs, sems):
        outs = [
            pltpu.make_async_copy(source, target, sems.at[index])
            for index, (source, target) in enumerate(
                ((gw2, f2), (gw1, f1), (oa, fa), (ob, fb), (gws, fs))
            )
        ]
        for out in outs:
            out.start()
        moved = mm(turn[...], gr[...].reshape(n_dp * in_local, slab_lanes), 1, 0)
        natural = regroup(moved, back_runs)
        ia[...] = natural[:, : qlanes[0]].reshape(in_local, n_dp, qlanes[0]).astype(bf16)
        tail = natural[:, qlanes[0] : qlanes[0] + qlanes[1]]
        ib[...] = tail.reshape(in_local, n_dp, qlanes[1]).astype(bf16)
        for ref, row in ((c1, 0), (h1, 1), (c2, 2), (h2, 3), (cs, 4), (hs, 3)):
            ref[...] = vecs[row : row + 1, :]
        for out in outs:
            out.wait()

    last = pl.pallas_call(
        closing,
        out_shape=[
            jax.ShapeDtypeStruct((sizes[0], chan_part), bf16),
            jax.ShapeDtypeStruct((sizes[1], chan_part), bf16),
            jax.ShapeDtypeStruct((in_local, n_dp, qlanes[0]), bf16),
            jax.ShapeDtypeStruct((in_local, n_dp, qlanes[1]), bf16),
            jax.ShapeDtypeStruct((9, in_local, LANES), f32),
            jax.ShapeDtypeStruct((9, out_rows, LANES), f32),
            jax.ShapeDtypeStruct((in_local, LANES), f32),
        ]
        + [jax.ShapeDtypeStruct((1, LANES), f32)] * 6,
        in_specs=[vmem] * 8,
        out_specs=[hbm, hbm, vmem, vmem, hbm, hbm, hbm] + [vmem] * 6,
        scratch_shapes=[pltpu.SemaphoreType.DMA((5,))],
        compiler_params=pltpu.CompilerParams(vmem_limit_bytes=32 * 2**20),
        name="closing",
    )
    total_rows = n_dp * in_local
    turn = np.zeros((total_rows, total_rows), np.float32)
    for c in range(in_local):
        for j in range(n_dp):
            turn[c * n_dp + j, j * in_local + c] = 1.0
    return (main, last) + tuple(m.astype(jnp.bfloat16) for m in (*patch_ms, cells_m, turn))


STOP = 99


def fused_body(
    input_a, input_b, boxes_a, boxes_b, weight_first, weight_second, weight_short,
    gain_first, shift_first, gain_second, shift_second, gain_short, shift_short,
    upstream_a, upstream_b,
):
    n_dp = lax.axis_size("dp")
    chan_part = weight_first.shape[2]
    in_local = input_a.shape[0]
    main, last, *matrices = make_fused(
        n_dp, in_local, (boxes_a.shape[0], boxes_b.shape[0]), (SA, SB),
        weight_first.shape[1], chan_part, STOP,
    )
    vectors = [
        v.reshape(1, chan_part)
        for v in (gain_first, shift_first, gain_second, shift_second, gain_short, shift_short)
    ]
    mid = main(
        input_a, input_b, boxes_a.T, boxes_b.T, weight_first, weight_second, weight_short,
        *vectors, upstream_a.T, upstream_b.T, *matrices,
    )
    res = last(*mid)
    return (
        res[0].T, res[1].T,
        res[2].reshape(in_local, n_dp, 1, -1), res[3].reshape(in_local, n_dp, 1, -1),
        res[4], res[5], res[6],
    ) + tuple(v.reshape(chan_part) for v in res[7:])


def choose_body(mesh):
    return fused_body if mesh.shape["dp"] == 8 and mesh.shape["chan"] == 4 else plain_body


def solution(mesh):
    placed = (
        P("dp", None),
        P("dp", None),
        P("dp", None),
        P("dp", None),
        P(None, None, "chan"),
        P(None, None, "chan"),
        P(None, "chan"),
        P("chan"),
        P("chan"),
        P("chan"),
        P("chan"),
        P("chan"),
        P("chan"),
        P("chan", "dp"),
        P("chan", "dp"),
    )
    return jax.shard_map(
        choose_body(mesh),
        mesh=mesh,
        in_specs=placed,
        out_specs=(
            P("chan", "dp"),
            P("chan", "dp"),
            P("dp", None, "chan", None),
            P("dp", None, "chan", None),
            P(None, "dp", "chan"),
            P(None, "dp", "chan"),
            P("dp", "chan"),
            P("chan"),
            P("chan"),
            P("chan"),
            P("chan"),
            P("chan"),
            P("chan"),
        ),
        check_vma=False,
    )
```

```python
import jax
import jax.numpy as jnp
from jax import lax
import numpy as np
from jax.experimental import pallas as pl
from jax.experimental.pallas import tpu as pltpu
from jax.sharding import PartitionSpec as P

SA = 14
SB = 6


epsilon = 1e-05


def box_mask(box_rows, extent):
    positions = jnp.arange(extent, dtype=jnp.int32)[None, :]
    row_inside = (positions >= box_rows[:, 0:1]) & (positions < box_rows[:, 0:1] + box_rows[:, 2:3])
    col_inside = (positions >= box_rows[:, 1:2]) & (positions < box_rows[:, 1:2] + box_rows[:, 3:4])
    return (row_inside[:, :, None] & col_inside[:, None, :]).astype(jnp.float32)


def taps_strided(feature, image_count, extent):
    channels = feature.shape[0]
    output_side = extent // 2
    padded = jnp.pad(
        feature.reshape(channels, image_count, extent, extent), ((0, 0), (0, 0), (1, 1), (1, 1))
    )
    pieces = [
        padded[:, :, tap_row : tap_row + extent : 2, tap_col : tap_col + extent : 2]
        for tap_row in range(3)
        for tap_col in range(3)
    ]
    return jnp.stack(pieces, axis=0).reshape(9 * channels, image_count * output_side * output_side)


def taps_plain(feature, image_count, extent):
    channels = feature.shape[0]
    padded = jnp.pad(
        feature.reshape(channels, image_count, extent, extent), ((0, 0), (0, 0), (1, 1), (1, 1))
    )
    pieces = [
        padded[:, :, tap_row : tap_row + extent, tap_col : tap_col + extent]
        for tap_row in range(3)
        for tap_col in range(3)
    ]
    return jnp.stack(pieces, axis=0).reshape(9 * channels, image_count * extent * extent)


def untaps_plain(columns, channels, image_count, extent):
    pieces = columns.reshape(9, channels, image_count, extent, extent)
    running = jnp.zeros((channels, image_count, extent + 2, extent + 2), jnp.float32)
    for tap_row in range(3):
        for tap_col in range(3):
            running = running + jnp.pad(
                pieces[3 * tap_row + tap_col],
                ((0, 0), (0, 0), (tap_row, 2 - tap_row), (tap_col, 2 - tap_col)),
            )
    return running[:, :, 1:-1, 1:-1].reshape(channels, image_count * extent * extent)


def untaps_strided(columns, shortcut, channels, image_count, extent):
    output_side = extent // 2
    pieces = columns.reshape(9, channels, image_count, output_side, output_side)
    parity_sums = {}
    for tap_row in range(3):
        for tap_col in range(3):
            block_row = tap_row // 2
            block_col = tap_col // 2
            placed = jnp.pad(
                pieces[3 * tap_row + tap_col],
                ((0, 0), (0, 0), (block_row, 1 - block_row), (block_col, 1 - block_col)),
            )
            parity = (tap_row % 2, tap_col % 2)
            parity_sums[parity] = (
                placed if parity not in parity_sums else parity_sums[parity] + placed
            )
    direct = jnp.pad(
        shortcut.reshape(channels, image_count, output_side, output_side),
        ((0, 0), (0, 0), (0, 1), (0, 1)),
    )
    parity_sums[1, 1] = parity_sums[1, 1] + direct
    rows_even = jnp.stack([parity_sums[0, 0], parity_sums[0, 1]], axis=-1)
    rows_odd = jnp.stack([parity_sums[1, 0], parity_sums[1, 1]], axis=-1)
    padded = jnp.stack([rows_even, rows_odd], axis=3).reshape(
        channels, image_count, extent + 2, extent + 2
    )
    return padded[:, :, 1:-1, 1:-1].reshape(channels, image_count * extent * extent)


def contract_first(weights, columns):
    return lax.dot_general(
        weights, columns, (((0,), (0,)), ((), ())), preferred_element_type=jnp.float32
    )


def weight_product(columns, gradient):
    return lax.dot_general(
        columns, gradient, (((1,), (1,)), ((), ())), preferred_element_type=jnp.float32
    )


def swish_slope(values):
    logistic = jax.nn.sigmoid(values)
    return logistic * (1.0 + values * (1.0 - logistic))


def moments(values, valid_list):
    running = 0.0
    squares = 0.0
    for tensor, valid in zip(values, valid_list):
        widened = tensor.astype(jnp.float32)
        running = running + jnp.sum(widened * valid, axis=1)
        squares = squares + jnp.sum(widened * widened * valid, axis=1)
    return (running, squares)


def standardize(values, running, squares, population):
    mean_value = running / population
    variance = squares / population - mean_value * mean_value
    scaling = lax.rsqrt(variance + epsilon)
    return (
        [
            (tensor.astype(jnp.float32) - mean_value[:, None]) * scaling[:, None]
            for tensor in values
        ],
        scaling,
    )


def norm_back(gradient, normed, valid, scaling, gain_values, shift_sum, gain_sum, population):
    return (gain_values * scaling)[:, None] * (
        gradient - valid * (shift_sum[:, None] + normed * gain_sum[:, None]) / population
    )


def plain_body(
    input_a,
    input_b,
    boxes_a,
    boxes_b,
    weight_first,
    weight_second,
    weight_short,
    gain_first,
    shift_first,
    gain_second,
    shift_second,
    gain_short,
    shift_short,
    upstream_a,
    upstream_b,
):
    image_groups = lax.axis_size("dp")
    in_local = input_a.shape[0]
    chan_in = weight_first.shape[1]
    chan_part = weight_first.shape[2]
    chan_full = weight_second.shape[1]
    image_counts = (boxes_a.shape[0], boxes_b.shape[0])
    extents = (SA, SB)
    whole_a, whole_b = (
        lax.all_to_all(
            input_a.reshape(in_local, image_groups, -1),
            "dp",
            split_axis=1,
            concat_axis=0,
            tiled=True,
        ),
        lax.all_to_all(
            input_b.reshape(in_local, image_groups, -1),
            "dp",
            split_axis=1,
            concat_axis=0,
            tiled=True,
        ),
    )
    features = (whole_a.reshape(chan_in, -1), whole_b.reshape(chan_in, -1))
    valid_list = (
        box_mask(boxes_a, SA // 2).reshape(1, -1),
        box_mask(boxes_b, SB // 2).reshape(1, -1),
    )
    first_mat = weight_first.reshape(9 * chan_in, chan_part)
    second_mat = weight_second.reshape(9 * chan_full, chan_part)
    first_cols = []
    sampled = []
    first_z = []
    short_z = []
    for feature, image_count, extent in zip(features, image_counts, extents):
        columns = taps_strided(feature, image_count, extent)
        picked = feature.reshape(chan_in, image_count, extent, extent)[:, :, ::2, ::2].reshape(
            chan_in, -1
        )
        first_cols.append(columns)
        sampled.append(picked)
        first_z.append(contract_first(first_mat, columns).astype(jnp.bfloat16))
        short_z.append(contract_first(weight_short, picked).astype(jnp.bfloat16))
    sum_first, square_first = moments(first_z, valid_list)
    sum_short, square_short = moments(short_z, valid_list)
    population = jnp.sum(valid_list[0]) + jnp.sum(valid_list[1])
    sum_first, square_first, sum_short, square_short, population = lax.psum(
        (sum_first, square_first, sum_short, square_short, population), "dp"
    )
    normed_first, scaling_first = standardize(first_z, sum_first, square_first, population)
    normed_short, scaling_short = standardize(short_z, sum_short, square_short, population)
    before_first = [normed * gain_first[:, None] + shift_first[:, None] for normed in normed_first]
    outgoing_a = (jax.nn.silu(before_first[0]) * valid_list[0]).astype(jnp.bfloat16)
    outgoing_b = (jax.nn.silu(before_first[1]) * valid_list[1]).astype(jnp.bfloat16)
    gathered_a, gathered_b = (
        lax.all_gather(outgoing_a, "chan", axis=0, tiled=True),
        lax.all_gather(outgoing_b, "chan", axis=0, tiled=True),
    )
    second_cols = []
    second_z = []
    for gathered, image_count, extent in zip((gathered_a, gathered_b), image_counts, extents):
        columns = taps_plain(gathered, image_count, extent // 2)
        second_cols.append(columns)
        second_z.append(contract_first(second_mat, columns).astype(jnp.bfloat16))
    sum_second, square_second = moments(second_z, valid_list)
    sum_second, square_second = lax.psum((sum_second, square_second), "dp")
    normed_second, scaling_second = standardize(second_z, sum_second, square_second, population)
    summed_pre = [
        main_part * gain_second[:, None]
        + shift_second[:, None]
        + side_part * gain_short[:, None]
        + shift_short[:, None]
        for main_part, side_part in zip(normed_second, normed_short)
    ]
    outputs = [
        (jax.nn.silu(tensor) * valid).astype(jnp.bfloat16)
        for tensor, valid in zip(summed_pre, valid_list)
    ]
    tail_grads = [
        upstream.astype(jnp.float32) * valid * swish_slope(tensor)
        for upstream, valid, tensor in zip((upstream_a, upstream_b), valid_list, summed_pre)
    ]
    shift_tail = sum((jnp.sum(gradient, axis=1) for gradient in tail_grads))
    gain_tail = sum(
        (jnp.sum(gradient * normed, axis=1) for gradient, normed in zip(tail_grads, normed_second))
    )
    gain_side = sum(
        (jnp.sum(gradient * normed, axis=1) for gradient, normed in zip(tail_grads, normed_short))
    )
    shift_tail, gain_tail, gain_side = lax.psum((shift_tail, gain_tail, gain_side), "dp")
    grad_second_local = 0.0
    partial_hidden = []
    short_dz = []
    for index_group in range(2):
        valid = valid_list[index_group]
        dz_second = norm_back(
            tail_grads[index_group],
            normed_second[index_group],
            valid,
            scaling_second,
            gain_second,
            shift_tail,
            gain_tail,
            population,
        ).astype(jnp.bfloat16)
        dz_short = norm_back(
            tail_grads[index_group],
            normed_short[index_group],
            valid,
            scaling_short,
            gain_short,
            shift_tail,
            gain_side,
            population,
        ).astype(jnp.bfloat16)
        short_dz.append(dz_short)
        grad_second_local = grad_second_local + weight_product(second_cols[index_group], dz_second)
        back_cols = jnp.dot(second_mat, dz_second, preferred_element_type=jnp.float32)
        partial_hidden.append(
            untaps_plain(back_cols, chan_full, image_counts[index_group], extents[index_group] // 2)
        )
    hidden_a, hidden_b = (
        lax.psum_scatter(
            partial_hidden[0].astype(jnp.bfloat16), "chan", scatter_dimension=0, tiled=True
        ).astype(jnp.float32),
        lax.psum_scatter(
            partial_hidden[1].astype(jnp.bfloat16), "chan", scatter_dimension=0, tiled=True
        ).astype(jnp.float32),
    )
    head_grads = [
        hidden * valid * swish_slope(tensor)
        for hidden, valid, tensor in zip((hidden_a, hidden_b), valid_list, before_first)
    ]
    shift_head = sum((jnp.sum(gradient, axis=1) for gradient in head_grads))
    gain_head = sum(
        (jnp.sum(gradient * normed, axis=1) for gradient, normed in zip(head_grads, normed_first))
    )
    shift_head, gain_head = lax.psum((shift_head, gain_head), "dp")
    grad_first_local = 0.0
    grad_short_local = 0.0
    partial_inputs = []
    for index_group in range(2):
        valid = valid_list[index_group]
        dz_first = norm_back(
            head_grads[index_group],
            normed_first[index_group],
            valid,
            scaling_first,
            gain_first,
            shift_head,
            gain_head,
            population,
        ).astype(jnp.bfloat16)
        grad_first_local = grad_first_local + weight_product(first_cols[index_group], dz_first)
        grad_short_local = grad_short_local + weight_product(
            sampled[index_group], short_dz[index_group]
        )
        back_cols = jnp.dot(first_mat, dz_first, preferred_element_type=jnp.float32)
        back_short = jnp.dot(
            weight_short, short_dz[index_group], preferred_element_type=jnp.float32
        )
        flat_input = untaps_strided(
            back_cols, back_short, chan_in, image_counts[index_group], extents[index_group]
        )
        partial_inputs.append(flat_input.reshape(chan_in, 1, lax.axis_size("chan"), -1))
    arrived_a, arrived_b = (
        lax.all_to_all(
            partial_inputs[0].astype(jnp.bfloat16), "dp", split_axis=0, concat_axis=1, tiled=True
        ).astype(jnp.float32),
        lax.all_to_all(
            partial_inputs[1].astype(jnp.bfloat16), "dp", split_axis=0, concat_axis=1, tiled=True
        ).astype(jnp.float32),
    )
    summed_a, summed_b = (
        lax.psum_scatter(
            arrived_a.astype(jnp.bfloat16), "chan", scatter_dimension=2, tiled=True
        ).astype(jnp.float32),
        lax.psum_scatter(
            arrived_b.astype(jnp.bfloat16), "chan", scatter_dimension=2, tiled=True
        ).astype(jnp.float32),
    )
    grad_input_a = summed_a.astype(jnp.bfloat16)
    grad_input_b = summed_b.astype(jnp.bfloat16)
    grad_first_local = grad_first_local.reshape(9, chan_in, chan_part)
    grad_second_local = grad_second_local.reshape(9, chan_full, chan_part)
    total_first, total_second, total_short = lax.psum(
        (grad_first_local, grad_second_local, grad_short_local), "dp"
    )
    position = lax.axis_index("dp")
    rows_first = chan_in // image_groups
    rows_second = chan_full // image_groups
    grad_first = lax.dynamic_slice_in_dim(total_first, position * rows_first, rows_first, 1)
    grad_second = lax.dynamic_slice_in_dim(total_second, position * rows_second, rows_second, 1)
    grad_short = lax.dynamic_slice_in_dim(total_short, position * rows_first, rows_first, 0)
    return (
        outputs[0],
        outputs[1],
        grad_input_a,
        grad_input_b,
        grad_first,
        grad_second,
        grad_short,
        gain_head,
        shift_head,
        gain_tail,
        shift_tail,
        gain_side,
        shift_tail,
    )


MESH = pl.DeviceIdType.MESH
TAPS = tuple((a, b) for a in range(3) for b in range(3))
PLANE_TAPS = (
    ((1, 1),),
    ((1, 0), (1, 2)),
    ((0, 1), (2, 1)),
    ((0, 0), (0, 2), (2, 0), (2, 2)),
)
ORDER = [tap for taps in PLANE_TAPS for tap in taps]
LANES = 128


class Links:
    def __init__(self, send_sems, recv_sems):
        self.send_sems, self.recv_sems = send_sems, recv_sems
        self.sends = self.slots = self.started = 0
        self.open, self.free = [], []

    def slot(self, count=1):
        first = self.slots
        self.slots += count
        return first

    def send(self, source, target, slot, where):
        if not self.free:
            self.free.append(self.sends)
            self.sends += 1
        index = self.free.pop(0)
        copy = pltpu.make_async_remote_copy(
            source, target, self.send_sems.at[index], self.recv_sems.at[slot],
            device_id=where, device_id_type=MESH,
        )
        copy.start()
        self.open.append((copy, index))
        self.started += 1

    def mark(self):
        return self.started

    def settle(self, last):
        count = last - self.started + len(self.open)
        for copy, index in self.open[:count]:
            copy.wait_send()
            self.free.append(index)
        self.open = self.open[count:]

    def arrived(self, target, slot, where):
        pltpu.make_async_remote_copy(
            target, target, self.send_sems.at[0], self.recv_sems.at[slot],
            device_id=where, device_id_type=MESH,
        ).wait_recv()

    def drain(self):
        self.settle(self.mark())


def mm(a, b, ca, cb):
    return lax.dot_general(a, b, (((ca,), (cb,)), ((), ())), preferred_element_type=jnp.float32)


def lanes_cat(parts):
    return jnp.concatenate(parts, axis=1) if len(parts) > 1 else parts[0]


def quarter_matrices(images, sides, segments, seg_lane, seg_row, q_rows, lanes):
    def lane(g, image, row, col):
        for (seg_g, r0, r1), first in zip(segments, seg_lane):
            if seg_g == g and 2 * r0 <= row < 2 * r1:
                return first + (image * 2 * (r1 - r0) + row - 2 * r0) * sides[g] + col

    taps = np.zeros((9, q_rows, lanes), np.float32)
    for (g, r0, r1), first in zip(segments, seg_row):
        half = sides[g] // 2
        for r in range(r0, r1):
            for s in range(half):
                for image in range(images[g]):
                    target = first + ((r - r0) * half + s) * images[g] + image
                    for t, (a, b) in enumerate(TAPS):
                        row, col = 2 * r + a - 1, 2 * s + b - 1
                        if row >= 0 and col >= 0:
                            taps[t, target, lane(g, image, row, col)] = 1.0
    sizes = [n * side * side for n, side in zip(images, sides)]
    cells = np.zeros((sum(sizes), lanes), np.float32)
    for g, (n, side) in enumerate(zip(images, sides)):
        for image in range(n):
            for row in range(side):
                for col in range(side):
                    cell = (row // 2) * (side // 2) + col // 2
                    target = g * sizes[0] + (cell * 4 + 2 * (row % 2) + col % 2) * n + image
                    cells[target, lane(g, image, row, col)] = 1.0
    return taps, cells


def regroup(value, runs):
    return jnp.concatenate([value[:, a:b] for a, b in runs], axis=1)


def fold(value):
    half = value.shape[1] // 2
    left = lax.broadcasted_iota(jnp.int32, (1, 1, LANES), 2) < LANES // 2
    return jnp.where(left, value[:, :half], pltpu.roll(value[:, half:], LANES // 2, 2))


def unfold(value):
    return jnp.concatenate([value, pltpu.roll(value, LANES // 2, 2)], axis=1)


def sigma(v):
    return 0.5 * jnp.tanh(0.5 * v) + 0.5


class Reduce:
    def __init__(self, net, i, k, part, bufs, windows, b4=None):
        self.b4 = b4
        self.net, self.part, self.windows = net, part, windows
        self.b1, self.s1, self.b2, self.s2, self.b3 = bufs
        self.ix, self.pz, self.hz = i % 2, (i // 2) % 2, i // 4
        self.peers = (
            (i + 1 - 2 * self.ix, k),
            (i + 2 - 4 * self.pz, k),
            (i + 4 - 8 * self.hz, k),
        )
        self.slots = [net.slot(3) for _ in windows]

    def first(self, w):
        cols = self.windows[w]
        self.net.send(
            self.part.at[:, :, 1 - self.ix, :, cols], self.b1.at[:, :, :, cols],
            self.slots[w], self.peers[0],
        )

    def second(self, w):
        cols = self.windows[w]
        self.net.arrived(self.b1.at[:, :, :, cols], self.slots[w], self.peers[0])
        for h in range(2):
            for p in range(2):
                value = self.part[h, p, self.ix, :, cols].astype(jnp.float32)
                value = value + self.b1[h, p, :, cols].astype(jnp.float32)
                self.s1[h, p, :, cols] = value.astype(jnp.bfloat16)
        self.net.send(
            self.s1.at[:, 1 - self.pz, :, cols], self.b2.at[:, :, cols],
            self.slots[w] + 1, self.peers[1],
        )

    def second_of(self, w, value):
        cols = self.windows[w]
        self.s1[:, :, :, cols] = value.reshape(2, 2, -1, value.shape[1])
        self.net.send(
            self.s1.at[:, 1 - self.pz, :, cols], self.b2.at[:, :, cols],
            self.slots[w] + 1, self.peers[1],
        )

    def spread_of(self, w, value):
        cols = self.windows[w]
        self.s1[:, :, :, cols] = value.reshape(2, 2, -1, value.shape[1])
        z = 2 * self.hz + self.pz
        self.direct = self.net.slot(4)
        for d in range(1, 4):
            to = (z + d) % 4
            self.net.send(
                self.s1.at[to // 2, to % 2, :, cols], self.b4.at[z],
                self.direct + z, (2 * to + self.ix, self.peers[0][1]),
            )

    def spread_last(self, w):
        cols = self.windows[w]
        z = 2 * self.hz + self.pz
        value = self.s1[self.hz, self.pz, :, cols].astype(jnp.float32)
        for d in range(1, 4):
            to = (z + d) % 4
            self.net.arrived(self.b4.at[to], self.direct + to, (2 * to + self.ix, self.peers[0][1]))
            value = value + self.b4[to].astype(jnp.float32)
        return value

    def third(self, w):
        cols = self.windows[w]
        self.net.arrived(self.b2.at[:, :, cols], self.slots[w] + 1, self.peers[1])
        for h in range(2):
            value = self.s1[h, self.pz, :, cols].astype(jnp.float32)
            value = value + self.b2[h, :, cols].astype(jnp.float32)
            self.s2[h, :, cols] = value.astype(jnp.bfloat16)
        self.net.send(
            self.s2.at[1 - self.hz, :, cols], self.b3.at[:, cols],
            self.slots[w] + 2, self.peers[2],
        )

    def last(self, w):
        cols = self.windows[w]
        self.net.arrived(self.b3.at[:, cols], self.slots[w] + 2, self.peers[2])
        return self.s2[self.hz, :, cols].astype(jnp.float32) + self.b3[:, cols].astype(jnp.float32)


def make_fused(n_dp, in_local, images, sides, chan_in, chan_part):
    f32, bf16 = jnp.float32, jnp.bfloat16
    halves = tuple(side // 2 for side in sides)
    sizes = tuple(h * h * n for h, n in zip(halves, images))
    rows = sum(sizes)
    quarter = tuple(n // 4 for n in images)
    qlanes = tuple(q * side * side for q, side in zip(quarter, sides))
    slab_lanes = -(-sum(qlanes) // LANES) * LANES
    chan_full = 4 * chan_part
    out_rows = chan_full // n_dp
    starts = (0, sizes[0])
    widths = tuple(h * n for h, n in zip(halves, images))
    chunks = [(g, r, starts[g] + r * widths[g], widths[g]) for g in range(2) for r in range(halves[g])]
    win = [-(-q // LANES) * LANES for q in qlanes]
    b_tile = qlanes[0] // LANES * LANES
    n_sends, n_slots = 68, 198
    b_skip = qlanes[0] - b_tile
    rs = halves[0] // 2
    segments = [(1, 0, halves[1]), (0, 0, rs), (0, rs, halves[0])]
    seg_lane, runs = [], []
    lane_of = 0
    for g, r0, r1 in segments:
        side, base = sides[g], (0, qlanes[0])[g]
        seg_lane.append(lane_of)
        lane_of += quarter[g] * 2 * (r1 - r0) * side
        runs += [
            (base + (image * side + 2 * r0) * side, base + (image * side + 2 * r1) * side)
            for image in range(quarter[g])
        ]
    runs.append((sum(qlanes), slab_lanes))
    at, order = 0, []
    for a, b in runs:
        order.append((a, at, at + b - a))
        at += b - a
    back_runs = [(a, b) for _, a, b in sorted(order)]
    cut_lane = -(-seg_lane[2] // LANES) * LANES
    lane_parts = (slice(0, cut_lane), slice(cut_lane, slab_lanes))
    seg_cells = [(r1 - r0) * halves[g] for g, r0, r1 in segments]
    seg_rows = [cells * quarter[seg[0]] for cells, seg in zip(seg_cells, segments)]
    top = -(-(seg_rows[0] + seg_rows[1]) // 16) * 16
    seg_row = [0, seg_rows[0], top]
    q_rows = top + -(-seg_rows[2] // 16) * 16
    row_parts = (slice(0, top), slice(top, q_rows))
    patch_win = (slice(0, cut_lane), slice(seg_lane[1] // LANES * LANES, slab_lanes))
    patch_m, cells_m = quarter_matrices(
        quarter, sides, segments, seg_lane, seg_row, q_rows, slab_lanes
    )
    patch_ms = [
        np.concatenate([m[rows_, lanes_] for m in patch_m], axis=0)
        for rows_, lanes_ in zip(row_parts, patch_win)
    ]
    low_lane = seg_lane[1] // LANES * LANES
    last_lane = slab_lanes - LANES
    assert sum(qlanes) - last_lane <= LANES // 2
    out_lanes = [slice(cut_lane, last_lane), slice(0, low_lane), slice(low_lane, cut_lane)]
    back_pieces = (((0, 0, 2),), ((0, 2, halves[0] - 1),), ((0, halves[0] - 1, halves[0]), (1, 0, halves[1])))
    row_halves = [
        slice(starts[p[0][0]] + p[0][1] * widths[p[0][0]], starts[p[-1][0]] + p[-1][2] * widths[p[-1][0]])
        for p in back_pieces
    ]
    cols2 = (slice(0, 4 * LANES), slice(4 * LANES, 9 * LANES))
    cols1 = (slice(6 * LANES, 10 * LANES), slice(0, 6 * LANES))

    def kernel(*refs):
        (xa_h, xb_h, bxa_h, bxb_h, w1_h, w2_h, ws_h, g1_h, b1_h, g2_h, b2_h, gs_h, bs_h, ua_h, ub_h,
         pm0_h, pm1_h, cells_h,
         turn_h,
         oa, ob, gr, grf, gw1, gws, gw2, vecs, turn,
         xa, xb, bxa, bxb, w1g, w2, wsg, vg, g2, b2, gs, bs, ua, ub, pm0, pm1, cells,
         xs, xt, xr, zb, zsq, zsr, zg, zpa, zpb, valid, vq, hat, mask, zs, a1a, a1b,
         cslots, slots, stat, up, outr, gv, dza, dzb, dzma, dzmb, apk, arx, gacc, dzsr,
         dd, hp, hr1, hs, hr2, gu, d1a, d1b,
         p22, p23, p24, p25, p26, wg1, p11, p12, p13, p14, p15,
         sq, si, dq, di, gt, gtf, lsem, ssem, rsem) = refs
        i, k = lax.axis_index("dp"), lax.axis_index("chan")
        k1 = k + 1 - 2 * (k % 2)
        k2 = (k + 2) % 4
        k3 = (k1 + 2) % 4
        ix = i % 2
        mate = (i + 1 - 2 * ix, k)
        net = Links(ssem, rsem)
        bits = n_dp.bit_length() - 1

        def flip(d):
            j = i
            for b in range(bits):
                if d >> b & 1:
                    j = j + (1 << b) * (1 - 2 * ((i // (1 << b)) % 2))
            return j

        peers = [flip(d) for d in sorted(range(n_dp), key=lambda d: (d == 0, -(d >> 1), d & 1))]
        peers, home = peers[:-1], peers[-1]
        zp, a1, dz, d1 = (zpa, zpb), (a1a, a1b), (dza, dzb), (d1a, d1b)
        dzm = (dzma, dzmb)

        def flat(value):
            return value.reshape(-1, value.shape[-1])

        def zeros(count):
            return [jnp.zeros((8, LANES), f32)] * count

        loads = {}
        pairs_of = (
            ("xa", xa_h, xa), ("xb", xb_h, xb),
            ("w1", w1_h, w1g.at[k]), ("ws", ws_h, wsg.at[k]), ("g1", g1_h, vg.at[k, 0]), ("b1", b1_h, vg.at[k, 1]),
            ("bxa", bxa_h, bxa), ("bxb", bxb_h, bxb), ("pm0", pm0_h, pm0), ("pm1", pm1_h, pm1),
            ("ua", ua_h, ua), ("ub", ub_h, ub), ("g2", g2_h, g2),
            ("b2", b2_h, b2), ("gs", gs_h, gs), ("bs", bs_h, bs), ("w2", w2_h, w2), ("cells", cells_h, cells),
            ("turn", turn_h, turn),
        )
        for index, (name, source, target) in enumerate(pairs_of):
            loads[name] = pltpu.make_async_copy(source, target, lsem.at[index])
        loads["xa"].start()
        loads["xb"].start()

        def need(*names):
            for name in names:
                loads.pop(name).wait()

        barrier = pltpu.get_barrier_semaphore()
        for j in peers:
            pl.semaphore_signal(barrier, inc=1, device_id=(j, k), device_id_type=MESH)
        for where in (k1, k2, k3):
            pl.semaphore_signal(barrier, inc=1, device_id=(i, where), device_id_type=MESH)

        need("xa", "xb")
        for copy in loads.values():
            copy.start()
        lane = lax.broadcasted_iota(jnp.int32, (in_local, LANES), 1)
        for d, j in enumerate(peers + [home]):
            begin = 4 * qlanes[0] * j + qlanes[0] * k
            tile = begin // LANES
            part_a = xa[:, pl.ds(pl.multiple_of(tile * LANES, LANES), win[0])].astype(f32)
            part_a = pltpu.roll(part_a, (win[0] - (begin - tile * LANES)) % win[0], 1)
            begin = 4 * qlanes[1] * j + qlanes[1] * k
            tile = begin // LANES
            part_b = xb[:, pl.ds(pl.multiple_of(tile * LANES, LANES), win[1])].astype(f32)
            part_b = jnp.concatenate([part_b, jnp.zeros((in_local, LANES), f32)], axis=1)
            wide = win[1] + LANES
            part_b = pltpu.roll(part_b, (wide + b_skip - (begin - tile * LANES)) % wide, 1)
            seam = jnp.where(lane < b_skip, part_a[:, b_tile : b_tile + LANES], part_b[:, :LANES])
            xs[d * in_local : (d + 1) * in_local, :] = jnp.concatenate(
                [part_a[:, :b_tile], seam, part_b[:, LANES : slab_lanes - b_tile]], axis=1
            ).astype(bf16)
        slot_x = [net.slot(n_dp) for _ in lane_parts]
        n_via = 2
        via = [pl.ds((9 - n_via) * e, n_via) for e in (ix, 1 - ix)]
        w_taps = [via[0], slice(n_via, 5), slice(5, 9 - n_via)]
        slot_w = [net.slot(4) for _ in range(6)]

        def weight_refs(q):
            return [w1g.at[q, taps] for taps in w_taps] + [wsg.at[q], vg.at[q], w1g.at[q, via[1]]]

        ordered = regroup(xs[...], runs)
        for c, cols in enumerate(lane_parts):
            moved = ordered[:, cols]
            xt[:, :, cols] = moved.reshape(n_dp, in_local, moved.shape[1])
            xr[i, :, cols] = moved[-in_local:]
            if c == 0:
                pl.semaphore_wait(barrier, n_dp + 2)
            for d, j in enumerate(peers):
                net.send(xt.at[d, :, cols], xr.at[i, :, cols], slot_x[c] + i, (j, k))
            if c == 0:
                need("w1", "ws", "g1", "b1")
                for ref, slot in zip(weight_refs(k)[:5], slot_w):
                    net.send(ref, ref, slot + k, (i, k2))
                for ref, slot in zip(weight_refs(k), slot_w):
                    net.send(ref, ref, slot + k, (i, k1))

        def weights_on(n):
            ref = weight_refs(k2)[n]
            net.arrived(ref, slot_w[n] + k2, mate if n == 5 else (i, k2))
            net.send(ref, ref, slot_w[n] + k2, (i, k1))
            if n == 0:
                net.send(ref, ref, slot_w[5] + k2, mate)

        def weights_in(parts):
            for q in (k1, k3):
                for n in parts:
                    net.arrived(weight_refs(q)[n], slot_w[n] + q, (i, k1))

        for buf in (zpa, zpb, a1a, a1b, dza, dzb, dzma, dzmb, d1a, d1b):
            side = buf.shape[1] if len(buf.shape) == 5 else buf.shape[0]
            lead = (slice(None),) if len(buf.shape) == 5 else ()
            for edge in (0, side - 1):
                for index in (lead + (edge,), lead + (slice(None), edge)):
                    region = buf.at[index]
                    region[...] = jnp.zeros(region.shape, buf.dtype)
        need("bxa", "bxb", "ua", "ub")
        population = zeros(1)[0]
        low = lax.broadcasted_iota(jnp.int32, (8, LANES), 0) < 4
        for g, box in enumerate((bxa, bxb)):
            n, half, count = images[g], halves[g], quarter[g]
            diag = lax.broadcasted_iota(jnp.int32, (n, n), 0) == lax.broadcasted_iota(jnp.int32, (n, n), 1)
            ends = [
                jnp.sum(jnp.where(diag, box[q : q + 1, :].astype(f32), 0.0), axis=1, keepdims=True)
                for q in range(4)
            ]
            ends = [jnp.broadcast_to(e, (n, LANES)) for e in ends]
            ends[2], ends[3] = ends[0] + ends[2], ends[1] + ends[3]

            def inside(ends, r, s):
                both = (r >= ends[0]) & (r < ends[2]) & (s >= ends[1]) & (s < ends[3])
                return both.astype(f32)

            for r in range(half):
                for s in range(half):
                    cell = inside(ends, r, s)
                    begin = starts[g] + (r * half + s) * n
                    valid[begin : begin + n, :] = cell
                    population = population + jnp.sum(cell.reshape(n // 8, 8, LANES), axis=0)
            mine = [pltpu.roll(e, (n - count * k) % n, 0)[:8] for e in ends]
            if count < 8:
                mine = [jnp.where(low, e, pltpu.roll(e, 4, 0)) for e in mine]
            for (seg_g, r0, r1), first, cells_n in zip(segments, seg_row, seg_cells):
                if seg_g != g:
                    continue
                per = 8 // count
                for t in range(-(-cells_n // per)):
                    spots = [divmod(min(per * t + e, cells_n - 1), half) for e in range(per)]
                    spots = [(float(r0 + r), float(s)) for r, s in spots]
                    if per == 2:
                        r, s = (jnp.where(low, spots[0][e], spots[1][e]) for e in range(2))
                    else:
                        r, s = spots[0]
                    cell = inside(mine, r, s)
                    if per == 2 and per * t + 1 >= cells_n:
                        cell = jnp.where(low, cell, 0.0)
                    vq[first + 8 * t : first + 8 * t + 8, :] = cell
        population = jnp.broadcast_to(jnp.sum(population, axis=0, keepdims=True), (8, LANES))
        for g, source in enumerate((ua, ub)):
            n, count = images[g], halves[g] ** 2
            gu[starts[g] : starts[g] + sizes[g], :] = source[...].astype(f32)
            for cell in range(count):
                up[starts[g] + cell * n : starts[g] + (cell + 1) * n, :] = gu[
                    pl.ds(starts[g] + cell, n, stride=count), :
                ]

        def rowsum(value):
            return jnp.sum(value.reshape(-1, 8, value.shape[-1]), axis=0)

        def message(sums):
            parts = [jnp.sum(v, axis=0, keepdims=True) if v.shape[0] > 1 else v for v in sums]
            if len(parts) % 8:
                parts.append(jnp.zeros((8 - len(parts) % 8, LANES), f32))
            return jnp.concatenate(parts, axis=0)

        def by_chan(value):
            return [value[:, q * LANES : (q + 1) * LANES] for q in range(4)]

        def share(rnd, value):
            mine = slots.at[rnd, i, : value.shape[0]]
            mine[...] = value
            first = net.slot(n_dp)
            for j in peers:
                net.send(mine, mine, first + i, (j, k))
            return first

        def total(rnd, first, count=8):
            for j in peers:
                net.arrived(slots.at[rnd, j, :count], first + j, (j, k))
            return jnp.sum(slots[rnd, :, :count], axis=0)

        def chan_share(rnd, value):
            mine = cslots.at[rnd, k, : value.shape[0]]
            mine[...] = value
            first = net.slot(4)
            for where in (k2, k3, k1):
                net.send(mine, mine, first + k, (i, where))
            return first

        def chan_total(rnd, first, count=8):
            for where in (k1, k2, k3):
                net.arrived(cslots.at[rnd, where, :count], first + where, (i, where))
            return jnp.sum(cslots[rnd, :, :count], axis=0)

        pop_first = share(4, population)

        def quarter_in(c):
            for j in peers:
                net.arrived(xr.at[j, :, lane_parts[c]], slot_x[c] + j, (j, k))

        def patches(c):
            whole = jnp.concatenate([xr[q, :, patch_win[c]] for q in range(n_dp)], axis=0)
            value = mm((pm0, pm1)[c][...], whole, 1, 1).astype(bf16)
            count = value.shape[0] // 9
            return [value[t * count : (t + 1) * count] for t in range(9)]

        slot_s = net.slot(4)

        z_cuts = (slice(0, top * 3 // 80 * 16), slice(top * 3 // 80 * 16, top), slice(top, q_rows))
        slot_z = [net.slot(4) for _ in z_cuts]

        def z_send(n):
            for where in (k2, k1):
                net.send(zb.at[k, z_cuts[n]], zb.at[k, z_cuts[n]], slot_z[n] + k, (i, where))

        def conv_taps(taps, some):
            weights = lanes_cat([w1g[q, some].reshape(-1, chan_part) for q in range(4)])
            return mm(lanes_cat(taps[some]), weights, 1, 0)

        def first_conv(c, value, acc):
            part = row_parts[c]
            value = value.astype(bf16)
            zb[k, part, :] = value
            if c == 0:
                z_send(0)
            z = value.astype(f32)
            u = z * lanes_cat([vq[part, :]] * 4)
            return [acc[0] + rowsum(u), acc[1] + rowsum(u * z)]

        def projection(c, patch, acc):
            side = mm(patch, lanes_cat([wsg[q] for q in range(4)]), 1, 0).astype(bf16)
            for q, z in enumerate(by_chan(side)):
                zsq[q, row_parts[c], :] = z
            z = side.astype(f32)
            u = z * lanes_cat([vq[row_parts[c], :]] * 4)
            return [acc[0] + rowsum(u), acc[1] + rowsum(u * z)]

        def act_on(n):
            part = zb.at[k2, z_cuts[n]]
            net.arrived(part, slot_z[n] + k2, (i, k2))
            net.send(part, part, slot_z[n] + k2, (i, k1))

        def act_in(n):
            net.arrived(zb.at[k1, z_cuts[n]], slot_z[n] + k1, (i, k1))
            net.arrived(zb.at[k3, z_cuts[n]], slot_z[n] + k3, (i, k1))

        acc = [jnp.zeros((8, chan_full), f32)] * 2
        need("pm0", "pm1")
        for n in (0, 1, 5, 2):
            weights_on(n)
        quarter_in(0)
        taps = patches(0)
        center = [taps[4]]
        weights_on(3)
        weights_on(4)
        weights_in((0, 1, 5))
        value = conv_taps(taps, slice(0, 5)) + conv_taps(taps, slice(9 - n_via, 9))
        weights_in((2,))
        acc = first_conv(0, value + conv_taps(taps, slice(5, 9 - n_via)), acc)
        quarter_in(1)
        taps = patches(1)
        center.append(taps[4])
        acc = first_conv(1, conv_taps(taps, slice(0, 9)), acc)
        acc = [jnp.sum(v, axis=0, keepdims=True) for v in acc]
        first = chan_share(0, message(sum((by_chan(v) for v in acc), [])))
        gone = net.mark()
        z_send(1)
        z_send(2)
        weights_in((3, 4))
        acc = [jnp.zeros((8, chan_full), f32)] * 2
        for c in range(2):
            acc = projection(c, center[c], acc)
        acc = [jnp.sum(v, axis=0, keepdims=True) for v in acc]
        side_first = share(5, message(sum((by_chan(v) for v in acc), [])))
        zsr[k] = zsq[k]

        need(*list(loads))
        row_cuts = (slice(0, rows // 32 * 16), slice(rows // 32 * 16, rows))
        slot_g0 = [net.slot(4) for _ in row_cuts]
        whole = jnp.concatenate([xr[q] for q in range(n_dp)], axis=0)
        for span in row_cuts:
            zg[k, span, :] = mm(cells[span, :], whole, 1, 1).astype(bf16)
        first = share(0, chan_total(0, first))
        for where in (k2, k3, k1):
            net.send(zsq.at[where], zsr.at[k], slot_s + k, (i, where))
        act_on(0)
        act_on(1)
        act_on(2)
        net.settle(gone)
        side_first = chan_share(2, total(5, side_first))
        gone = net.mark()
        for span, slot in zip(row_cuts, slot_g0):
            for where in (k2, k1):
                net.send(zg.at[k, span], zg.at[k, span], slot + k, (i, where))

        def slab_on(n):
            span, slot = row_cuts[n], slot_g0[n]
            net.arrived(zg.at[k2, span], slot + k2, (i, k2))
            net.send(zg.at[k2, span], zg.at[k2, span], slot + k2, (i, k1))

        def slab_in(n):
            span, slot = row_cuts[n], slot_g0[n]
            net.arrived(zg.at[k1, span], slot + k1, (i, k1))
            net.arrived(zg.at[k3, span], slot + k3, (i, k1))

        inv_pop = 1.0 / total(4, pop_first)[0:1]
        turn_low = lax.broadcasted_iota(jnp.int32, (8, 1), 0) < 4

        def whole_cells(read, c):
            for begin in range(row_parts[c].start, row_parts[c].stop, 16):
                blocks = [read(q, slice(begin, begin + 16)).astype(f32) for q in range(4)]
                for at in (begin, begin + 8):
                    seg = max(e for e in range(3) if seg_row[e] <= at)
                    g, r0, r1 = segments[seg]
                    per = 8 // quarter[g]
                    v = [block[at - begin : at - begin + 8] for block in blocks]
                    cell = (at - seg_row[seg]) // 8 * per
                    if per == 1:
                        found = [jnp.concatenate(v, axis=0)]
                    else:
                        t = [pltpu.roll(e, 4, 0) for e in v]
                        found = [
                            jnp.concatenate(
                                [jnp.where(turn_low, v[0], t[1]), jnp.where(turn_low, v[2], t[3])], axis=0
                            ),
                            jnp.concatenate(
                                [jnp.where(turn_low, t[0], v[1]), jnp.where(turn_low, t[2], v[3])], axis=0
                            ),
                        ]
                    for e, value in enumerate(found):
                        if cell + e < seg_cells[seg]:
                            r, s = divmod(cell + e, halves[g])
                            yield g, r0 + r, s, value

        def gather_cells(c):
            for g, r, s, z in whole_cells(lambda q, span: zb[q, span, :], c):
                begin = starts[g] + (r * halves[g] + s) * images[g]
                hat[begin : begin + images[g], :] = z

        for n in range(2):
            act_in(n)
        gather_cells(0)
        act_in(2)
        gather_cells(1)
        tot = total(0, first)
        stat[0:8, :] = tot
        tot_first = (stat[pl.ds(k, 1), :], stat[pl.ds(4 + k, 1), :])
        def moments(total_, square):
            mean = total_ * inv_pop
            return mean, lax.rsqrt(square * inv_pop - mean * mean + epsilon)

        mean1, sc1 = moments(tot[0:4], tot[4:8])
        mean1, sc1 = (lanes_cat([v[q : q + 1] for q in range(4)]) for v in (mean1, sc1))
        gain1, shift1 = (lanes_cat([vg[q, e] for q in range(4)]) for e in range(2))

        scale1 = sc1 * gain1
        offset1 = shift1 - mean1 * scale1

        def activate(c):
            for g, r0, r1 in (segments[:2], segments[2:])[c]:
                for r in range(r0, r1):
                    for s in range(halves[g]):
                        begin = starts[g] + (r * halves[g] + s) * images[g]
                        span = slice(begin, begin + images[g])
                        v = hat[span, :] * scale1 + offset1
                        act = v * sigma(v) * lanes_cat([valid[span, :]] * 4)
                        a1[g][1 + r, 1 + s] = act.astype(bf16)

        def second_conv(parts, acc):
            value = None
            for a, b in TAPS:
                patch = jnp.concatenate(
                    [flat(a1[g][r0 + a : r1 + a, b : b + halves[g]]) for g, r0, r1 in parts], axis=0
                )
                part = mm(patch, w2[3 * a + b], 1, 0)
                value = part if value is None else value + part
            at = 0
            for g, r0, r1 in parts:
                for r in range(r0, r1):
                    begin = starts[g] + r * widths[g]
                    span = slice(begin, begin + widths[g])
                    u = value[at : at + widths[g]]
                    at += widths[g]
                    gv[span, :] = u
                    uv = u * valid[span, :]
                    acc = [acc[0] + rowsum(uv), acc[1] + rowsum(uv * u)]
            return acc

        left = lax.broadcasted_iota(jnp.int32, (1, LANES), 1) < out_rows

        def pack(g, r0, r1):
            for r in range(r0, r1):
                v = by_chan(flat(a1[g][1 + r, 1 : 1 + halves[g]]).astype(f32))
                t = [pltpu.roll(e, out_rows, 1) for e in v]
                begin = starts[g] + r * widths[g]
                span = slice(begin, begin + widths[g])
                for p in range(2):
                    cols = slice(p * LANES, (p + 1) * LANES)
                    apk[0, span, cols] = jnp.where(left, v[2 * p], t[2 * p + 1]).astype(bf16)
                    apk[1, span, cols] = jnp.where(left, t[2 * p], v[2 * p + 1]).astype(bf16)

        near = sizes[1]
        far = sizes[0] * 9 // 16 // 16 * 16
        pack_spans = [
            [slice(starts[1], starts[1] + near)],
            [slice(0, far)],
            [slice(far, sizes[0])],
        ]
        slot_p = [[net.slot() for _ in spans_] for spans_ in pack_spans]

        def pack_send(n):
            for span, slot in zip(pack_spans[n], slot_p[n]):
                net.send(apk.at[1 - ix, span], arx.at[span], slot, mate)

        activate(0)
        pack(1, 0, halves[1])
        pack(0, 0, rs)
        pack_send(0)
        acc = second_conv([(1, 0, halves[1]), (0, 0, rs - 1)], zeros(2))
        activate(1)
        pack(0, rs, halves[0])
        acc = second_conv([(0, rs - 1, halves[0])], acc)
        first = share(1, message(acc))
        pack_send(1)

        stat[0:8, :] = chan_total(2, side_first)
        means, scs = moments(stat[pl.ds(k, 1), :], stat[pl.ds(4 + k, 1), :])
        for where in (k2, k3, k1):
            net.arrived(zsr.at[where], slot_s + where, (i, where))
        for c in range(2):
            for g, r, s, z in whole_cells(lambda q, span: zsr[q, span, :], c):
                begin = starts[g] + (r * halves[g] + s) * images[g]
                zs[begin : begin + images[g], :] = (z - means) * scs

        def planes_of(quarters, g):
            count = quarter[g]
            if count % 8 == 0:
                return [
                    jnp.concatenate([v[:, count * p : count * (p + 1)] for v in quarters], axis=1)
                    for p in range(4)
                ]
            low = lax.broadcasted_iota(jnp.int32, (1, 8, 1), 1) < 4
            parts = [[v[:, 8 * h : 8 * h + 8] for v in quarters] for h in range(2)]
            turned = [[pltpu.roll(v, 4, 1) for v in side] for side in parts]
            result = []
            for p in range(4):
                v, t = parts[p // 2], turned[p // 2]
                if p % 2 == 0:
                    both = [jnp.where(low, v[0], t[1]), jnp.where(low, v[2], t[3])]
                else:
                    both = [jnp.where(low, t[0], v[1]), jnp.where(low, t[2], v[3])]
                result.append(jnp.concatenate(both, axis=1))
            return result

        def make_planes():
            for g, r, begin, count in chunks:
                quarters = [
                    zg[q, begin : begin + count, :].astype(f32).reshape(halves[g], images[g], chan_in)
                    for q in range(4)
                ]
                for p, value in enumerate(planes_of(quarters, g)):
                    zp[g][p, 1 + r, 1 : 1 + halves[g]] = value.astype(bf16)

        tot = total(1, first)
        mean2, sc2 = moments(tot[0:1], tot[1:2])
        gain2, gains = g2[...], gs[...]
        shifts = b2[...] + bs[...]
        acc = zeros(3)
        for g, r, begin, count in chunks:
            span = slice(begin, begin + count)
            ok = valid[span, :]
            hat2 = (gv[span, :] - mean2) * sc2
            hats = zs[span, :]
            v = hat2 * gain2 + hats * gains + shifts
            sig = sigma(v)
            outr[span, :] = v * sig * ok
            grad = up[span, :] * ok * (sig * (1.0 + v * (1.0 - sig)))
            up[span, :] = grad
            gv[span, :] = hat2
            acc = [acc[0] + rowsum(grad), acc[1] + rowsum(grad * hat2), acc[2] + rowsum(grad * hats)]
        first = share(2, message(acc))
        pack_send(2)
        for g, target in enumerate((oa, ob)):
            n, count = images[g], halves[g] ** 2
            for cell in range(count):
                gu[pl.ds(starts[g] + cell, n, stride=count), :] = outr[
                    starts[g] + cell * n : starts[g] + (cell + 1) * n, :
                ]
            target[...] = gu[starts[g] : starts[g] + sizes[g], :].astype(bf16)
        for begin in range(0, rows, 16):
            span = slice(begin, begin + 16)
            h = (hat[span, :] - mean1) * sc1
            hat[span, :] = h
            v = h * gain1 + shift1
            sig = sigma(v)
            mask[span, :] = sig * (1.0 + v * (1.0 - sig)) * lanes_cat([valid[span, :]] * 4)
        net.settle(gone)
        gone = net.mark()
        tot = total(2, first)
        sum_tail, sum_gain2, sum_gains = tot[0:1], tot[1:2], tot[2:3]
        k2g, ksg = gain2 * sc2, gains * scs
        db, dg2, dgs = sum_tail * inv_pop, sum_gain2 * inv_pop, sum_gains * inv_pop
        for g, r, begin, count in chunks:
            span = slice(begin, begin + count)
            value = k2g * (up[span, :] - valid[span, :] * (db + gv[span, :] * dg2))
            dz[g][1 + r, 1 : 1 + halves[g]] = value.astype(bf16).reshape(halves[g], images[g], chan_part)
        slot_d = net.slot(2)

        def dz_inner(buf, g):
            return buf[g].at[1 : 1 + halves[g], 1 : 1 + halves[g]]

        for g in range(2):
            net.send(dz_inner(dz, g), dz_inner(dzm, g), slot_d + g, mate)

        def columns(buf, piece, taps=range(9)):
            for g, r0, r1 in piece:
                for t in taps:
                    a, b = TAPS[t]
                    dd[
                        starts[g] + r0 * widths[g] : starts[g] + r1 * widths[g],
                        t * LANES : (t + 1) * LANES,
                    ] = flat(buf[g][r0 + 2 - a : r1 + 2 - a, 2 - b : 2 - b + halves[g]])

        def back_second(first, span):
            begin = pl.multiple_of(first * chan_part, LANES)
            weights = lanes_cat([w2[t, pl.ds(begin, 2 * chan_part), :] for t in range(9)])
            value = mm(dd[span, :], weights, 1, 1).astype(bf16)
            hp[first, span, :] = value[:, :chan_part]
            hp[first + 1, span, :] = value[:, chan_part:]

        slot_h = [net.slot(3) for _ in row_halves]
        def other_pair(n):
            columns(dz, back_pieces[n])
            back_second(2 * (k2 // 2), row_halves[n])
            net.send(hp.at[k3, row_halves[n]], hr1.at[1, row_halves[n]], slot_h[n] + 1, (i, k1))

        def cross_second(n):
            span = row_halves[n]
            net.arrived(hr1.at[1, span], slot_h[n] + 1, (i, k1))
            hs[span, :] = (hp[k2, span, :].astype(f32) + hr1[1, span, :].astype(f32)).astype(bf16)
            net.send(hs.at[span], hr2.at[span], slot_h[n] + 2, (i, k2))

        def pair_sums(first):
            acc = [jnp.zeros((8, 2 * chan_part), f32)] * 2
            cols = pl.ds(pl.multiple_of(first * chan_part, 2 * LANES), 2 * chan_part)
            for begin in range(0, rows, 16):
                span = slice(begin, begin + 16)
                part = lanes_cat([hp[first + e, span, :] for e in range(2)]).astype(f32) * mask[span, cols]
                acc = [acc[0] + rowsum(part), acc[1] + rowsum(part * hat[span, cols])]
            acc = [jnp.sum(v, axis=0, keepdims=True) for v in acc]
            for e in range(2):
                for n in range(2):
                    stat[pl.ds(4 * n + first + e, 1), :] = acc[n][:, e * LANES : (e + 1) * LANES]

        other_pair(0)
        other_pair(1)
        cross_second(0)
        other_pair(2)
        cross_second(1)
        back_second(2 * (k // 2), slice(0, rows))
        pair_sums(2 * (k2 // 2))
        cross_second(2)
        for span, slot in zip(row_halves, slot_h):
            net.send(hp.at[k1, span], hr1.at[0, span], slot, (i, k1))
        pair_sums(2 * (k // 2))
        first = share(3, stat[0:8, :])

        sum2 = Reduce(net, i, k, None, (None, p22, p23, p24, p25), cols2, p26)
        gacc[...] = mm(apk[ix], dd[...], 0, 0)
        net.settle(gone)
        first = chan_share(1, total(3, first))
        def split_cells(read, target, c):
            for begin in range(row_parts[c].start, row_parts[c].stop, 16):
                tiles = []
                for at in (begin, begin + 8):
                    seg = max(e for e in range(3) if seg_row[e] <= at)
                    g, r0, r1 = segments[seg]
                    per = 8 // quarter[g]
                    cell = (at - seg_row[seg]) // 8 * per
                    blocks = []
                    for e in range(per):
                        if cell + e < seg_cells[seg]:
                            r, s = divmod(cell + e, halves[g])
                            blocks.append(read(g, r0 + r, s))
                        else:
                            blocks.append(jnp.zeros((images[g], chan_part), f32))
                    if per == 1:
                        tiles.append([blocks[0][8 * q : 8 * q + 8] for q in range(4)])
                    else:
                        found = []
                        for h in range(2):
                            v = [block[8 * h : 8 * h + 8] for block in blocks]
                            t = [pltpu.roll(e, 4, 0) for e in v]
                            found += [jnp.where(turn_low, v[0], t[1]), jnp.where(turn_low, t[0], v[1])]
                        tiles.append(found)
                for q in range(4):
                    both = jnp.concatenate([tiles[0][q], tiles[1][q]], axis=0)
                    target[q, begin : begin + 16, :] = both.astype(bf16)

        def cell_span(g, r, s):
            begin = starts[g] + (r * halves[g] + s) * images[g]
            return slice(begin, begin + images[g])

        def short_cell(g, r, s):
            span = cell_span(g, r, s)
            value = ksg * (up[span, :] - valid[span, :] * (db + zs[span, :] * dgs))
            dzsr[span, :] = value.astype(bf16)
            return value

        slot_q = [net.slot(4) for _ in range(3)]

        def quarters_out(source, target, span, slot):
            for where in (k2, k3, k1):
                net.send(source.at[where, span], target.at[k, span], slot + k, (i, where))
            target[k, span, :] = source[k, span, :]

        def quarters_in(target, span, slot):
            for where in (k1, k2, k3):
                net.arrived(target.at[where, span], slot + where, (i, where))

        for c in range(2):
            split_cells(short_cell, sq, c)
        quarters_out(sq, si, slice(0, q_rows), slot_q[2])
        for n in range(2):
            slab_on(n)
        for spans_, slots_ in zip(pack_spans, slot_p):
            for span, slot in zip(spans_, slots_):
                net.arrived(arx.at[span], slot, mate)
        for g in range(2):
            net.arrived(dz_inner(dzm, g), slot_d + g, mate)
        gone = net.mark()
        for w, cols in enumerate(cols2):
            for piece in back_pieces:
                columns(dzm, piece, range(cols.start // LANES, cols.stop // LANES))
            value = (gacc[:, cols] + mm(arx[...], dd[:, cols], 0, 0)).astype(bf16)
            (sum2.spread_of, sum2.second_of)[w](w, value)
        tot = chan_total(1, first)
        stat[0:8, :] = tot
        sum_head, sum_gain1 = stat[pl.ds(k, 1), :], stat[pl.ds(4 + k, 1), :]

        def close_second():
            for w, cols in enumerate(cols2):
                value = (sum2.spread_last, sum2.last)[w](w)
                for t in range(cols.start // LANES, cols.stop // LANES):
                    gw2[t] = value[:, t * LANES - cols.start : (t + 1) * LANES - cols.start]

        own = pl.ds(pl.multiple_of(k * chan_part, LANES), chan_part)
        mean1, sc1 = moments(tot_first[0], tot_first[1])
        k1g = vg[k, 0] * sc1
        db, dg1 = sum_head * inv_pop, sum_gain1 * inv_pop
        for span, slot in zip(row_halves, slot_h):
            net.arrived(hr1.at[0, span], slot, (i, k1))
            net.arrived(hr2.at[span], slot + 2, (i, k2))

        def first_cell(g, r, s):
            span = cell_span(g, r, s)
            grad = hp[k, span, :].astype(f32) + hr1[0, span, :].astype(f32) + hr2[span, :].astype(f32)
            grad = grad * mask[span, own]
            value = k1g * (grad - valid[span, :] * (db + hat[span, own] * dg1))
            d1[g][r, s] = value.astype(bf16)
            return value

        for c in (1, 0):
            split_cells(first_cell, dq, c)
            quarters_out(dq, di, row_parts[c], slot_q[c])

        def back_patch(pieces, p):
            parts = []
            for g, r0, r1 in pieces:
                width = halves[g] * images[g]
                taps = [
                    flat(d1[g][r0 + (a == 0) : r1 + (a == 0), (b == 0) : (b == 0) + halves[g]])
                    for a, b in PLANE_TAPS[p]
                ]
                if p == 0:
                    taps.append(dzsr[starts[g] + r0 * width : starts[g] + r1 * width, :])
                parts.append(lanes_cat(taps))
            return jnp.concatenate(parts, axis=0) if len(parts) > 1 else parts[0]

        slot_o = [net.slot(n_dp) for _ in out_lanes]

        def back_taps(c):
            part = row_parts[c]
            quarters_in(di, part, slot_q[c])
            grads = lanes_cat([di[q, part, :] for q in range(4)])
            weights = lanes_cat([w1g[q].reshape(9 * chan_in, chan_part) for q in range(4)])
            value = mm(grads, weights, 1, 1)
            taps = [value[:, t * chan_in : (t + 1) * chan_in] for t in range(9)]
            side = lanes_cat([si[q, part, :] for q in range(4)])
            taps[4] = taps[4] + mm(side, lanes_cat([wsg[q] for q in range(4)]), 1, 1)
            return jnp.concatenate([tap.astype(bf16) for tap in taps], axis=0)

        slot_f = net.slot(n_dp)

        def out_send(n, value):
            cols = out_lanes[n]
            if n == 0:
                last_tile = value[:, value.shape[1] - LANES :].reshape(n_dp, in_local, LANES)
                gtf[...] = fold(last_tile).astype(bf16)
                grf[i] = gtf[i]
                for j in peers:
                    net.send(gtf.at[j], grf.at[i], slot_f + i, (j, k))
                value = value[:, : value.shape[1] - LANES]
            gt[:, :, cols] = value.astype(bf16).reshape(n_dp, in_local, value.shape[1])
            for j in peers:
                net.send(gt.at[j, :, cols], gr.at[i, :, cols], slot_o[n] + i, (j, k))

        sum1 = Reduce(net, i, k, wg1, (p11, p12, p13, p14, p15), cols1)

        def weight_first(w):
            cols = cols1[w]
            blocks = []
            for p in ((3,), (0, 1, 2))[w]:
                value = 0.0
                for g, r0, r1 in ((0, 0, halves[0]), (1, 0, halves[1])):
                    cell = flat(zp[g][p, 1 : 1 + halves[g], 1 : 1 + halves[g]])
                    value = value + mm(cell, back_patch([(g, r0, r1)], p), 0, 0)
                blocks.append(value.astype(bf16))
            wg1[:, :, :, :, cols] = lanes_cat(blocks).reshape(2, 2, 2, in_local, cols.stop - cols.start)
            sum1.first(w)

        for n in range(2):
            slab_in(n)
        make_planes()
        weight_first(0)
        weight_first(1)
        net.settle(gone)
        quarters_in(si, slice(0, q_rows), slot_q[2])
        late = back_taps(1)
        edge = cut_lane - patch_win[1].start
        out_send(0, mm(late, pm1[:, edge:], 0, 0))
        early_ = back_taps(0)
        out_send(1, mm(early_, pm0[:, :low_lane], 0, 0))
        rest = mm(early_, pm0[:, low_lane:], 0, 0)
        shared = mm(late, pm1[:, low_lane - patch_win[1].start : edge], 0, 0)
        sum2.third(1)
        sum1.second(0)
        sum1.second(1)
        out_send(2, rest + shared)
        sum1.third(0)
        sum1.third(1)
        gr[i] = gt[i]
        close_second()
        for w, cols in enumerate(cols1):
            value = sum1.last(w)
            for t, tap in enumerate(TAPS):
                place = ORDER.index(tap)
                place = (place + (place > 0)) * LANES
                if cols.start <= place < cols.stop:
                    gw1[t] = value[:, place - cols.start : place - cols.start + LANES]
            if cols.start <= LANES < cols.stop:
                gws[...] = value[:, LANES - cols.start : 2 * LANES - cols.start]
        vecs[...] = message([sum_gain1, sum_head, sum_gain2, sum_tail, sum_gains])
        for j in peers:
            net.arrived(grf.at[j], slot_f + j, (j, k))
        for c, cols in enumerate(out_lanes):
            for j in peers:
                net.arrived(gr.at[j, :, cols], slot_o[c] + j, (j, k))
        net.drain()
        assert net.sends <= n_sends and net.slots <= n_slots

    V = pltpu.VMEM
    pads = [(h + 2, h + 2, n, chan_part) for h, n in zip(halves, images)]
    half_pads = [(h + 1, h + 1, n) for h, n in zip(halves, images)]

    def ladder(count, width):
        return [
            V((2, 2, 2, count, width), bf16), V((2, 2, count, width), bf16), V((2, 2, count, width), bf16),
            V((2, count, width), bf16), V((2, count, width), bf16), V((count, width), bf16),
        ]

    inputs = [
        V((in_local, n_dp * 4 * qlanes[0]), bf16), V((in_local, n_dp * 4 * qlanes[1]), bf16),
        V((4, images[0]), jnp.int32), V((4, images[1]), jnp.int32),
        V((4, 9, chan_in, chan_part), bf16), V((9, chan_full, chan_part), bf16),
        V((4, chan_in, chan_part), bf16), V((4, 2, 1, chan_part), f32),
    ] + [V((1, chan_part), f32)] * 4 + [
        V((sizes[0], chan_part), bf16), V((sizes[1], chan_part), bf16),
    ] + [V(m.shape, bf16) for m in patch_ms] + [V((rows, slab_lanes), bf16)]
    scratch = inputs + [
        V((n_dp * in_local, slab_lanes), bf16),
        V((n_dp, in_local, slab_lanes), bf16),
        V((n_dp, in_local, slab_lanes), bf16),
        V((4, q_rows, chan_full), bf16),
        V((4, q_rows, chan_part), bf16),
        V((4, q_rows, chan_part), bf16),
        V((4, rows, chan_in), bf16),
        V((4,) + half_pads[0] + (chan_in,), bf16),
        V((4,) + half_pads[1] + (chan_in,), bf16),
        V((rows, LANES), f32),
        V((q_rows, LANES), f32),
        V((rows, chan_full), f32),
        V((rows, chan_full), f32),
        V((rows, chan_part), f32),
        V(pads[0][:3] + (chan_full,), bf16),
        V(pads[1][:3] + (chan_full,), bf16),
        V((3, 4, 16, LANES), f32),
        V((6, n_dp, 16, LANES), f32),
        V((16, LANES), f32),
        V((rows, chan_part), f32),
        V((rows, chan_part), f32),
        V((rows, chan_part), f32),
        V(pads[0], bf16),
        V(pads[1], bf16),
        V(pads[0], bf16),
        V(pads[1], bf16),
        V((2, rows, chan_full // 2), bf16),
        V((rows, chan_full // 2), bf16),
        V((chan_full // 2, 9 * chan_part), f32),
        V((rows, chan_part), bf16),
        V((rows, 9 * chan_part), bf16),
        V((4, rows, chan_part), bf16),
        V((2, rows, chan_part), bf16),
        V((rows, chan_part), bf16),
        V((rows, chan_part), bf16),
        V((rows, chan_part), f32),
        V(half_pads[0] + (chan_part,), bf16),
        V(half_pads[1] + (chan_part,), bf16),
    ]
    scratch += ladder(out_rows, 9 * LANES)[2:]
    scratch += [V((n_dp // 2, out_rows, cols2[0].stop), bf16)] + ladder(in_local, 10 * LANES)
    scratch += [
        V((4, q_rows, chan_part), bf16),
        V((4, q_rows, chan_part), bf16),
        V((4, q_rows, chan_part), bf16),
        V((4, q_rows, chan_part), bf16),
        V((n_dp, in_local, last_lane), bf16),
        V((n_dp, in_local // 2, LANES), bf16),
        pltpu.SemaphoreType.DMA((20,)),
        pltpu.SemaphoreType.DMA((n_sends,)),
        pltpu.SemaphoreType.DMA((n_slots,)),
    ]
    mid_outs = [
        V((sizes[0], chan_part), bf16),
        V((sizes[1], chan_part), bf16),
        V((n_dp, in_local, last_lane), bf16),
        V((n_dp, in_local // 2, LANES), bf16),
        V((9, in_local, LANES), f32),
        V((in_local, LANES), f32),
        V((9, out_rows, LANES), f32),
        V((8, LANES), f32),
        V((n_dp * in_local, n_dp * in_local), bf16),
    ]
    vmem = pl.BlockSpec(memory_space=pltpu.VMEM)
    hbm = pl.BlockSpec(memory_space=pl.ANY)
    main = pl.pallas_call(
        kernel,
        out_shape=mid_outs,
        in_specs=[hbm] * 19,
        out_specs=[vmem] * len(mid_outs),
        scratch_shapes=scratch,
        compiler_params=pltpu.CompilerParams(
            collective_id=1, has_side_effects=True, vmem_limit_bytes=58 * 2**20
        ),
        name="block",
    )

    def closing(oa, ob, gr, grf, gw1, gws, gw2, vecs, turn,
                fa, fb, ia, ib, f1, f2, fs, c1, h1, c2, h2, cs, hs, iav, ibv, sems):
        outs = [
            pltpu.make_async_copy(source, target, sems.at[index])
            for index, (source, target) in enumerate(
                ((gw2, f2), (gw1, f1), (oa, fa), (ob, fb), (gws, fs))
            )
        ]
        for out in outs:
            out.start()
        tail = unfold(grf[...].astype(f32)).astype(bf16).reshape(n_dp * in_local, LANES)
        moved = jnp.concatenate([gr[...].reshape(n_dp * in_local, last_lane), tail], axis=1)
        n_half = in_local // 2
        for h in range(2):
            part = slice(h * n_half, (h + 1) * n_half)
            natural = regroup(mm(turn[h * n_half * n_dp : (h + 1) * n_half * n_dp, :], moved, 1, 0), back_runs)
            iav[part] = natural[:, : qlanes[0]].reshape(n_half, n_dp, qlanes[0]).astype(bf16)
            tail = natural[:, qlanes[0] : qlanes[0] + qlanes[1]]
            ibv[part] = tail.reshape(n_half, n_dp, qlanes[1]).astype(bf16)
            for e, (source, target) in enumerate(((iav, ia), (ibv, ib))):
                out = pltpu.make_async_copy(source.at[part], target.at[part], sems.at[5 + 2 * h + e])
                out.start()
                outs.append(out)
        for ref, row in ((c1, 0), (h1, 1), (c2, 2), (h2, 3), (cs, 4), (hs, 3)):
            ref[...] = vecs[row : row + 1, :]
        for out in outs:
            out.wait()

    last = pl.pallas_call(
        closing,
        out_shape=[
            jax.ShapeDtypeStruct((sizes[0], chan_part), bf16),
            jax.ShapeDtypeStruct((sizes[1], chan_part), bf16),
            jax.ShapeDtypeStruct((in_local, n_dp, qlanes[0]), bf16),
            jax.ShapeDtypeStruct((in_local, n_dp, qlanes[1]), bf16),
            jax.ShapeDtypeStruct((9, in_local, LANES), f32),
            jax.ShapeDtypeStruct((9, out_rows, LANES), f32),
            jax.ShapeDtypeStruct((in_local, LANES), f32),
        ]
        + [jax.ShapeDtypeStruct((1, LANES), f32)] * 6,
        in_specs=[vmem] * 9,
        out_specs=[hbm] * 7 + [vmem] * 6,
        scratch_shapes=[
            V((in_local, n_dp, qlanes[0]), bf16),
            V((in_local, n_dp, qlanes[1]), bf16),
            pltpu.SemaphoreType.DMA((9,)),
        ],
        compiler_params=pltpu.CompilerParams(vmem_limit_bytes=32 * 2**20),
        name="closing",
    )
    total_rows = n_dp * in_local
    turn = np.zeros((total_rows, total_rows), np.float32)
    for c in range(in_local):
        for j in range(n_dp):
            turn[c * n_dp + j, j * in_local + c] = 1.0
    return (main, last) + tuple(m.astype(jnp.bfloat16) for m in (*patch_ms, cells_m, turn))


def fused_body(
    input_a, input_b, boxes_a, boxes_b, weight_first, weight_second, weight_short,
    gain_first, shift_first, gain_second, shift_second, gain_short, shift_short,
    upstream_a, upstream_b,
):
    n_dp = lax.axis_size("dp")
    chan_part = weight_first.shape[2]
    in_local = input_a.shape[0]
    main, last, *matrices = make_fused(
        n_dp, in_local, (boxes_a.shape[0], boxes_b.shape[0]), (SA, SB),
        weight_first.shape[1], chan_part,
    )
    vectors = [
        v.reshape(1, chan_part)
        for v in (gain_first, shift_first, gain_second, shift_second, gain_short, shift_short)
    ]
    mid = main(
        input_a, input_b, boxes_a.T, boxes_b.T, weight_first, weight_second, weight_short,
        *vectors, upstream_a.T, upstream_b.T, *matrices,
    )
    res = last(*mid)
    return (
        res[0].T, res[1].T,
        res[2].reshape(in_local, n_dp, 1, -1), res[3].reshape(in_local, n_dp, 1, -1),
        res[4], res[5], res[6],
    ) + tuple(v.reshape(chan_part) for v in res[7:])


def choose_body(mesh):
    return fused_body if mesh.shape["dp"] == 8 and mesh.shape["chan"] == 4 else plain_body


def solution(mesh):
    placed = (
        P("dp", None),
        P("dp", None),
        P("dp", None),
        P("dp", None),
        P(None, None, "chan"),
        P(None, None, "chan"),
        P(None, "chan"),
        P("chan"),
        P("chan"),
        P("chan"),
        P("chan"),
        P("chan"),
        P("chan"),
        P("chan", "dp"),
        P("chan", "dp"),
    )
    return jax.shard_map(
        choose_body(mesh),
        mesh=mesh,
        in_specs=placed,
        out_specs=(
            P("chan", "dp"),
            P("chan", "dp"),
            P("dp", None, "chan", None),
            P("dp", None, "chan", None),
            P(None, "dp", "chan"),
            P(None, "dp", "chan"),
            P("dp", "chan"),
            P("chan"),
            P("chan"),
            P("chan"),
            P("chan"),
            P("chan"),
            P("chan"),
        ),
        check_vma=False,
    )
```

```python
import jax
import jax.numpy as jnp
from jax import lax
import numpy as np
from jax.experimental import pallas as pl
from jax.experimental.pallas import tpu as pltpu
from jax.sharding import PartitionSpec as P

SA = 14
SB = 6


epsilon = 1e-05


def box_mask(box_rows, extent):
    positions = jnp.arange(extent, dtype=jnp.int32)[None, :]
    row_inside = (positions >= box_rows[:, 0:1]) & (positions < box_rows[:, 0:1] + box_rows[:, 2:3])
    col_inside = (positions >= box_rows[:, 1:2]) & (positions < box_rows[:, 1:2] + box_rows[:, 3:4])
    return (row_inside[:, :, None] & col_inside[:, None, :]).astype(jnp.float32)


def taps_strided(feature, image_count, extent):
    channels = feature.shape[0]
    output_side = extent // 2
    padded = jnp.pad(
        feature.reshape(channels, image_count, extent, extent), ((0, 0), (0, 0), (1, 1), (1, 1))
    )
    pieces = [
        padded[:, :, tap_row : tap_row + extent : 2, tap_col : tap_col + extent : 2]
        for tap_row in range(3)
        for tap_col in range(3)
    ]
    return jnp.stack(pieces, axis=0).reshape(9 * channels, image_count * output_side * output_side)


def taps_plain(feature, image_count, extent):
    channels = feature.shape[0]
    padded = jnp.pad(
        feature.reshape(channels, image_count, extent, extent), ((0, 0), (0, 0), (1, 1), (1, 1))
    )
    pieces = [
        padded[:, :, tap_row : tap_row + extent, tap_col : tap_col + extent]
        for tap_row in range(3)
        for tap_col in range(3)
    ]
    return jnp.stack(pieces, axis=0).reshape(9 * channels, image_count * extent * extent)


def untaps_plain(columns, channels, image_count, extent):
    pieces = columns.reshape(9, channels, image_count, extent, extent)
    running = jnp.zeros((channels, image_count, extent + 2, extent + 2), jnp.float32)
    for tap_row in range(3):
        for tap_col in range(3):
            running = running + jnp.pad(
                pieces[3 * tap_row + tap_col],
                ((0, 0), (0, 0), (tap_row, 2 - tap_row), (tap_col, 2 - tap_col)),
            )
    return running[:, :, 1:-1, 1:-1].reshape(channels, image_count * extent * extent)


def untaps_strided(columns, shortcut, channels, image_count, extent):
    output_side = extent // 2
    pieces = columns.reshape(9, channels, image_count, output_side, output_side)
    parity_sums = {}
    for tap_row in range(3):
        for tap_col in range(3):
            block_row = tap_row // 2
            block_col = tap_col // 2
            placed = jnp.pad(
                pieces[3 * tap_row + tap_col],
                ((0, 0), (0, 0), (block_row, 1 - block_row), (block_col, 1 - block_col)),
            )
            parity = (tap_row % 2, tap_col % 2)
            parity_sums[parity] = (
                placed if parity not in parity_sums else parity_sums[parity] + placed
            )
    direct = jnp.pad(
        shortcut.reshape(channels, image_count, output_side, output_side),
        ((0, 0), (0, 0), (0, 1), (0, 1)),
    )
    parity_sums[1, 1] = parity_sums[1, 1] + direct
    rows_even = jnp.stack([parity_sums[0, 0], parity_sums[0, 1]], axis=-1)
    rows_odd = jnp.stack([parity_sums[1, 0], parity_sums[1, 1]], axis=-1)
    padded = jnp.stack([rows_even, rows_odd], axis=3).reshape(
        channels, image_count, extent + 2, extent + 2
    )
    return padded[:, :, 1:-1, 1:-1].reshape(channels, image_count * extent * extent)


def contract_first(weights, columns):
    return lax.dot_general(
        weights, columns, (((0,), (0,)), ((), ())), preferred_element_type=jnp.float32
    )


def weight_product(columns, gradient):
    return lax.dot_general(
        columns, gradient, (((1,), (1,)), ((), ())), preferred_element_type=jnp.float32
    )


def swish_slope(values):
    logistic = jax.nn.sigmoid(values)
    return logistic * (1.0 + values * (1.0 - logistic))


def moments(values, valid_list):
    running = 0.0
    squares = 0.0
    for tensor, valid in zip(values, valid_list):
        widened = tensor.astype(jnp.float32)
        running = running + jnp.sum(widened * valid, axis=1)
        squares = squares + jnp.sum(widened * widened * valid, axis=1)
    return (running, squares)


def standardize(values, running, squares, population):
    mean_value = running / population
    variance = squares / population - mean_value * mean_value
    scaling = lax.rsqrt(variance + epsilon)
    return (
        [
            (tensor.astype(jnp.float32) - mean_value[:, None]) * scaling[:, None]
            for tensor in values
        ],
        scaling,
    )


def norm_back(gradient, normed, valid, scaling, gain_values, shift_sum, gain_sum, population):
    return (gain_values * scaling)[:, None] * (
        gradient - valid * (shift_sum[:, None] + normed * gain_sum[:, None]) / population
    )


def plain_body(
    input_a,
    input_b,
    boxes_a,
    boxes_b,
    weight_first,
    weight_second,
    weight_short,
    gain_first,
    shift_first,
    gain_second,
    shift_second,
    gain_short,
    shift_short,
    upstream_a,
    upstream_b,
):
    image_groups = lax.axis_size("dp")
    in_local = input_a.shape[0]
    chan_in = weight_first.shape[1]
    chan_part = weight_first.shape[2]
    chan_full = weight_second.shape[1]
    image_counts = (boxes_a.shape[0], boxes_b.shape[0])
    extents = (SA, SB)
    whole_a, whole_b = (
        lax.all_to_all(
            input_a.reshape(in_local, image_groups, -1),
            "dp",
            split_axis=1,
            concat_axis=0,
            tiled=True,
        ),
        lax.all_to_all(
            input_b.reshape(in_local, image_groups, -1),
            "dp",
            split_axis=1,
            concat_axis=0,
            tiled=True,
        ),
    )
    features = (whole_a.reshape(chan_in, -1), whole_b.reshape(chan_in, -1))
    valid_list = (
        box_mask(boxes_a, SA // 2).reshape(1, -1),
        box_mask(boxes_b, SB // 2).reshape(1, -1),
    )
    first_mat = weight_first.reshape(9 * chan_in, chan_part)
    second_mat = weight_second.reshape(9 * chan_full, chan_part)
    first_cols = []
    sampled = []
    first_z = []
    short_z = []
    for feature, image_count, extent in zip(features, image_counts, extents):
        columns = taps_strided(feature, image_count, extent)
        picked = feature.reshape(chan_in, image_count, extent, extent)[:, :, ::2, ::2].reshape(
            chan_in, -1
        )
        first_cols.append(columns)
        sampled.append(picked)
        first_z.append(contract_first(first_mat, columns).astype(jnp.bfloat16))
        short_z.append(contract_first(weight_short, picked).astype(jnp.bfloat16))
    sum_first, square_first = moments(first_z, valid_list)
    sum_short, square_short = moments(short_z, valid_list)
    population = jnp.sum(valid_list[0]) + jnp.sum(valid_list[1])
    sum_first, square_first, sum_short, square_short, population = lax.psum(
        (sum_first, square_first, sum_short, square_short, population), "dp"
    )
    normed_first, scaling_first = standardize(first_z, sum_first, square_first, population)
    normed_short, scaling_short = standardize(short_z, sum_short, square_short, population)
    before_first = [normed * gain_first[:, None] + shift_first[:, None] for normed in normed_first]
    outgoing_a = (jax.nn.silu(before_first[0]) * valid_list[0]).astype(jnp.bfloat16)
    outgoing_b = (jax.nn.silu(before_first[1]) * valid_list[1]).astype(jnp.bfloat16)
    gathered_a, gathered_b = (
        lax.all_gather(outgoing_a, "chan", axis=0, tiled=True),
        lax.all_gather(outgoing_b, "chan", axis=0, tiled=True),
    )
    second_cols = []
    second_z = []
    for gathered, image_count, extent in zip((gathered_a, gathered_b), image_counts, extents):
        columns = taps_plain(gathered, image_count, extent // 2)
        second_cols.append(columns)
        second_z.append(contract_first(second_mat, columns).astype(jnp.bfloat16))
    sum_second, square_second = moments(second_z, valid_list)
    sum_second, square_second = lax.psum((sum_second, square_second), "dp")
    normed_second, scaling_second = standardize(second_z, sum_second, square_second, population)
    summed_pre = [
        main_part * gain_second[:, None]
        + shift_second[:, None]
        + side_part * gain_short[:, None]
        + shift_short[:, None]
        for main_part, side_part in zip(normed_second, normed_short)
    ]
    outputs = [
        (jax.nn.silu(tensor) * valid).astype(jnp.bfloat16)
        for tensor, valid in zip(summed_pre, valid_list)
    ]
    tail_grads = [
        upstream.astype(jnp.float32) * valid * swish_slope(tensor)
        for upstream, valid, tensor in zip((upstream_a, upstream_b), valid_list, summed_pre)
    ]
    shift_tail = sum((jnp.sum(gradient, axis=1) for gradient in tail_grads))
    gain_tail = sum(
        (jnp.sum(gradient * normed, axis=1) for gradient, normed in zip(tail_grads, normed_second))
    )
    gain_side = sum(
        (jnp.sum(gradient * normed, axis=1) for gradient, normed in zip(tail_grads, normed_short))
    )
    shift_tail, gain_tail, gain_side = lax.psum((shift_tail, gain_tail, gain_side), "dp")
    grad_second_local = 0.0
    partial_hidden = []
    short_dz = []
    for index_group in range(2):
        valid = valid_list[index_group]
        dz_second = norm_back(
            tail_grads[index_group],
            normed_second[index_group],
            valid,
            scaling_second,
            gain_second,
            shift_tail,
            gain_tail,
            population,
        ).astype(jnp.bfloat16)
        dz_short = norm_back(
            tail_grads[index_group],
            normed_short[index_group],
            valid,
            scaling_short,
            gain_short,
            shift_tail,
            gain_side,
            population,
        ).astype(jnp.bfloat16)
        short_dz.append(dz_short)
        grad_second_local = grad_second_local + weight_product(second_cols[index_group], dz_second)
        back_cols = jnp.dot(second_mat, dz_second, preferred_element_type=jnp.float32)
        partial_hidden.append(
            untaps_plain(back_cols, chan_full, image_counts[index_group], extents[index_group] // 2)
        )
    hidden_a, hidden_b = (
        lax.psum_scatter(
            partial_hidden[0].astype(jnp.bfloat16), "chan", scatter_dimension=0, tiled=True
        ).astype(jnp.float32),
        lax.psum_scatter(
            partial_hidden[1].astype(jnp.bfloat16), "chan", scatter_dimension=0, tiled=True
        ).astype(jnp.float32),
    )
    head_grads = [
        hidden * valid * swish_slope(tensor)
        for hidden, valid, tensor in zip((hidden_a, hidden_b), valid_list, before_first)
    ]
    shift_head = sum((jnp.sum(gradient, axis=1) for gradient in head_grads))
    gain_head = sum(
        (jnp.sum(gradient * normed, axis=1) for gradient, normed in zip(head_grads, normed_first))
    )
    shift_head, gain_head = lax.psum((shift_head, gain_head), "dp")
    grad_first_local = 0.0
    grad_short_local = 0.0
    partial_inputs = []
    for index_group in range(2):
        valid = valid_list[index_group]
        dz_first = norm_back(
            head_grads[index_group],
            normed_first[index_group],
            valid,
            scaling_first,
            gain_first,
            shift_head,
            gain_head,
            population,
        ).astype(jnp.bfloat16)
        grad_first_local = grad_first_local + weight_product(first_cols[index_group], dz_first)
        grad_short_local = grad_short_local + weight_product(
            sampled[index_group], short_dz[index_group]
        )
        back_cols = jnp.dot(first_mat, dz_first, preferred_element_type=jnp.float32)
        back_short = jnp.dot(
            weight_short, short_dz[index_group], preferred_element_type=jnp.float32
        )
        flat_input = untaps_strided(
            back_cols, back_short, chan_in, image_counts[index_group], extents[index_group]
        )
        partial_inputs.append(flat_input.reshape(chan_in, 1, lax.axis_size("chan"), -1))
    arrived_a, arrived_b = (
        lax.all_to_all(
            partial_inputs[0].astype(jnp.bfloat16), "dp", split_axis=0, concat_axis=1, tiled=True
        ).astype(jnp.float32),
        lax.all_to_all(
            partial_inputs[1].astype(jnp.bfloat16), "dp", split_axis=0, concat_axis=1, tiled=True
        ).astype(jnp.float32),
    )
    summed_a, summed_b = (
        lax.psum_scatter(
            arrived_a.astype(jnp.bfloat16), "chan", scatter_dimension=2, tiled=True
        ).astype(jnp.float32),
        lax.psum_scatter(
            arrived_b.astype(jnp.bfloat16), "chan", scatter_dimension=2, tiled=True
        ).astype(jnp.float32),
    )
    grad_input_a = summed_a.astype(jnp.bfloat16)
    grad_input_b = summed_b.astype(jnp.bfloat16)
    grad_first_local = grad_first_local.reshape(9, chan_in, chan_part)
    grad_second_local = grad_second_local.reshape(9, chan_full, chan_part)
    total_first, total_second, total_short = lax.psum(
        (grad_first_local, grad_second_local, grad_short_local), "dp"
    )
    position = lax.axis_index("dp")
    rows_first = chan_in // image_groups
    rows_second = chan_full // image_groups
    grad_first = lax.dynamic_slice_in_dim(total_first, position * rows_first, rows_first, 1)
    grad_second = lax.dynamic_slice_in_dim(total_second, position * rows_second, rows_second, 1)
    grad_short = lax.dynamic_slice_in_dim(total_short, position * rows_first, rows_first, 0)
    return (
        outputs[0],
        outputs[1],
        grad_input_a,
        grad_input_b,
        grad_first,
        grad_second,
        grad_short,
        gain_head,
        shift_head,
        gain_tail,
        shift_tail,
        gain_side,
        shift_tail,
    )


MESH = pl.DeviceIdType.MESH
TAPS = tuple((a, b) for a in range(3) for b in range(3))
PLANE_TAPS = (
    ((1, 1),),
    ((1, 0), (1, 2)),
    ((0, 1), (2, 1)),
    ((0, 0), (0, 2), (2, 0), (2, 2)),
)
ORDER = [tap for taps in PLANE_TAPS for tap in taps]
LANES = 128


class Links:
    def __init__(self, send_sems, recv_sems):
        self.send_sems, self.recv_sems = send_sems, recv_sems
        self.sends = self.slots = self.started = 0
        self.open, self.free = [], []
        self.spare, self.spare_dp = set(), set()

    def slot(self, count=1, dp_only=False):
        for spare in (self.spare_dp, self.spare) if dp_only else (self.spare,):
            for first in sorted(spare):
                run = set(range(first, first + count))
                if run <= spare:
                    spare -= run
                    return first
        first = self.slots
        self.slots += count
        return first

    def send(self, source, target, slot, where):
        if not self.free:
            self.free.append(self.sends)
            self.sends += 1
        index = self.free.pop(0)
        copy = pltpu.make_async_remote_copy(
            source, target, self.send_sems.at[index], self.recv_sems.at[slot],
            device_id=where, device_id_type=MESH,
        )
        copy.start()
        self.open.append((copy, index))
        self.started += 1

    def mark(self):
        return self.started

    def settle(self, last):
        count = last - self.started + len(self.open)
        for copy, index in self.open[:count]:
            copy.wait_send()
            self.free.append(index)
        self.open = self.open[count:]

    def arrived(self, target, slot, where):
        pltpu.make_async_remote_copy(
            target, target, self.send_sems.at[0], self.recv_sems.at[slot],
            device_id=where, device_id_type=MESH,
        ).wait_recv()

    def drain(self):
        self.settle(self.mark())


def mm(a, b, ca, cb):
    return lax.dot_general(a, b, (((ca,), (cb,)), ((), ())), preferred_element_type=jnp.float32)


def lanes_cat(parts):
    return jnp.concatenate(parts, axis=1) if len(parts) > 1 else parts[0]


def quarter_matrices(images, sides, segments, seg_lane, seg_row, q_rows, lanes):
    def lane(g, image, row, col):
        for (seg_g, r0, r1), first in zip(segments, seg_lane):
            if seg_g == g and 2 * r0 <= row < 2 * r1:
                return first + (image * 2 * (r1 - r0) + row - 2 * r0) * sides[g] + col

    taps = np.zeros((9, q_rows, lanes), np.float32)
    for (g, r0, r1), first in zip(segments, seg_row):
        half = sides[g] // 2
        for r in range(r0, r1):
            for s in range(half):
                for image in range(images[g]):
                    target = first + ((r - r0) * half + s) * images[g] + image
                    for t, (a, b) in enumerate(TAPS):
                        row, col = 2 * r + a - 1, 2 * s + b - 1
                        if row >= 0 and col >= 0:
                            taps[t, target, lane(g, image, row, col)] = 1.0
    sizes = [n * side * side for n, side in zip(images, sides)]
    cells = np.zeros((sum(sizes), lanes), np.float32)
    for g, (n, side) in enumerate(zip(images, sides)):
        for image in range(n):
            for row in range(side):
                for col in range(side):
                    cell = (row // 2) * (side // 2) + col // 2
                    target = g * sizes[0] + (cell * 4 + 2 * (row % 2) + col % 2) * n + image
                    cells[target, lane(g, image, row, col)] = 1.0
    return taps, cells


def regroup(value, runs):
    return jnp.concatenate([value[:, a:b] for a, b in runs], axis=1)


def fold(value):
    half = value.shape[1] // 2
    left = lax.broadcasted_iota(jnp.int32, (1, 1, LANES), 2) < LANES // 2
    return jnp.where(left, value[:, :half], pltpu.roll(value[:, half:], LANES // 2, 2))


def unfold(value):
    return jnp.concatenate([value, pltpu.roll(value, LANES // 2, 2)], axis=1)


def sigma(v):
    return 0.5 * jnp.tanh(0.5 * v) + 0.5


class Reduce:
    def __init__(self, net, i, k, part, bufs, windows, b4=None):
        self.b4 = b4
        self.net, self.part, self.windows = net, part, windows
        self.b1, self.s1, self.b2, self.s2, self.b3 = bufs
        self.ix, self.pz, self.hz = i % 2, (i // 2) % 2, i // 4
        self.peers = (
            (i + 1 - 2 * self.ix, k),
            (i + 2 - 4 * self.pz, k),
            (i + 4 - 8 * self.hz, k),
        )
        self.slots = [net.slot(3, True) for _ in windows]

    def first(self, w):
        cols = self.windows[w]
        self.net.send(
            self.part.at[:, :, 1 - self.ix, :, cols], self.b1.at[:, :, :, cols],
            self.slots[w], self.peers[0],
        )

    def second(self, w):
        cols = self.windows[w]
        self.net.arrived(self.b1.at[:, :, :, cols], self.slots[w], self.peers[0])
        for h in range(2):
            for p in range(2):
                value = self.part[h, p, self.ix, :, cols].astype(jnp.float32)
                value = value + self.b1[h, p, :, cols].astype(jnp.float32)
                self.s1[h, p, :, cols] = value.astype(jnp.bfloat16)
        self.net.send(
            self.s1.at[:, 1 - self.pz, :, cols], self.b2.at[:, :, cols],
            self.slots[w] + 1, self.peers[1],
        )

    def second_of(self, w, value):
        cols = self.windows[w]
        self.s1[:, :, :, cols] = value.reshape(2, 2, -1, value.shape[1])
        self.net.send(
            self.s1.at[:, 1 - self.pz, :, cols], self.b2.at[:, :, cols],
            self.slots[w] + 1, self.peers[1],
        )

    def spread_of(self, w, value):
        cols = self.windows[w]
        self.s1[:, :, :, cols] = value.reshape(2, 2, -1, value.shape[1])
        z = 2 * self.hz + self.pz
        self.direct = self.net.slot(4, True)
        for d in range(1, 4):
            to = (z + d) % 4
            self.net.send(
                self.s1.at[to // 2, to % 2, :, cols], self.b4.at[z],
                self.direct + z, (2 * to + self.ix, self.peers[0][1]),
            )

    def spread_last(self, w):
        cols = self.windows[w]
        z = 2 * self.hz + self.pz
        value = self.s1[self.hz, self.pz, :, cols].astype(jnp.float32)
        for d in range(1, 4):
            to = (z + d) % 4
            self.net.arrived(self.b4.at[to], self.direct + to, (2 * to + self.ix, self.peers[0][1]))
            value = value + self.b4[to].astype(jnp.float32)
        return value

    def third(self, w):
        cols = self.windows[w]
        self.net.arrived(self.b2.at[:, :, cols], self.slots[w] + 1, self.peers[1])
        for h in range(2):
            value = self.s1[h, self.pz, :, cols].astype(jnp.float32)
            value = value + self.b2[h, :, cols].astype(jnp.float32)
            self.s2[h, :, cols] = value.astype(jnp.bfloat16)
        self.net.send(
            self.s2.at[1 - self.hz, :, cols], self.b3.at[:, cols],
            self.slots[w] + 2, self.peers[2],
        )

    def last(self, w):
        cols = self.windows[w]
        self.net.arrived(self.b3.at[:, cols], self.slots[w] + 2, self.peers[2])
        return self.s2[self.hz, :, cols].astype(jnp.float32) + self.b3[:, cols].astype(jnp.float32)


def make_fused(n_dp, in_local, images, sides, chan_in, chan_part):
    f32, bf16 = jnp.float32, jnp.bfloat16
    halves = tuple(side // 2 for side in sides)
    sizes = tuple(h * h * n for h, n in zip(halves, images))
    rows = sum(sizes)
    quarter = tuple(n // 4 for n in images)
    qlanes = tuple(q * side * side for q, side in zip(quarter, sides))
    slab_lanes = -(-sum(qlanes) // LANES) * LANES
    chan_full = 4 * chan_part
    out_rows = chan_full // n_dp
    starts = (0, sizes[0])
    widths = tuple(h * n for h, n in zip(halves, images))
    chunks = [(g, r, starts[g] + r * widths[g], widths[g]) for g in range(2) for r in range(halves[g])]
    win = [-(-q // LANES) * LANES for q in qlanes]
    b_tile = qlanes[0] // LANES * LANES
    n_sends, n_slots = 68, 107
    b_skip = qlanes[0] - b_tile
    rs = halves[0] // 2
    segments = [(1, 0, halves[1]), (0, 0, rs), (0, rs, halves[0])]
    seg_lane, runs = [], []
    lane_of = 0
    for g, r0, r1 in segments:
        side, base = sides[g], (0, qlanes[0])[g]
        seg_lane.append(lane_of)
        lane_of += quarter[g] * 2 * (r1 - r0) * side
        runs += [
            (base + (image * side + 2 * r0) * side, base + (image * side + 2 * r1) * side)
            for image in range(quarter[g])
        ]
    runs.append((sum(qlanes), slab_lanes))
    at, order = 0, []
    for a, b in runs:
        order.append((a, at, at + b - a))
        at += b - a
    back_runs = [(a, b) for _, a, b in sorted(order)]
    cut_lane = -(-seg_lane[2] // LANES) * LANES
    lane_parts = (slice(0, cut_lane), slice(cut_lane, slab_lanes))
    seg_cells = [(r1 - r0) * halves[g] for g, r0, r1 in segments]
    seg_rows = [cells * quarter[seg[0]] for cells, seg in zip(seg_cells, segments)]
    top = -(-(seg_rows[0] + seg_rows[1]) // 16) * 16
    seg_row = [0, seg_rows[0], top]
    q_rows = top + -(-seg_rows[2] // 16) * 16
    row_parts = (slice(0, top), slice(top, q_rows))
    patch_win = (slice(0, cut_lane), slice(seg_lane[1] // LANES * LANES, slab_lanes))
    patch_m, cells_m = quarter_matrices(
        quarter, sides, segments, seg_lane, seg_row, q_rows, slab_lanes
    )
    patch_ms = [
        np.concatenate([m[rows_, lanes_] for m in patch_m], axis=0)
        for rows_, lanes_ in zip(row_parts, patch_win)
    ]
    low_lane = seg_lane[1] // LANES * LANES
    last_lane = slab_lanes - LANES
    assert sum(qlanes) - last_lane <= LANES // 2
    out_lanes = [slice(cut_lane, last_lane), slice(0, low_lane), slice(low_lane, cut_lane)]
    back_pieces = (((0, 0, 2),), ((0, 2, halves[0] - 1),), ((0, halves[0] - 1, halves[0]), (1, 0, halves[1])))
    row_halves = [
        slice(starts[p[0][0]] + p[0][1] * widths[p[0][0]], starts[p[-1][0]] + p[-1][2] * widths[p[-1][0]])
        for p in back_pieces
    ]
    cols2 = (slice(0, 4 * LANES), slice(4 * LANES, 9 * LANES))
    cols1 = (slice(6 * LANES, 10 * LANES), slice(0, 6 * LANES))

    def kernel(*refs):
        (xa_h, xb_h, bxa_h, bxb_h, w1_h, w2_h, ws_h, g1_h, b1_h, g2_h, b2_h, gs_h, bs_h, ua_h, ub_h,
         pm0_h, pm1_h, cells_h,
         turn_h,
         oa, ob, gr, grf, gw1, gws, gw2, vecs, turn,
         xa, xb, bxa, bxb, w1g, w2, wsg, vg, g2, b2, gs, bs, ua, ub, pm0, pm1, cells,
         xs, xt, xr, zb, zsq, zsr, zg, zpa, zpb, valid, vq, hat, mask, zs, a1a, a1b,
         cslots, slots, stat, up, outr, gv, dza, dzb, dzma, dzmb, apk, arx, gacc, dzsr,
         dd, hp, hr1, hs, hr2, gu, d1a, d1b,
         p22, p23, p24, p25, p26, wg1, p11, p12, p13, p14, p15,
         sq, si, dq, di, gt, gtf, lsem, ssem, rsem) = refs
        i, k = lax.axis_index("dp"), lax.axis_index("chan")
        k1 = k + 1 - 2 * (k % 2)
        k2 = (k + 2) % 4
        k3 = (k1 + 2) % 4
        ix = i % 2
        mate = (i + 1 - 2 * ix, k)
        net = Links(ssem, rsem)
        bits = n_dp.bit_length() - 1

        def flip(d):
            j = i
            for b in range(bits):
                if d >> b & 1:
                    j = j + (1 << b) * (1 - 2 * ((i // (1 << b)) % 2))
            return j

        peers = [flip(d) for d in sorted(range(n_dp), key=lambda d: (d == 0, -(d >> 1), d & 1))]
        peers, home = peers[:-1], peers[-1]
        zp, a1, dz, d1 = (zpa, zpb), (a1a, a1b), (dza, dzb), (d1a, d1b)
        dzm = (dzma, dzmb)

        def flat(value):
            return value.reshape(-1, value.shape[-1])

        def zeros(count):
            return [jnp.zeros((8, LANES), f32)] * count

        loads = {}
        pairs_of = (
            ("xa", xa_h, xa), ("xb", xb_h, xb),
            ("w1", w1_h, w1g.at[k]), ("ws", ws_h, wsg.at[k]), ("g1", g1_h, vg.at[k, 0]), ("b1", b1_h, vg.at[k, 1]),
            ("bxa", bxa_h, bxa), ("bxb", bxb_h, bxb), ("pm0", pm0_h, pm0), ("pm1", pm1_h, pm1),
            ("ua", ua_h, ua), ("ub", ub_h, ub), ("g2", g2_h, g2),
            ("b2", b2_h, b2), ("gs", gs_h, gs), ("bs", bs_h, bs), ("w2", w2_h, w2), ("cells", cells_h, cells),
            ("turn", turn_h, turn),
        )
        for index, (name, source, target) in enumerate(pairs_of):
            loads[name] = pltpu.make_async_copy(source, target, lsem.at[index])
        loads["xa"].start()
        loads["xb"].start()

        def need(*names):
            for name in names:
                loads.pop(name).wait()

        barrier = pltpu.get_barrier_semaphore()
        for j in peers:
            pl.semaphore_signal(barrier, inc=1, device_id=(j, k), device_id_type=MESH)
        for where in (k1, k2, k3):
            pl.semaphore_signal(barrier, inc=1, device_id=(i, where), device_id_type=MESH)

        need("xa", "xb")
        for copy in loads.values():
            copy.start()
        lane = lax.broadcasted_iota(jnp.int32, (in_local, LANES), 1)
        for d, j in enumerate(peers + [home]):
            begin = 4 * qlanes[0] * j + qlanes[0] * k
            tile = begin // LANES
            part_a = xa[:, pl.ds(pl.multiple_of(tile * LANES, LANES), win[0])].astype(f32)
            part_a = pltpu.roll(part_a, (win[0] - (begin - tile * LANES)) % win[0], 1)
            begin = 4 * qlanes[1] * j + qlanes[1] * k
            tile = begin // LANES
            part_b = xb[:, pl.ds(pl.multiple_of(tile * LANES, LANES), win[1])].astype(f32)
            part_b = jnp.concatenate([part_b, jnp.zeros((in_local, LANES), f32)], axis=1)
            wide = win[1] + LANES
            part_b = pltpu.roll(part_b, (wide + b_skip - (begin - tile * LANES)) % wide, 1)
            seam = jnp.where(lane < b_skip, part_a[:, b_tile : b_tile + LANES], part_b[:, :LANES])
            xs[d * in_local : (d + 1) * in_local, :] = jnp.concatenate(
                [part_a[:, :b_tile], seam, part_b[:, LANES : slab_lanes - b_tile]], axis=1
            ).astype(bf16)
        slot_x = [net.slot(n_dp) for _ in lane_parts]
        n_via = 2
        via = [pl.ds((9 - n_via) * e, n_via) for e in (ix, 1 - ix)]
        w_taps = [via[0], slice(n_via, 5), slice(5, 9 - n_via)]
        slot_w = [net.slot(4) for _ in range(6)]

        def weight_refs(q):
            return [w1g.at[q, taps] for taps in w_taps] + [wsg.at[q], vg.at[q], w1g.at[q, via[1]]]

        ordered = regroup(xs[...], runs)
        for c, cols in enumerate(lane_parts):
            moved = ordered[:, cols]
            xt[:, :, cols] = moved.reshape(n_dp, in_local, moved.shape[1])
            xr[i, :, cols] = moved[-in_local:]
            if c == 0:
                pl.semaphore_wait(barrier, n_dp + 2)
            for d, j in enumerate(peers):
                net.send(xt.at[d, :, cols], xr.at[i, :, cols], slot_x[c] + i, (j, k))
            if c == 0:
                need("w1", "ws", "g1", "b1")
                for ref, slot in zip(weight_refs(k)[:5], slot_w):
                    net.send(ref, ref, slot + k, (i, k2))
                for ref, slot in zip(weight_refs(k), slot_w):
                    net.send(ref, ref, slot + k, (i, k1))

        def weights_on(n):
            ref = weight_refs(k2)[n]
            net.arrived(ref, slot_w[n] + k2, mate if n == 5 else (i, k2))
            net.send(ref, ref, slot_w[n] + k2, (i, k1))
            if n == 0:
                net.send(ref, ref, slot_w[5] + k2, mate)

        def weights_in(parts):
            for q in (k1, k3):
                for n in parts:
                    net.arrived(weight_refs(q)[n], slot_w[n] + q, (i, k1))

        for buf in (zpa, zpb, a1a, a1b, dza, dzb, dzma, dzmb, d1a, d1b):
            side = buf.shape[1] if len(buf.shape) == 5 else buf.shape[0]
            lead = (slice(None),) if len(buf.shape) == 5 else ()
            for edge in (0, side - 1):
                for index in (lead + (edge,), lead + (slice(None), edge)):
                    region = buf.at[index]
                    region[...] = jnp.zeros(region.shape, buf.dtype)
        need("bxa", "bxb", "ua", "ub")
        population = zeros(1)[0]
        low = lax.broadcasted_iota(jnp.int32, (8, LANES), 0) < 4
        for g, box in enumerate((bxa, bxb)):
            n, half, count = images[g], halves[g], quarter[g]
            diag = lax.broadcasted_iota(jnp.int32, (n, n), 0) == lax.broadcasted_iota(jnp.int32, (n, n), 1)
            ends = [
                jnp.sum(jnp.where(diag, box[q : q + 1, :].astype(f32), 0.0), axis=1, keepdims=True)
                for q in range(4)
            ]
            ends = [jnp.broadcast_to(e, (n, LANES)) for e in ends]
            ends[2], ends[3] = ends[0] + ends[2], ends[1] + ends[3]

            def inside(ends, r, s):
                both = (r >= ends[0]) & (r < ends[2]) & (s >= ends[1]) & (s < ends[3])
                return both.astype(f32)

            for r in range(half):
                for s in range(half):
                    cell = inside(ends, r, s)
                    begin = starts[g] + (r * half + s) * n
                    valid[begin : begin + n, :] = cell
                    population = population + jnp.sum(cell.reshape(n // 8, 8, LANES), axis=0)
            mine = [pltpu.roll(e, (n - count * k) % n, 0)[:8] for e in ends]
            if count < 8:
                mine = [jnp.where(low, e, pltpu.roll(e, 4, 0)) for e in mine]
            for (seg_g, r0, r1), first, cells_n in zip(segments, seg_row, seg_cells):
                if seg_g != g:
                    continue
                per = 8 // count
                for t in range(-(-cells_n // per)):
                    spots = [divmod(min(per * t + e, cells_n - 1), half) for e in range(per)]
                    spots = [(float(r0 + r), float(s)) for r, s in spots]
                    if per == 2:
                        r, s = (jnp.where(low, spots[0][e], spots[1][e]) for e in range(2))
                    else:
                        r, s = spots[0]
                    cell = inside(mine, r, s)
                    if per == 2 and per * t + 1 >= cells_n:
                        cell = jnp.where(low, cell, 0.0)
                    vq[first + 8 * t : first + 8 * t + 8, :] = cell
        population = jnp.broadcast_to(jnp.sum(population, axis=0, keepdims=True), (8, LANES))
        for g, source in enumerate((ua, ub)):
            n, count = images[g], halves[g] ** 2
            gu[starts[g] : starts[g] + sizes[g], :] = source[...].astype(f32)
            for cell in range(count):
                up[starts[g] + cell * n : starts[g] + (cell + 1) * n, :] = gu[
                    pl.ds(starts[g] + cell, n, stride=count), :
                ]

        def rowsum(value):
            return jnp.sum(value.reshape(-1, 8, value.shape[-1]), axis=0)

        def message(sums):
            parts = [jnp.sum(v, axis=0, keepdims=True) if v.shape[0] > 1 else v for v in sums]
            if len(parts) % 8:
                parts.append(jnp.zeros((8 - len(parts) % 8, LANES), f32))
            return jnp.concatenate(parts, axis=0)

        def by_chan(value):
            return [value[:, q * LANES : (q + 1) * LANES] for q in range(4)]

        used = []

        def share(rnd, value):
            mine = slots.at[rnd, i, : value.shape[0]]
            mine[...] = value
            first = net.slot(n_dp, True)
            used.append((first, n_dp))
            for j in peers:
                net.send(mine, mine, first + i, (j, k))
            return first

        def total(rnd, first, count=8):
            for j in peers:
                net.arrived(slots.at[rnd, j, :count], first + j, (j, k))
            return jnp.sum(slots[rnd, :, :count], axis=0)

        def chan_share(rnd, value):
            mine = cslots.at[rnd, k, : value.shape[0]]
            mine[...] = value
            first = net.slot(4)
            used.append((first, 4))
            for where in (k2, k3, k1):
                net.send(mine, mine, first + k, (i, where))
            return first

        def chan_total(rnd, first, count=8):
            for where in (k1, k2, k3):
                net.arrived(cslots.at[rnd, where, :count], first + where, (i, where))
            return jnp.sum(cslots[rnd, :, :count], axis=0)

        pop_first = share(4, population)

        def quarter_in(c):
            for j in peers:
                net.arrived(xr.at[j, :, lane_parts[c]], slot_x[c] + j, (j, k))

        def patches(c):
            whole = jnp.concatenate([xr[q, :, patch_win[c]] for q in range(n_dp)], axis=0)
            value = mm((pm0, pm1)[c][...], whole, 1, 1).astype(bf16)
            count = value.shape[0] // 9
            return [value[t * count : (t + 1) * count] for t in range(9)]

        slot_s = net.slot(4)

        z_cuts = (slice(0, top * 3 // 80 * 16), slice(top * 3 // 80 * 16, top), slice(top, q_rows))
        slot_z = [net.slot(4) for _ in z_cuts]

        def z_send(n):
            for where in (k2, k1):
                net.send(zb.at[k, z_cuts[n]], zb.at[k, z_cuts[n]], slot_z[n] + k, (i, where))

        def conv_taps(taps, some):
            weights = lanes_cat([w1g[q, some].reshape(-1, chan_part) for q in range(4)])
            return mm(lanes_cat(taps[some]), weights, 1, 0)

        def first_conv(c, value, acc):
            part = row_parts[c]
            value = value.astype(bf16)
            zb[k, part, :] = value
            if c == 0:
                z_send(0)
            z = value.astype(f32)
            u = z * lanes_cat([vq[part, :]] * 4)
            return [acc[0] + rowsum(u), acc[1] + rowsum(u * z)]

        def projection(c, patch, acc):
            side = mm(patch, lanes_cat([wsg[q] for q in range(4)]), 1, 0).astype(bf16)
            for q, z in enumerate(by_chan(side)):
                zsq[q, row_parts[c], :] = z
            z = side.astype(f32)
            u = z * lanes_cat([vq[row_parts[c], :]] * 4)
            return [acc[0] + rowsum(u), acc[1] + rowsum(u * z)]

        def act_on(n):
            part = zb.at[k2, z_cuts[n]]
            net.arrived(part, slot_z[n] + k2, (i, k2))
            net.send(part, part, slot_z[n] + k2, (i, k1))

        def act_in(n):
            net.arrived(zb.at[k1, z_cuts[n]], slot_z[n] + k1, (i, k1))
            net.arrived(zb.at[k3, z_cuts[n]], slot_z[n] + k3, (i, k1))

        acc = [jnp.zeros((8, chan_full), f32)] * 2
        need("pm0", "pm1")
        for n in (0, 1, 5, 2):
            weights_on(n)
        quarter_in(0)
        taps = patches(0)
        center = [taps[4]]
        weights_on(3)
        weights_on(4)
        weights_in((0, 1, 5))
        value = conv_taps(taps, slice(0, 5)) + conv_taps(taps, slice(9 - n_via, 9))
        weights_in((2,))
        acc = first_conv(0, value + conv_taps(taps, slice(5, 9 - n_via)), acc)
        quarter_in(1)
        taps = patches(1)
        center.append(taps[4])
        acc = first_conv(1, conv_taps(taps, slice(0, 9)), acc)
        acc = [jnp.sum(v, axis=0, keepdims=True) for v in acc]
        first = chan_share(0, message(sum((by_chan(v) for v in acc), [])))
        gone = net.mark()
        z_send(1)
        z_send(2)
        weights_in((3, 4))
        acc = [jnp.zeros((8, chan_full), f32)] * 2
        for c in range(2):
            acc = projection(c, center[c], acc)
        acc = [jnp.sum(v, axis=0, keepdims=True) for v in acc]
        side_first = share(5, message(sum((by_chan(v) for v in acc), [])))
        zsr[k] = zsq[k]

        need(*list(loads))
        row_cuts = (slice(0, rows // 32 * 16), slice(rows // 32 * 16, rows))
        slot_g0 = [net.slot(4) for _ in row_cuts]
        whole = jnp.concatenate([xr[q] for q in range(n_dp)], axis=0)
        for span in row_cuts:
            zg[k, span, :] = mm(cells[span, :], whole, 1, 1).astype(bf16)
        first = share(0, chan_total(0, first))
        for where in (k2, k3, k1):
            net.send(zsq.at[where], zsr.at[k], slot_s + k, (i, where))
        act_on(0)
        act_on(1)
        act_on(2)
        net.settle(gone)
        side_first = chan_share(2, total(5, side_first))
        gone = net.mark()
        for span, slot in zip(row_cuts, slot_g0):
            for where in (k2, k1):
                net.send(zg.at[k, span], zg.at[k, span], slot + k, (i, where))

        def slab_on(n):
            span, slot = row_cuts[n], slot_g0[n]
            net.arrived(zg.at[k2, span], slot + k2, (i, k2))
            net.send(zg.at[k2, span], zg.at[k2, span], slot + k2, (i, k1))

        def slab_in(n):
            span, slot = row_cuts[n], slot_g0[n]
            net.arrived(zg.at[k1, span], slot + k1, (i, k1))
            net.arrived(zg.at[k3, span], slot + k3, (i, k1))

        inv_pop = 1.0 / total(4, pop_first)[0:1]
        turn_low = lax.broadcasted_iota(jnp.int32, (8, 1), 0) < 4

        def whole_cells(read, c):
            for begin in range(row_parts[c].start, row_parts[c].stop, 16):
                blocks = [read(q, slice(begin, begin + 16)).astype(f32) for q in range(4)]
                for at in (begin, begin + 8):
                    seg = max(e for e in range(3) if seg_row[e] <= at)
                    g, r0, r1 = segments[seg]
                    per = 8 // quarter[g]
                    v = [block[at - begin : at - begin + 8] for block in blocks]
                    cell = (at - seg_row[seg]) // 8 * per
                    if per == 1:
                        found = [jnp.concatenate(v, axis=0)]
                    else:
                        t = [pltpu.roll(e, 4, 0) for e in v]
                        found = [
                            jnp.concatenate(
                                [jnp.where(turn_low, v[0], t[1]), jnp.where(turn_low, v[2], t[3])], axis=0
                            ),
                            jnp.concatenate(
                                [jnp.where(turn_low, t[0], v[1]), jnp.where(turn_low, t[2], v[3])], axis=0
                            ),
                        ]
                    for e, value in enumerate(found):
                        if cell + e < seg_cells[seg]:
                            r, s = divmod(cell + e, halves[g])
                            yield g, r0 + r, s, value

        def gather_cells(c):
            for g, r, s, z in whole_cells(lambda q, span: zb[q, span, :], c):
                begin = starts[g] + (r * halves[g] + s) * images[g]
                hat[begin : begin + images[g], :] = z

        for n in range(2):
            act_in(n)
        gather_cells(0)
        act_in(2)
        gather_cells(1)
        tot = total(0, first)
        stat[0:8, :] = tot
        tot_first = (stat[pl.ds(k, 1), :], stat[pl.ds(4 + k, 1), :])
        def moments(total_, square):
            mean = total_ * inv_pop
            return mean, lax.rsqrt(square * inv_pop - mean * mean + epsilon)

        mean1, sc1 = moments(tot[0:4], tot[4:8])
        mean1, sc1 = (lanes_cat([v[q : q + 1] for q in range(4)]) for v in (mean1, sc1))
        gain1, shift1 = (lanes_cat([vg[q, e] for q in range(4)]) for e in range(2))

        scale1 = sc1 * gain1
        offset1 = shift1 - mean1 * scale1

        def activate(c):
            for g, r0, r1 in (segments[:2], segments[2:])[c]:
                for r in range(r0, r1):
                    for s in range(halves[g]):
                        begin = starts[g] + (r * halves[g] + s) * images[g]
                        span = slice(begin, begin + images[g])
                        v = hat[span, :] * scale1 + offset1
                        act = v * sigma(v) * lanes_cat([valid[span, :]] * 4)
                        a1[g][1 + r, 1 + s] = act.astype(bf16)

        def second_conv(parts, acc):
            value = None
            for a, b in TAPS:
                patch = jnp.concatenate(
                    [flat(a1[g][r0 + a : r1 + a, b : b + halves[g]]) for g, r0, r1 in parts], axis=0
                )
                part = mm(patch, w2[3 * a + b], 1, 0)
                value = part if value is None else value + part
            at = 0
            for g, r0, r1 in parts:
                for r in range(r0, r1):
                    begin = starts[g] + r * widths[g]
                    span = slice(begin, begin + widths[g])
                    u = value[at : at + widths[g]]
                    at += widths[g]
                    gv[span, :] = u
                    uv = u * valid[span, :]
                    acc = [acc[0] + rowsum(uv), acc[1] + rowsum(uv * u)]
            return acc

        left = lax.broadcasted_iota(jnp.int32, (1, LANES), 1) < out_rows

        def pack(g, r0, r1):
            for r in range(r0, r1):
                v = by_chan(flat(a1[g][1 + r, 1 : 1 + halves[g]]).astype(f32))
                t = [pltpu.roll(e, out_rows, 1) for e in v]
                begin = starts[g] + r * widths[g]
                span = slice(begin, begin + widths[g])
                for p in range(2):
                    cols = slice(p * LANES, (p + 1) * LANES)
                    apk[0, span, cols] = jnp.where(left, v[2 * p], t[2 * p + 1]).astype(bf16)
                    apk[1, span, cols] = jnp.where(left, t[2 * p], v[2 * p + 1]).astype(bf16)

        near = sizes[1]
        far = sizes[0] * 9 // 16 // 16 * 16
        pack_spans = [
            [slice(starts[1], starts[1] + near)],
            [slice(0, far)],
            [slice(far, sizes[0])],
        ]
        slot_p = [[net.slot() for _ in spans_] for spans_ in pack_spans]

        def pack_send(n):
            for span, slot in zip(pack_spans[n], slot_p[n]):
                net.send(apk.at[1 - ix, span], arx.at[span], slot, mate)

        activate(0)
        pack(1, 0, halves[1])
        pack(0, 0, rs)
        pack_send(0)
        acc = second_conv([(1, 0, halves[1]), (0, 0, rs - 1)], zeros(2))
        activate(1)
        pack(0, rs, halves[0])
        acc = second_conv([(0, rs - 1, halves[0])], acc)
        first = share(1, message(acc))
        pack_send(1)

        stat[0:8, :] = chan_total(2, side_first)
        means, scs = moments(stat[pl.ds(k, 1), :], stat[pl.ds(4 + k, 1), :])
        for where in (k2, k3, k1):
            net.arrived(zsr.at[where], slot_s + where, (i, where))
        for c in range(2):
            for g, r, s, z in whole_cells(lambda q, span: zsr[q, span, :], c):
                begin = starts[g] + (r * halves[g] + s) * images[g]
                zs[begin : begin + images[g], :] = (z - means) * scs

        def planes_of(quarters, g):
            count = quarter[g]
            if count % 8 == 0:
                return [
                    jnp.concatenate([v[:, count * p : count * (p + 1)] for v in quarters], axis=1)
                    for p in range(4)
                ]
            low = lax.broadcasted_iota(jnp.int32, (1, 8, 1), 1) < 4
            parts = [[v[:, 8 * h : 8 * h + 8] for v in quarters] for h in range(2)]
            turned = [[pltpu.roll(v, 4, 1) for v in side] for side in parts]
            result = []
            for p in range(4):
                v, t = parts[p // 2], turned[p // 2]
                if p % 2 == 0:
                    both = [jnp.where(low, v[0], t[1]), jnp.where(low, v[2], t[3])]
                else:
                    both = [jnp.where(low, t[0], v[1]), jnp.where(low, t[2], v[3])]
                result.append(jnp.concatenate(both, axis=1))
            return result

        def make_planes():
            for g, r, begin, count in chunks:
                quarters = [
                    zg[q, begin : begin + count, :].astype(f32).reshape(halves[g], images[g], chan_in)
                    for q in range(4)
                ]
                for p, value in enumerate(planes_of(quarters, g)):
                    zp[g][p, 1 + r, 1 : 1 + halves[g]] = value.astype(bf16)

        tot = total(1, first)
        net.spare |= set(range(slot_x[0], slot_x[-1] + n_dp)) | set(range(slot_w[0], slot_w[-1] + 4))
        mean2, sc2 = moments(tot[0:1], tot[1:2])
        gain2, gains = g2[...], gs[...]
        shifts = b2[...] + bs[...]
        acc = zeros(3)
        for g, r, begin, count in chunks:
            span = slice(begin, begin + count)
            ok = valid[span, :]
            hat2 = (gv[span, :] - mean2) * sc2
            hats = zs[span, :]
            v = hat2 * gain2 + hats * gains + shifts
            sig = sigma(v)
            outr[span, :] = v * sig * ok
            grad = up[span, :] * ok * (sig * (1.0 + v * (1.0 - sig)))
            up[span, :] = grad
            gv[span, :] = hat2
            acc = [acc[0] + rowsum(grad), acc[1] + rowsum(grad * hat2), acc[2] + rowsum(grad * hats)]
        first = share(2, message(acc))
        pack_send(2)
        for g, target in enumerate((oa, ob)):
            n, count = images[g], halves[g] ** 2
            for cell in range(count):
                gu[pl.ds(starts[g] + cell, n, stride=count), :] = outr[
                    starts[g] + cell * n : starts[g] + (cell + 1) * n, :
                ]
            target[...] = gu[starts[g] : starts[g] + sizes[g], :].astype(bf16)
        for begin in range(0, rows, 16):
            span = slice(begin, begin + 16)
            h = (hat[span, :] - mean1) * sc1
            hat[span, :] = h
            v = h * gain1 + shift1
            sig = sigma(v)
            mask[span, :] = sig * (1.0 + v * (1.0 - sig)) * lanes_cat([valid[span, :]] * 4)
        net.settle(gone)
        gone = net.mark()
        tot = total(2, first)
        done = used[:-1] + [(begin, 4) for begin in slot_z] + [(slot_s, 4)]
        net.spare_dp |= {begin + e for begin, count in done for e in range(count)}
        sum_tail, sum_gain2, sum_gains = tot[0:1], tot[1:2], tot[2:3]
        k2g, ksg = gain2 * sc2, gains * scs
        db, dg2, dgs = sum_tail * inv_pop, sum_gain2 * inv_pop, sum_gains * inv_pop
        for g, r, begin, count in chunks:
            span = slice(begin, begin + count)
            value = k2g * (up[span, :] - valid[span, :] * (db + gv[span, :] * dg2))
            dz[g][1 + r, 1 : 1 + halves[g]] = value.astype(bf16).reshape(halves[g], images[g], chan_part)
        slot_d = net.slot(2)

        def dz_inner(buf, g):
            return buf[g].at[1 : 1 + halves[g], 1 : 1 + halves[g]]

        for g in range(2):
            net.send(dz_inner(dz, g), dz_inner(dzm, g), slot_d + g, mate)

        def columns(buf, piece, taps=range(9)):
            for g, r0, r1 in piece:
                for t in taps:
                    a, b = TAPS[t]
                    dd[
                        starts[g] + r0 * widths[g] : starts[g] + r1 * widths[g],
                        t * LANES : (t + 1) * LANES,
                    ] = flat(buf[g][r0 + 2 - a : r1 + 2 - a, 2 - b : 2 - b + halves[g]])

        def back_second(first, span):
            begin = pl.multiple_of(first * chan_part, LANES)
            weights = lanes_cat([w2[t, pl.ds(begin, 2 * chan_part), :] for t in range(9)])
            value = mm(dd[span, :], weights, 1, 1).astype(bf16)
            hp[first, span, :] = value[:, :chan_part]
            hp[first + 1, span, :] = value[:, chan_part:]

        slot_h = [net.slot(3) for _ in row_halves]
        def other_pair(n):
            columns(dz, back_pieces[n])
            back_second(2 * (k2 // 2), row_halves[n])
            net.send(hp.at[k3, row_halves[n]], hr1.at[1, row_halves[n]], slot_h[n] + 1, (i, k1))

        def cross_second(n):
            span = row_halves[n]
            net.arrived(hr1.at[1, span], slot_h[n] + 1, (i, k1))
            hs[span, :] = (hp[k2, span, :].astype(f32) + hr1[1, span, :].astype(f32)).astype(bf16)
            net.send(hs.at[span], hr2.at[span], slot_h[n] + 2, (i, k2))

        def pair_sums(first):
            acc = [jnp.zeros((8, 2 * chan_part), f32)] * 2
            cols = pl.ds(pl.multiple_of(first * chan_part, 2 * LANES), 2 * chan_part)
            for begin in range(0, rows, 16):
                span = slice(begin, begin + 16)
                part = lanes_cat([hp[first + e, span, :] for e in range(2)]).astype(f32) * mask[span, cols]
                acc = [acc[0] + rowsum(part), acc[1] + rowsum(part * hat[span, cols])]
            acc = [jnp.sum(v, axis=0, keepdims=True) for v in acc]
            for e in range(2):
                for n in range(2):
                    stat[pl.ds(4 * n + first + e, 1), :] = acc[n][:, e * LANES : (e + 1) * LANES]

        other_pair(0)
        other_pair(1)
        cross_second(0)
        other_pair(2)
        cross_second(1)
        back_second(2 * (k // 2), slice(0, rows))
        pair_sums(2 * (k2 // 2))
        cross_second(2)
        for span, slot in zip(row_halves, slot_h):
            net.send(hp.at[k1, span], hr1.at[0, span], slot, (i, k1))
        pair_sums(2 * (k // 2))
        first = share(3, stat[0:8, :])

        sum2 = Reduce(net, i, k, None, (None, p22, p23, p24, p25), cols2, p26)
        gacc[...] = mm(apk[ix], dd[...], 0, 0)
        net.settle(gone)
        first = chan_share(1, total(3, first))
        def split_cells(read, target, c):
            for begin in range(row_parts[c].start, row_parts[c].stop, 16):
                tiles = []
                for at in (begin, begin + 8):
                    seg = max(e for e in range(3) if seg_row[e] <= at)
                    g, r0, r1 = segments[seg]
                    per = 8 // quarter[g]
                    cell = (at - seg_row[seg]) // 8 * per
                    blocks = []
                    for e in range(per):
                        if cell + e < seg_cells[seg]:
                            r, s = divmod(cell + e, halves[g])
                            blocks.append(read(g, r0 + r, s))
                        else:
                            blocks.append(jnp.zeros((images[g], chan_part), f32))
                    if per == 1:
                        tiles.append([blocks[0][8 * q : 8 * q + 8] for q in range(4)])
                    else:
                        found = []
                        for h in range(2):
                            v = [block[8 * h : 8 * h + 8] for block in blocks]
                            t = [pltpu.roll(e, 4, 0) for e in v]
                            found += [jnp.where(turn_low, v[0], t[1]), jnp.where(turn_low, t[0], v[1])]
                        tiles.append(found)
                for q in range(4):
                    both = jnp.concatenate([tiles[0][q], tiles[1][q]], axis=0)
                    target[q, begin : begin + 16, :] = both.astype(bf16)

        def cell_span(g, r, s):
            begin = starts[g] + (r * halves[g] + s) * images[g]
            return slice(begin, begin + images[g])

        def short_cell(g, r, s):
            span = cell_span(g, r, s)
            value = ksg * (up[span, :] - valid[span, :] * (db + zs[span, :] * dgs))
            dzsr[span, :] = value.astype(bf16)
            return value

        slot_q = [net.slot(4) for _ in range(3)]

        def quarters_out(source, target, span, slot):
            for where in (k2, k3, k1):
                net.send(source.at[where, span], target.at[k, span], slot + k, (i, where))
            target[k, span, :] = source[k, span, :]

        def quarters_in(target, span, slot):
            for where in (k1, k2, k3):
                net.arrived(target.at[where, span], slot + where, (i, where))

        for c in range(2):
            split_cells(short_cell, sq, c)
        quarters_out(sq, si, slice(0, q_rows), slot_q[2])
        for n in range(2):
            slab_on(n)
        for spans_, slots_ in zip(pack_spans, slot_p):
            for span, slot in zip(spans_, slots_):
                net.arrived(arx.at[span], slot, mate)
        for g in range(2):
            net.arrived(dz_inner(dzm, g), slot_d + g, mate)
        gone = net.mark()
        for w, cols in enumerate(cols2):
            for piece in back_pieces:
                columns(dzm, piece, range(cols.start // LANES, cols.stop // LANES))
            value = (gacc[:, cols] + mm(arx[...], dd[:, cols], 0, 0)).astype(bf16)
            (sum2.spread_of, sum2.second_of)[w](w, value)
        tot = chan_total(1, first)
        stat[0:8, :] = tot
        sum_head, sum_gain1 = stat[pl.ds(k, 1), :], stat[pl.ds(4 + k, 1), :]

        def close_second():
            for w, cols in enumerate(cols2):
                value = (sum2.spread_last, sum2.last)[w](w)
                for t in range(cols.start // LANES, cols.stop // LANES):
                    gw2[t] = value[:, t * LANES - cols.start : (t + 1) * LANES - cols.start]

        own = pl.ds(pl.multiple_of(k * chan_part, LANES), chan_part)
        mean1, sc1 = moments(tot_first[0], tot_first[1])
        k1g = vg[k, 0] * sc1
        db, dg1 = sum_head * inv_pop, sum_gain1 * inv_pop
        for span, slot in zip(row_halves, slot_h):
            net.arrived(hr1.at[0, span], slot, (i, k1))
            net.arrived(hr2.at[span], slot + 2, (i, k2))

        def first_cell(g, r, s):
            span = cell_span(g, r, s)
            grad = hp[k, span, :].astype(f32) + hr1[0, span, :].astype(f32) + hr2[span, :].astype(f32)
            grad = grad * mask[span, own]
            value = k1g * (grad - valid[span, :] * (db + hat[span, own] * dg1))
            d1[g][r, s] = value.astype(bf16)
            return value

        for c in (1, 0):
            split_cells(first_cell, dq, c)
            quarters_out(dq, di, row_parts[c], slot_q[c])

        def back_patch(pieces, p):
            parts = []
            for g, r0, r1 in pieces:
                width = halves[g] * images[g]
                taps = [
                    flat(d1[g][r0 + (a == 0) : r1 + (a == 0), (b == 0) : (b == 0) + halves[g]])
                    for a, b in PLANE_TAPS[p]
                ]
                if p == 0:
                    taps.append(dzsr[starts[g] + r0 * width : starts[g] + r1 * width, :])
                parts.append(lanes_cat(taps))
            return jnp.concatenate(parts, axis=0) if len(parts) > 1 else parts[0]

        slot_o = [net.slot(n_dp, True) for _ in out_lanes]

        def back_taps(c):
            part = row_parts[c]
            quarters_in(di, part, slot_q[c])
            grads = lanes_cat([di[q, part, :] for q in range(4)])
            weights = lanes_cat([w1g[q].reshape(9 * chan_in, chan_part) for q in range(4)])
            value = mm(grads, weights, 1, 1)
            taps = [value[:, t * chan_in : (t + 1) * chan_in] for t in range(9)]
            side = lanes_cat([si[q, part, :] for q in range(4)])
            taps[4] = taps[4] + mm(side, lanes_cat([wsg[q] for q in range(4)]), 1, 1)
            return jnp.concatenate([tap.astype(bf16) for tap in taps], axis=0)

        slot_f = net.slot(n_dp, True)

        def out_send(n, value):
            cols = out_lanes[n]
            if n == 0:
                last_tile = value[:, value.shape[1] - LANES :].reshape(n_dp, in_local, LANES)
                gtf[...] = fold(last_tile).astype(bf16)
                grf[i] = gtf[i]
                for j in peers:
                    net.send(gtf.at[j], grf.at[i], slot_f + i, (j, k))
                value = value[:, : value.shape[1] - LANES]
            gt[:, :, cols] = value.astype(bf16).reshape(n_dp, in_local, value.shape[1])
            for j in peers:
                net.send(gt.at[j, :, cols], gr.at[i, :, cols], slot_o[n] + i, (j, k))

        sum1 = Reduce(net, i, k, wg1, (p11, p12, p13, p14, p15), cols1)

        def weight_first(w):
            cols = cols1[w]
            blocks = []
            for p in ((3,), (0, 1, 2))[w]:
                value = 0.0
                for g, r0, r1 in ((0, 0, halves[0]), (1, 0, halves[1])):
                    cell = flat(zp[g][p, 1 : 1 + halves[g], 1 : 1 + halves[g]])
                    value = value + mm(cell, back_patch([(g, r0, r1)], p), 0, 0)
                blocks.append(value.astype(bf16))
            wg1[:, :, :, :, cols] = lanes_cat(blocks).reshape(2, 2, 2, in_local, cols.stop - cols.start)
            sum1.first(w)

        for n in range(2):
            slab_in(n)
        make_planes()
        weight_first(0)
        weight_first(1)
        net.settle(gone)
        quarters_in(si, slice(0, q_rows), slot_q[2])
        late = back_taps(1)
        edge = cut_lane - patch_win[1].start
        out_send(0, mm(late, pm1[:, edge:], 0, 0))
        early_ = back_taps(0)
        out_send(1, mm(early_, pm0[:, :low_lane], 0, 0))
        rest = mm(early_, pm0[:, low_lane:], 0, 0)
        shared = mm(late, pm1[:, low_lane - patch_win[1].start : edge], 0, 0)
        sum2.third(1)
        sum1.second(0)
        sum1.second(1)
        out_send(2, rest + shared)
        sum1.third(0)
        sum1.third(1)
        gr[i] = gt[i]
        close_second()
        for w, cols in enumerate(cols1):
            value = sum1.last(w)
            for t, tap in enumerate(TAPS):
                place = ORDER.index(tap)
                place = (place + (place > 0)) * LANES
                if cols.start <= place < cols.stop:
                    gw1[t] = value[:, place - cols.start : place - cols.start + LANES]
            if cols.start <= LANES < cols.stop:
                gws[...] = value[:, LANES - cols.start : 2 * LANES - cols.start]
        vecs[...] = message([sum_gain1, sum_head, sum_gain2, sum_tail, sum_gains])
        for j in peers:
            net.arrived(grf.at[j], slot_f + j, (j, k))
        for c, cols in enumerate(out_lanes):
            for j in peers:
                net.arrived(gr.at[j, :, cols], slot_o[c] + j, (j, k))
        net.drain()
        assert net.sends <= n_sends and net.slots <= n_slots

    V = pltpu.VMEM
    pads = [(h + 2, h + 2, n, chan_part) for h, n in zip(halves, images)]
    half_pads = [(h + 1, h + 1, n) for h, n in zip(halves, images)]

    def ladder(count, width):
        return [
            V((2, 2, 2, count, width), bf16), V((2, 2, count, width), bf16), V((2, 2, count, width), bf16),
            V((2, count, width), bf16), V((2, count, width), bf16), V((count, width), bf16),
        ]

    inputs = [
        V((in_local, n_dp * 4 * qlanes[0]), bf16), V((in_local, n_dp * 4 * qlanes[1]), bf16),
        V((4, images[0]), jnp.int32), V((4, images[1]), jnp.int32),
        V((4, 9, chan_in, chan_part), bf16), V((9, chan_full, chan_part), bf16),
        V((4, chan_in, chan_part), bf16), V((4, 2, 1, chan_part), f32),
    ] + [V((1, chan_part), f32)] * 4 + [
        V((sizes[0], chan_part), bf16), V((sizes[1], chan_part), bf16),
    ] + [V(m.shape, bf16) for m in patch_ms] + [V((rows, slab_lanes), bf16)]
    scratch = inputs + [
        V((n_dp * in_local, slab_lanes), bf16),
        V((n_dp, in_local, slab_lanes), bf16),
        V((n_dp, in_local, slab_lanes), bf16),
        V((4, q_rows, chan_full), bf16),
        V((4, q_rows, chan_part), bf16),
        V((4, q_rows, chan_part), bf16),
        V((4, rows, chan_in), bf16),
        V((4,) + half_pads[0] + (chan_in,), bf16),
        V((4,) + half_pads[1] + (chan_in,), bf16),
        V((rows, LANES), f32),
        V((q_rows, LANES), f32),
        V((rows, chan_full), f32),
        V((rows, chan_full), f32),
        V((rows, chan_part), f32),
        V(pads[0][:3] + (chan_full,), bf16),
        V(pads[1][:3] + (chan_full,), bf16),
        V((3, 4, 16, LANES), f32),
        V((6, n_dp, 16, LANES), f32),
        V((16, LANES), f32),
        V((rows, chan_part), f32),
        V((rows, chan_part), f32),
        V((rows, chan_part), f32),
        V(pads[0], bf16),
        V(pads[1], bf16),
        V(pads[0], bf16),
        V(pads[1], bf16),
        V((2, rows, chan_full // 2), bf16),
        V((rows, chan_full // 2), bf16),
        V((chan_full // 2, 9 * chan_part), f32),
        V((rows, chan_part), bf16),
        V((rows, 9 * chan_part), bf16),
        V((4, rows, chan_part), bf16),
        V((2, rows, chan_part), bf16),
        V((rows, chan_part), bf16),
        V((rows, chan_part), bf16),
        V((rows, chan_part), f32),
        V(half_pads[0] + (chan_part,), bf16),
        V(half_pads[1] + (chan_part,), bf16),
    ]
    scratch += ladder(out_rows, 9 * LANES)[2:]
    scratch += [V((n_dp // 2, out_rows, cols2[0].stop), bf16)] + ladder(in_local, 10 * LANES)
    scratch += [
        V((4, q_rows, chan_part), bf16),
        V((4, q_rows, chan_part), bf16),
        V((4, q_rows, chan_part), bf16),
        V((4, q_rows, chan_part), bf16),
        V((n_dp, in_local, last_lane), bf16),
        V((n_dp, in_local // 2, LANES), bf16),
        pltpu.SemaphoreType.DMA((20,)),
        pltpu.SemaphoreType.DMA((n_sends,)),
        pltpu.SemaphoreType.DMA((n_slots,)),
    ]
    mid_outs = [
        V((sizes[0], chan_part), bf16),
        V((sizes[1], chan_part), bf16),
        V((n_dp, in_local, last_lane), bf16),
        V((n_dp, in_local // 2, LANES), bf16),
        V((9, in_local, LANES), f32),
        V((in_local, LANES), f32),
        V((9, out_rows, LANES), f32),
        V((8, LANES), f32),
        V((n_dp * in_local, n_dp * in_local), bf16),
    ]
    vmem = pl.BlockSpec(memory_space=pltpu.VMEM)
    hbm = pl.BlockSpec(memory_space=pl.ANY)
    main = pl.pallas_call(
        kernel,
        out_shape=mid_outs,
        in_specs=[hbm] * 19,
        out_specs=[vmem] * len(mid_outs),
        scratch_shapes=scratch,
        compiler_params=pltpu.CompilerParams(
            collective_id=1, has_side_effects=True, vmem_limit_bytes=58 * 2**20
        ),
        name="block",
    )

    def closing(oa, ob, gr, grf, gw1, gws, gw2, vecs, turn,
                fa, fb, ia, ib, f1, f2, fs, c1, h1, c2, h2, cs, hs, iav, ibv, sems):
        outs = [
            pltpu.make_async_copy(source, target, sems.at[index])
            for index, (source, target) in enumerate(
                ((gw2, f2), (gw1, f1), (oa, fa), (ob, fb), (gws, fs))
            )
        ]
        for out in outs:
            out.start()
        tail = unfold(grf[...].astype(f32)).astype(bf16).reshape(n_dp * in_local, LANES)
        moved = jnp.concatenate([gr[...].reshape(n_dp * in_local, last_lane), tail], axis=1)
        n_half = in_local // 2
        for h in range(2):
            part = slice(h * n_half, (h + 1) * n_half)
            natural = regroup(mm(turn[h * n_half * n_dp : (h + 1) * n_half * n_dp, :], moved, 1, 0), back_runs)
            iav[part] = natural[:, : qlanes[0]].reshape(n_half, n_dp, qlanes[0]).astype(bf16)
            tail = natural[:, qlanes[0] : qlanes[0] + qlanes[1]]
            ibv[part] = tail.reshape(n_half, n_dp, qlanes[1]).astype(bf16)
            for e, (source, target) in enumerate(((iav, ia), (ibv, ib))):
                out = pltpu.make_async_copy(source.at[part], target.at[part], sems.at[5 + 2 * h + e])
                out.start()
                outs.append(out)
        for ref, row in ((c1, 0), (h1, 1), (c2, 2), (h2, 3), (cs, 4), (hs, 3)):
            ref[...] = vecs[row : row + 1, :]
        for out in outs:
            out.wait()

    last = pl.pallas_call(
        closing,
        out_shape=[
            jax.ShapeDtypeStruct((sizes[0], chan_part), bf16),
            jax.ShapeDtypeStruct((sizes[1], chan_part), bf16),
            jax.ShapeDtypeStruct((in_local, n_dp, qlanes[0]), bf16),
            jax.ShapeDtypeStruct((in_local, n_dp, qlanes[1]), bf16),
            jax.ShapeDtypeStruct((9, in_local, LANES), f32),
            jax.ShapeDtypeStruct((9, out_rows, LANES), f32),
            jax.ShapeDtypeStruct((in_local, LANES), f32),
        ]
        + [jax.ShapeDtypeStruct((1, LANES), f32)] * 6,
        in_specs=[vmem] * 9,
        out_specs=[hbm] * 7 + [vmem] * 6,
        scratch_shapes=[
            V((in_local, n_dp, qlanes[0]), bf16),
            V((in_local, n_dp, qlanes[1]), bf16),
            pltpu.SemaphoreType.DMA((9,)),
        ],
        compiler_params=pltpu.CompilerParams(vmem_limit_bytes=32 * 2**20),
        name="closing",
    )
    total_rows = n_dp * in_local
    turn = np.zeros((total_rows, total_rows), np.float32)
    for c in range(in_local):
        for j in range(n_dp):
            turn[c * n_dp + j, j * in_local + c] = 1.0
    return (main, last) + tuple(m.astype(jnp.bfloat16) for m in (*patch_ms, cells_m, turn))


def fused_body(
    input_a, input_b, boxes_a, boxes_b, weight_first, weight_second, weight_short,
    gain_first, shift_first, gain_second, shift_second, gain_short, shift_short,
    upstream_a, upstream_b,
):
    n_dp = lax.axis_size("dp")
    chan_part = weight_first.shape[2]
    in_local = input_a.shape[0]
    main, last, *matrices = make_fused(
        n_dp, in_local, (boxes_a.shape[0], boxes_b.shape[0]), (SA, SB),
        weight_first.shape[1], chan_part,
    )
    vectors = [
        v.reshape(1, chan_part)
        for v in (gain_first, shift_first, gain_second, shift_second, gain_short, shift_short)
    ]
    mid = main(
        input_a, input_b, boxes_a.T, boxes_b.T, weight_first, weight_second, weight_short,
        *vectors, upstream_a.T, upstream_b.T, *matrices,
    )
    res = last(*mid)
    return (
        res[0].T, res[1].T,
        res[2].reshape(in_local, n_dp, 1, -1), res[3].reshape(in_local, n_dp, 1, -1),
        res[4], res[5], res[6],
    ) + tuple(v.reshape(chan_part) for v in res[7:])


def choose_body(mesh):
    return fused_body if mesh.shape["dp"] == 8 and mesh.shape["chan"] == 4 else plain_body


def solution(mesh):
    placed = (
        P("dp", None),
        P("dp", None),
        P("dp", None),
        P("dp", None),
        P(None, None, "chan"),
        P(None, None, "chan"),
        P(None, "chan"),
        P("chan"),
        P("chan"),
        P("chan"),
        P("chan"),
        P("chan"),
        P("chan"),
        P("chan", "dp"),
        P("chan", "dp"),
    )
    return jax.shard_map(
        choose_body(mesh),
        mesh=mesh,
        in_specs=placed,
        out_specs=(
            P("chan", "dp"),
            P("chan", "dp"),
            P("dp", None, "chan", None),
            P("dp", None, "chan", None),
            P(None, "dp", "chan"),
            P(None, "dp", "chan"),
            P("dp", "chan"),
            P("chan"),
            P("chan"),
            P("chan"),
            P("chan"),
            P("chan"),
            P("chan"),
        ),
        check_vma=False,
    )
```

```python
import jax
import jax.numpy as jnp
from jax import lax
import numpy as np
from jax.experimental import pallas as pl
from jax.experimental.pallas import tpu as pltpu
from jax.sharding import PartitionSpec as P

SA = 14
SB = 6


epsilon = 1e-05


def box_mask(box_rows, extent):
    positions = jnp.arange(extent, dtype=jnp.int32)[None, :]
    row_inside = (positions >= box_rows[:, 0:1]) & (positions < box_rows[:, 0:1] + box_rows[:, 2:3])
    col_inside = (positions >= box_rows[:, 1:2]) & (positions < box_rows[:, 1:2] + box_rows[:, 3:4])
    return (row_inside[:, :, None] & col_inside[:, None, :]).astype(jnp.float32)


def taps_strided(feature, image_count, extent):
    channels = feature.shape[0]
    output_side = extent // 2
    padded = jnp.pad(
        feature.reshape(channels, image_count, extent, extent), ((0, 0), (0, 0), (1, 1), (1, 1))
    )
    pieces = [
        padded[:, :, tap_row : tap_row + extent : 2, tap_col : tap_col + extent : 2]
        for tap_row in range(3)
        for tap_col in range(3)
    ]
    return jnp.stack(pieces, axis=0).reshape(9 * channels, image_count * output_side * output_side)


def taps_plain(feature, image_count, extent):
    channels = feature.shape[0]
    padded = jnp.pad(
        feature.reshape(channels, image_count, extent, extent), ((0, 0), (0, 0), (1, 1), (1, 1))
    )
    pieces = [
        padded[:, :, tap_row : tap_row + extent, tap_col : tap_col + extent]
        for tap_row in range(3)
        for tap_col in range(3)
    ]
    return jnp.stack(pieces, axis=0).reshape(9 * channels, image_count * extent * extent)


def untaps_plain(columns, channels, image_count, extent):
    pieces = columns.reshape(9, channels, image_count, extent, extent)
    running = jnp.zeros((channels, image_count, extent + 2, extent + 2), jnp.float32)
    for tap_row in range(3):
        for tap_col in range(3):
            running = running + jnp.pad(
                pieces[3 * tap_row + tap_col],
                ((0, 0), (0, 0), (tap_row, 2 - tap_row), (tap_col, 2 - tap_col)),
            )
    return running[:, :, 1:-1, 1:-1].reshape(channels, image_count * extent * extent)


def untaps_strided(columns, shortcut, channels, image_count, extent):
    output_side = extent // 2
    pieces = columns.reshape(9, channels, image_count, output_side, output_side)
    parity_sums = {}
    for tap_row in range(3):
        for tap_col in range(3):
            block_row = tap_row // 2
            block_col = tap_col // 2
            placed = jnp.pad(
                pieces[3 * tap_row + tap_col],
                ((0, 0), (0, 0), (block_row, 1 - block_row), (block_col, 1 - block_col)),
            )
            parity = (tap_row % 2, tap_col % 2)
            parity_sums[parity] = (
                placed if parity not in parity_sums else parity_sums[parity] + placed
            )
    direct = jnp.pad(
        shortcut.reshape(channels, image_count, output_side, output_side),
        ((0, 0), (0, 0), (0, 1), (0, 1)),
    )
    parity_sums[1, 1] = parity_sums[1, 1] + direct
    rows_even = jnp.stack([parity_sums[0, 0], parity_sums[0, 1]], axis=-1)
    rows_odd = jnp.stack([parity_sums[1, 0], parity_sums[1, 1]], axis=-1)
    padded = jnp.stack([rows_even, rows_odd], axis=3).reshape(
        channels, image_count, extent + 2, extent + 2
    )
    return padded[:, :, 1:-1, 1:-1].reshape(channels, image_count * extent * extent)


def contract_first(weights, columns):
    return lax.dot_general(
        weights, columns, (((0,), (0,)), ((), ())), preferred_element_type=jnp.float32
    )


def weight_product(columns, gradient):
    return lax.dot_general(
        columns, gradient, (((1,), (1,)), ((), ())), preferred_element_type=jnp.float32
    )


def swish_slope(values):
    logistic = jax.nn.sigmoid(values)
    return logistic * (1.0 + values * (1.0 - logistic))


def moments(values, valid_list):
    running = 0.0
    squares = 0.0
    for tensor, valid in zip(values, valid_list):
        widened = tensor.astype(jnp.float32)
        running = running + jnp.sum(widened * valid, axis=1)
        squares = squares + jnp.sum(widened * widened * valid, axis=1)
    return (running, squares)


def standardize(values, running, squares, population):
    mean_value = running / population
    variance = squares / population - mean_value * mean_value
    scaling = lax.rsqrt(variance + epsilon)
    return (
        [
            (tensor.astype(jnp.float32) - mean_value[:, None]) * scaling[:, None]
            for tensor in values
        ],
        scaling,
    )


def norm_back(gradient, normed, valid, scaling, gain_values, shift_sum, gain_sum, population):
    return (gain_values * scaling)[:, None] * (
        gradient - valid * (shift_sum[:, None] + normed * gain_sum[:, None]) / population
    )


def plain_body(
    input_a,
    input_b,
    boxes_a,
    boxes_b,
    weight_first,
    weight_second,
    weight_short,
    gain_first,
    shift_first,
    gain_second,
    shift_second,
    gain_short,
    shift_short,
    upstream_a,
    upstream_b,
):
    image_groups = lax.axis_size("dp")
    in_local = input_a.shape[0]
    chan_in = weight_first.shape[1]
    chan_part = weight_first.shape[2]
    chan_full = weight_second.shape[1]
    image_counts = (boxes_a.shape[0], boxes_b.shape[0])
    extents = (SA, SB)
    whole_a, whole_b = (
        lax.all_to_all(
            input_a.reshape(in_local, image_groups, -1),
            "dp",
            split_axis=1,
            concat_axis=0,
            tiled=True,
        ),
        lax.all_to_all(
            input_b.reshape(in_local, image_groups, -1),
            "dp",
            split_axis=1,
            concat_axis=0,
            tiled=True,
        ),
    )
    features = (whole_a.reshape(chan_in, -1), whole_b.reshape(chan_in, -1))
    valid_list = (
        box_mask(boxes_a, SA // 2).reshape(1, -1),
        box_mask(boxes_b, SB // 2).reshape(1, -1),
    )
    first_mat = weight_first.reshape(9 * chan_in, chan_part)
    second_mat = weight_second.reshape(9 * chan_full, chan_part)
    first_cols = []
    sampled = []
    first_z = []
    short_z = []
    for feature, image_count, extent in zip(features, image_counts, extents):
        columns = taps_strided(feature, image_count, extent)
        picked = feature.reshape(chan_in, image_count, extent, extent)[:, :, ::2, ::2].reshape(
            chan_in, -1
        )
        first_cols.append(columns)
        sampled.append(picked)
        first_z.append(contract_first(first_mat, columns).astype(jnp.bfloat16))
        short_z.append(contract_first(weight_short, picked).astype(jnp.bfloat16))
    sum_first, square_first = moments(first_z, valid_list)
    sum_short, square_short = moments(short_z, valid_list)
    population = jnp.sum(valid_list[0]) + jnp.sum(valid_list[1])
    sum_first, square_first, sum_short, square_short, population = lax.psum(
        (sum_first, square_first, sum_short, square_short, population), "dp"
    )
    normed_first, scaling_first = standardize(first_z, sum_first, square_first, population)
    normed_short, scaling_short = standardize(short_z, sum_short, square_short, population)
    before_first = [normed * gain_first[:, None] + shift_first[:, None] for normed in normed_first]
    outgoing_a = (jax.nn.silu(before_first[0]) * valid_list[0]).astype(jnp.bfloat16)
    outgoing_b = (jax.nn.silu(before_first[1]) * valid_list[1]).astype(jnp.bfloat16)
    gathered_a, gathered_b = (
        lax.all_gather(outgoing_a, "chan", axis=0, tiled=True),
        lax.all_gather(outgoing_b, "chan", axis=0, tiled=True),
    )
    second_cols = []
    second_z = []
    for gathered, image_count, extent in zip((gathered_a, gathered_b), image_counts, extents):
        columns = taps_plain(gathered, image_count, extent // 2)
        second_cols.append(columns)
        second_z.append(contract_first(second_mat, columns).astype(jnp.bfloat16))
    sum_second, square_second = moments(second_z, valid_list)
    sum_second, square_second = lax.psum((sum_second, square_second), "dp")
    normed_second, scaling_second = standardize(second_z, sum_second, square_second, population)
    summed_pre = [
        main_part * gain_second[:, None]
        + shift_second[:, None]
        + side_part * gain_short[:, None]
        + shift_short[:, None]
        for main_part, side_part in zip(normed_second, normed_short)
    ]
    outputs = [
        (jax.nn.silu(tensor) * valid).astype(jnp.bfloat16)
        for tensor, valid in zip(summed_pre, valid_list)
    ]
    tail_grads = [
        upstream.astype(jnp.float32) * valid * swish_slope(tensor)
        for upstream, valid, tensor in zip((upstream_a, upstream_b), valid_list, summed_pre)
    ]
    shift_tail = sum((jnp.sum(gradient, axis=1) for gradient in tail_grads))
    gain_tail = sum(
        (jnp.sum(gradient * normed, axis=1) for gradient, normed in zip(tail_grads, normed_second))
    )
    gain_side = sum(
        (jnp.sum(gradient * normed, axis=1) for gradient, normed in zip(tail_grads, normed_short))
    )
    shift_tail, gain_tail, gain_side = lax.psum((shift_tail, gain_tail, gain_side), "dp")
    grad_second_local = 0.0
    partial_hidden = []
    short_dz = []
    for index_group in range(2):
        valid = valid_list[index_group]
        dz_second = norm_back(
            tail_grads[index_group],
            normed_second[index_group],
            valid,
            scaling_second,
            gain_second,
            shift_tail,
            gain_tail,
            population,
        ).astype(jnp.bfloat16)
        dz_short = norm_back(
            tail_grads[index_group],
            normed_short[index_group],
            valid,
            scaling_short,
            gain_short,
            shift_tail,
            gain_side,
            population,
        ).astype(jnp.bfloat16)
        short_dz.append(dz_short)
        grad_second_local = grad_second_local + weight_product(second_cols[index_group], dz_second)
        back_cols = jnp.dot(second_mat, dz_second, preferred_element_type=jnp.float32)
        partial_hidden.append(
            untaps_plain(back_cols, chan_full, image_counts[index_group], extents[index_group] // 2)
        )
    hidden_a, hidden_b = (
        lax.psum_scatter(
            partial_hidden[0].astype(jnp.bfloat16), "chan", scatter_dimension=0, tiled=True
        ).astype(jnp.float32),
        lax.psum_scatter(
            partial_hidden[1].astype(jnp.bfloat16), "chan", scatter_dimension=0, tiled=True
        ).astype(jnp.float32),
    )
    head_grads = [
        hidden * valid * swish_slope(tensor)
        for hidden, valid, tensor in zip((hidden_a, hidden_b), valid_list, before_first)
    ]
    shift_head = sum((jnp.sum(gradient, axis=1) for gradient in head_grads))
    gain_head = sum(
        (jnp.sum(gradient * normed, axis=1) for gradient, normed in zip(head_grads, normed_first))
    )
    shift_head, gain_head = lax.psum((shift_head, gain_head), "dp")
    grad_first_local = 0.0
    grad_short_local = 0.0
    partial_inputs = []
    for index_group in range(2):
        valid = valid_list[index_group]
        dz_first = norm_back(
            head_grads[index_group],
            normed_first[index_group],
            valid,
            scaling_first,
            gain_first,
            shift_head,
            gain_head,
            population,
        ).astype(jnp.bfloat16)
        grad_first_local = grad_first_local + weight_product(first_cols[index_group], dz_first)
        grad_short_local = grad_short_local + weight_product(
            sampled[index_group], short_dz[index_group]
        )
        back_cols = jnp.dot(first_mat, dz_first, preferred_element_type=jnp.float32)
        back_short = jnp.dot(
            weight_short, short_dz[index_group], preferred_element_type=jnp.float32
        )
        flat_input = untaps_strided(
            back_cols, back_short, chan_in, image_counts[index_group], extents[index_group]
        )
        partial_inputs.append(flat_input.reshape(chan_in, 1, lax.axis_size("chan"), -1))
    arrived_a, arrived_b = (
        lax.all_to_all(
            partial_inputs[0].astype(jnp.bfloat16), "dp", split_axis=0, concat_axis=1, tiled=True
        ).astype(jnp.float32),
        lax.all_to_all(
            partial_inputs[1].astype(jnp.bfloat16), "dp", split_axis=0, concat_axis=1, tiled=True
        ).astype(jnp.float32),
    )
    summed_a, summed_b = (
        lax.psum_scatter(
            arrived_a.astype(jnp.bfloat16), "chan", scatter_dimension=2, tiled=True
        ).astype(jnp.float32),
        lax.psum_scatter(
            arrived_b.astype(jnp.bfloat16), "chan", scatter_dimension=2, tiled=True
        ).astype(jnp.float32),
    )
    grad_input_a = summed_a.astype(jnp.bfloat16)
    grad_input_b = summed_b.astype(jnp.bfloat16)
    grad_first_local = grad_first_local.reshape(9, chan_in, chan_part)
    grad_second_local = grad_second_local.reshape(9, chan_full, chan_part)
    total_first, total_second, total_short = lax.psum(
        (grad_first_local, grad_second_local, grad_short_local), "dp"
    )
    position = lax.axis_index("dp")
    rows_first = chan_in // image_groups
    rows_second = chan_full // image_groups
    grad_first = lax.dynamic_slice_in_dim(total_first, position * rows_first, rows_first, 1)
    grad_second = lax.dynamic_slice_in_dim(total_second, position * rows_second, rows_second, 1)
    grad_short = lax.dynamic_slice_in_dim(total_short, position * rows_first, rows_first, 0)
    return (
        outputs[0],
        outputs[1],
        grad_input_a,
        grad_input_b,
        grad_first,
        grad_second,
        grad_short,
        gain_head,
        shift_head,
        gain_tail,
        shift_tail,
        gain_side,
        shift_tail,
    )


MESH = pl.DeviceIdType.MESH
TAPS = tuple((a, b) for a in range(3) for b in range(3))
PLANE_TAPS = (
    ((1, 1),),
    ((1, 0), (1, 2)),
    ((0, 1), (2, 1)),
    ((0, 0), (0, 2), (2, 0), (2, 2)),
)
ORDER = [tap for taps in PLANE_TAPS for tap in taps]
LANES = 128


class Links:
    def __init__(self, send_sems, recv_sems):
        self.send_sems, self.recv_sems = send_sems, recv_sems
        self.sends = self.slots = self.started = 0
        self.open, self.free = [], []
        self.spare, self.spare_dp = set(), set()

    def slot(self, count=1, dp_only=False):
        for spare in (self.spare_dp, self.spare) if dp_only else (self.spare,):
            for first in sorted(spare):
                run = set(range(first, first + count))
                if run <= spare:
                    spare -= run
                    return first
        first = self.slots
        self.slots += count
        return first

    def send(self, source, target, slot, where):
        if not self.free:
            self.free.append(self.sends)
            self.sends += 1
        index = self.free.pop(0)
        copy = pltpu.make_async_remote_copy(
            source, target, self.send_sems.at[index], self.recv_sems.at[slot],
            device_id=where, device_id_type=MESH,
        )
        copy.start()
        self.open.append((copy, index))
        self.started += 1

    def mark(self):
        return self.started

    def settle(self, last):
        count = last - self.started + len(self.open)
        for copy, index in self.open[:count]:
            copy.wait_send()
            self.free.append(index)
        self.open = self.open[count:]

    def arrived(self, target, slot, where):
        pltpu.make_async_remote_copy(
            target, target, self.send_sems.at[0], self.recv_sems.at[slot],
            device_id=where, device_id_type=MESH,
        ).wait_recv()

    def drain(self):
        self.settle(self.mark())


def mm(a, b, ca, cb):
    return lax.dot_general(a, b, (((ca,), (cb,)), ((), ())), preferred_element_type=jnp.float32)


def lanes_cat(parts):
    return jnp.concatenate(parts, axis=1) if len(parts) > 1 else parts[0]


def quarter_matrices(images, sides, segments, seg_lane, seg_row, q_rows, lanes):
    def lane(g, image, row, col):
        for (seg_g, r0, r1), first in zip(segments, seg_lane):
            if seg_g == g and 2 * r0 <= row < 2 * r1:
                return first + (image * 2 * (r1 - r0) + row - 2 * r0) * sides[g] + col

    taps = np.zeros((9, q_rows, lanes), np.float32)
    for (g, r0, r1), first in zip(segments, seg_row):
        half = sides[g] // 2
        for r in range(r0, r1):
            for s in range(half):
                for image in range(images[g]):
                    target = first + ((r - r0) * half + s) * images[g] + image
                    for t, (a, b) in enumerate(TAPS):
                        row, col = 2 * r + a - 1, 2 * s + b - 1
                        if row >= 0 and col >= 0:
                            taps[t, target, lane(g, image, row, col)] = 1.0
    sizes = [n * side * side for n, side in zip(images, sides)]
    cells = np.zeros((sum(sizes), lanes), np.float32)
    for g, (n, side) in enumerate(zip(images, sides)):
        for image in range(n):
            for row in range(side):
                for col in range(side):
                    cell = (row // 2) * (side // 2) + col // 2
                    target = g * sizes[0] + (cell * 4 + 2 * (row % 2) + col % 2) * n + image
                    cells[target, lane(g, image, row, col)] = 1.0
    return taps, cells


def regroup(value, runs):
    return jnp.concatenate([value[:, a:b] for a, b in runs], axis=1)


def fold(value):
    half = value.shape[1] // 2
    left = lax.broadcasted_iota(jnp.int32, (1, 1, LANES), 2) < LANES // 2
    return jnp.where(left, value[:, :half], pltpu.roll(value[:, half:], LANES // 2, 2))


def unfold(value):
    return jnp.concatenate([value, pltpu.roll(value, LANES // 2, 2)], axis=1)


def sigma(v):
    return 0.5 * jnp.tanh(0.5 * v) + 0.5


class Reduce:
    def __init__(self, net, i, k, part, bufs, windows, b4=None):
        self.b4 = b4
        self.net, self.part, self.windows = net, part, windows
        self.b1, self.s1, self.b2, self.s2, self.b3 = bufs
        self.ix, self.pz, self.hz = i % 2, (i // 2) % 2, i // 4
        self.peers = (
            (i + 1 - 2 * self.ix, k),
            (i + 2 - 4 * self.pz, k),
            (i + 4 - 8 * self.hz, k),
        )
        self.slots = [net.slot(3, True) for _ in windows]

    def first(self, w):
        cols = self.windows[w]
        self.net.send(
            self.part.at[:, :, 1 - self.ix, :, cols], self.b1.at[:, :, :, cols],
            self.slots[w], self.peers[0],
        )

    def second(self, w):
        cols = self.windows[w]
        self.net.arrived(self.b1.at[:, :, :, cols], self.slots[w], self.peers[0])
        for h in range(2):
            for p in range(2):
                value = self.part[h, p, self.ix, :, cols].astype(jnp.float32)
                value = value + self.b1[h, p, :, cols].astype(jnp.float32)
                self.s1[h, p, :, cols] = value.astype(jnp.bfloat16)
        self.net.send(
            self.s1.at[:, 1 - self.pz, :, cols], self.b2.at[:, :, cols],
            self.slots[w] + 1, self.peers[1],
        )

    def second_of(self, w, value):
        cols = self.windows[w]
        self.s1[:, :, :, cols] = value.reshape(2, 2, -1, value.shape[1])
        self.net.send(
            self.s1.at[:, 1 - self.pz, :, cols], self.b2.at[:, :, cols],
            self.slots[w] + 1, self.peers[1],
        )

    def spread_of(self, w, value):
        cols = self.windows[w]
        self.s1[:, :, :, cols] = value.reshape(2, 2, -1, value.shape[1])
        z = 2 * self.hz + self.pz
        self.direct = self.net.slot(4, True)
        for d in range(1, 4):
            to = (z + d) % 4
            self.net.send(
                self.s1.at[to // 2, to % 2, :, cols], self.b4.at[z],
                self.direct + z, (2 * to + self.ix, self.peers[0][1]),
            )

    def spread_last(self, w):
        cols = self.windows[w]
        z = 2 * self.hz + self.pz
        value = self.s1[self.hz, self.pz, :, cols].astype(jnp.float32)
        for d in range(1, 4):
            to = (z + d) % 4
            self.net.arrived(self.b4.at[to], self.direct + to, (2 * to + self.ix, self.peers[0][1]))
            value = value + self.b4[to].astype(jnp.float32)
        return value

    def third(self, w):
        cols = self.windows[w]
        self.net.arrived(self.b2.at[:, :, cols], self.slots[w] + 1, self.peers[1])
        for h in range(2):
            value = self.s1[h, self.pz, :, cols].astype(jnp.float32)
            value = value + self.b2[h, :, cols].astype(jnp.float32)
            self.s2[h, :, cols] = value.astype(jnp.bfloat16)
        self.net.send(
            self.s2.at[1 - self.hz, :, cols], self.b3.at[:, cols],
            self.slots[w] + 2, self.peers[2],
        )

    def last(self, w):
        cols = self.windows[w]
        self.net.arrived(self.b3.at[:, cols], self.slots[w] + 2, self.peers[2])
        return self.s2[self.hz, :, cols].astype(jnp.float32) + self.b3[:, cols].astype(jnp.float32)


def make_fused(n_dp, in_local, images, sides, chan_in, chan_part):
    f32, bf16 = jnp.float32, jnp.bfloat16
    halves = tuple(side // 2 for side in sides)
    sizes = tuple(h * h * n for h, n in zip(halves, images))
    rows = sum(sizes)
    quarter = tuple(n // 4 for n in images)
    qlanes = tuple(q * side * side for q, side in zip(quarter, sides))
    slab_lanes = -(-sum(qlanes) // LANES) * LANES
    chan_full = 4 * chan_part
    out_rows = chan_full // n_dp
    starts = (0, sizes[0])
    widths = tuple(h * n for h, n in zip(halves, images))
    chunks = [(g, r, starts[g] + r * widths[g], widths[g]) for g in range(2) for r in range(halves[g])]
    win = [-(-q // LANES) * LANES for q in qlanes]
    b_tile = qlanes[0] // LANES * LANES
    n_sends, n_slots = 55, 107
    b_skip = qlanes[0] - b_tile
    rs = halves[0] // 2
    segments = [(1, 0, halves[1]), (0, 0, rs), (0, rs, halves[0])]
    seg_lane, runs = [], []
    lane_of = 0
    for g, r0, r1 in segments:
        side, base = sides[g], (0, qlanes[0])[g]
        seg_lane.append(lane_of)
        lane_of += quarter[g] * 2 * (r1 - r0) * side
        runs += [
            (base + (image * side + 2 * r0) * side, base + (image * side + 2 * r1) * side)
            for image in range(quarter[g])
        ]
    runs.append((sum(qlanes), slab_lanes))
    at, order = 0, []
    for a, b in runs:
        order.append((a, at, at + b - a))
        at += b - a
    back_runs = [(a, b) for _, a, b in sorted(order)]
    cut_lane = -(-seg_lane[2] // LANES) * LANES
    lane_parts = (slice(0, cut_lane), slice(cut_lane, slab_lanes))
    seg_cells = [(r1 - r0) * halves[g] for g, r0, r1 in segments]
    seg_rows = [cells * quarter[seg[0]] for cells, seg in zip(seg_cells, segments)]
    top = -(-(seg_rows[0] + seg_rows[1]) // 16) * 16
    seg_row = [0, seg_rows[0], top]
    q_rows = top + -(-seg_rows[2] // 16) * 16
    row_parts = (slice(0, top), slice(top, q_rows))
    patch_win = (slice(0, cut_lane), slice(seg_lane[1] // LANES * LANES, slab_lanes))
    patch_m, cells_m = quarter_matrices(
        quarter, sides, segments, seg_lane, seg_row, q_rows, slab_lanes
    )
    patch_ms = [
        np.concatenate([m[rows_, lanes_] for m in patch_m], axis=0)
        for rows_, lanes_ in zip(row_parts, patch_win)
    ]
    low_lane = seg_lane[1] // LANES * LANES
    last_lane = slab_lanes - LANES
    assert sum(qlanes) - last_lane <= LANES // 2
    out_lanes = [slice(cut_lane, last_lane), slice(0, low_lane), slice(low_lane, cut_lane)]
    back_pieces = (((0, 0, 2),), ((0, 2, halves[0] - 1),), ((0, halves[0] - 1, halves[0]), (1, 0, halves[1])))
    row_halves = [
        slice(starts[p[0][0]] + p[0][1] * widths[p[0][0]], starts[p[-1][0]] + p[-1][2] * widths[p[-1][0]])
        for p in back_pieces
    ]
    cols2 = (slice(0, 4 * LANES), slice(4 * LANES, 9 * LANES))
    cols1 = (slice(6 * LANES, 10 * LANES), slice(0, 6 * LANES))

    def kernel(*refs):
        (xa_h, xb_h, bxa_h, bxb_h, w1_h, w2_h, ws_h, g1_h, b1_h, g2_h, b2_h, gs_h, bs_h, ua_h, ub_h,
         pm0_h, pm1_h, cells_h,
         turn_h,
         oa, ob, gr, grf, gw1, gws, gw2, vecs, turn,
         xa, xb, bxa, bxb, w1g, w2, wsg, vg, g2, b2, gs, bs, ua, ub, pm0, pm1, cells,
         xs, xt, xr, zb, zsq, zsr, zg, zpa, zpb, valid, vq, hat, mask, zs, a1a, a1b,
         cslots, slots, stat, up, outr, gv, dza, dzb, dzma, dzmb, apk, arx, gacc, dzsr,
         dd, hp, hr1, hs, hr2, gu, d1a, d1b,
         p22, p23, p24, p25, p26, wg1, p11, p12, p13, p14, p15,
         sq, si, dq, di, gt, gtf, lsem, ssem, rsem) = refs
        i, k = lax.axis_index("dp"), lax.axis_index("chan")
        k1 = k + 1 - 2 * (k % 2)
        k2 = (k + 2) % 4
        k3 = (k1 + 2) % 4
        ix = i % 2
        mate = (i + 1 - 2 * ix, k)
        net = Links(ssem, rsem)
        bits = n_dp.bit_length() - 1

        def flip(d):
            j = i
            for b in range(bits):
                if d >> b & 1:
                    j = j + (1 << b) * (1 - 2 * ((i // (1 << b)) % 2))
            return j

        peers = [flip(d) for d in sorted(range(n_dp), key=lambda d: (d == 0, -(d >> 1), d & 1))]
        peers, home = peers[:-1], peers[-1]
        zp, a1, dz, d1 = (zpa, zpb), (a1a, a1b), (dza, dzb), (d1a, d1b)
        dzm = (dzma, dzmb)

        def flat(value):
            return value.reshape(-1, value.shape[-1])

        def zeros(count):
            return [jnp.zeros((8, LANES), f32)] * count

        loads = {}
        pairs_of = (
            ("xa", xa_h, xa), ("xb", xb_h, xb),
            ("w1", w1_h, w1g.at[k]), ("ws", ws_h, wsg.at[k]), ("g1", g1_h, vg.at[k, 0]), ("b1", b1_h, vg.at[k, 1]),
            ("bxa", bxa_h, bxa), ("bxb", bxb_h, bxb), ("pm0", pm0_h, pm0), ("pm1", pm1_h, pm1),
            ("ua", ua_h, ua), ("ub", ub_h, ub), ("g2", g2_h, g2),
            ("b2", b2_h, b2), ("gs", gs_h, gs), ("bs", bs_h, bs), ("w2", w2_h, w2), ("cells", cells_h, cells),
            ("turn", turn_h, turn),
        )
        for index, (name, source, target) in enumerate(pairs_of):
            loads[name] = pltpu.make_async_copy(source, target, lsem.at[index])
        loads["xa"].start()
        loads["xb"].start()

        def need(*names):
            for name in names:
                loads.pop(name).wait()

        barrier = pltpu.get_barrier_semaphore()
        for j in peers:
            pl.semaphore_signal(barrier, inc=1, device_id=(j, k), device_id_type=MESH)
        for where in (k1, k2, k3):
            pl.semaphore_signal(barrier, inc=1, device_id=(i, where), device_id_type=MESH)

        need("xa", "xb")
        for copy in loads.values():
            copy.start()
        lane = lax.broadcasted_iota(jnp.int32, (in_local, LANES), 1)
        for d, j in enumerate(peers + [home]):
            begin = 4 * qlanes[0] * j + qlanes[0] * k
            tile = begin // LANES
            part_a = xa[:, pl.ds(pl.multiple_of(tile * LANES, LANES), win[0])].astype(f32)
            part_a = pltpu.roll(part_a, (win[0] - (begin - tile * LANES)) % win[0], 1)
            begin = 4 * qlanes[1] * j + qlanes[1] * k
            tile = begin // LANES
            part_b = xb[:, pl.ds(pl.multiple_of(tile * LANES, LANES), win[1])].astype(f32)
            part_b = jnp.concatenate([part_b, jnp.zeros((in_local, LANES), f32)], axis=1)
            wide = win[1] + LANES
            part_b = pltpu.roll(part_b, (wide + b_skip - (begin - tile * LANES)) % wide, 1)
            seam = jnp.where(lane < b_skip, part_a[:, b_tile : b_tile + LANES], part_b[:, :LANES])
            xs[d * in_local : (d + 1) * in_local, :] = jnp.concatenate(
                [part_a[:, :b_tile], seam, part_b[:, LANES : slab_lanes - b_tile]], axis=1
            ).astype(bf16)
        slot_x = [net.slot(n_dp) for _ in lane_parts]
        n_via = 2
        via = [pl.ds((9 - n_via) * e, n_via) for e in (ix, 1 - ix)]
        w_taps = [via[0], slice(n_via, 5), slice(5, 9 - n_via)]
        slot_w = [net.slot(4) for _ in range(6)]

        def weight_refs(q):
            return [w1g.at[q, taps] for taps in w_taps] + [wsg.at[q], vg.at[q], w1g.at[q, via[1]]]

        ordered = regroup(xs[...], runs)
        for c, cols in enumerate(lane_parts):
            moved = ordered[:, cols]
            xt[:, :, cols] = moved.reshape(n_dp, in_local, moved.shape[1])
            xr[i, :, cols] = moved[-in_local:]
            if c == 0:
                pl.semaphore_wait(barrier, n_dp + 2)
            for d, j in enumerate(peers):
                net.send(xt.at[d, :, cols], xr.at[i, :, cols], slot_x[c] + i, (j, k))
            if c == 0:
                need("w1", "ws", "g1", "b1")
                for ref, slot in zip(weight_refs(k)[:5], slot_w):
                    net.send(ref, ref, slot + k, (i, k2))
                for ref, slot in zip(weight_refs(k), slot_w):
                    net.send(ref, ref, slot + k, (i, k1))

        def weights_on(n):
            ref = weight_refs(k2)[n]
            net.arrived(ref, slot_w[n] + k2, mate if n == 5 else (i, k2))
            net.send(ref, ref, slot_w[n] + k2, (i, k1))
            if n == 0:
                net.send(ref, ref, slot_w[5] + k2, mate)

        def weights_in(parts):
            for q in (k1, k3):
                for n in parts:
                    net.arrived(weight_refs(q)[n], slot_w[n] + q, (i, k1))

        for buf in (zpa, zpb, a1a, a1b, dza, dzb, dzma, dzmb, d1a, d1b):
            side = buf.shape[1] if len(buf.shape) == 5 else buf.shape[0]
            lead = (slice(None),) if len(buf.shape) == 5 else ()
            for edge in (0, side - 1):
                for index in (lead + (edge,), lead + (slice(None), edge)):
                    region = buf.at[index]
                    region[...] = jnp.zeros(region.shape, buf.dtype)
        need("bxa", "bxb", "ua", "ub")
        population = zeros(1)[0]
        low = lax.broadcasted_iota(jnp.int32, (8, LANES), 0) < 4
        for g, box in enumerate((bxa, bxb)):
            n, half, count = images[g], halves[g], quarter[g]
            diag = lax.broadcasted_iota(jnp.int32, (n, n), 0) == lax.broadcasted_iota(jnp.int32, (n, n), 1)
            ends = [
                jnp.sum(jnp.where(diag, box[q : q + 1, :].astype(f32), 0.0), axis=1, keepdims=True)
                for q in range(4)
            ]
            ends = [jnp.broadcast_to(e, (n, LANES)) for e in ends]
            ends[2], ends[3] = ends[0] + ends[2], ends[1] + ends[3]

            def inside(ends, r, s):
                both = (r >= ends[0]) & (r < ends[2]) & (s >= ends[1]) & (s < ends[3])
                return both.astype(f32)

            for r in range(half):
                for s in range(half):
                    cell = inside(ends, r, s)
                    begin = starts[g] + (r * half + s) * n
                    valid[begin : begin + n, :] = cell
                    population = population + jnp.sum(cell.reshape(n // 8, 8, LANES), axis=0)
            mine = [pltpu.roll(e, (n - count * k) % n, 0)[:8] for e in ends]
            if count < 8:
                mine = [jnp.where(low, e, pltpu.roll(e, 4, 0)) for e in mine]
            for (seg_g, r0, r1), first, cells_n in zip(segments, seg_row, seg_cells):
                if seg_g != g:
                    continue
                per = 8 // count
                for t in range(-(-cells_n // per)):
                    spots = [divmod(min(per * t + e, cells_n - 1), half) for e in range(per)]
                    spots = [(float(r0 + r), float(s)) for r, s in spots]
                    if per == 2:
                        r, s = (jnp.where(low, spots[0][e], spots[1][e]) for e in range(2))
                    else:
                        r, s = spots[0]
                    cell = inside(mine, r, s)
                    if per == 2 and per * t + 1 >= cells_n:
                        cell = jnp.where(low, cell, 0.0)
                    vq[first + 8 * t : first + 8 * t + 8, :] = cell
        population = jnp.broadcast_to(jnp.sum(population, axis=0, keepdims=True), (8, LANES))
        for g, source in enumerate((ua, ub)):
            n, count = images[g], halves[g] ** 2
            gu[starts[g] : starts[g] + sizes[g], :] = source[...].astype(f32)
            for cell in range(count):
                up[starts[g] + cell * n : starts[g] + (cell + 1) * n, :] = gu[
                    pl.ds(starts[g] + cell, n, stride=count), :
                ]

        def rowsum(value):
            return jnp.sum(value.reshape(-1, 8, value.shape[-1]), axis=0)

        def message(sums):
            parts = [jnp.sum(v, axis=0, keepdims=True) if v.shape[0] > 1 else v for v in sums]
            if len(parts) % 8:
                parts.append(jnp.zeros((8 - len(parts) % 8, LANES), f32))
            return jnp.concatenate(parts, axis=0)

        def by_chan(value):
            return [value[:, q * LANES : (q + 1) * LANES] for q in range(4)]

        used = []

        def share(rnd, value):
            mine = slots.at[rnd, i, : value.shape[0]]
            mine[...] = value
            first = net.slot(n_dp, True)
            used.append((first, n_dp))
            for j in peers:
                net.send(mine, mine, first + i, (j, k))
            return first

        def total(rnd, first, count=8):
            for j in peers:
                net.arrived(slots.at[rnd, j, :count], first + j, (j, k))
            return jnp.sum(slots[rnd, :, :count], axis=0)

        def chan_share(rnd, value):
            mine = cslots.at[rnd, k, : value.shape[0]]
            mine[...] = value
            first = net.slot(4)
            used.append((first, 4))
            for where in (k2, k3, k1):
                net.send(mine, mine, first + k, (i, where))
            return first

        def chan_total(rnd, first, count=8):
            for where in (k1, k2, k3):
                net.arrived(cslots.at[rnd, where, :count], first + where, (i, where))
            return jnp.sum(cslots[rnd, :, :count], axis=0)

        pop_first = share(4, population)

        def quarter_in(c):
            for j in peers:
                net.arrived(xr.at[j, :, lane_parts[c]], slot_x[c] + j, (j, k))

        def patches(c):
            whole = jnp.concatenate([xr[q, :, patch_win[c]] for q in range(n_dp)], axis=0)
            value = mm((pm0, pm1)[c][...], whole, 1, 1).astype(bf16)
            count = value.shape[0] // 9
            return [value[t * count : (t + 1) * count] for t in range(9)]

        slot_s = net.slot(4)

        z_cuts = (slice(0, top * 3 // 80 * 16), slice(top * 3 // 80 * 16, top), slice(top, q_rows))
        slot_z = [net.slot(4) for _ in z_cuts]

        def z_send(n):
            for where in (k2, k1):
                net.send(zb.at[k, z_cuts[n]], zb.at[k, z_cuts[n]], slot_z[n] + k, (i, where))

        def conv_taps(taps, some):
            weights = lanes_cat([w1g[q, some].reshape(-1, chan_part) for q in range(4)])
            return mm(lanes_cat(taps[some]), weights, 1, 0)

        def first_conv(c, value, acc):
            part = row_parts[c]
            value = value.astype(bf16)
            zb[k, part, :] = value
            if c == 0:
                z_send(0)
            z = value.astype(f32)
            u = z * lanes_cat([vq[part, :]] * 4)
            return [acc[0] + rowsum(u), acc[1] + rowsum(u * z)]

        def projection(c, patch, acc):
            side = mm(patch, lanes_cat([wsg[q] for q in range(4)]), 1, 0).astype(bf16)
            for q, z in enumerate(by_chan(side)):
                zsq[q, row_parts[c], :] = z
            z = side.astype(f32)
            u = z * lanes_cat([vq[row_parts[c], :]] * 4)
            return [acc[0] + rowsum(u), acc[1] + rowsum(u * z)]

        def act_on(n):
            part = zb.at[k2, z_cuts[n]]
            net.arrived(part, slot_z[n] + k2, (i, k2))
            net.send(part, part, slot_z[n] + k2, (i, k1))

        def act_in(n):
            net.arrived(zb.at[k1, z_cuts[n]], slot_z[n] + k1, (i, k1))
            net.arrived(zb.at[k3, z_cuts[n]], slot_z[n] + k3, (i, k1))

        acc = [jnp.zeros((8, chan_full), f32)] * 2
        need("pm0", "pm1")
        for n in (0, 1, 5, 2):
            weights_on(n)
        quarter_in(0)
        taps = patches(0)
        center = [taps[4]]
        weights_on(3)
        weights_on(4)
        weights_in((0, 1, 5))
        value = conv_taps(taps, slice(0, 5)) + conv_taps(taps, slice(9 - n_via, 9))
        weights_in((2,))
        acc = first_conv(0, value + conv_taps(taps, slice(5, 9 - n_via)), acc)
        quarter_in(1)
        taps = patches(1)
        center.append(taps[4])
        acc = first_conv(1, conv_taps(taps, slice(0, 9)), acc)
        acc = [jnp.sum(v, axis=0, keepdims=True) for v in acc]
        first = chan_share(0, message(sum((by_chan(v) for v in acc), [])))
        gone = net.mark()
        z_send(1)
        z_send(2)
        weights_in((3, 4))
        acc = [jnp.zeros((8, chan_full), f32)] * 2
        for c in range(2):
            acc = projection(c, center[c], acc)
        acc = [jnp.sum(v, axis=0, keepdims=True) for v in acc]
        side_first = share(5, message(sum((by_chan(v) for v in acc), [])))
        zsr[k] = zsq[k]

        need(*list(loads))
        row_cuts = (slice(0, rows // 32 * 16), slice(rows // 32 * 16, rows))
        slot_g0 = [net.slot(4) for _ in row_cuts]
        whole = jnp.concatenate([xr[q] for q in range(n_dp)], axis=0)
        for span in row_cuts:
            zg[k, span, :] = mm(cells[span, :], whole, 1, 1).astype(bf16)
        net.settle(gone)
        first = share(0, chan_total(0, first))
        for where in (k2, k3, k1):
            net.send(zsq.at[where], zsr.at[k], slot_s + k, (i, where))
        act_on(0)
        act_on(1)
        act_on(2)
        side_first = chan_share(2, total(5, side_first))
        gone = net.mark()
        for span, slot in zip(row_cuts, slot_g0):
            for where in (k2, k1):
                net.send(zg.at[k, span], zg.at[k, span], slot + k, (i, where))

        def slab_on(n):
            span, slot = row_cuts[n], slot_g0[n]
            net.arrived(zg.at[k2, span], slot + k2, (i, k2))
            net.send(zg.at[k2, span], zg.at[k2, span], slot + k2, (i, k1))

        def slab_in(n):
            span, slot = row_cuts[n], slot_g0[n]
            net.arrived(zg.at[k1, span], slot + k1, (i, k1))
            net.arrived(zg.at[k3, span], slot + k3, (i, k1))

        inv_pop = 1.0 / total(4, pop_first)[0:1]
        turn_low = lax.broadcasted_iota(jnp.int32, (8, 1), 0) < 4

        def whole_cells(read, c):
            for begin in range(row_parts[c].start, row_parts[c].stop, 16):
                blocks = [read(q, slice(begin, begin + 16)).astype(f32) for q in range(4)]
                for at in (begin, begin + 8):
                    seg = max(e for e in range(3) if seg_row[e] <= at)
                    g, r0, r1 = segments[seg]
                    per = 8 // quarter[g]
                    v = [block[at - begin : at - begin + 8] for block in blocks]
                    cell = (at - seg_row[seg]) // 8 * per
                    if per == 1:
                        found = [jnp.concatenate(v, axis=0)]
                    else:
                        t = [pltpu.roll(e, 4, 0) for e in v]
                        found = [
                            jnp.concatenate(
                                [jnp.where(turn_low, v[0], t[1]), jnp.where(turn_low, v[2], t[3])], axis=0
                            ),
                            jnp.concatenate(
                                [jnp.where(turn_low, t[0], v[1]), jnp.where(turn_low, t[2], v[3])], axis=0
                            ),
                        ]
                    for e, value in enumerate(found):
                        if cell + e < seg_cells[seg]:
                            r, s = divmod(cell + e, halves[g])
                            yield g, r0 + r, s, value

        def gather_cells(c):
            for g, r, s, z in whole_cells(lambda q, span: zb[q, span, :], c):
                begin = starts[g] + (r * halves[g] + s) * images[g]
                hat[begin : begin + images[g], :] = z

        for n in range(2):
            act_in(n)
        gather_cells(0)
        act_in(2)
        gather_cells(1)
        tot = total(0, first)
        stat[0:8, :] = tot
        tot_first = (stat[pl.ds(k, 1), :], stat[pl.ds(4 + k, 1), :])
        def moments(total_, square):
            mean = total_ * inv_pop
            return mean, lax.rsqrt(square * inv_pop - mean * mean + epsilon)

        mean1, sc1 = moments(tot[0:4], tot[4:8])
        mean1, sc1 = (lanes_cat([v[q : q + 1] for q in range(4)]) for v in (mean1, sc1))
        gain1, shift1 = (lanes_cat([vg[q, e] for q in range(4)]) for e in range(2))

        scale1 = sc1 * gain1
        offset1 = shift1 - mean1 * scale1

        def activate(c):
            for g, r0, r1 in (segments[:2], segments[2:])[c]:
                for r in range(r0, r1):
                    for s in range(halves[g]):
                        begin = starts[g] + (r * halves[g] + s) * images[g]
                        span = slice(begin, begin + images[g])
                        v = hat[span, :] * scale1 + offset1
                        act = v * sigma(v) * lanes_cat([valid[span, :]] * 4)
                        a1[g][1 + r, 1 + s] = act.astype(bf16)

        def second_conv(parts, acc):
            value = None
            for a, b in TAPS:
                patch = jnp.concatenate(
                    [flat(a1[g][r0 + a : r1 + a, b : b + halves[g]]) for g, r0, r1 in parts], axis=0
                )
                part = mm(patch, w2[3 * a + b], 1, 0)
                value = part if value is None else value + part
            at = 0
            for g, r0, r1 in parts:
                for r in range(r0, r1):
                    begin = starts[g] + r * widths[g]
                    span = slice(begin, begin + widths[g])
                    u = value[at : at + widths[g]]
                    at += widths[g]
                    gv[span, :] = u
                    uv = u * valid[span, :]
                    acc = [acc[0] + rowsum(uv), acc[1] + rowsum(uv * u)]
            return acc

        left = lax.broadcasted_iota(jnp.int32, (1, LANES), 1) < out_rows

        def pack(g, r0, r1):
            for r in range(r0, r1):
                v = by_chan(flat(a1[g][1 + r, 1 : 1 + halves[g]]).astype(f32))
                t = [pltpu.roll(e, out_rows, 1) for e in v]
                begin = starts[g] + r * widths[g]
                span = slice(begin, begin + widths[g])
                for p in range(2):
                    cols = slice(p * LANES, (p + 1) * LANES)
                    apk[0, span, cols] = jnp.where(left, v[2 * p], t[2 * p + 1]).astype(bf16)
                    apk[1, span, cols] = jnp.where(left, t[2 * p], v[2 * p + 1]).astype(bf16)

        near = sizes[1]
        far = sizes[0] * 9 // 16 // 16 * 16
        pack_spans = [
            [slice(starts[1], starts[1] + near)],
            [slice(0, far)],
            [slice(far, sizes[0])],
        ]
        slot_p = [[net.slot() for _ in spans_] for spans_ in pack_spans]

        def pack_send(n):
            for span, slot in zip(pack_spans[n], slot_p[n]):
                net.send(apk.at[1 - ix, span], arx.at[span], slot, mate)

        activate(0)
        pack(1, 0, halves[1])
        pack(0, 0, rs)
        pack_send(0)
        acc = second_conv([(1, 0, halves[1]), (0, 0, rs - 1)], zeros(2))
        activate(1)
        pack(0, rs, halves[0])
        acc = second_conv([(0, rs - 1, halves[0])], acc)
        first = share(1, message(acc))
        pack_send(1)

        stat[0:8, :] = chan_total(2, side_first)
        means, scs = moments(stat[pl.ds(k, 1), :], stat[pl.ds(4 + k, 1), :])
        for where in (k2, k3, k1):
            net.arrived(zsr.at[where], slot_s + where, (i, where))
        for c in range(2):
            for g, r, s, z in whole_cells(lambda q, span: zsr[q, span, :], c):
                begin = starts[g] + (r * halves[g] + s) * images[g]
                zs[begin : begin + images[g], :] = (z - means) * scs

        def planes_of(quarters, g):
            count = quarter[g]
            if count % 8 == 0:
                return [
                    jnp.concatenate([v[:, count * p : count * (p + 1)] for v in quarters], axis=1)
                    for p in range(4)
                ]
            low = lax.broadcasted_iota(jnp.int32, (1, 8, 1), 1) < 4
            parts = [[v[:, 8 * h : 8 * h + 8] for v in quarters] for h in range(2)]
            turned = [[pltpu.roll(v, 4, 1) for v in side] for side in parts]
            result = []
            for p in range(4):
                v, t = parts[p // 2], turned[p // 2]
                if p % 2 == 0:
                    both = [jnp.where(low, v[0], t[1]), jnp.where(low, v[2], t[3])]
                else:
                    both = [jnp.where(low, t[0], v[1]), jnp.where(low, t[2], v[3])]
                result.append(jnp.concatenate(both, axis=1))
            return result

        def make_planes():
            for g, r, begin, count in chunks:
                quarters = [
                    zg[q, begin : begin + count, :].astype(f32).reshape(halves[g], images[g], chan_in)
                    for q in range(4)
                ]
                for p, value in enumerate(planes_of(quarters, g)):
                    zp[g][p, 1 + r, 1 : 1 + halves[g]] = value.astype(bf16)

        net.settle(gone)
        tot = total(1, first)
        net.spare |= set(range(slot_x[0], slot_x[-1] + n_dp)) | set(range(slot_w[0], slot_w[-1] + 4))
        mean2, sc2 = moments(tot[0:1], tot[1:2])
        gain2, gains = g2[...], gs[...]
        shifts = b2[...] + bs[...]
        acc = zeros(3)
        for g, r, begin, count in chunks:
            span = slice(begin, begin + count)
            ok = valid[span, :]
            hat2 = (gv[span, :] - mean2) * sc2
            hats = zs[span, :]
            v = hat2 * gain2 + hats * gains + shifts
            sig = sigma(v)
            outr[span, :] = v * sig * ok
            grad = up[span, :] * ok * (sig * (1.0 + v * (1.0 - sig)))
            up[span, :] = grad
            gv[span, :] = hat2
            acc = [acc[0] + rowsum(grad), acc[1] + rowsum(grad * hat2), acc[2] + rowsum(grad * hats)]
        first = share(2, message(acc))
        pack_send(2)
        for g, target in enumerate((oa, ob)):
            n, count = images[g], halves[g] ** 2
            for cell in range(count):
                gu[pl.ds(starts[g] + cell, n, stride=count), :] = outr[
                    starts[g] + cell * n : starts[g] + (cell + 1) * n, :
                ]
            target[...] = gu[starts[g] : starts[g] + sizes[g], :].astype(bf16)
        for begin in range(0, rows, 16):
            span = slice(begin, begin + 16)
            h = (hat[span, :] - mean1) * sc1
            hat[span, :] = h
            v = h * gain1 + shift1
            sig = sigma(v)
            mask[span, :] = sig * (1.0 + v * (1.0 - sig)) * lanes_cat([valid[span, :]] * 4)
        net.settle(gone)
        gone = net.mark()
        tot = total(2, first)
        done = used[:-1] + [(begin, 4) for begin in slot_z] + [(slot_s, 4)]
        net.spare_dp |= {begin + e for begin, count in done for e in range(count)}
        sum_tail, sum_gain2, sum_gains = tot[0:1], tot[1:2], tot[2:3]
        k2g, ksg = gain2 * sc2, gains * scs
        db, dg2, dgs = sum_tail * inv_pop, sum_gain2 * inv_pop, sum_gains * inv_pop
        for g, r, begin, count in chunks:
            span = slice(begin, begin + count)
            value = k2g * (up[span, :] - valid[span, :] * (db + gv[span, :] * dg2))
            dz[g][1 + r, 1 : 1 + halves[g]] = value.astype(bf16).reshape(halves[g], images[g], chan_part)
        slot_d = net.slot(2)

        def dz_inner(buf, g):
            return buf[g].at[1 : 1 + halves[g], 1 : 1 + halves[g]]

        for g in range(2):
            net.send(dz_inner(dz, g), dz_inner(dzm, g), slot_d + g, mate)

        def columns(buf, piece, taps=range(9)):
            for g, r0, r1 in piece:
                for t in taps:
                    a, b = TAPS[t]
                    dd[
                        starts[g] + r0 * widths[g] : starts[g] + r1 * widths[g],
                        t * LANES : (t + 1) * LANES,
                    ] = flat(buf[g][r0 + 2 - a : r1 + 2 - a, 2 - b : 2 - b + halves[g]])

        def back_second(first, span):
            begin = pl.multiple_of(first * chan_part, LANES)
            weights = lanes_cat([w2[t, pl.ds(begin, 2 * chan_part), :] for t in range(9)])
            value = mm(dd[span, :], weights, 1, 1).astype(bf16)
            hp[first, span, :] = value[:, :chan_part]
            hp[first + 1, span, :] = value[:, chan_part:]

        slot_h = [net.slot(3) for _ in row_halves]
        def other_pair(n):
            columns(dz, back_pieces[n])
            back_second(2 * (k2 // 2), row_halves[n])
            net.send(hp.at[k3, row_halves[n]], hr1.at[1, row_halves[n]], slot_h[n] + 1, (i, k1))

        def cross_second(n):
            span = row_halves[n]
            net.arrived(hr1.at[1, span], slot_h[n] + 1, (i, k1))
            hs[span, :] = (hp[k2, span, :].astype(f32) + hr1[1, span, :].astype(f32)).astype(bf16)
            net.send(hs.at[span], hr2.at[span], slot_h[n] + 2, (i, k2))

        def pair_sums(first):
            acc = [jnp.zeros((8, 2 * chan_part), f32)] * 2
            cols = pl.ds(pl.multiple_of(first * chan_part, 2 * LANES), 2 * chan_part)
            for begin in range(0, rows, 16):
                span = slice(begin, begin + 16)
                part = lanes_cat([hp[first + e, span, :] for e in range(2)]).astype(f32) * mask[span, cols]
                acc = [acc[0] + rowsum(part), acc[1] + rowsum(part * hat[span, cols])]
            acc = [jnp.sum(v, axis=0, keepdims=True) for v in acc]
            for e in range(2):
                for n in range(2):
                    stat[pl.ds(4 * n + first + e, 1), :] = acc[n][:, e * LANES : (e + 1) * LANES]

        other_pair(0)
        other_pair(1)
        cross_second(0)
        other_pair(2)
        cross_second(1)
        back_second(2 * (k // 2), slice(0, rows))
        pair_sums(2 * (k2 // 2))
        cross_second(2)
        for span, slot in zip(row_halves, slot_h):
            net.send(hp.at[k1, span], hr1.at[0, span], slot, (i, k1))
        pair_sums(2 * (k // 2))
        first = share(3, stat[0:8, :])

        sum2 = Reduce(net, i, k, None, (None, p22, p23, p24, p25), cols2, p26)
        gacc[...] = mm(apk[ix], dd[...], 0, 0)
        net.settle(gone)
        first = chan_share(1, total(3, first))
        def split_cells(read, target, c):
            for begin in range(row_parts[c].start, row_parts[c].stop, 16):
                tiles = []
                for at in (begin, begin + 8):
                    seg = max(e for e in range(3) if seg_row[e] <= at)
                    g, r0, r1 = segments[seg]
                    per = 8 // quarter[g]
                    cell = (at - seg_row[seg]) // 8 * per
                    blocks = []
                    for e in range(per):
                        if cell + e < seg_cells[seg]:
                            r, s = divmod(cell + e, halves[g])
                            blocks.append(read(g, r0 + r, s))
                        else:
                            blocks.append(jnp.zeros((images[g], chan_part), f32))
                    if per == 1:
                        tiles.append([blocks[0][8 * q : 8 * q + 8] for q in range(4)])
                    else:
                        found = []
                        for h in range(2):
                            v = [block[8 * h : 8 * h + 8] for block in blocks]
                            t = [pltpu.roll(e, 4, 0) for e in v]
                            found += [jnp.where(turn_low, v[0], t[1]), jnp.where(turn_low, t[0], v[1])]
                        tiles.append(found)
                for q in range(4):
                    both = jnp.concatenate([tiles[0][q], tiles[1][q]], axis=0)
                    target[q, begin : begin + 16, :] = both.astype(bf16)

        def cell_span(g, r, s):
            begin = starts[g] + (r * halves[g] + s) * images[g]
            return slice(begin, begin + images[g])

        def short_cell(g, r, s):
            span = cell_span(g, r, s)
            value = ksg * (up[span, :] - valid[span, :] * (db + zs[span, :] * dgs))
            dzsr[span, :] = value.astype(bf16)
            return value

        slot_q = [net.slot(4) for _ in range(3)]

        def quarters_out(source, target, span, slot):
            for where in (k2, k3, k1):
                net.send(source.at[where, span], target.at[k, span], slot + k, (i, where))
            target[k, span, :] = source[k, span, :]

        def quarters_in(target, span, slot):
            for where in (k1, k2, k3):
                net.arrived(target.at[where, span], slot + where, (i, where))

        for c in range(2):
            split_cells(short_cell, sq, c)
        quarters_out(sq, si, slice(0, q_rows), slot_q[2])
        for n in range(2):
            slab_on(n)
        for spans_, slots_ in zip(pack_spans, slot_p):
            for span, slot in zip(spans_, slots_):
                net.arrived(arx.at[span], slot, mate)
        for g in range(2):
            net.arrived(dz_inner(dzm, g), slot_d + g, mate)
        gone = net.mark()
        for w, cols in enumerate(cols2):
            for piece in back_pieces:
                columns(dzm, piece, range(cols.start // LANES, cols.stop // LANES))
            value = (gacc[:, cols] + mm(arx[...], dd[:, cols], 0, 0)).astype(bf16)
            (sum2.spread_of, sum2.second_of)[w](w, value)
        tot = chan_total(1, first)
        stat[0:8, :] = tot
        sum_head, sum_gain1 = stat[pl.ds(k, 1), :], stat[pl.ds(4 + k, 1), :]

        def close_second():
            for w, cols in enumerate(cols2):
                value = (sum2.spread_last, sum2.last)[w](w)
                for t in range(cols.start // LANES, cols.stop // LANES):
                    gw2[t] = value[:, t * LANES - cols.start : (t + 1) * LANES - cols.start]

        own = pl.ds(pl.multiple_of(k * chan_part, LANES), chan_part)
        mean1, sc1 = moments(tot_first[0], tot_first[1])
        k1g = vg[k, 0] * sc1
        db, dg1 = sum_head * inv_pop, sum_gain1 * inv_pop
        for span, slot in zip(row_halves, slot_h):
            net.arrived(hr1.at[0, span], slot, (i, k1))
            net.arrived(hr2.at[span], slot + 2, (i, k2))

        def first_cell(g, r, s):
            span = cell_span(g, r, s)
            grad = hp[k, span, :].astype(f32) + hr1[0, span, :].astype(f32) + hr2[span, :].astype(f32)
            grad = grad * mask[span, own]
            value = k1g * (grad - valid[span, :] * (db + hat[span, own] * dg1))
            d1[g][r, s] = value.astype(bf16)
            return value

        for c in (1, 0):
            split_cells(first_cell, dq, c)
            quarters_out(dq, di, row_parts[c], slot_q[c])

        def back_patch(pieces, p):
            parts = []
            for g, r0, r1 in pieces:
                width = halves[g] * images[g]
                taps = [
                    flat(d1[g][r0 + (a == 0) : r1 + (a == 0), (b == 0) : (b == 0) + halves[g]])
                    for a, b in PLANE_TAPS[p]
                ]
                if p == 0:
                    taps.append(dzsr[starts[g] + r0 * width : starts[g] + r1 * width, :])
                parts.append(lanes_cat(taps))
            return jnp.concatenate(parts, axis=0) if len(parts) > 1 else parts[0]

        slot_o = [net.slot(n_dp, True) for _ in out_lanes]

        def back_taps(c):
            part = row_parts[c]
            quarters_in(di, part, slot_q[c])
            grads = lanes_cat([di[q, part, :] for q in range(4)])
            weights = lanes_cat([w1g[q].reshape(9 * chan_in, chan_part) for q in range(4)])
            value = mm(grads, weights, 1, 1)
            taps = [value[:, t * chan_in : (t + 1) * chan_in] for t in range(9)]
            side = lanes_cat([si[q, part, :] for q in range(4)])
            taps[4] = taps[4] + mm(side, lanes_cat([wsg[q] for q in range(4)]), 1, 1)
            return jnp.concatenate([tap.astype(bf16) for tap in taps], axis=0)

        slot_f = net.slot(n_dp, True)

        def out_send(n, value):
            cols = out_lanes[n]
            if n == 0:
                last_tile = value[:, value.shape[1] - LANES :].reshape(n_dp, in_local, LANES)
                gtf[...] = fold(last_tile).astype(bf16)
                grf[i] = gtf[i]
                for j in peers:
                    net.send(gtf.at[j], grf.at[i], slot_f + i, (j, k))
                value = value[:, : value.shape[1] - LANES]
            gt[:, :, cols] = value.astype(bf16).reshape(n_dp, in_local, value.shape[1])
            for j in peers:
                net.send(gt.at[j, :, cols], gr.at[i, :, cols], slot_o[n] + i, (j, k))

        sum1 = Reduce(net, i, k, wg1, (p11, p12, p13, p14, p15), cols1)

        def weight_first(w):
            cols = cols1[w]
            blocks = []
            for p in ((3,), (0, 1, 2))[w]:
                value = 0.0
                for g, r0, r1 in ((0, 0, halves[0]), (1, 0, halves[1])):
                    cell = flat(zp[g][p, 1 : 1 + halves[g], 1 : 1 + halves[g]])
                    value = value + mm(cell, back_patch([(g, r0, r1)], p), 0, 0)
                blocks.append(value.astype(bf16))
            wg1[:, :, :, :, cols] = lanes_cat(blocks).reshape(2, 2, 2, in_local, cols.stop - cols.start)
            sum1.first(w)

        for n in range(2):
            slab_in(n)
        make_planes()
        weight_first(0)
        weight_first(1)
        net.settle(gone)
        quarters_in(si, slice(0, q_rows), slot_q[2])
        late = back_taps(1)
        edge = cut_lane - patch_win[1].start
        out_send(0, mm(late, pm1[:, edge:], 0, 0))
        early_ = back_taps(0)
        out_send(1, mm(early_, pm0[:, :low_lane], 0, 0))
        rest = mm(early_, pm0[:, low_lane:], 0, 0)
        shared = mm(late, pm1[:, low_lane - patch_win[1].start : edge], 0, 0)
        sum2.third(1)
        sum1.second(0)
        sum1.second(1)
        out_send(2, rest + shared)
        sum1.third(0)
        sum1.third(1)
        gr[i] = gt[i]
        close_second()
        for w, cols in enumerate(cols1):
            value = sum1.last(w)
            for t, tap in enumerate(TAPS):
                place = ORDER.index(tap)
                place = (place + (place > 0)) * LANES
                if cols.start <= place < cols.stop:
                    gw1[t] = value[:, place - cols.start : place - cols.start + LANES]
            if cols.start <= LANES < cols.stop:
                gws[...] = value[:, LANES - cols.start : 2 * LANES - cols.start]
        vecs[...] = message([sum_gain1, sum_head, sum_gain2, sum_tail, sum_gains])
        for j in peers:
            net.arrived(grf.at[j], slot_f + j, (j, k))
        for c, cols in enumerate(out_lanes):
            for j in peers:
                net.arrived(gr.at[j, :, cols], slot_o[c] + j, (j, k))
        net.drain()
        assert net.sends <= n_sends and net.slots <= n_slots

    V = pltpu.VMEM
    pads = [(h + 2, h + 2, n, chan_part) for h, n in zip(halves, images)]
    half_pads = [(h + 1, h + 1, n) for h, n in zip(halves, images)]

    def ladder(count, width):
        return [
            V((2, 2, 2, count, width), bf16), V((2, 2, count, width), bf16), V((2, 2, count, width), bf16),
            V((2, count, width), bf16), V((2, count, width), bf16), V((count, width), bf16),
        ]

    inputs = [
        V((in_local, n_dp * 4 * qlanes[0]), bf16), V((in_local, n_dp * 4 * qlanes[1]), bf16),
        V((4, images[0]), jnp.int32), V((4, images[1]), jnp.int32),
        V((4, 9, chan_in, chan_part), bf16), V((9, chan_full, chan_part), bf16),
        V((4, chan_in, chan_part), bf16), V((4, 2, 1, chan_part), f32),
    ] + [V((1, chan_part), f32)] * 4 + [
        V((sizes[0], chan_part), bf16), V((sizes[1], chan_part), bf16),
    ] + [V(m.shape, bf16) for m in patch_ms] + [V((rows, slab_lanes), bf16)]
    scratch = inputs + [
        V((n_dp * in_local, slab_lanes), bf16),
        V((n_dp, in_local, slab_lanes), bf16),
        V((n_dp, in_local, slab_lanes), bf16),
        V((4, q_rows, chan_full), bf16),
        V((4, q_rows, chan_part), bf16),
        V((4, q_rows, chan_part), bf16),
        V((4, rows, chan_in), bf16),
        V((4,) + half_pads[0] + (chan_in,), bf16),
        V((4,) + half_pads[1] + (chan_in,), bf16),
        V((rows, LANES), f32),
        V((q_rows, LANES), f32),
        V((rows, chan_full), f32),
        V((rows, chan_full), f32),
        V((rows, chan_part), f32),
        V(pads[0][:3] + (chan_full,), bf16),
        V(pads[1][:3] + (chan_full,), bf16),
        V((3, 4, 16, LANES), f32),
        V((6, n_dp, 16, LANES), f32),
        V((16, LANES), f32),
        V((rows, chan_part), f32),
        V((rows, chan_part), f32),
        V((rows, chan_part), f32),
        V(pads[0], bf16),
        V(pads[1], bf16),
        V(pads[0], bf16),
        V(pads[1], bf16),
        V((2, rows, chan_full // 2), bf16),
        V((rows, chan_full // 2), bf16),
        V((chan_full // 2, 9 * chan_part), f32),
        V((rows, chan_part), bf16),
        V((rows, 9 * chan_part), bf16),
        V((4, rows, chan_part), bf16),
        V((2, rows, chan_part), bf16),
        V((rows, chan_part), bf16),
        V((rows, chan_part), bf16),
        V((rows, chan_part), f32),
        V(half_pads[0] + (chan_part,), bf16),
        V(half_pads[1] + (chan_part,), bf16),
    ]
    scratch += ladder(out_rows, 9 * LANES)[2:]
    scratch += [V((n_dp // 2, out_rows, cols2[0].stop), bf16)] + ladder(in_local, 10 * LANES)
    scratch += [
        V((4, q_rows, chan_part), bf16),
        V((4, q_rows, chan_part), bf16),
        V((4, q_rows, chan_part), bf16),
        V((4, q_rows, chan_part), bf16),
        V((n_dp, in_local, last_lane), bf16),
        V((n_dp, in_local // 2, LANES), bf16),
        pltpu.SemaphoreType.DMA((20,)),
        pltpu.SemaphoreType.DMA((n_sends,)),
        pltpu.SemaphoreType.DMA((n_slots,)),
    ]
    mid_outs = [
        V((sizes[0], chan_part), bf16),
        V((sizes[1], chan_part), bf16),
        V((n_dp, in_local, last_lane), bf16),
        V((n_dp, in_local // 2, LANES), bf16),
        V((9, in_local, LANES), f32),
        V((in_local, LANES), f32),
        V((9, out_rows, LANES), f32),
        V((8, LANES), f32),
        V((n_dp * in_local, n_dp * in_local), bf16),
    ]
    vmem = pl.BlockSpec(memory_space=pltpu.VMEM)
    hbm = pl.BlockSpec(memory_space=pl.ANY)
    main = pl.pallas_call(
        kernel,
        out_shape=mid_outs,
        in_specs=[hbm] * 19,
        out_specs=[vmem] * len(mid_outs),
        scratch_shapes=scratch,
        compiler_params=pltpu.CompilerParams(
            collective_id=1, has_side_effects=True, vmem_limit_bytes=58 * 2**20
        ),
        name="block",
    )

    def closing(oa, ob, gr, grf, gw1, gws, gw2, vecs, turn,
                fa, fb, ia, ib, f1, f2, fs, c1, h1, c2, h2, cs, hs, iav, ibv, sems):
        outs = [
            pltpu.make_async_copy(source, target, sems.at[index])
            for index, (source, target) in enumerate(
                ((gw2, f2), (gw1, f1), (oa, fa), (ob, fb), (gws, fs))
            )
        ]
        for out in outs:
            out.start()
        tail = unfold(grf[...].astype(f32)).astype(bf16).reshape(n_dp * in_local, LANES)
        moved = jnp.concatenate([gr[...].reshape(n_dp * in_local, last_lane), tail], axis=1)
        n_half = in_local // 2
        for h in range(2):
            part = slice(h * n_half, (h + 1) * n_half)
            natural = regroup(mm(turn[h * n_half * n_dp : (h + 1) * n_half * n_dp, :], moved, 1, 0), back_runs)
            iav[part] = natural[:, : qlanes[0]].reshape(n_half, n_dp, qlanes[0]).astype(bf16)
            tail = natural[:, qlanes[0] : qlanes[0] + qlanes[1]]
            ibv[part] = tail.reshape(n_half, n_dp, qlanes[1]).astype(bf16)
            for e, (source, target) in enumerate(((iav, ia), (ibv, ib))):
                out = pltpu.make_async_copy(source.at[part], target.at[part], sems.at[5 + 2 * h + e])
                out.start()
                outs.append(out)
        for ref, row in ((c1, 0), (h1, 1), (c2, 2), (h2, 3), (cs, 4), (hs, 3)):
            ref[...] = vecs[row : row + 1, :]
        for out in outs:
            out.wait()

    last = pl.pallas_call(
        closing,
        out_shape=[
            jax.ShapeDtypeStruct((sizes[0], chan_part), bf16),
            jax.ShapeDtypeStruct((sizes[1], chan_part), bf16),
            jax.ShapeDtypeStruct((in_local, n_dp, qlanes[0]), bf16),
            jax.ShapeDtypeStruct((in_local, n_dp, qlanes[1]), bf16),
            jax.ShapeDtypeStruct((9, in_local, LANES), f32),
            jax.ShapeDtypeStruct((9, out_rows, LANES), f32),
            jax.ShapeDtypeStruct((in_local, LANES), f32),
        ]
        + [jax.ShapeDtypeStruct((1, LANES), f32)] * 6,
        in_specs=[vmem] * 9,
        out_specs=[hbm] * 7 + [vmem] * 6,
        scratch_shapes=[
            V((in_local, n_dp, qlanes[0]), bf16),
            V((in_local, n_dp, qlanes[1]), bf16),
            pltpu.SemaphoreType.DMA((9,)),
        ],
        compiler_params=pltpu.CompilerParams(vmem_limit_bytes=32 * 2**20),
        name="closing",
    )
    total_rows = n_dp * in_local
    turn = np.zeros((total_rows, total_rows), np.float32)
    for c in range(in_local):
        for j in range(n_dp):
            turn[c * n_dp + j, j * in_local + c] = 1.0
    return (main, last) + tuple(m.astype(jnp.bfloat16) for m in (*patch_ms, cells_m, turn))


def fused_body(
    input_a, input_b, boxes_a, boxes_b, weight_first, weight_second, weight_short,
    gain_first, shift_first, gain_second, shift_second, gain_short, shift_short,
    upstream_a, upstream_b,
):
    n_dp = lax.axis_size("dp")
    chan_part = weight_first.shape[2]
    in_local = input_a.shape[0]
    main, last, *matrices = make_fused(
        n_dp, in_local, (boxes_a.shape[0], boxes_b.shape[0]), (SA, SB),
        weight_first.shape[1], chan_part,
    )
    vectors = [
        v.reshape(1, chan_part)
        for v in (gain_first, shift_first, gain_second, shift_second, gain_short, shift_short)
    ]
    mid = main(
        input_a, input_b, boxes_a.T, boxes_b.T, weight_first, weight_second, weight_short,
        *vectors, upstream_a.T, upstream_b.T, *matrices,
    )
    res = last(*mid)
    return (
        res[0].T, res[1].T,
        res[2].reshape(in_local, n_dp, 1, -1), res[3].reshape(in_local, n_dp, 1, -1),
        res[4], res[5], res[6],
    ) + tuple(v.reshape(chan_part) for v in res[7:])


def choose_body(mesh):
    return fused_body if mesh.shape["dp"] == 8 and mesh.shape["chan"] == 4 else plain_body


def solution(mesh):
    placed = (
        P("dp", None),
        P("dp", None),
        P("dp", None),
        P("dp", None),
        P(None, None, "chan"),
        P(None, None, "chan"),
        P(None, "chan"),
        P("chan"),
        P("chan"),
        P("chan"),
        P("chan"),
        P("chan"),
        P("chan"),
        P("chan", "dp"),
        P("chan", "dp"),
    )
    return jax.shard_map(
        choose_body(mesh),
        mesh=mesh,
        in_specs=placed,
        out_specs=(
            P("chan", "dp"),
            P("chan", "dp"),
            P("dp", None, "chan", None),
            P("dp", None, "chan", None),
            P(None, "dp", "chan"),
            P(None, "dp", "chan"),
            P("dp", "chan"),
            P("chan"),
            P("chan"),
            P("chan"),
            P("chan"),
            P("chan"),
            P("chan"),
        ),
        check_vma=False,
    )
```
